512 devices in a mesh: gx: 16 (over y, x_lo), yz: 16 (over z, core), lvl: 2 (over x_hi).
Axes of the slice: x: 4 (x_hi: 2, x_lo: 2; x = x_hi * 2 + x_lo), y: 8, z: 8, core: 2. Of those that a mesh axis runs over, the one named last changes fastest.
Arguments:
- input_residual: float32 [64, 16, 128, 256], P(None, 'gx', 'yz', 'lvl'), may hold values from -6 to 6
- coefficient: float32 [16, 128, 256], P('gx', 'yz', 'lvl'), may hold values from 0.1 to 1.35
- element_block: float32 [64, 64], replicated, may hold values from -0.03125 to 3, as said below
- face_blocks: float32 [4, 16, 16], replicated, may hold values from -0.5 to 12, as said below
- face_block_kind: int32 [6, 16, 128, 256], P(None, 'gx', 'yz', 'lvl'), may hold values from 0 to 3, as said below
- face_wall_flag: int32 [6, 16, 128, 256], P(None, 'gx', 'yz', 'lvl'), may hold values from 0 to 1, as said below
Outputs:
- correction: float32 [64, 16, 128, 256], P(None, 'gx', 'yz', 'lvl')
- residual: float32 [64, 16, 128, 256], P(None, 'gx', 'yz', 'lvl')
The draws below stay inside these ranges and needn't reach their ends.
Inputs may be any that keep to these rules, and one draw needn't show every extreme that they name: `element_block`: symmetric. `face_blocks`: each block symmetric. `face_block_kind`: the entry of an element for its + face along a direction equals the entry of its neighbour on that side for its - face. `face_wall_flag`: 1 marks a wall; the entry of an element for its + face along a direction equals the entry of its neighbour on that side for its - face.
All inputs are finite; a program needn't handle non-finite values.
Results may differ from the reference program's by a relative error of at most 0.00027.
Values sent between devices are 32-bit elements; how exact they have to be, the bound alone decides.
No kernel may reach another device: no remote copies, remote signals or barrier semaphores. Data moves between devices by JAX's collectives and lax.ppermute only.
A program may use at most 64 MiB of HBM per device.

```python
import math
import jax
import jax.numpy as jnp
from jax import lax

FACE_BLOCK_KINDS = 4
CHEB = 3
CITERS = 8
ELEMENTS_X = 16
ELEMENTS_Y = 128
ELEMENTS_Z = 256


def assemble(tables):
    along_x, along_y, along_z = tables
    pieces = [along_x[:-1], along_x[1:], along_y[:, :-1], along_y[:, 1:], along_z[:, :, :-1], along_z[:, :, 1:]]
    return jnp.stack(pieces).astype(jnp.int32)


def face_tables(key):
    array_shapes = ((ELEMENTS_X + 1, ELEMENTS_Y, ELEMENTS_Z), (ELEMENTS_X, ELEMENTS_Y + 1, ELEMENTS_Z), (ELEMENTS_X, ELEMENTS_Y, ELEMENTS_Z + 1))
    kind_tables = []
    wall_tables = []
    for d in range(3):
        kind_tables.append(jax.random.randint(jax.random.fold_in(key, 101 + d), array_shapes[d], 0, FACE_BLOCK_KINDS))
        wall_draws = jax.random.randint(jax.random.fold_in(key, 201 + d), array_shapes[d], 0, 8)
        wall_tables.append(jnp.where(wall_draws == 0, 1, 0).astype(jnp.int32))
    return (assemble(kind_tables), assemble(wall_tables))


def place_ramp(shape, axis):
    position = lax.broadcasted_iota(jnp.int32, shape, axis).astype(jnp.float32)
    return position / float(max(ELEMENTS_X - 1, 1))


def draw_input_residual(key, part):
    key = jax.random.fold_in(key, 11)
    first = jax.random.fold_in(key, 0)
    shape = (64, ELEMENTS_X, ELEMENTS_Y, ELEMENTS_Z)
    ramp = place_ramp(shape, 1)
    noise = jax.random.normal(first, shape, jnp.float32)
    amplitude = 1.0 + 3.0 * ramp
    level = 0.5
    values = amplitude * (level + noise)
    return jnp.clip(values, -6.0, 6.0)


def draw_coefficient(key, part):
    key = jax.random.fold_in(key, 13)
    shape = (ELEMENTS_X, ELEMENTS_Y, ELEMENTS_Z)
    ramp = place_ramp(shape, 0)
    base = jnp.exp(jax.random.uniform(key, shape, jnp.float32, math.log(0.1), math.log(0.33)))
    falling = 3.0 - 2.0 * ramp
    return jnp.clip(base * falling, 0.1, 1.32)


def draw_face_block_kind(key, part):
    kinds_out, walls_out = face_tables(key)
    return kinds_out


def draw_face_wall_flag(key, part):
    kinds_out, walls_out = face_tables(key)
    return walls_out


def draw_element_block(key, part):
    key = jax.random.fold_in(key, 5)
    first, second = jax.random.split(key, 2)
    raw_vals = jax.random.uniform(first, (64, 64), jnp.float32, -1.0 / 32.0, 1.0 / 32.0)
    offdiag = (raw_vals + raw_vals.T) * 0.5
    ident = jnp.eye(64, dtype=jnp.float32)
    diagonal = jax.random.uniform(second, (64,), jnp.float32, 2.0, 3.0)
    return offdiag * (1.0 - ident) + ident * diagonal[None, :]


def draw_face_blocks(key, part):
    key = jax.random.fold_in(key, 7)
    first, second, third = jax.random.split(key, 3)
    raw_vals = jax.random.uniform(first, (FACE_BLOCK_KINDS, 16, 16), jnp.float32, -1.0 / 16.0, 1.0 / 16.0)
    offdiag = (raw_vals + jnp.swapaxes(raw_vals, 1, 2)) * 0.5
    ident = jnp.eye(16, dtype=jnp.float32)[None, :, :]
    diagonal = jax.random.uniform(second, (FACE_BLOCK_KINDS, 16), jnp.float32, 1.0, 1.5)
    factor = jnp.exp(jax.random.uniform(third, (FACE_BLOCK_KINDS,), jnp.float32, 0.0, math.log(8.0)))
    blocks = offdiag * (1.0 - ident) + ident * diagonal[:, None, :]
    return blocks * factor[:, None, None]


def setup_inputs(seed: int = 0) -> dict:
    key_list = jax.random.split(jax.random.key(seed), 7)
    input_residual = draw_input_residual(jax.random.fold_in(key_list[6], 71), 0)
    coefficient = draw_coefficient(jax.random.fold_in(key_list[6], 71), 0)
    element_block = draw_element_block(jax.random.fold_in(key_list[6], 71), 0)
    face_blocks = draw_face_blocks(jax.random.fold_in(key_list[6], 71), 0)
    face_block_kind = draw_face_block_kind(jax.random.fold_in(key_list[6], 71), 0)
    face_wall_flag = draw_face_wall_flag(jax.random.fold_in(key_list[6], 71), 0)
    return dict(input_residual=input_residual, coefficient=coefficient, element_block=element_block, face_blocks=face_blocks, face_block_kind=face_block_kind, face_wall_flag=face_wall_flag)


HIGHEST = lax.Precision.HIGHEST
LOW_EIG = 0.3
HIGH_EIG = 3.0

def prolong_tables():
    node_points = jnp.array([-1.0, -1.0 / math.sqrt(5.0), 1.0 / math.sqrt(5.0), 1.0], dtype=jnp.float32)
    basis_table = jnp.stack([(1.0 - node_points) * 0.5, (1.0 + node_points) * 0.5], axis=1)
    volume = (basis_table[:, None, None, :, None, None] * basis_table[None, :, None, None, :, None] * basis_table[None, None, :, None, None, :]).reshape(64, 8)
    surface = (basis_table[:, None, :, None] * basis_table[None, :, None, :]).reshape(16, 4)
    return (volume, surface)

def level_tables(element_block, face_blocks, volume, surface):
    elem_mid = jnp.dot(volume.T, jnp.dot(element_block, volume, precision=HIGHEST), precision=HIGHEST)
    face_mid = jnp.einsum('kij,jb->kib', face_blocks, surface, precision=HIGHEST)
    face_mid = jnp.einsum('ia,kib->kab', surface, face_mid, precision=HIGHEST)
    elem_coarse = jnp.sum(elem_mid).reshape(1, 1)
    face_coarse = lax.optimization_barrier(jnp.sum(face_mid, axis=(1, 2))).reshape(-1, 1, 1)
    return (elem_mid, face_mid, elem_coarse, face_coarse)

def build_weights(face_block_kind, face_wall_flag, offsets, totals, kinds):
    shape = face_block_kind.shape[1:]
    places = [offsets[d] + lax.broadcasted_iota(jnp.int32, shape, d) for d in range(3)]
    has_next = [places[d] < totals[d] - 1 for d in range(3)]
    has_prev = [places[d] > 0 for d in range(3)]
    kind_ids = jnp.arange(kinds, dtype=jnp.int32).reshape(kinds, 1, 1, 1)

    def weigh_faces(row, allowed):
        chosen = (face_block_kind[row][None] == kind_ids) & (face_wall_flag[row][None] == 0) & allowed[None]
        return chosen.astype(jnp.float32)
    plus_side_weight = [weigh_faces(2 * d + 1, has_next[d]) for d in range(3)]
    minus_side_weight = [weigh_faces(2 * d, has_prev[d]) for d in range(3)]
    return (plus_side_weight, minus_side_weight)

def shift_ahead(values, axis):
    count = values.shape[axis]
    return jnp.concatenate([lax.slice_in_dim(values, 1, count, axis=axis), jnp.zeros_like(lax.slice_in_dim(values, 0, 1, axis=axis))], axis=axis)

def shift_behind(values, axis):
    count = values.shape[axis]
    return jnp.concatenate([jnp.zeros_like(lax.slice_in_dim(values, 0, 1, axis=axis)), lax.slice_in_dim(values, 0, count - 1, axis=axis)], axis=axis)

def trace_of(values, points, direction, at):
    shaped = values.reshape((points, points, points) + values.shape[1:])
    picked = lax.index_in_dim(shaped, at, axis=direction, keepdims=False)
    return picked.reshape((points * points,) + values.shape[1:])

def add_to_trace(values, points, direction, at, addend):
    shaped = values.reshape((points, points, points) + values.shape[1:])
    face_piece = addend.reshape((points, points) + values.shape[1:])
    index_list = [slice(None)] * direction + [at]
    shaped = shaped.at[tuple(index_list)].add(face_piece)
    return shaped.reshape(values.shape)

def select(blocks, weights, jump_vals):
    running = jnp.zeros_like(jump_vals)
    for k in range(blocks.shape[0]):
        running = running + weights[k][None] * jnp.einsum('ij,jxyz->ixyz', blocks[k], jump_vals, precision=HIGHEST)
    return running

def pick_diag(face_diag, weights):
    running = jnp.zeros((face_diag.shape[1],) + weights.shape[1:], jnp.float32)
    for k in range(face_diag.shape[0]):
        running = running + face_diag[k][:, None, None, None] * weights[k][None]
    return running

def diag_of(points, element, blocks, coefficient, plus_side_weight, minus_side_weight):
    result = coefficient[None] * jnp.diagonal(element)[:, None, None, None]
    face_diag = jnp.diagonal(blocks, axis1=1, axis2=2)
    for d in range(3):
        result = add_to_trace(result, points, d, points - 1, pick_diag(face_diag, plus_side_weight[d]))
        result = add_to_trace(result, points, d, 0, pick_diag(face_diag, minus_side_weight[d]))
    return result

def operate(values, points, element, blocks, coefficient, plus_side_weight):
    result = coefficient[None] * jnp.einsum('ij,jxyz->ixyz', element, values, precision=HIGHEST)
    for d in range(3):
        axis = 1 + d
        upper = trace_of(values, points, d, points - 1)
        bottom = trace_of(values, points, d, 0)
        face_flux = select(blocks, plus_side_weight[d], upper - shift_ahead(bottom, axis))
        result = add_to_trace(result, points, d, points - 1, face_flux)
        result = add_to_trace(result, points, d, 0, -shift_behind(face_flux, axis))
    return result

def smooth(operate_fn, inverse, start_vec, residual, keep_last):
    middle = 0.5 * (HIGH_EIG + LOW_EIG)
    spread = 0.5 * (HIGH_EIG - LOW_EIG)
    scaled = middle / spread
    rho_now = 1.0 / scaled
    update = inverse * residual / middle
    solution = start_vec
    for k in range(CHEB):
        solution = solution + update
        is_last = k == CHEB - 1
        if keep_last or not is_last:
            residual = residual - operate_fn(update)
        if not is_last:
            rho_next = 1.0 / (2.0 * scaled - rho_now)
            update = rho_next * rho_now * update + 2.0 * rho_next / spread * (inverse * residual)
            rho_now = rho_next
    return (solution, residual)

def conjugate(operate_fn, rhs):
    solution = jnp.zeros_like(rhs)
    residual = rhs
    search = rhs
    norm_now = jnp.sum(residual * residual)
    for k in range(CITERS):
        image_vec = operate_fn(search)
        step_len = norm_now / jnp.sum(search * image_vec)
        solution = solution + step_len * search
        residual = residual - step_len * image_vec
        norm_next = jnp.sum(residual * residual)
        search = residual + norm_next / norm_now * search
        norm_now = norm_next
    return solution

def reference(input_residual, coefficient, element_block, face_blocks, face_block_kind, face_wall_flag):
    volume, surface = prolong_tables()
    elem_mid, face_mid, elem_coarse, face_coarse = level_tables(element_block, face_blocks, volume, surface)
    plus_side_weight, minus_side_weight = build_weights(face_block_kind, face_wall_flag, (0, 0, 0), (ELEMENTS_X, ELEMENTS_Y, ELEMENTS_Z), FACE_BLOCK_KINDS)

    def fine_apply(values):
        return operate(values, 4, element_block, face_blocks, coefficient, plus_side_weight)

    def mid_apply(values):
        return operate(values, 2, elem_mid, face_mid, coefficient, plus_side_weight)

    def coarse_apply(values):
        return operate(values, 1, elem_coarse, face_coarse, coefficient, plus_side_weight)
    fine_inverse = 1.0 / diag_of(4, element_block, face_blocks, coefficient, plus_side_weight, minus_side_weight)
    mid_inverse = 1.0 / diag_of(2, elem_mid, face_mid, coefficient, plus_side_weight, minus_side_weight)
    fine_pre, fine_res = smooth(fine_apply, fine_inverse, jnp.zeros_like(input_residual), input_residual, True)
    mid_rhs = jnp.einsum('ij,jxyz->ixyz', volume.T, fine_res, precision=HIGHEST)
    mid_pre, mid_res = smooth(mid_apply, mid_inverse, jnp.zeros_like(mid_rhs), mid_rhs, True)
    coarse_rhs = lax.optimization_barrier(jnp.sum(mid_res, axis=0, keepdims=True))
    coarse_sol = conjugate(coarse_apply, coarse_rhs)
    spread_sol = jnp.broadcast_to(coarse_sol, mid_pre.shape)
    mid_sol, unused = smooth(mid_apply, mid_inverse, mid_pre + spread_sol, mid_res - mid_apply(spread_sol), False)
    lifted = jnp.einsum('ij,jxyz->ixyz', volume, mid_sol, precision=HIGHEST)
    correction, residual = smooth(fine_apply, fine_inverse, fine_pre + lifted, fine_res - fine_apply(lifted), True)
    return (correction, residual)
```

```python
import functools
import math

import jax
import jax.numpy as jnp
import numpy as np
from jax import lax
from jax.experimental import pallas as pl
from jax.experimental.pallas import tpu as pltpu
from jax.sharding import PartitionSpec as P

NX = 16
NY = 128
NZ = 256
KINDS = 4
F32 = jnp.float32
BF16 = jnp.bfloat16
HIGHEST = lax.Precision.HIGHEST
LOW_EIG = 0.3
HIGH_EIG = 3.0
MIDDLE = 0.5 * (HIGH_EIG + LOW_EIG)
SPREAD = 0.5 * (HIGH_EIG - LOW_EIG)
SCALED = MIDDLE / SPREAD
RHO0 = 1.0 / SCALED
RHO1 = 1.0 / (2.0 * SCALED - RHO0)
RHO2 = 1.0 / (2.0 * SCALED - RHO1)
STEPS = ((RHO1 * RHO0, 2.0 * RHO1 / SPREAD), (RHO2 * RHO1, 2.0 * RHO2 / SPREAD))
BASIS = 8
VMEM_LIMIT = 48 * 2**20


def lanes(shape):
    return lax.broadcasted_iota(jnp.int32, shape, len(shape) - 1)


def roll(x, shift, axis=None):
    axis = x.ndim - 1 if axis is None else axis
    shift = shift % x.shape[axis]
    return x if shift == 0 else pltpu.roll(x, shift, axis)


def call(body, name, out_shape, in_specs, scratch=(), flops=1000000):
    single = not isinstance(out_shape, (tuple, list))
    outs = [out_shape] if single else list(out_shape)
    vm = pl.BlockSpec(memory_space=pltpu.VMEM)
    return pl.pallas_call(
        body,
        out_shape=outs[0] if single else outs,
        in_specs=[pl.BlockSpec(memory_space=pltpu.SMEM) if s else vm for s in in_specs],
        out_specs=vm if single else [vm] * len(outs),
        scratch_shapes=list(scratch),
        compiler_params=pltpu.CompilerParams(vmem_limit_bytes=VMEM_LIMIT),
        cost_estimate=pl.CostEstimate(flops=flops, bytes_accessed=1000000, transcendentals=0),
        name=name,
    )


def f32s(*shape):
    return jax.ShapeDtypeStruct(shape, F32)


def split3(x):
    high = x.astype(BF16).astype(F32)
    low = x - high
    return high, low


def stack_hlh(x):
    high, low = split3(x)
    return jnp.concatenate([high, low, high], axis=0).astype(BF16)


def mm(a, b):
    return jnp.dot(a, b, preferred_element_type=F32)


def edges_body(pos, res, cf, out):
    first = pos[2] == 0
    lane = lanes((16, 128))
    acc = [jnp.zeros((16, 128), F32)]
    packed = jnp.zeros((16, 128), F32)
    packed_cf = jnp.zeros((8, 128), F32)
    lane8 = lanes((8, 128))
    for y in range(8):
        rows = res[pl.ds(y, 64, stride=8), :]
        rows = jnp.where(first, roll(rows, 4), rows)
        for j in range(4):
            at = 32 * j + 4 * y
            packed = jnp.where(
                (lane >= at) & (lane < at + 4), roll(rows[16 * j : 16 * j + 16], at), packed
            )
        rows = cf[pl.ds(y, 8, stride=8), :]
        rows = jnp.where(first, roll(rows, 12), rows)
        at = 12 * y
        packed_cf = jnp.where((lane8 >= at) & (lane8 < at + 12), roll(rows, at), packed_cf)
    out[0:16, :] = packed
    out[16:24, :] = packed_cf


def slots_body(pos, res, cf, halo, out, rows, rows_cf):
    first = pos[2] == 0
    lane = lanes((64, 128))
    lane8 = lanes((8, 128))
    for y in range(8):
        mine = res[pl.ds(y, 64, stride=8), :]
        got = jnp.concatenate([roll(halo[0:16, :], -(32 * j + 4 * y)) for j in range(4)], axis=0)
        rows[0, y] = jnp.where(lane >= 124, jnp.where(first, 0.0, roll(got, 124)), mine)
        rows[1, y] = mine
        rows[2, y] = jnp.where(lane < 4, jnp.where(first, got, 0.0), mine)
        mine = cf[pl.ds(y, 8, stride=8), :]
        got = roll(halo[16:24, :], -12 * y)
        rows_cf[0, y] = jnp.where(lane8 >= 116, jnp.where(first, 0.0, roll(got, 116)), mine)
        rows_cf[1, y] = mine
        rows_cf[2, y] = jnp.where(lane8 < 12, jnp.where(first, got, 0.0), mine)
    for g in range(NX):
        source = 0 if g == 0 else (2 if g == NX - 1 else 1)
        acc = jnp.zeros((64, 128), F32)
        for y in range(8):
            acc = jnp.where(lane // 16 == y, roll(rows[source, y], 16 * y - (8 * g - 4)), acc)
        out[g, 0:64, :] = acc
        source = 0 if g <= 1 else (2 if g >= NX - 2 else 1)
        for h in range(2):
            acc = jnp.zeros((8, 128), F32)
            for y in range(4):
                acc = jnp.where(
                    lane8 // 32 == y, roll(rows_cf[source, 4 * h + y], 32 * y - (8 * g - 12)), acc
                )
            out[g, 64 + 8 * h : 72 + 8 * h, :] = acc


def fine_update(x, u, r, sol, inv, step):
    if step is None:
        return
    keep, gain = STEPS[step]
    new = keep * u[x] + gain * (inv[x] * r[x])
    u[x] = new
    sol[x] = sol[x] + new


def fine_apply(u, r, w, coef, wide, spread, px, qx, step, sol, inv):
    def first(x, carry):
        prod = mm(wide[...], stack_hlh(u[x]))

        def pick(base, row):
            total = w[x, pl.ds(row, 1), :] * prod[base : base + 16]
            for k in range(1, KINDS):
                total = total + w[x, pl.ds(row + k, 1), :] * prod[base + 16 * k : base + 16 * k + 16]
            return total

        px[x + 1] = pick(64, 0)
        py = pick(128, 4)
        pz = pick(192, 8)
        qx[x] = pick(256, 12)
        qy = pick(320, 16)
        qz = pick(384, 20)
        flux = jnp.concatenate(
            [py - roll(qy, -16), roll(py, 16) - qy, pz - roll(qz, -1), roll(pz, 1) - qz], axis=0
        )
        high, low = split3(flux)
        faces = mm(spread[...], jnp.concatenate([high, low], axis=0).astype(BF16))
        r[x] = r[x] - (coef[x, pl.ds(0, 1), :] * prod[0:64] + faces)
        return carry

    lax.fori_loop(0, NX, first, 0)

    def second(x, carry):
        r[x, 48:64, :] = r[x, 48:64, :] - (px[x + 1] - qx[x + 1])
        r[x, 0:16, :] = r[x, 0:16, :] + (px[x] - qx[x])
        fine_update(x, u, r, sol, inv, step)
        return carry

    lax.fori_loop(0, NX, second, 0)


def fine_pre_body(
    pos,
    own,
    below,
    above,
    wide,
    spread,
    diag_w,
    diag_e,
    down,
    mid_diag_w,
    mid_diag_e,
    sol,
    r,
    w,
    coef,
    inv,
    cfm,
    send_up,
    send_down,
    u,
    px,
    qx,
    gather,
):
    low = lanes((64, 128)) < 64
    low8 = lanes((8, 128)) < 64
    lane8 = lanes((8, 128))
    place = lanes((1, 256))
    y_at = pos[0] * 8 - 4 + place // 16
    z_at = pos[1] * 8 - 4 + place % 16
    inside = (y_at >= 0) & (y_at < NY) & (z_at >= 0) & (z_at < NZ)
    has_y = inside & (y_at < NY - 1)
    has_z = inside & (z_at < NZ - 1)
    inside_f = jnp.where(inside, 1.0, 0.0)
    px[0] = jnp.zeros((16, 256), F32)
    qx[NX] = jnp.zeros((16, 256), F32)
    cfm[:, 0:128] = jnp.zeros((128, 128), F32)
    cfm[:, 896:1024] = jnp.zeros((128, 128), F32)
    for x in range(NX):
        turned = roll(own[x, 0:64, :], 64)
        r[x, :, 0:128] = jnp.where(low, roll(below[x, 0:64, :], 64), turned)
        r[x, :, 128:256] = jnp.where(low, turned, roll(above[x, 0:64, :], 64))
        blocks = [
            below[x, 64:72, :],
            below[x, 72:80, :],
            own[x, 64:72, :],
            own[x, 72:80, :],
            above[x, 64:72, :],
            above[x, 72:80, :],
        ]
        for m in range(6):
            gather[pl.ds(128 * m + x, 8, stride=16), :] = blocks[m]
        for half in range(2):
            acc = jnp.zeros((8, 128), F32)
            for row in range(8):
                n = 8 * half + row
                acc = jnp.where(
                    lane8 // 16 == row,
                    roll(blocks[1 + n // 4], 16 * row - (n % 4) * 32 - 8),
                    acc,
                )
            coef[x, :, 128 * half : 128 * half + 128] = acc
    for m in range(6):
        cfm[:, 128 * (m + 1) : 128 * (m + 2)] = gather[128 * m : 128 * m + 128, :]
    for x in range(NX):
        rows = coef[x]
        opens = [
            inside & (rows[4:5] == 0.0) if x < NX - 1 else jnp.zeros((1, 256), jnp.bool_),
            has_y & (rows[5:6] == 0.0),
            has_z & (rows[6:7] == 0.0),
        ]
        plus = [
            [jnp.where(opens[d] & (rows[1 + d : 2 + d] == float(k)), 1.0, 0.0) for k in range(KINDS)]
            for d in range(3)
        ]
        plus_all = jnp.concatenate(plus[0] + plus[1] + plus[2] , axis=0)
        w[x, 0:12, :] = plus_all
        if x == 0:
            w[0, 12:16, :] = jnp.zeros((4, 256), F32)
        if x < NX - 1:
            w[x + 1, 12:16, :] = plus_all[0:4]
        w[x, 16:20, :] = roll(plus_all[4:8], 16)
        w[x, 20:24, :] = roll(plus_all[8:12], 1)

    def prepare(x, carry):
        ws = w[x]
        ws = jnp.concatenate([ws, ws, ws, jnp.zeros((8, 256), F32)], axis=0).astype(BF16)
        diag = diag_e[...] * coef[x, pl.ds(0, 1), :] + mm(diag_w[...], ws)
        inverse = jnp.where(inside, 1.0 / diag, 0.0)
        inv[x] = inverse
        update = inverse * r[x] / MIDDLE
        u[x] = update
        sol[x] = update
        return carry

    lax.fori_loop(0, NX, prepare, 0)
    fine_apply(u, r, w, coef, wide, spread, px, qx, 0, sol, inv)
    fine_apply(u, r, w, coef, wide, spread, px, qx, 1, sol, inv)
    fine_apply(u, r, w, coef, wide, spread, px, qx, None, sol, inv)
    lane16 = lanes((16, 128)) % 16 // 4
    for x in range(NX):
        rx = r[x]
        ws = w[x]
        ws = jnp.concatenate([ws, ws, ws, jnp.zeros((8, 256), F32)], axis=0).astype(BF16)
        rhs = mm(down[...], stack_hlh(rx))
        diag = mid_diag_e[...] * coef[x, 0:1, :] + mm(mid_diag_w[...], ws)
        update = jnp.where(inside, 1.0 / diag, 0.0) * rhs / MIDDLE
        for half in range(2):
            piece = update[:, 128 * half : 128 * half + 128]
            send_up[pl.ds(128 * half + x, 8, stride=16), :] = piece
            send_down[pl.ds(128 * half + x, 8, stride=16), :] = piece
        mine = jnp.where(low, roll(rx[:, 0:128], 64), roll(rx[:, 128:256], 64))
        up = jnp.zeros((16, 128), F32)
        dn = jnp.zeros((16, 128), F32)
        for j in range(4):
            part = mine[16 * j : 16 * j + 16]
            up = jnp.where(lane16 == j, roll(part, 4 * j - 8), up)
            dn = jnp.where(lane16 == j, roll(part, 4 * j - 4), dn)
        send_up[256 + 16 * x : 272 + 16 * x, :] = up
        send_down[256 + 16 * x : 272 + 16 * x, :] = dn


def mid_z_body(own, dn, up, r, cfm, slab, fwd, bwd, frz):
    lane = lanes((128, 128))
    for m in range(4):
        acc = jnp.zeros((128, 128), F32)
        for n in range(4):
            y = 4 * (m - 1) + n
            if y < -1 or y > 8:
                continue
            to = 32 * n
            half, at = (y + 4) // 8, 16 * ((y + 4) % 8)
            rows = slice(128 * half, 128 * half + 128)
            acc = jnp.where((lane >= to + 12) & (lane < to + 20), roll(own[rows, :], to + 8 - at), acc)
            acc = jnp.where((lane >= to + 3) & (lane < to + 12), roll(dn[rows, :], to - at), acc)
            acc = jnp.where((lane >= to + 20) & (lane < to + 29), roll(up[rows, :], to + 16 - at), acc)
        if 1 <= m <= 2:
            slab[:, 128 * (m - 1) : 128 * m] = acc
        if m <= 2:
            fwd[128 * m : 128 * m + 128, :] = acc
        if m >= 1:
            bwd[128 * (m - 1) : 128 * m, :] = acc
    fwd[896:912, :] = cfm[32:48, 256:384]
    fwd[912:928, :] = cfm[80:96, 256:384]
    low = lanes((64, 128)) < 64
    l16 = lanes((16, 128)) % 16
    for x in range(NX):
        rx = r[x]
        mine = jnp.where(low, roll(rx[:, 0:128], 64), roll(rx[:, 128:256], 64))
        pack_dn = dn[256 + 16 * x : 272 + 16 * x, :]
        pack_up = up[256 + 16 * x : 272 + 16 * x, :]
        for j in range(4):
            rows = slice(16 * j, 16 * j + 16)
            part = jnp.where(l16 < 4, roll(pack_dn, -4 * j), mine[rows])
            part = jnp.where(l16 >= 12, roll(pack_up, 12 - 4 * j), part)
            frz[x, rows, :] = part
    for x in range(8):
        fwd[384 + 64 * x : 448 + 64 * x, :] = jnp.where(low, roll(frz[x], 64), frz[x + 8])
        bwd[384 + 64 * x : 448 + 64 * x, :] = jnp.where(low, frz[x], roll(frz[x + 8], 64))


MID_PAIRS = ((0, 0), (0, 1), (0, 2), (0, 3), (1, 1), (1, 2), (1, 3), (2, 2), (2, 3), (3, 3))
MID_SLOT = {}
for _n, (_i, _j) in enumerate(MID_PAIRS):
    MID_SLOT[(_i, _j)] = _n
    MID_SLOT[(_j, _i)] = _n
LOWS = ((0, 1, 2, 3), (0, 1, 4, 5), (0, 2, 4, 6))
HIGHS = ((4, 5, 6, 7), (2, 3, 6, 7), (1, 3, 5, 7))


def ahead(v, d):
    if d == 0:
        return roll(v, -1, 0)
    return roll(v, -32 if d == 1 else -1, 1)


def behind(v, d):
    if d == 0:
        return roll(v, 1, 0)
    return roll(v, 32 if d == 1 else 1, 1)


def mid_setup(pos, scal, cfm, sel, faces, inv, diag):
    place = lanes((16, 1024))
    x_at = lax.broadcasted_iota(jnp.int32, (16, 1024), 0)
    y_at = pos[0] * 8 - 12 + place // 32
    z_at = pos[1] * 8 - 12 + place % 32
    domain = (y_at >= 0) & (y_at < NY) & (z_at >= 0) & (z_at < NZ)
    known = domain & (place >= 128) & (place < 896)
    lasts = (x_at < NX - 1, y_at < NY - 1, z_at < NZ - 1)
    for d in range(3):
        is_open = domain & lasts[d] & (cfm[64 + 16 * d : 80 + 16 * d, :] == 0.0)
        sel[d] = jnp.where(is_open, cfm[16 + 16 * d : 32 + 16 * d, :], 4.0)
    coef = cfm[0:16, :]

    def table(n, carry):
        at = 64 + n
        for d in range(3):
            kind = sel[d]
            value = jnp.zeros((16, 1024), F32)
            for k in range(KINDS):
                value = jnp.where(kind == float(k), scal[at + 16 * k], value)
            faces[d, n] = value
        return carry

    lax.fori_loop(0, 16, table, 0)
    if inv is None:
        return known
    for i in range(8):
        total = coef * scal[9 * i]
        for d in range(3):
            if i in HIGHS[d]:
                total = total + faces[d, 5 * HIGHS[d].index(i)]
            else:
                total = total + behind(faces[d, 5 * LOWS[d].index(i)], d)
        if diag is not None:
            diag[i] = total
        inv[i] = jnp.where(known, 1.0 / total, 0.0)
    return known


def mid_apply(v, r, scal, cfm, faces, jump, flux):
    for d in range(3):
        for j in range(4):
            jump[j] = v[HIGHS[d][j]] - ahead(v[LOWS[d][j]], d)

        def face(c, carry):
            at = pl.ds(pl.multiple_of(c * 128, 128), 128)
            jumps = [jump[j, :, at] for j in range(4)]
            for i in range(4):
                total = faces[d, 4 * i, :, at] * jumps[0]
                for j in range(1, 4):
                    total = total + faces[d, 4 * i + j, :, at] * jumps[j]
                flux[4 * d + i, :, at] = total
            return carry

        lax.fori_loop(0, 8, face, 0)

    def block(c, carry):
        at = pl.ds(pl.multiple_of(c * 128, 128), 128)
        values = [v[j, :, at] for j in range(8)]
        coef = cfm[0:16, at]
        for i in range(8):
            total = scal[8 * i] * values[0]
            for j in range(1, 8):
                total = total + scal[8 * i + j] * values[j]
            r[i, :, at] = r[i, :, at] - coef * total
        return carry

    lax.fori_loop(0, 8, block, 0)
    for d in range(3):
        for j in range(4):
            value = flux[4 * d + j]
            r[HIGHS[d][j]] = r[HIGHS[d][j]] - value
            r[LOWS[d][j]] = r[LOWS[d][j]] + behind(value, d)


def mid_step(step, u, r, sol, inv):
    keep, gain = STEPS[step]
    for i in range(8):
        new = keep * u[i] + gain * (inv[i] * r[i])
        u[i] = new
        sol[i] = sol[i] + new


def mid_pre_body(
    pos, scal, slab, below, above, cfm_in, sol, r, coarse, send_up, send_down,
    cfm, sel, faces, inv, diag, u, jump, flux,
):
    cfm[...] = cfm_in[...]
    cfm[32:48, 0:128] = below[896:912, :]
    cfm[80:96, 0:128] = below[912:928, :]
    for i in range(8):
        rows = slice(16 * i, 16 * i + 16)
        for m in range(3):
            u[i, :, 128 * m : 128 * m + 128] = below[128 * m + 16 * i : 128 * m + 16 * i + 16, :]
            u[i, :, 128 * (m + 5) : 128 * (m + 6)] = above[128 * m + 16 * i : 128 * m + 16 * i + 16, :]
        u[i, :, 384:640] = slab[rows, :]
    mid_setup(pos, scal, cfm, sel, faces, inv, diag)
    for i in range(8):
        r[i] = (MIDDLE * diag[i]) * u[i]
        sol[i] = u[i]
    mid_apply(u, r, scal, cfm, faces, jump, flux)
    mid_step(0, u, r, sol, inv)
    mid_apply(u, r, scal, cfm, faces, jump, flux)
    mid_step(1, u, r, sol, inv)
    mid_apply(u, r, scal, cfm, faces, jump, flux)
    total = r[0]
    for i in range(1, 8):
        total = total + r[i]
    coarse[0] = total
    center = cfm[0:16, :] * scal[128]
    for d in range(3):
        kind = sel[d]
        value = jnp.zeros((16, 1024), F32)
        for k in range(KINDS):
            value = jnp.where(kind == float(k), scal[129 + k], value)
        coarse[2 + d] = value
        center = center + value + behind(value, d)
    coarse[1] = center
    l32 = lanes((16, 768)) % 32
    for out, first in ((send_up, 6), (send_down, 18)):
        acc = jnp.zeros((16, 768), F32)
        for f in range(4):
            acc = jnp.where(l32 // 8 == f, roll(coarse[f, :, 128:896], 8 * f - first), acc)
        out[0] = acc
        out[1] = roll(coarse[4, :, 128:896], -first)


def coarse_z_body(own, dn, up, slab, fwd, bwd):
    lane = lanes((16, 128))
    for f in range(5):
        part = 0 if f < 4 else 1
        shift = 8 * f if f < 4 else 0
        for m in range(10):
            acc = jnp.zeros((16, 128), F32)
            for n in range(2):
                y = 2 * m + n - 6
                tile, at = (y + 12) // 4, 32 * ((y + 12) % 4)
                to = 64 * n
                mine = own[f, :, 128 * tile : 128 * tile + 128]
                left = dn[part, :, 128 * (tile - 1) : 128 * tile]
                right = up[part, :, 128 * (tile - 1) : 128 * tile]
                acc = jnp.where(
                    (lane >= to + 22) & (lane < to + 42), roll(mine, to + 22 - (at + 6)), acc
                )
                acc = jnp.where(
                    (lane >= to + 14) & (lane < to + 22), roll(left, to + 14 - (at + shift)), acc
                )
                acc = jnp.where(
                    (lane >= to + 42) & (lane < to + 50), roll(right, to + 42 - (at + shift)), acc
                )
            slab[f, :, 128 * m : 128 * m + 128] = acc
            if m < 4:
                fwd[f, :, 128 * m : 128 * m + 128] = acc
            if m >= 6:
                bwd[f, :, 128 * (m - 6) : 128 * (m - 5)] = acc


def two_sum(a, b):
    s = a + b
    t = s - a
    return s, (a - (s - t)) + (b - t)


def halves(a):
    t = a * 4097.0
    high = t - (t - a)
    return high, a - high


def two_prod(a, b):
    ah, al = halves(a)
    bh, bl = halves(b)
    p = a * b
    return p, ((ah * bh - p) + ah * bl + al * bh) + al * bl


def pair_mul(a, b):
    p, e = two_prod(a[0], b[0])
    return two_sum(p, e + (a[0] * b[1] + a[1] * b[0]))


def pair_sub(a, b):
    s, e = two_sum(a[0], -b[0])
    return two_sum(s, e + (a[1] - b[1]))


def pair_div(a, b):
    first = a[0] / b[0]
    rest = pair_sub(a, pair_mul((first, jnp.zeros_like(first)), b))
    return two_sum(first, rest[0] / b[0])


START = (0, 9, 17, 24, 30, 35, 39, 42)
PAIRS = sum(9 - i for i in range(BASIS))


def krylov_body(scal, own, below, above, basis, gram, field, hold):
    for f in range(5):
        field[f, :, 0:512] = below[f]
        field[f, :, 512:1792] = own[f]
        field[f, :, 1792:2304] = above[f]
    center, half = scal[133], scal[134]
    lane8 = lanes((8, 128))

    def apply(v):
        total = field[1] * v
        for d in range(3):
            cond = field[2 + d]
            axis, step = ((0, 1), (1, 64), (1, 1))[d]
            total = total - cond * roll(v, -step, axis) - roll(cond * v, step, axis)
        return total

    def compact(v):
        acc = jnp.zeros((8, 128), F32)
        for t in range(2):
            for y in range(8):
                tile, at = (y + 14) // 2, 64 * ((y + 14) % 2) + 28
                to = 64 * t + 8 * y
                piece = v[8 * t : 8 * t + 8, 128 * tile : 128 * tile + 128]
                acc = jnp.where((lane8 >= to) & (lane8 < to + 8), roll(piece, to - at), acc)
        return acc

    before = None
    now = field[0]
    for j in range(BASIS):
        basis[j] = now[:, 384:1920]
        hold[j] = compact(now)
        image = apply(now)
        hold[BASIS + j] = compact(image)
        if j + 1 < BASIS:
            nxt = (image - center * now) * half
            if j > 0:
                nxt = 2.0 * nxt - before
            before, now = now, nxt
    high_rows, low_rows = [], []
    for i in range(BASIS):
        for j in range(i, BASIS + 1):
            other = hold[BASIS + j] if j < BASIS else hold[0]
            p, e = two_prod(hold[i], other)
            high_rows.append(p)
            low_rows.append(e)
    high = jnp.stack(high_rows)
    low = jnp.stack(low_rows)
    for axis, shifts in ((1, (4, 2, 1)), (2, (64, 32, 16, 8, 4, 2, 1))):
        for s in shifts:
            high, e = two_sum(high, roll(high, s, axis))
            low = low + roll(low, s, axis) + e
    row = jnp.zeros((8, 128), F32)
    for n in range(PAIRS):
        row = jnp.where(lane8 == n, high[n], row)
        row = jnp.where(lane8 == 64 + n, low[n], row)
    for m in range(64):
        gram[8 * m : 8 * m + 8, :] = row


def mid_post_body(
    pos, scal, gram, basis, cfm, pre, res, out,
    sel, faces, inv, u, r, sol, jump, flux,
):
    high = gram[...].reshape(64, 8, 128)
    low = jnp.zeros((64, 8, 128), F32)
    count = 64
    while count > 1:
        count //= 2
        high, e = two_sum(high[:count], high[count : 2 * count])
        low = low[:count] + low[count : 2 * count] + e
    high, low = high[0], low[0]
    for s in (4, 2, 1):
        high, e = two_sum(high, roll(high, s, 0))
        low = low + roll(low, s, 0) + e
    low = low + roll(high, 64)
    high, low = two_sum(high, low)
    lane = lanes((8, 128))
    sub = lax.broadcasted_iota(jnp.int32, (8, 128), 0)
    mat_h = jnp.zeros((8, 128), F32)
    mat_l = jnp.zeros((8, 128), F32)
    for i in range(BASIS):
        here = (sub == i) & (lane >= i) & (lane <= BASIS)
        mat_h = jnp.where(here, roll(high, i - START[i]), mat_h)
        mat_l = jnp.where(here, roll(low, i - START[i]), mat_l)
        for j in range(i + 1, BASIS):
            here = (sub == j) & (lane == i)
            shift = i - (START[i] + j - i)
            mat_h = jnp.where(here, roll(high, shift), mat_h)
            mat_l = jnp.where(here, roll(low, shift), mat_l)

    def spread_at(v, row, col):
        return jnp.broadcast_to(v[row : row + 1, col : col + 1], (8, 128))

    answers = []
    pivots = []
    for k in range(BASIS):
        start = spread_at(high, 0, START[k])
        piv = (spread_at(mat_h, k, k), spread_at(mat_l, k, k))
        good = jnp.abs(piv[0]) > 1e-12 * jnp.abs(start)
        safe = (jnp.where(good, piv[0], 1.0), jnp.where(good, piv[1], 0.0))
        pivots.append((safe, good))
        row = (
            jnp.broadcast_to(mat_h[k : k + 1, :], (8, 128)),
            jnp.broadcast_to(mat_l[k : k + 1, :], (8, 128)),
        )
        col = (
            jnp.broadcast_to(mat_h[:, k : k + 1], (8, 128)),
            jnp.broadcast_to(mat_l[:, k : k + 1], (8, 128)),
        )
        factor = pair_div(col, safe)
        use = good & (sub != k)
        factor = (jnp.where(use, factor[0], 0.0), jnp.where(use, factor[1], 0.0))
        mat_h, mat_l = pair_sub((mat_h, mat_l), pair_mul(factor, row))
    for k in range(BASIS):
        safe, good = pivots[k]
        value = pair_div((spread_at(mat_h, k, BASIS), spread_at(mat_l, k, BASIS)), safe)[0]
        answers.append(jnp.where(good, value, 0.0))
    weights = [jnp.concatenate([a, a], axis=0) for a in answers]
    lane16 = lanes((16, 128))
    tiles = []
    for m in range(12):
        total = weights[0] * basis[0, :, 128 * m : 128 * m + 128]
        for j in range(1, BASIS):
            total = total + weights[j] * basis[j, :, 128 * m : 128 * m + 128]
        tiles.append(total)
    for m in range(8):
        acc = jnp.zeros((16, 128), F32)
        if 1 <= m <= 6:
            for n in range(4):
                y = 4 * m + n - 12
                tile, at = (y + 14) // 2 - 3, 64 * ((y + 14) % 2)
                to = 32 * n
                acc = jnp.where(
                    (lane16 >= to + 5) & (lane16 < to + 27), roll(tiles[tile], to + 5 - (at + 21)), acc
                )
        for i in range(8):
            u[i, :, 128 * m : 128 * m + 128] = acc
    mid_setup(pos, scal, cfm, sel, faces, inv, None)
    for i in range(8):
        r[i] = res[i]
        sol[i] = pre[i] + u[i]
    mid_apply(u, r, scal, cfm, faces, jump, flux)
    for i in range(8):
        new = inv[i] * r[i] / MIDDLE
        u[i] = new
        sol[i] = sol[i] + new
    mid_apply(u, r, scal, cfm, faces, jump, flux)
    mid_step(0, u, r, sol, inv)
    mid_apply(u, r, scal, cfm, faces, jump, flux)
    mid_step(1, u, r, sol, inv)
    for i in range(8):
        for half in range(2):
            acc = jnp.zeros((16, 128), F32)
            for n in range(8):
                y = 8 * half + n - 4
                tile, at = (y + 12) // 4, 32 * ((y + 12) % 4) + 8
                acc = jnp.where(
                    lane16 // 16 == n,
                    roll(sol[i, :, 128 * tile : 128 * tile + 128], 16 * n - at),
                    acc,
                )
            out[128 * half + 16 * i : 128 * half + 16 * i + 16, :] = acc


def fine_post_body(
    mid, pre, frz, below, above, w, coef, inv, wide, spread, lift, out, u, r, sol, px, qx,
):
    low = lanes((64, 128)) < 64
    px[0] = jnp.zeros((16, 256), F32)
    qx[NX] = jnp.zeros((16, 256), F32)
    for x in range(NX):
        turned = roll(frz[x], 64)
        at = 384 + 64 * (x % 8)
        down = below[at : at + 64, :]
        over = above[at : at + 64, :]
        if x >= 8:
            down = roll(down, 64)
        else:
            over = roll(over, 64)
        r[x, :, 0:128] = jnp.where(low, down, turned)
        r[x, :, 128:256] = jnp.where(low, turned, over)
        halved = [mid[pl.ds(128 * half + x, 8, stride=16), :] for half in range(2)]
        high, rest = split3(jnp.concatenate(halved, axis=1))
        stacked = jnp.concatenate([high, rest, high, jnp.zeros((8, 256), F32)], axis=0)
        lifted = mm(lift[...], stacked.astype(BF16))
        u[x] = lifted
        sol[x] = pre[x] + lifted
    fine_apply(u, r, w, coef, wide, spread, px, qx, None, sol, inv)

    def begin(x, carry):
        new = inv[x] * r[x] / MIDDLE
        u[x] = new
        sol[x] = sol[x] + new
        return carry

    lax.fori_loop(0, NX, begin, 0)
    fine_apply(u, r, w, coef, wide, spread, px, qx, 0, sol, inv)
    fine_apply(u, r, w, coef, wide, spread, px, qx, 1, sol, inv)
    fine_apply(u, r, w, coef, wide, spread, px, qx, None, sol, inv)
    lane = lanes((64, 128))
    for x in range(NX):
        acc = jnp.zeros((64, 128), F32)
        for part, ref in enumerate((sol, r)):
            for y in range(8):
                half, at = (y + 4) // 8, 16 * ((y + 4) % 8) + 4
                acc = jnp.where(
                    lane // 8 == 8 * part + y,
                    roll(ref[x, :, 128 * half : 128 * half + 128], 64 * part + 8 * y - at),
                    acc,
                )
        out[x] = acc


def unpack_body(got, first, second):
    lane = lanes((64, 128)) // 8
    for part, out in enumerate((first, second)):
        for y in range(8):
            acc = jnp.zeros((64, 128), F32)
            for g in range(NX):
                acc = jnp.where(lane == g, roll(got[g], 8 * g - 8 * y - 64 * part), acc)
            out[pl.ds(y, 64, stride=8), :] = acc


def trace_tables():
    high = np.zeros((3, 16, 64), np.float32)
    low = np.zeros((3, 16, 64), np.float32)
    for p in range(4):
        for q in range(4):
            for d in range(3):
                for table, at in ((high, 3), (low, 0)):
                    index = [p, q]
                    index.insert(d, at)
                    table[d, 4 * p + q, 16 * index[0] + 4 * index[1] + index[2]] = 1.0
    return high, low


def mid_traces():
    high = np.zeros((3, 4, 8), np.float32)
    low = np.zeros((3, 4, 8), np.float32)
    for d in range(3):
        for n in range(4):
            high[d, n, HIGHS[d][n]] = 1.0
            low[d, n, LOWS[d][n]] = 1.0
    return high, low


def prolong_tables():
    node_points = jnp.array(
        [-1.0, -1.0 / math.sqrt(5.0), 1.0 / math.sqrt(5.0), 1.0], dtype=jnp.float32
    )
    basis_table = jnp.stack([(1.0 - node_points) * 0.5, (1.0 + node_points) * 0.5], axis=1)
    volume = (
        basis_table[:, None, None, :, None, None]
        * basis_table[None, :, None, None, :, None]
        * basis_table[None, None, :, None, None, :]
    ).reshape(64, 8)
    surface = (basis_table[:, None, :, None] * basis_table[None, :, None, :]).reshape(16, 4)
    return (volume, surface)


def cut(x):
    return lax.reduce_precision(x, 8, 7)


def two_parts(x):
    high = cut(x)
    return high, cut(x - high)


def three_parts(x):
    high = cut(x)
    rest = x - high
    mid = cut(rest)
    return high, mid, cut(rest - mid)


def tables(element, faces):
    volume, surface = prolong_tables()
    elem_mid = jnp.dot(volume.T, jnp.dot(element, volume, precision=HIGHEST), precision=HIGHEST)
    face_mid = jnp.einsum("kij,jb->kib", faces, surface, precision=HIGHEST)
    face_mid = jnp.einsum("ia,kib->kab", surface, face_mid, precision=HIGHEST)
    elem_coarse = jnp.sum(elem_mid)
    face_coarse = jnp.sum(face_mid, axis=(1, 2))
    high, low = trace_tables()
    both = np.concatenate([high, low], axis=0)
    rows = jnp.einsum("kij,djm->dkim", faces, both, precision=HIGHEST).reshape(384, 64)
    wide = jnp.concatenate([element, rows], axis=0)
    wh, wl = two_parts(wide)
    wide = jnp.concatenate([wh, wh, wl], axis=1).astype(BF16)
    spread = np.concatenate([high[1], -low[1], high[2], -low[2]], axis=0).T
    spread = np.concatenate([spread, spread], axis=1)
    face_diag = jnp.diagonal(faces, axis1=1, axis2=2)
    diag = jnp.einsum("dim,ki->mdk", both, face_diag, precision=HIGHEST).reshape(64, 24)
    diag_w = jnp.concatenate(three_parts(diag) + (jnp.zeros((64, 8), F32),), axis=1).astype(BF16)
    diag_e = jnp.diagonal(element)[:, None]
    mh, ml = mid_traces()
    both = np.concatenate([mh, ml], axis=0)
    diag = jnp.einsum(
        "dim,ki->mdk", both, jnp.diagonal(face_mid, axis1=1, axis2=2), precision=HIGHEST
    ).reshape(8, 24)
    mid_diag_w = jnp.concatenate(three_parts(diag) + (jnp.zeros((8, 8), F32),), axis=1).astype(BF16)
    mid_diag_e = jnp.diagonal(elem_mid)[:, None]
    vh, vl = two_parts(volume)
    down = jnp.concatenate([vh.T, vh.T, vl.T], axis=1).astype(BF16)
    lift = jnp.concatenate([vh, vh, vl, jnp.zeros((64, 8), F32)], axis=1).astype(BF16)
    least = 0.1 * elem_coarse
    most = 1.35 * elem_coarse + 9.0 * jnp.max(jnp.abs(face_coarse))
    half = 0.5 * (most - least)
    half = jnp.where(jnp.abs(half) > 0.0, half, 1.0)
    scal = jnp.concatenate(
        [
            elem_mid.reshape(-1),
            face_mid.reshape(-1),
            elem_coarse[None],
            face_coarse,
            (0.5 * (most + least))[None],
            (1.0 / half)[None],
            jnp.zeros((9,), F32),
        ]
    )
    return (
        wide,
        jnp.asarray(spread, BF16),
        diag_w,
        diag_e,
        down,
        mid_diag_w,
        mid_diag_e,
        lift,
        scal,
    )


def local(residual, coefficient, element, faces, kind, flag):
    shift_up = [(i, i + 1) for i in range(15)]
    shift_dn = [(i + 1, i) for i in range(15)]

    def z_index(zb):
        return (zb % 16) * 2 + zb // 16

    z_up = [(z_index(i), z_index(i + 1)) for i in range(31)]
    z_dn = [(z_index(i + 1), z_index(i)) for i in range(31)]
    z_axes = ("gx", "lvl")
    side = lax.axis_index("lvl")
    pos = jnp.stack(
        [
            lax.axis_index("yz"),
            side * 16 + lax.axis_index("gx"),
            side,
            jnp.zeros_like(side),
        ]
    ).astype(jnp.int32)
    wide, spread, diag_w, diag_e, down, mid_diag_w, mid_diag_e, lift, scal = tables(element, faces)
    res = residual.reshape(512, 128)
    cf = jnp.concatenate(
        [
            coefficient,
            kind[1].astype(F32),
            kind[3].astype(F32),
            kind[5].astype(F32),
            flag[1].astype(F32),
            flag[3].astype(F32),
            flag[5].astype(F32),
            jnp.zeros_like(coefficient),
        ],
        axis=0,
    ).reshape(64, 128)
    edges = call(edges_body, "edges", f32s(24, 128), (1, 0, 0))(pos, res, cf)
    halo = lax.ppermute(edges, "lvl", [(0, 1), (1, 0)])
    slots = call(
        slots_body,
        "slots",
        f32s(16, 80, 128),
        (1, 0, 0, 0),
        [pltpu.VMEM((3, 8, 64, 128), F32), pltpu.VMEM((3, 8, 8, 128), F32)],
    )(pos, res, cf, halo)
    own = lax.all_to_all(slots, "gx", 0, 0, tiled=True)
    below = lax.ppermute(own, "yz", shift_up)
    above = lax.ppermute(own, "yz", shift_dn)
    plane = (NX, 64, 256)
    pre, r, w, coef, inv, cfm, send_up, send_down = call(
        fine_pre_body,
        "fine_pre",
        [
            f32s(*plane),
            f32s(*plane),
            f32s(NX, 24, 256),
            f32s(NX, 8, 256),
            f32s(*plane),
            f32s(128, 1024),
            f32s(512, 128),
            f32s(512, 128),
        ],
        (1,) + (0,) * 10,
        [
            pltpu.VMEM(plane, F32),
            pltpu.VMEM((NX + 1, 16, 256), F32),
            pltpu.VMEM((NX + 1, 16, 256), F32),
            pltpu.VMEM((768, 128), F32),
        ],
    )(pos, own, below, above, wide, spread, diag_w, diag_e, down, mid_diag_w, mid_diag_e)
    dn = lax.ppermute(send_up, z_axes, z_up)
    up = lax.ppermute(send_down, z_axes, z_dn)
    slab, fwd, bwd, frz = call(
        mid_z_body,
        "mid_z",
        [f32s(128, 256), f32s(928, 128), f32s(896, 128), f32s(NX, 64, 128)],
        (0,) * 5,
    )(send_up, dn, up, r, cfm)
    below = lax.ppermute(fwd, "yz", shift_up)
    above = lax.ppermute(bwd, "yz", shift_dn)
    mid = (8, 16, 1024)
    mid_scratch = [
        pltpu.VMEM((3, 16, 1024), F32),
        pltpu.VMEM((3, 16, 16, 1024), F32),
        pltpu.VMEM(mid, F32),
    ]
    tail_scratch = [pltpu.VMEM((4, 16, 1024), F32), pltpu.VMEM((12, 16, 1024), F32)]
    mid_pre, mid_res, coarse, send_up, send_down = call(
        mid_pre_body,
        "mid_pre",
        [f32s(*mid), f32s(*mid), f32s(5, 16, 1024), f32s(2, 16, 768), f32s(2, 16, 768)],
        (1, 1, 0, 0, 0, 0),
        [pltpu.VMEM((128, 1024), F32)]
        + mid_scratch
        + [pltpu.VMEM(mid, F32), pltpu.VMEM(mid, F32)]
        + tail_scratch,
    )(pos, scal, slab, below, above, cfm)
    dn = lax.ppermute(send_up, z_axes, z_up)
    up = lax.ppermute(send_down, z_axes, z_dn)
    coarse_slab, fwd, bwd = call(
        coarse_z_body,
        "coarse_z",
        [f32s(5, 16, 1280), f32s(5, 16, 512), f32s(5, 16, 512)],
        (0, 0, 0),
    )(coarse, dn, up)
    coarse_below = lax.ppermute(fwd, "yz", shift_up)
    coarse_above = lax.ppermute(bwd, "yz", shift_dn)
    basis, gram = call(
        krylov_body,
        "krylov",
        [f32s(BASIS, 16, 1536), f32s(512, 128)],
        (1, 0, 0, 0),
        [pltpu.VMEM((5, 16, 2304), F32), pltpu.VMEM((2 * BASIS, 8, 128), F32)],
    )(scal, coarse_slab, coarse_below, coarse_above)
    grams = lax.all_to_all(gram, ("gx", "yz", "lvl"), 0, 0, tiled=True)
    mid_sol = call(
        mid_post_body,
        "mid_post",
        f32s(256, 128),
        (1, 1, 0, 0, 0, 0, 0),
        mid_scratch + [pltpu.VMEM(mid, F32)] * 3 + tail_scratch,
    )(pos, scal, grams, basis, cfm, mid_pre, mid_res)
    packed = call(
        fine_post_body,
        "fine_post",
        f32s(16, 64, 128),
        (0,) * 11,
        [
            pltpu.VMEM(plane, F32),
            pltpu.VMEM(plane, F32),
            pltpu.VMEM(plane, F32),
            pltpu.VMEM((NX + 1, 16, 256), F32),
            pltpu.VMEM((NX + 1, 16, 256), F32),
        ],
    )(mid_sol, pre, frz, below, above, w, coef, inv, wide, spread, lift)
    got = lax.all_to_all(packed, "gx", 0, 0, tiled=True)
    correction, rest = call(unpack_body, "unpack", [f32s(512, 128), f32s(512, 128)], (0,))(got)
    return (correction.reshape(64, 1, 8, 128), rest.reshape(64, 1, 8, 128))


def solution(mesh):
    in_specs = (
        P(None, "gx", "yz", "lvl"),
        P("gx", "yz", "lvl"),
        P(),
        P(),
        P(None, "gx", "yz", "lvl"),
        P(None, "gx", "yz", "lvl"),
    )
    out_specs = (P(None, "gx", "yz", "lvl"), P(None, "gx", "yz", "lvl"))
    return jax.shard_map(local, mesh=mesh, in_specs=in_specs, out_specs=out_specs, check_vma=False)
```

```python
import functools
import math

import jax
import jax.numpy as jnp
import numpy as np
from jax import lax
from jax.experimental import pallas as pl
from jax.experimental.pallas import tpu as pltpu
from jax.sharding import PartitionSpec as P

NX = 16
NY = 128
NZ = 256
KINDS = 4
F32 = jnp.float32
BF16 = jnp.bfloat16
HIGHEST = lax.Precision.HIGHEST
LOW_EIG = 0.3
HIGH_EIG = 3.0
MIDDLE = 0.5 * (HIGH_EIG + LOW_EIG)
SPREAD = 0.5 * (HIGH_EIG - LOW_EIG)
SCALED = MIDDLE / SPREAD
RHO0 = 1.0 / SCALED
RHO1 = 1.0 / (2.0 * SCALED - RHO0)
RHO2 = 1.0 / (2.0 * SCALED - RHO1)
STEPS = ((RHO1 * RHO0, 2.0 * RHO1 / SPREAD), (RHO2 * RHO1, 2.0 * RHO2 / SPREAD))
BASIS = 8
VMEM_LIMIT = 24 * 2**20


def lanes(shape):
    return lax.broadcasted_iota(jnp.int32, shape, len(shape) - 1)


def roll(x, shift, axis=None):
    axis = x.ndim - 1 if axis is None else axis
    shift = shift % x.shape[axis]
    return x if shift == 0 else pltpu.roll(x, shift, axis)


def call(body, name, out_shape, in_specs, scratch=(), flops=1000000):
    single = not isinstance(out_shape, (tuple, list))
    outs = [out_shape] if single else list(out_shape)
    vm = pl.BlockSpec(memory_space=pltpu.VMEM)
    return pl.pallas_call(
        body,
        out_shape=outs[0] if single else outs,
        in_specs=[pl.BlockSpec(memory_space=pltpu.SMEM) if s else vm for s in in_specs],
        out_specs=vm if single else [vm] * len(outs),
        scratch_shapes=list(scratch),
        compiler_params=pltpu.CompilerParams(vmem_limit_bytes=VMEM_LIMIT),
        cost_estimate=pl.CostEstimate(flops=flops, bytes_accessed=1000000, transcendentals=0),
        name=name,
    )


def f32s(*shape):
    return jax.ShapeDtypeStruct(shape, F32)


def split3(x):
    high = x.astype(BF16).astype(F32)
    low = x - high
    return high, low


def stack_hlh(x):
    high, low = split3(x)
    return jnp.concatenate([high, low, high], axis=0).astype(BF16)


def mm(a, b):
    return jnp.dot(a, b, preferred_element_type=F32)


def edges_body(pos, res, cf, out):
    first = pos[2] == 0
    lane = lanes((16, 128))
    acc = [jnp.zeros((16, 128), F32)]
    packed = jnp.zeros((16, 128), F32)
    packed_cf = jnp.zeros((8, 128), F32)
    lane8 = lanes((8, 128))
    for y in range(8):
        rows = res[pl.ds(y, 64, stride=8), :]
        rows = jnp.where(first, roll(rows, 4), rows)
        for j in range(4):
            at = 32 * j + 4 * y
            packed = jnp.where(
                (lane >= at) & (lane < at + 4), roll(rows[16 * j : 16 * j + 16], at), packed
            )
        rows = cf[pl.ds(y, 8, stride=8), :]
        rows = jnp.where(first, roll(rows, 12), rows)
        at = 12 * y
        packed_cf = jnp.where((lane8 >= at) & (lane8 < at + 12), roll(rows, at), packed_cf)
    out[0:16, :] = packed
    out[16:24, :] = packed_cf


def slots_body(pos, res, cf, halo, out, rows, rows_cf):
    first = pos[2] == 0
    lane = lanes((64, 128))
    lane8 = lanes((8, 128))
    for y in range(8):
        mine = res[pl.ds(y, 64, stride=8), :]
        got = jnp.concatenate([roll(halo[0:16, :], -(32 * j + 4 * y)) for j in range(4)], axis=0)
        rows[0, y] = jnp.where(lane >= 124, jnp.where(first, 0.0, roll(got, 124)), mine)
        rows[1, y] = mine
        rows[2, y] = jnp.where(lane < 4, jnp.where(first, got, 0.0), mine)
        mine = cf[pl.ds(y, 8, stride=8), :]
        got = roll(halo[16:24, :], -12 * y)
        rows_cf[0, y] = jnp.where(lane8 >= 116, jnp.where(first, 0.0, roll(got, 116)), mine)
        rows_cf[1, y] = mine
        rows_cf[2, y] = jnp.where(lane8 < 12, jnp.where(first, got, 0.0), mine)
    for g in range(NX):
        source = 0 if g == 0 else (2 if g == NX - 1 else 1)
        acc = jnp.zeros((64, 128), F32)
        for y in range(8):
            acc = jnp.where(lane // 16 == y, roll(rows[source, y], 16 * y - (8 * g - 4)), acc)
        out[g, 0:64, :] = acc
        source = 0 if g <= 1 else (2 if g >= NX - 2 else 1)
        for h in range(2):
            acc = jnp.zeros((8, 128), F32)
            for y in range(4):
                acc = jnp.where(
                    lane8 // 32 == y, roll(rows_cf[source, 4 * h + y], 32 * y - (8 * g - 12)), acc
                )
            out[g, 64 + 8 * h : 72 + 8 * h, :] = acc


CHUNK = 4096
CHUNKS = NX * 256 // CHUNK


def fine_apply(u, r, w, coef, wide, spread, px, qx, step, sol, inv):
    for c in range(CHUNKS):
        at = slice(CHUNK * c, CHUNK * (c + 1))
        after = slice(CHUNK * c + 256, CHUNK * (c + 1) + 256)
        prod = mm(wide[...], stack_hlh(u[:, at]))

        def pick(base, row):
            total = w[row : row + 1, at] * prod[base : base + 16]
            for k in range(1, KINDS):
                total = total + w[row + k : row + k + 1, at] * prod[base + 16 * k : base + 16 * k + 16]
            return total

        px[:, after] = pick(64, 0)
        py = pick(128, 4)
        pz = pick(192, 8)
        qx[:, at] = pick(256, 12)
        qy = pick(320, 16)
        qz = pick(384, 20)
        flux = jnp.concatenate(
            [py - roll(qy, -16), roll(py, 16) - qy, pz - roll(qz, -1), roll(pz, 1) - qz], axis=0
        )
        high, low = split3(flux)
        faces = mm(spread[...], jnp.concatenate([high, low], axis=0).astype(BF16))
        r[:, at] = r[:, at] - (coef[0:1, at] * prod[0:64] + faces)

    for c in range(CHUNKS):
        at = slice(CHUNK * c, CHUNK * (c + 1))
        after = slice(CHUNK * c + 256, CHUNK * (c + 1) + 256)
        r[48:64, at] = r[48:64, at] - (px[:, after] - qx[:, after])
        r[0:16, at] = r[0:16, at] + (px[:, at] - qx[:, at])
        if step is not None:
            keep, gain = STEPS[step]
            new = keep * u[:, at] + gain * (inv[:, at] * r[:, at])
            u[:, at] = new
            sol[:, at] = sol[:, at] + new


def fine_pre_body(
    pos,
    own,
    below,
    above,
    wide,
    spread,
    diag_w,
    diag_e,
    down,
    mid_diag_w,
    mid_diag_e,
    sol,
    r,
    w,
    coef,
    inv,
    cfm,
    send_up,
    send_down,
    u,
    px,
    qx,
    gather,
):
    low = lanes((64, 128)) < 64
    low8 = lanes((8, 128)) < 64
    lane8 = lanes((8, 128))
    place = lanes((1, 256)) % 256
    y_at = pos[0] * 8 - 4 + place // 16
    z_at = pos[1] * 8 - 4 + place % 16
    inside = (y_at >= 0) & (y_at < NY) & (z_at >= 0) & (z_at < NZ)
    has_y = inside & (y_at < NY - 1)
    has_z = inside & (z_at < NZ - 1)
    inside_f = jnp.where(inside, 1.0, 0.0)
    px[:, 0:256] = jnp.zeros((16, 256), F32)
    qx[:, NX * 256 :] = jnp.zeros((16, 256), F32)
    cfm[:, 0:128] = jnp.zeros((128, 128), F32)
    cfm[:, 896:1024] = jnp.zeros((128, 128), F32)
    for x in range(NX):
        first, second = slice(256 * x, 256 * x + 128), slice(256 * x + 128, 256 * x + 256)
        turned = roll(own[x, 0:64, :], 64)
        r[:, first] = jnp.where(low, roll(below[x, 0:64, :], 64), turned)
        r[:, second] = jnp.where(low, turned, roll(above[x, 0:64, :], 64))
        blocks = [
            below[x, 64:72, :],
            below[x, 72:80, :],
            own[x, 64:72, :],
            own[x, 72:80, :],
            above[x, 64:72, :],
            above[x, 72:80, :],
        ]
        for m in range(6):
            gather[pl.ds(128 * m + x, 8, stride=16), :] = blocks[m]
        for half, at in enumerate((first, second)):
            acc = jnp.zeros((8, 128), F32)
            for row in range(8):
                n = 8 * half + row
                acc = jnp.where(
                    lane8 // 16 == row,
                    roll(blocks[1 + n // 4], 16 * row - (n % 4) * 32 - 8),
                    acc,
                )
            coef[:, at] = acc
    for m in range(6):
        cfm[:, 128 * (m + 1) : 128 * (m + 2)] = gather[128 * m : 128 * m + 128, :]
    w[12:16, 0:256] = jnp.zeros((4, 256), F32)
    for x in range(NX):
        at = slice(256 * x, 256 * x + 256)
        rows = coef[:, at]
        opens = [
            inside & (rows[4:5] == 0.0) if x < NX - 1 else jnp.zeros((1, 256), jnp.bool_),
            has_y & (rows[5:6] == 0.0),
            has_z & (rows[6:7] == 0.0),
        ]
        plus = [
            [jnp.where(opens[d] & (rows[1 + d : 2 + d] == float(k)), 1.0, 0.0) for k in range(KINDS)]
            for d in range(3)
        ]
        plus_all = jnp.concatenate(plus[0] + plus[1] + plus[2], axis=0)
        w[0:12, at] = plus_all
        if x < NX - 1:
            w[12:16, 256 * x + 256 : 256 * x + 512] = plus_all[0:4]
        w[16:20, at] = roll(plus_all[4:8], 16)
        w[20:24, at] = roll(plus_all[8:12], 1)
    wide_inside = jnp.concatenate([inside] * (CHUNK // 256), axis=1)

    def kinds_of(at):
        ws = w[:, at]
        return jnp.concatenate([ws, ws, ws, jnp.zeros((8, CHUNK), F32)], axis=0).astype(BF16)

    for c in range(CHUNKS):
        at = slice(CHUNK * c, CHUNK * (c + 1))
        diag = diag_e[...] * coef[0:1, at] + mm(diag_w[...], kinds_of(at))
        inverse = jnp.where(wide_inside, 1.0 / diag, 0.0)
        inv[:, at] = inverse
        update = inverse * r[:, at] / MIDDLE
        u[:, at] = update
        sol[:, at] = update
    fine_apply(u, r, w, coef, wide, spread, px, qx, 0, sol, inv)
    fine_apply(u, r, w, coef, wide, spread, px, qx, 1, sol, inv)
    fine_apply(u, r, w, coef, wide, spread, px, qx, None, sol, inv)
    lane16 = lanes((16, 128)) % 16 // 4
    for c in range(CHUNKS):
        at = slice(CHUNK * c, CHUNK * (c + 1))
        rhs = mm(down[...], stack_hlh(r[:, at]))
        diag = mid_diag_e[...] * coef[0:1, at] + mm(mid_diag_w[...], kinds_of(at))
        update = jnp.where(wide_inside, 1.0 / diag, 0.0) * rhs / MIDDLE
        for n in range(CHUNK // 256):
            x = (CHUNK // 256) * c + n
            for half in range(2):
                piece = update[:, 256 * n + 128 * half : 256 * n + 128 * half + 128]
                send_up[pl.ds(128 * half + x, 8, stride=16), :] = piece
                send_down[pl.ds(128 * half + x, 8, stride=16), :] = piece
    for x in range(NX):
        first, second = slice(256 * x, 256 * x + 128), slice(256 * x + 128, 256 * x + 256)
        mine = jnp.where(low, roll(r[:, first], 64), roll(r[:, second], 64))
        up = jnp.zeros((16, 128), F32)
        dn = jnp.zeros((16, 128), F32)
        for j in range(4):
            part = mine[16 * j : 16 * j + 16]
            up = jnp.where(lane16 == j, roll(part, 4 * j - 8), up)
            dn = jnp.where(lane16 == j, roll(part, 4 * j - 4), dn)
        send_up[256 + 16 * x : 272 + 16 * x, :] = up
        send_down[256 + 16 * x : 272 + 16 * x, :] = dn


def mid_z_body(own, dn, up, r, cfm, slab, fwd, bwd, frz):
    lane = lanes((128, 128))
    for m in range(4):
        acc = jnp.zeros((128, 128), F32)
        for n in range(4):
            y = 4 * (m - 1) + n
            if y < -1 or y > 8:
                continue
            to = 32 * n
            half, at = (y + 4) // 8, 16 * ((y + 4) % 8)
            rows = slice(128 * half, 128 * half + 128)
            acc = jnp.where((lane >= to + 12) & (lane < to + 20), roll(own[rows, :], to + 8 - at), acc)
            acc = jnp.where((lane >= to + 3) & (lane < to + 12), roll(dn[rows, :], to - at), acc)
            acc = jnp.where((lane >= to + 20) & (lane < to + 29), roll(up[rows, :], to + 16 - at), acc)
        if 1 <= m <= 2:
            slab[:, 128 * (m - 1) : 128 * m] = acc
        if m <= 2:
            fwd[128 * m : 128 * m + 128, :] = acc
        if m >= 1:
            bwd[128 * (m - 1) : 128 * m, :] = acc
    fwd[896:912, :] = cfm[32:48, 256:384]
    fwd[912:928, :] = cfm[80:96, 256:384]
    low = lanes((64, 128)) < 64
    l16 = lanes((16, 128)) % 16
    for x in range(NX):
        at = 256 * x
        mine = jnp.where(low, roll(r[:, at : at + 128], 64), roll(r[:, at + 128 : at + 256], 64))
        pack_dn = dn[256 + 16 * x : 272 + 16 * x, :]
        pack_up = up[256 + 16 * x : 272 + 16 * x, :]
        for j in range(4):
            rows = slice(16 * j, 16 * j + 16)
            part = jnp.where(l16 < 4, roll(pack_dn, -4 * j), mine[rows])
            part = jnp.where(l16 >= 12, roll(pack_up, 12 - 4 * j), part)
            frz[x, rows, :] = part
    for x in range(8):
        fwd[384 + 64 * x : 448 + 64 * x, :] = jnp.where(low, roll(frz[x], 64), frz[x + 8])
        bwd[384 + 64 * x : 448 + 64 * x, :] = jnp.where(low, frz[x], roll(frz[x + 8], 64))


LOWS = ((0, 1, 2, 3), (0, 1, 4, 5), (0, 2, 4, 6))
HIGHS = ((4, 5, 6, 7), (2, 3, 6, 7), (1, 3, 5, 7))


def ahead(v, d):
    if d == 0:
        return roll(v, -1, 0)
    return roll(v, -32 if d == 1 else -1, 1)


def behind(v, d):
    if d == 0:
        return roll(v, 1, 0)
    return roll(v, 32 if d == 1 else 1, 1)


def mid_setup(pos, scal, cfm, sel, faces, inv, diag):
    place = lanes((16, 1024))
    x_at = lax.broadcasted_iota(jnp.int32, (16, 1024), 0)
    y_at = pos[0] * 8 - 12 + place // 32
    z_at = pos[1] * 8 - 12 + place % 32
    domain = (y_at >= 0) & (y_at < NY) & (z_at >= 0) & (z_at < NZ)
    known = domain & (place >= 128) & (place < 896)
    lasts = (x_at < NX - 1, y_at < NY - 1, z_at < NZ - 1)
    for d in range(3):
        is_open = domain & lasts[d] & (cfm[64 + 16 * d : 80 + 16 * d, :] == 0.0)
        sel[d] = jnp.where(is_open, cfm[16 + 16 * d : 32 + 16 * d, :], 4.0)
    coef = cfm[0:16, :]

    for d in range(3):
        for c in range(8):
            at = slice(128 * c, 128 * c + 128)
            kind = sel[d, :, at]
            ones = [kind == float(k) for k in range(KINDS)]
            for i in range(4):
                for j in range(i, 4):
                    value = jnp.zeros((16, 128), F32)
                    for k in range(KINDS):
                        value = jnp.where(ones[k], scal[64 + 16 * k + 4 * i + j], value)
                    faces[d, 4 * i + j, :, at] = value
    if inv is None:
        return known
    for i in range(8):
        total = coef * scal[9 * i]
        for d in range(3):
            if i in HIGHS[d]:
                total = total + faces[d, 5 * HIGHS[d].index(i)]
            else:
                total = total + behind(faces[d, 5 * LOWS[d].index(i)], d)
        if diag is not None:
            diag[i] = total
        inv[i] = jnp.where(known, 1.0 / total, 0.0)
    return known


def mid_apply(v, r, scal, cfm, faces, jump, flux):
    for d in range(3):
        for j in range(4):
            jump[j] = v[HIGHS[d][j]] - ahead(v[LOWS[d][j]], d)

        for c in range(8):
            at = slice(128 * c, 128 * c + 128)
            jumps = [jump[j, :, at] for j in range(4)]
            for i in range(4):
                total = faces[d, i, :, at] * jumps[0]
                for j in range(1, 4):
                    total = total + faces[d, 4 * min(i, j) + max(i, j), :, at] * jumps[j]
                flux[4 * d + i, :, at] = total

    for c in range(1, 7):
        at = slice(128 * c, 128 * c + 128)
        values = [v[j, :, at] for j in range(8)]
        coef = cfm[0:16, at]
        for i in range(8):
            total = scal[8 * i] * values[0]
            for j in range(1, 8):
                total = total + scal[8 * i + j] * values[j]
            r[i, :, at] = r[i, :, at] - coef * total
    for d in range(3):
        for j in range(4):
            value = flux[4 * d + j]
            r[HIGHS[d][j]] = r[HIGHS[d][j]] - value
            r[LOWS[d][j]] = r[LOWS[d][j]] + behind(value, d)


def mid_step(step, u, r, sol, inv):
    keep, gain = STEPS[step]
    for i in range(8):
        new = keep * u[i] + gain * (inv[i] * r[i])
        u[i] = new
        sol[i] = sol[i] + new


def mid_pre_body(
    pos, scal, slab, below, above, cfm_in, sol, r, coarse, send_up, send_down,
    cfm, sel, faces, inv, diag, u, jump, flux,
):
    cfm[...] = cfm_in[...]
    cfm[32:48, 0:128] = below[896:912, :]
    cfm[80:96, 0:128] = below[912:928, :]
    for i in range(8):
        rows = slice(16 * i, 16 * i + 16)
        for m in range(3):
            u[i, :, 128 * m : 128 * m + 128] = below[128 * m + 16 * i : 128 * m + 16 * i + 16, :]
            u[i, :, 128 * (m + 5) : 128 * (m + 6)] = above[128 * m + 16 * i : 128 * m + 16 * i + 16, :]
        u[i, :, 384:640] = slab[rows, :]
    mid_setup(pos, scal, cfm, sel, faces, inv, diag)
    for i in range(8):
        r[i] = (MIDDLE * diag[i]) * u[i]
        sol[i] = u[i]
    mid_apply(u, r, scal, cfm, faces, jump, flux)
    mid_step(0, u, r, sol, inv)
    mid_apply(u, r, scal, cfm, faces, jump, flux)
    mid_step(1, u, r, sol, inv)
    mid_apply(u, r, scal, cfm, faces, jump, flux)
    total = r[0]
    for i in range(1, 8):
        total = total + r[i]
    coarse[0] = total
    center = cfm[0:16, :] * scal[128]
    for d in range(3):
        kind = sel[d]
        value = jnp.zeros((16, 1024), F32)
        for k in range(KINDS):
            value = jnp.where(kind == float(k), scal[129 + k], value)
        coarse[2 + d] = value
        center = center + value + behind(value, d)
    coarse[1] = center
    l32 = lanes((16, 768)) % 32
    for out, first in ((send_up, 6), (send_down, 18)):
        acc = jnp.zeros((16, 768), F32)
        for f in range(4):
            acc = jnp.where(l32 // 8 == f, roll(coarse[f, :, 128:896], 8 * f - first), acc)
        out[0] = acc
        out[1] = roll(coarse[4, :, 128:896], -first)


def coarse_z_body(own, dn, up, slab, fwd, bwd):
    lane = lanes((16, 128))
    for f in range(5):
        part = 0 if f < 4 else 1
        shift = 8 * f if f < 4 else 0
        for m in range(10):
            acc = jnp.zeros((16, 128), F32)
            for n in range(2):
                y = 2 * m + n - 6
                tile, at = (y + 12) // 4, 32 * ((y + 12) % 4)
                to = 64 * n
                mine = own[f, :, 128 * tile : 128 * tile + 128]
                left = dn[part, :, 128 * (tile - 1) : 128 * tile]
                right = up[part, :, 128 * (tile - 1) : 128 * tile]
                acc = jnp.where(
                    (lane >= to + 22) & (lane < to + 42), roll(mine, to + 22 - (at + 6)), acc
                )
                acc = jnp.where(
                    (lane >= to + 14) & (lane < to + 22), roll(left, to + 14 - (at + shift)), acc
                )
                acc = jnp.where(
                    (lane >= to + 42) & (lane < to + 50), roll(right, to + 42 - (at + shift)), acc
                )
            slab[f, :, 128 * m : 128 * m + 128] = acc
            if m < 4:
                fwd[f, :, 128 * m : 128 * m + 128] = acc
            if m >= 6:
                bwd[f, :, 128 * (m - 6) : 128 * (m - 5)] = acc


def two_sum(a, b):
    s = a + b
    t = s - a
    return s, (a - (s - t)) + (b - t)


def halves(a):
    t = a * 4097.0
    high = t - (t - a)
    return high, a - high


def two_prod(a, b):
    ah, al = halves(a)
    bh, bl = halves(b)
    p = a * b
    return p, ((ah * bh - p) + ah * bl + al * bh) + al * bl


def pair_mul(a, b):
    p, e = two_prod(a[0], b[0])
    return two_sum(p, e + (a[0] * b[1] + a[1] * b[0]))


def pair_sub(a, b):
    s, e = two_sum(a[0], -b[0])
    return two_sum(s, e + (a[1] - b[1]))


def pair_div(a, b):
    first = a[0] / b[0]
    rest = pair_sub(a, pair_mul((first, jnp.zeros_like(first)), b))
    return two_sum(first, rest[0] / b[0])


START = (0, 9, 17, 24, 30, 35, 39, 42)
PAIRS = sum(9 - i for i in range(BASIS))


def krylov_body(scal, own, below, above, basis, gram, field, hold):
    for f in range(5):
        field[f, :, 0:512] = below[f]
        field[f, :, 512:1792] = own[f]
        field[f, :, 1792:2304] = above[f]
    center, half = scal[133], scal[134]
    lane8 = lanes((8, 128))

    def apply(v):
        total = field[1] * v
        for d in range(3):
            cond = field[2 + d]
            axis, step = ((0, 1), (1, 64), (1, 1))[d]
            total = total - cond * roll(v, -step, axis) - roll(cond * v, step, axis)
        return total

    def compact(v):
        acc = jnp.zeros((8, 128), F32)
        for t in range(2):
            for y in range(8):
                tile, at = (y + 14) // 2, 64 * ((y + 14) % 2) + 28
                to = 64 * t + 8 * y
                piece = v[8 * t : 8 * t + 8, 128 * tile : 128 * tile + 128]
                acc = jnp.where((lane8 >= to) & (lane8 < to + 8), roll(piece, to - at), acc)
        return acc

    before = None
    now = field[0]
    for j in range(BASIS):
        basis[j] = now[:, 384:1920]
        hold[j] = compact(now)
        image = apply(now)
        hold[BASIS + j] = compact(image)
        if j + 1 < BASIS:
            nxt = (image - center * now) * half
            if j > 0:
                nxt = 2.0 * nxt - before
            before, now = now, nxt
    high_rows, low_rows = [], []
    for i in range(BASIS):
        for j in range(i, BASIS + 1):
            other = hold[BASIS + j] if j < BASIS else hold[0]
            p, e = two_prod(hold[i], other)
            high_rows.append(p)
            low_rows.append(e)
    high = jnp.stack(high_rows)
    low = jnp.stack(low_rows)
    for axis, shifts in ((1, (4, 2, 1)), (2, (64, 32, 16, 8, 4, 2, 1))):
        for s in shifts:
            high, e = two_sum(high, roll(high, s, axis))
            low = low + roll(low, s, axis) + e
    row = jnp.zeros((8, 128), F32)
    for n in range(PAIRS):
        row = jnp.where(lane8 == n, high[n], row)
        row = jnp.where(lane8 == 64 + n, low[n], row)
    for m in range(64):
        gram[8 * m : 8 * m + 8, :] = row


def mid_post_body(
    pos, scal, gram, basis, cfm, pre, res, out,
    sel, faces, inv, u, r, sol, jump, flux,
):
    high = gram[...].reshape(64, 8, 128)
    low = jnp.zeros((64, 8, 128), F32)
    count = 64
    while count > 1:
        count //= 2
        high, e = two_sum(high[:count], high[count : 2 * count])
        low = low[:count] + low[count : 2 * count] + e
    high, low = high[0], low[0]
    for s in (4, 2, 1):
        high, e = two_sum(high, roll(high, s, 0))
        low = low + roll(low, s, 0) + e
    low = low + roll(high, 64)
    high, low = two_sum(high, low)
    lane = lanes((8, 128))
    sub = lax.broadcasted_iota(jnp.int32, (8, 128), 0)
    mat_h = jnp.zeros((8, 128), F32)
    mat_l = jnp.zeros((8, 128), F32)
    for i in range(BASIS):
        here = (sub == i) & (lane >= i) & (lane <= BASIS)
        mat_h = jnp.where(here, roll(high, i - START[i]), mat_h)
        mat_l = jnp.where(here, roll(low, i - START[i]), mat_l)
        for j in range(i + 1, BASIS):
            here = (sub == j) & (lane == i)
            shift = i - (START[i] + j - i)
            mat_h = jnp.where(here, roll(high, shift), mat_h)
            mat_l = jnp.where(here, roll(low, shift), mat_l)

    def spread_at(v, row, col):
        return jnp.broadcast_to(v[row : row + 1, col : col + 1], (8, 128))

    answers = []
    pivots = []
    for k in range(BASIS):
        start = spread_at(high, 0, START[k])
        piv = (spread_at(mat_h, k, k), spread_at(mat_l, k, k))
        good = jnp.abs(piv[0]) > 1e-12 * jnp.abs(start)
        safe = (jnp.where(good, piv[0], 1.0), jnp.where(good, piv[1], 0.0))
        pivots.append((safe, good))
        row = (
            jnp.broadcast_to(mat_h[k : k + 1, :], (8, 128)),
            jnp.broadcast_to(mat_l[k : k + 1, :], (8, 128)),
        )
        col = (
            jnp.broadcast_to(mat_h[:, k : k + 1], (8, 128)),
            jnp.broadcast_to(mat_l[:, k : k + 1], (8, 128)),
        )
        factor = pair_div(col, safe)
        use = good & (sub != k)
        factor = (jnp.where(use, factor[0], 0.0), jnp.where(use, factor[1], 0.0))
        mat_h, mat_l = pair_sub((mat_h, mat_l), pair_mul(factor, row))
    for k in range(BASIS):
        safe, good = pivots[k]
        value = pair_div((spread_at(mat_h, k, BASIS), spread_at(mat_l, k, BASIS)), safe)[0]
        answers.append(jnp.where(good, value, 0.0))
    weights = [jnp.concatenate([a, a], axis=0) for a in answers]
    lane16 = lanes((16, 128))
    tiles = []
    for m in range(12):
        total = weights[0] * basis[0, :, 128 * m : 128 * m + 128]
        for j in range(1, BASIS):
            total = total + weights[j] * basis[j, :, 128 * m : 128 * m + 128]
        tiles.append(total)
    for m in range(8):
        acc = jnp.zeros((16, 128), F32)
        if 1 <= m <= 6:
            for n in range(4):
                y = 4 * m + n - 12
                tile, at = (y + 14) // 2 - 3, 64 * ((y + 14) % 2)
                to = 32 * n
                acc = jnp.where(
                    (lane16 >= to + 5) & (lane16 < to + 27), roll(tiles[tile], to + 5 - (at + 21)), acc
                )
        for i in range(8):
            u[i, :, 128 * m : 128 * m + 128] = acc
    mid_setup(pos, scal, cfm, sel, faces, inv, None)
    for i in range(8):
        r[i] = res[i]
        sol[i] = pre[i] + u[i]
    mid_apply(u, r, scal, cfm, faces, jump, flux)
    for i in range(8):
        new = inv[i] * r[i] / MIDDLE
        u[i] = new
        sol[i] = sol[i] + new
    mid_apply(u, r, scal, cfm, faces, jump, flux)
    mid_step(0, u, r, sol, inv)
    mid_apply(u, r, scal, cfm, faces, jump, flux)
    mid_step(1, u, r, sol, inv)
    for i in range(8):
        for half in range(2):
            acc = jnp.zeros((16, 128), F32)
            for n in range(8):
                y = 8 * half + n - 4
                tile, at = (y + 12) // 4, 32 * ((y + 12) % 4) + 8
                acc = jnp.where(
                    lane16 // 16 == n,
                    roll(sol[i, :, 128 * tile : 128 * tile + 128], 16 * n - at),
                    acc,
                )
            out[128 * half + 16 * i : 128 * half + 16 * i + 16, :] = acc


def fine_post_body(
    mid, pre, frz, below, above, w, coef, inv, wide, spread, lift, out, u, r, sol, px, qx,
):
    low = lanes((64, 128)) < 64
    px[:, 0:256] = jnp.zeros((16, 256), F32)
    qx[:, NX * 256 :] = jnp.zeros((16, 256), F32)
    for x in range(NX):
        first, second = slice(256 * x, 256 * x + 128), slice(256 * x + 128, 256 * x + 256)
        turned = roll(frz[x], 64)
        at = 384 + 64 * (x % 8)
        down = below[at : at + 64, :]
        over = above[at : at + 64, :]
        if x >= 8:
            down = roll(down, 64)
        else:
            over = roll(over, 64)
        r[:, first] = jnp.where(low, down, turned)
        r[:, second] = jnp.where(low, turned, over)
    planes = CHUNK // 256
    for c in range(CHUNKS):
        at = slice(CHUNK * c, CHUNK * (c + 1))
        pieces = [
            mid[pl.ds(128 * half + planes * c + n, 8, stride=16), :]
            for n in range(planes)
            for half in range(2)
        ]
        high, rest = split3(jnp.concatenate(pieces, axis=1))
        stacked = jnp.concatenate([high, rest, high, jnp.zeros((8, CHUNK), F32)], axis=0)
        lifted = mm(lift[...], stacked.astype(BF16))
        u[:, at] = lifted
        sol[:, at] = pre[:, at] + lifted
    fine_apply(u, r, w, coef, wide, spread, px, qx, None, sol, inv)
    for c in range(CHUNKS):
        at = slice(CHUNK * c, CHUNK * (c + 1))
        new = inv[:, at] * r[:, at] / MIDDLE
        u[:, at] = new
        sol[:, at] = sol[:, at] + new
    fine_apply(u, r, w, coef, wide, spread, px, qx, 0, sol, inv)
    fine_apply(u, r, w, coef, wide, spread, px, qx, 1, sol, inv)
    fine_apply(u, r, w, coef, wide, spread, px, qx, None, sol, inv)
    lane = lanes((64, 128))
    for x in range(NX):
        acc = jnp.zeros((64, 128), F32)
        for part, ref in enumerate((sol, r)):
            for y in range(8):
                half, at = (y + 4) // 8, 16 * ((y + 4) % 8) + 4
                start = 256 * x + 128 * half
                acc = jnp.where(
                    lane // 8 == 8 * part + y,
                    roll(ref[:, start : start + 128], 64 * part + 8 * y - at),
                    acc,
                )
        out[x] = acc


def unpack_body(got, first, second):
    lane = lanes((64, 128)) // 8
    for part, out in enumerate((first, second)):
        for y in range(8):
            acc = jnp.zeros((64, 128), F32)
            for g in range(NX):
                acc = jnp.where(lane == g, roll(got[g], 8 * g - 8 * y - 64 * part), acc)
            out[pl.ds(y, 64, stride=8), :] = acc


def trace_tables():
    high = np.zeros((3, 16, 64), np.float32)
    low = np.zeros((3, 16, 64), np.float32)
    for p in range(4):
        for q in range(4):
            for d in range(3):
                for table, at in ((high, 3), (low, 0)):
                    index = [p, q]
                    index.insert(d, at)
                    table[d, 4 * p + q, 16 * index[0] + 4 * index[1] + index[2]] = 1.0
    return high, low


def mid_traces():
    high = np.zeros((3, 4, 8), np.float32)
    low = np.zeros((3, 4, 8), np.float32)
    for d in range(3):
        for n in range(4):
            high[d, n, HIGHS[d][n]] = 1.0
            low[d, n, LOWS[d][n]] = 1.0
    return high, low


def prolong_tables():
    node_points = jnp.array(
        [-1.0, -1.0 / math.sqrt(5.0), 1.0 / math.sqrt(5.0), 1.0], dtype=jnp.float32
    )
    basis_table = jnp.stack([(1.0 - node_points) * 0.5, (1.0 + node_points) * 0.5], axis=1)
    volume = (
        basis_table[:, None, None, :, None, None]
        * basis_table[None, :, None, None, :, None]
        * basis_table[None, None, :, None, None, :]
    ).reshape(64, 8)
    surface = (basis_table[:, None, :, None] * basis_table[None, :, None, :]).reshape(16, 4)
    return (volume, surface)


def cut(x):
    return lax.reduce_precision(x, 8, 7)


def two_parts(x):
    high = cut(x)
    return high, cut(x - high)


def three_parts(x):
    high = cut(x)
    rest = x - high
    mid = cut(rest)
    return high, mid, cut(rest - mid)


def tables(element, faces):
    volume, surface = prolong_tables()
    elem_mid = jnp.dot(volume.T, jnp.dot(element, volume, precision=HIGHEST), precision=HIGHEST)
    face_mid = jnp.einsum("kij,jb->kib", faces, surface, precision=HIGHEST)
    face_mid = jnp.einsum("ia,kib->kab", surface, face_mid, precision=HIGHEST)
    elem_coarse = jnp.sum(elem_mid)
    face_coarse = jnp.sum(face_mid, axis=(1, 2))
    high, low = trace_tables()
    both = np.concatenate([high, low], axis=0)
    rows = jnp.einsum("kij,djm->dkim", faces, both, precision=HIGHEST).reshape(384, 64)
    wide = jnp.concatenate([element, rows], axis=0)
    wh, wl = two_parts(wide)
    wide = jnp.concatenate([wh, wh, wl], axis=1).astype(BF16)
    spread = np.concatenate([high[1], -low[1], high[2], -low[2]], axis=0).T
    spread = np.concatenate([spread, spread], axis=1)
    face_diag = jnp.diagonal(faces, axis1=1, axis2=2)
    diag = jnp.einsum("dim,ki->mdk", both, face_diag, precision=HIGHEST).reshape(64, 24)
    diag_w = jnp.concatenate(three_parts(diag) + (jnp.zeros((64, 8), F32),), axis=1).astype(BF16)
    diag_e = jnp.diagonal(element)[:, None]
    mh, ml = mid_traces()
    both = np.concatenate([mh, ml], axis=0)
    diag = jnp.einsum(
        "dim,ki->mdk", both, jnp.diagonal(face_mid, axis1=1, axis2=2), precision=HIGHEST
    ).reshape(8, 24)
    mid_diag_w = jnp.concatenate(three_parts(diag) + (jnp.zeros((8, 8), F32),), axis=1).astype(BF16)
    mid_diag_e = jnp.diagonal(elem_mid)[:, None]
    vh, vl = two_parts(volume)
    down = jnp.concatenate([vh.T, vh.T, vl.T], axis=1).astype(BF16)
    lift = jnp.concatenate([vh, vh, vl, jnp.zeros((64, 8), F32)], axis=1).astype(BF16)
    least = 0.1 * elem_coarse
    most = 1.35 * elem_coarse + 9.0 * jnp.max(jnp.abs(face_coarse))
    half = 0.5 * (most - least)
    half = jnp.where(jnp.abs(half) > 0.0, half, 1.0)
    scal = jnp.concatenate(
        [
            elem_mid.reshape(-1),
            face_mid.reshape(-1),
            elem_coarse[None],
            face_coarse,
            (0.5 * (most + least))[None],
            (1.0 / half)[None],
            jnp.zeros((9,), F32),
        ]
    )
    return (
        wide,
        jnp.asarray(spread, BF16),
        diag_w,
        diag_e,
        down,
        mid_diag_w,
        mid_diag_e,
        lift,
        scal,
    )


def local(residual, coefficient, element, faces, kind, flag):
    shift_up = [(i, i + 1) for i in range(15)]
    shift_dn = [(i + 1, i) for i in range(15)]

    def z_index(zb):
        return (zb % 16) * 2 + zb // 16

    z_up = [(z_index(i), z_index(i + 1)) for i in range(31)]
    z_dn = [(z_index(i + 1), z_index(i)) for i in range(31)]
    z_axes = ("gx", "lvl")
    side = lax.axis_index("lvl")
    pos = jnp.stack(
        [
            lax.axis_index("yz"),
            side * 16 + lax.axis_index("gx"),
            side,
            jnp.zeros_like(side),
        ]
    ).astype(jnp.int32)
    res = residual.reshape(512, 128)
    cf = jnp.concatenate(
        [
            coefficient,
            kind[1].astype(F32),
            kind[3].astype(F32),
            kind[5].astype(F32),
            flag[1].astype(F32),
            flag[3].astype(F32),
            flag[5].astype(F32),
            jnp.zeros_like(coefficient),
        ],
        axis=0,
    ).reshape(64, 128)
    edges = call(edges_body, "edges", f32s(24, 128), (1, 0, 0))(pos, res, cf)
    halo = lax.ppermute(edges, "lvl", [(0, 1), (1, 0)])
    slots = call(
        slots_body,
        "slots",
        f32s(16, 80, 128),
        (1, 0, 0, 0),
        [pltpu.VMEM((3, 8, 64, 128), F32), pltpu.VMEM((3, 8, 8, 128), F32)],
    )(pos, res, cf, halo)
    element, faces, slots = lax.optimization_barrier((element, faces, slots))
    wide, spread, diag_w, diag_e, down, mid_diag_w, mid_diag_e, lift, scal = tables(element, faces)
    own = lax.all_to_all(slots, "gx", 0, 0, tiled=True)
    below = lax.ppermute(own, "yz", shift_up)
    above = lax.ppermute(own, "yz", shift_dn)
    plane = (64, NX * 256)
    strip = (16, NX * 256 + 256)
    pre, r, w, coef, inv, cfm, send_up, send_down = call(
        fine_pre_body,
        "fine_pre",
        [
            f32s(*plane),
            f32s(*plane),
            f32s(24, NX * 256),
            f32s(8, NX * 256),
            f32s(*plane),
            f32s(128, 1024),
            f32s(512, 128),
            f32s(512, 128),
        ],
        (1,) + (0,) * 10,
        [
            pltpu.VMEM(plane, F32),
            pltpu.VMEM(strip, F32),
            pltpu.VMEM(strip, F32),
            pltpu.VMEM((768, 128), F32),
        ],
    )(pos, own, below, above, wide, spread, diag_w, diag_e, down, mid_diag_w, mid_diag_e)
    dn = lax.ppermute(send_up, z_axes, z_up)
    up = lax.ppermute(send_down, z_axes, z_dn)
    slab, fwd, bwd, frz = call(
        mid_z_body,
        "mid_z",
        [f32s(128, 256), f32s(928, 128), f32s(896, 128), f32s(NX, 64, 128)],
        (0,) * 5,
    )(send_up, dn, up, r, cfm)
    below = lax.ppermute(fwd, "yz", shift_up)
    above = lax.ppermute(bwd, "yz", shift_dn)
    mid = (8, 16, 1024)
    mid_scratch = [
        pltpu.VMEM((3, 16, 1024), F32),
        pltpu.VMEM((3, 16, 16, 1024), F32),
        pltpu.VMEM(mid, F32),
    ]
    tail_scratch = [pltpu.VMEM((4, 16, 1024), F32), pltpu.VMEM((12, 16, 1024), F32)]
    mid_pre, mid_res, coarse, send_up, send_down = call(
        mid_pre_body,
        "mid_pre",
        [f32s(*mid), f32s(*mid), f32s(5, 16, 1024), f32s(2, 16, 768), f32s(2, 16, 768)],
        (1, 1, 0, 0, 0, 0),
        [pltpu.VMEM((128, 1024), F32)]
        + mid_scratch
        + [pltpu.VMEM(mid, F32), pltpu.VMEM(mid, F32)]
        + tail_scratch,
    )(pos, scal, slab, below, above, cfm)
    dn = lax.ppermute(send_up, z_axes, z_up)
    up = lax.ppermute(send_down, z_axes, z_dn)
    coarse_slab, fwd, bwd = call(
        coarse_z_body,
        "coarse_z",
        [f32s(5, 16, 1280), f32s(5, 16, 512), f32s(5, 16, 512)],
        (0, 0, 0),
    )(coarse, dn, up)
    coarse_below = lax.ppermute(fwd, "yz", shift_up)
    coarse_above = lax.ppermute(bwd, "yz", shift_dn)
    basis, gram = call(
        krylov_body,
        "krylov",
        [f32s(BASIS, 16, 1536), f32s(512, 128)],
        (1, 0, 0, 0),
        [pltpu.VMEM((5, 16, 2304), F32), pltpu.VMEM((2 * BASIS, 8, 128), F32)],
    )(scal, coarse_slab, coarse_below, coarse_above)
    grams = lax.all_to_all(gram, ("gx", "yz", "lvl"), 0, 0, tiled=True)
    mid_sol = call(
        mid_post_body,
        "mid_post",
        f32s(256, 128),
        (1, 1, 0, 0, 0, 0, 0),
        mid_scratch + [pltpu.VMEM(mid, F32)] * 3 + tail_scratch,
    )(pos, scal, grams, basis, cfm, mid_pre, mid_res)
    packed = call(
        fine_post_body,
        "fine_post",
        f32s(16, 64, 128),
        (0,) * 11,
        [
            pltpu.VMEM(plane, F32),
            pltpu.VMEM(plane, F32),
            pltpu.VMEM(plane, F32),
            pltpu.VMEM(strip, F32),
            pltpu.VMEM(strip, F32),
        ],
    )(mid_sol, pre, frz, below, above, w, coef, inv, wide, spread, lift)
    got = lax.all_to_all(packed, "gx", 0, 0, tiled=True)
    correction, rest = call(unpack_body, "unpack", [f32s(512, 128), f32s(512, 128)], (0,))(got)
    return (correction.reshape(64, 1, 8, 128), rest.reshape(64, 1, 8, 128))


def solution(mesh):
    in_specs = (
        P(None, "gx", "yz", "lvl"),
        P("gx", "yz", "lvl"),
        P(),
        P(),
        P(None, "gx", "yz", "lvl"),
        P(None, "gx", "yz", "lvl"),
    )
    out_specs = (P(None, "gx", "yz", "lvl"), P(None, "gx", "yz", "lvl"))
    return jax.shard_map(local, mesh=mesh, in_specs=in_specs, out_specs=out_specs, check_vma=False)
```

```python
import functools
import math

import jax
import jax.numpy as jnp
import numpy as np
from jax import lax
from jax.experimental import pallas as pl
from jax.experimental.pallas import tpu as pltpu
from jax.sharding import PartitionSpec as P

NX = 16
NY = 128
NZ = 256
KINDS = 4
F32 = jnp.float32
BF16 = jnp.bfloat16
HIGHEST = lax.Precision.HIGHEST
LOW_EIG = 0.3
HIGH_EIG = 3.0
MIDDLE = 0.5 * (HIGH_EIG + LOW_EIG)
SPREAD = 0.5 * (HIGH_EIG - LOW_EIG)
SCALED = MIDDLE / SPREAD
RHO0 = 1.0 / SCALED
RHO1 = 1.0 / (2.0 * SCALED - RHO0)
RHO2 = 1.0 / (2.0 * SCALED - RHO1)
STEPS = ((RHO1 * RHO0, 2.0 * RHO1 / SPREAD), (RHO2 * RHO1, 2.0 * RHO2 / SPREAD))
BASIS = 8
VMEM_LIMIT = 24 * 2**20


def lanes(shape):
    return lax.broadcasted_iota(jnp.int32, shape, len(shape) - 1)


def roll(x, shift, axis=None):
    axis = x.ndim - 1 if axis is None else axis
    shift = shift % x.shape[axis]
    return x if shift == 0 else pltpu.roll(x, shift, axis)


SPACES = {
    0: pl.BlockSpec(memory_space=pltpu.VMEM),
    1: pl.BlockSpec(memory_space=pltpu.SMEM),
    2: pl.BlockSpec(memory_space=pltpu.HBM),
}


def call(body, name, out_shape, in_specs, scratch=(), out_specs=None):
    out_specs = out_specs or (0,) * len(out_shape)
    return pl.pallas_call(
        body,
        out_shape=list(out_shape),
        in_specs=[SPACES[i] for i in in_specs],
        out_specs=[SPACES[i] for i in out_specs],
        scratch_shapes=list(scratch),
        compiler_params=pltpu.CompilerParams(vmem_limit_bytes=VMEM_LIMIT),
        cost_estimate=pl.CostEstimate(flops=1000000, bytes_accessed=1000000, transcendentals=0),
        name=name,
    )


def f32s(*shape):
    return jax.ShapeDtypeStruct(shape, F32)


def split3(x):
    high = x.astype(BF16).astype(F32)
    low = x - high
    return high, low


def stack_hlh(x):
    high, low = split3(x)
    return jnp.concatenate([high, low, high], axis=0).astype(BF16)


def mm(a, b):
    return jnp.dot(a, b, preferred_element_type=F32)


def exchange(arrays, lane_block):
    arrays = list(arrays)
    group = lanes(arrays[0].shape) // lane_block
    for bit in (1, 2, 4):
        upper = (group // bit) % 2 == 1
        for n in range(8):
            if n & bit:
                continue
            a, b = arrays[n], arrays[n | bit]
            arrays[n] = jnp.where(upper, roll(b, lane_block * bit), a)
            arrays[n | bit] = jnp.where(upper, b, roll(a, -lane_block * bit))
    return arrays


def slots_body(res, cf, out):
    low = lanes((32, 128)) < 64
    low8 = lanes((8, 128)) < 64
    values = exchange([res[pl.ds(y, 64, stride=8), :] for y in range(8)], 8)
    kinds = exchange([cf[pl.ds(y, 16, stride=8), :] for y in range(8)], 8)
    for j in range(8):
        a, b = values[j][0:32], values[j][32:64]
        out[j, 0:32, :] = jnp.where(low, a, roll(b, 64))
        out[j + 8, 0:32, :] = jnp.where(low, roll(a, 64), b)
        a, b = kinds[j][0:8], kinds[j][8:16]
        out[j, 32:40, :] = jnp.where(low8, a, roll(b, 64))
        out[j + 8, 32:40, :] = jnp.where(low8, roll(a, 64), b)


def place_tables():
    values = np.zeros((256, 256), np.float32)
    kinds = np.zeros((384, 512), np.float32)
    for half in range(2):
        for y in range(8):
            for z in range(8):
                lane = 64 * half + 8 * y + z
                values[lane, 128 * half + 16 * y + z + 4] = 1.0
                beside = z + 12 if z < 4 else z - 4
                values[128 + lane, 128 * half + 16 * y + beside] = 1.0
                for n, first in enumerate((12, 4, 20)):
                    kinds[128 * n + lane, 256 * half + 32 * y + first + z] = 1.0
    return values, kinds


def three_rows(x):
    high = x.astype(BF16).astype(F32)
    rest = x - high
    mid = rest.astype(BF16).astype(F32)
    return jnp.concatenate([high, mid, rest - mid], axis=0).astype(BF16)


def moved(x, table):
    count = x.shape[0]
    out = mm(three_rows(x), table)
    return out[0:count] + out[count : 2 * count] + out[2 * count :]


def join_body(own, dn, up, place_values, place_kinds, rows, fwd, bwd):
    near = lanes((512, 128)) % 8 < 4
    mine = own[:, 0:32, :].reshape(512, 128)
    beside = jnp.where(near, up[:, 0:32, :].reshape(512, 128), dn[:, 0:32, :].reshape(512, 128))
    out = moved(jnp.concatenate([mine, beside], axis=1), place_values[...])
    for x in range(NX):
        rows[x, 0:32, :] = out[32 * x : 32 * x + 32, 0:128]
        rows[x, 32:64, :] = out[32 * x : 32 * x + 32, 128:256]
    low = lanes((64, 128)) < 64
    for x in range(8):
        fwd[64 * x : 64 * x + 64, :] = jnp.where(low, roll(rows[x], 64), rows[x + 8])
        bwd[64 * x : 64 * x + 64, :] = jnp.where(low, rows[x], roll(rows[x + 8], 64))
    kinds = jnp.concatenate([v[:, 32:40, :].reshape(128, 128) for v in (own, dn, up)], axis=1)
    out = moved(kinds, place_kinds[...])
    array = lax.broadcasted_iota(jnp.int32, (128, 128), 0) % 8
    edge = (lanes((128, 128)) % 32 == 3) & ((array == 3) | (array == 6))
    for h in range(2):
        minus = out[:, 256 + 128 * h : 384 + 128 * h]
        plus = jnp.where(edge, roll(minus, -1), out[:, 128 * h : 128 * h + 128])
        fwd[512 + 128 * h : 640 + 128 * h, :] = plus
        bwd[512 + 128 * h : 640 + 128 * h, :] = plus
    fwd[768:896, :] = out[:, 256:384]


CHUNK = 4096
CHUNKS = NX * 256 // CHUNK


def fine_apply(u, r, w, coef, wide, spread, px, qx, step, sol, inv):
    for c in range(CHUNKS):
        at = slice(CHUNK * c, CHUNK * (c + 1))
        after = slice(CHUNK * c + 256, CHUNK * (c + 1) + 256)
        prod = mm(wide[...], stack_hlh(u[:, at]))

        def pick(base, row):
            total = w[row : row + 1, at] * prod[base : base + 16]
            for k in range(1, KINDS):
                total = total + w[row + k : row + k + 1, at] * prod[base + 16 * k : base + 16 * k + 16]
            return total

        px[:, after] = pick(64, 0)
        py = pick(128, 4)
        pz = pick(192, 8)
        qx[:, at] = pick(256, 12)
        qy = pick(320, 16)
        qz = pick(384, 20)
        flux = jnp.concatenate(
            [py - roll(qy, -16), roll(py, 16) - qy, pz - roll(qz, -1), roll(pz, 1) - qz], axis=0
        )
        high, low = split3(flux)
        faces = mm(spread[...], jnp.concatenate([high, low], axis=0).astype(BF16))
        r[:, at] = r[:, at] - (coef[0:1, at] * prod[0:64] + faces)

    for c in range(CHUNKS):
        at = slice(CHUNK * c, CHUNK * (c + 1))
        after = slice(CHUNK * c + 256, CHUNK * (c + 1) + 256)
        r[48:64, at] = r[48:64, at] - (px[:, after] - qx[:, after])
        r[0:16, at] = r[0:16, at] + (px[:, at] - qx[:, at])
        if step is not None:
            keep, gain = STEPS[step]
            new = keep * u[:, at] + gain * (inv[:, at] * r[:, at])
            u[:, at] = new
            sol[:, at] = sol[:, at] + new


def fine_pre_body(
    pos,
    rows_in,
    own,
    below,
    above,
    wide,
    spread,
    diag_w,
    diag_e,
    down,
    mid_diag_w,
    mid_diag_e,
    sol_out,
    r,
    w_out,
    coef_out,
    inv_out,
    cfm,
    send_up,
    send_down,
    sol,
    w,
    coef,
    inv,
    u,
    px,
    qx,
    gather,
    sems,
):
    low = lanes((64, 128)) < 64
    lane8 = lanes((8, 128))
    place = lanes((1, 256))
    y_at = pos[0] * 8 - 4 + place // 16
    z_at = pos[1] * 8 - 4 + place % 16
    inside = (y_at >= 0) & (y_at < NY) & (z_at >= 0) & (z_at < NZ)
    has_y = inside & (y_at < NY - 1)
    has_z = inside & (z_at < NZ - 1)
    inside_f = jnp.where(inside, 1.0, 0.0)
    px[:, 0:256] = jnp.zeros((16, 256), F32)
    qx[:, NX * 256 :] = jnp.zeros((16, 256), F32)
    cfm[:, 896:1024] = jnp.zeros((128, 128), F32)
    array = lax.broadcasted_iota(jnp.int32, (8, 128), 0)
    edge = (lane8 >= 96) & ((array == 2) | (array == 5))
    for x in range(NX):
        first, second = slice(256 * x, 256 * x + 128), slice(256 * x + 128, 256 * x + 256)
        turned = roll(rows_in[x], 64)
        at = 64 * (x % 8)
        under = below[at : at + 64, :]
        over = above[at : at + 64, :]
        if x >= 8:
            under = roll(under, 64)
        else:
            over = roll(over, 64)
        r[:, first] = jnp.where(low, under, turned)
        r[:, second] = jnp.where(low, turned, over)
        blocks = [
            ref[512 + 128 * h + 8 * x : 520 + 128 * h + 8 * x, :]
            for ref in (below, own, above)
            for h in range(2)
        ]
        minus = below[768 + 8 * x : 776 + 8 * x, :]
        gather[pl.ds(x, 8, stride=16), :] = jnp.where(edge, roll(minus, 96), 0.0)
        for m in range(6):
            gather[pl.ds(128 * (m + 1) + x, 8, stride=16), :] = blocks[m]
        for half, at in enumerate((first, second)):
            acc = jnp.zeros((8, 128), F32)
            for row in range(8):
                n = 8 * half + row
                acc = jnp.where(
                    lane8 // 16 == row,
                    roll(blocks[1 + n // 4], 16 * row - (n % 4) * 32 - 8),
                    acc,
                )
            coef[:, at] = acc
    for m in range(7):
        cfm[:, 128 * m : 128 * m + 128] = gather[128 * m : 128 * m + 128, :]
    w[12:16, 0:256] = jnp.zeros((4, 256), F32)
    for x in range(NX):
        at = slice(256 * x, 256 * x + 256)
        rows = coef[:, at]
        opens = [
            inside & (rows[4:5] == 0.0) if x < NX - 1 else jnp.zeros((1, 256), jnp.bool_),
            has_y & (rows[5:6] == 0.0),
            has_z & (rows[6:7] == 0.0),
        ]
        plus = [
            [jnp.where(opens[d] & (rows[1 + d : 2 + d] == float(k)), 1.0, 0.0) for k in range(KINDS)]
            for d in range(3)
        ]
        plus_all = jnp.concatenate(plus[0] + plus[1] + plus[2], axis=0)
        w[0:12, at] = plus_all
        if x < NX - 1:
            w[12:16, 256 * x + 256 : 256 * x + 512] = plus_all[0:4]
        w[16:20, at] = roll(plus_all[4:8], 16)
        w[20:24, at] = roll(plus_all[8:12], 1)
    wide_inside = jnp.concatenate([inside] * (CHUNK // 256), axis=1)

    def kinds_of(at):
        ws = w[:, at]
        return jnp.concatenate([ws, ws, ws, jnp.zeros((8, CHUNK), F32)], axis=0).astype(BF16)

    for c in range(CHUNKS):
        at = slice(CHUNK * c, CHUNK * (c + 1))
        diag = diag_e[...] * coef[0:1, at] + mm(diag_w[...], kinds_of(at))
        inverse = jnp.where(wide_inside, 1.0 / diag, 0.0)
        inv[:, at] = inverse
        update = inverse * r[:, at] / MIDDLE
        u[:, at] = update
        sol[:, at] = update
    copies = [
        pltpu.make_async_copy(held, out, sems.at[n])
        for n, (held, out) in enumerate(
            ((w, w_out), (coef, coef_out), (inv, inv_out), (sol, sol_out))
        )
    ]
    for copy in copies[:3]:
        copy.start()
    fine_apply(u, r, w, coef, wide, spread, px, qx, 0, sol, inv)
    fine_apply(u, r, w, coef, wide, spread, px, qx, 1, sol, inv)
    copies[3].start()
    fine_apply(u, r, w, coef, wide, spread, px, qx, None, sol, inv)
    lane16 = lanes((16, 128)) % 16 // 4
    for c in range(CHUNKS):
        at = slice(CHUNK * c, CHUNK * (c + 1))
        rhs = mm(down[...], stack_hlh(r[:, at]))
        diag = mid_diag_e[...] * coef[0:1, at] + mm(mid_diag_w[...], kinds_of(at))
        update = jnp.where(wide_inside, 1.0 / diag, 0.0) * rhs / MIDDLE
        for n in range(CHUNK // 256):
            x = (CHUNK // 256) * c + n
            for half in range(2):
                piece = update[:, 256 * n + 128 * half : 256 * n + 128 * half + 128]
                send_up[pl.ds(128 * half + x, 8, stride=16), :] = piece
                send_down[pl.ds(128 * half + x, 8, stride=16), :] = piece
    for x in range(NX):
        first, second = slice(256 * x, 256 * x + 128), slice(256 * x + 128, 256 * x + 256)
        mine = jnp.where(low, roll(r[:, first], 64), roll(r[:, second], 64))
        up = jnp.zeros((16, 128), F32)
        dn = jnp.zeros((16, 128), F32)
        for j in range(4):
            part = mine[16 * j : 16 * j + 16]
            up = jnp.where(lane16 == j, roll(part, 4 * j - 8), up)
            dn = jnp.where(lane16 == j, roll(part, 4 * j - 4), dn)
        send_up[256 + 16 * x : 272 + 16 * x, :] = up
        send_down[256 + 16 * x : 272 + 16 * x, :] = dn
    for copy in copies:
        copy.wait()


def mid_z_body(own, dn, up, r, slab, fwd, bwd, frz_out, frz, sem):
    low = lanes((64, 128)) < 64
    l16 = lanes((16, 128)) % 16
    for x in range(NX):
        at = 256 * x
        mine = jnp.where(low, roll(r[:, at : at + 128], 64), roll(r[:, at + 128 : at + 256], 64))
        pack_dn = dn[256 + 16 * x : 272 + 16 * x, :]
        pack_up = up[256 + 16 * x : 272 + 16 * x, :]
        for j in range(4):
            rows = slice(16 * j, 16 * j + 16)
            part = jnp.where(l16 < 4, roll(pack_dn, -4 * j), mine[rows])
            part = jnp.where(l16 >= 12, roll(pack_up, 12 - 4 * j), part)
            frz[x, rows, :] = part
    copy = pltpu.make_async_copy(frz, frz_out, sem)
    copy.start()
    for x in range(8):
        fwd[384 + 64 * x : 448 + 64 * x, :] = jnp.where(low, roll(frz[x], 64), frz[x + 8])
        bwd[384 + 64 * x : 448 + 64 * x, :] = jnp.where(low, frz[x], roll(frz[x + 8], 64))
    lane = lanes((128, 128))
    for m in range(4):
        acc = jnp.zeros((128, 128), F32)
        for n in range(4):
            y = 4 * (m - 1) + n
            if y < -1 or y > 8:
                continue
            to = 32 * n
            half, at = (y + 4) // 8, 16 * ((y + 4) % 8)
            rows = slice(128 * half, 128 * half + 128)
            acc = jnp.where((lane >= to + 12) & (lane < to + 20), roll(own[rows, :], to + 8 - at), acc)
            acc = jnp.where((lane >= to + 3) & (lane < to + 12), roll(dn[rows, :], to - at), acc)
            acc = jnp.where((lane >= to + 20) & (lane < to + 29), roll(up[rows, :], to + 16 - at), acc)
        if 1 <= m <= 2:
            slab[:, 128 * (m - 1) : 128 * m] = acc
        if m <= 2:
            fwd[128 * m : 128 * m + 128, :] = acc
        if m >= 1:
            bwd[128 * (m - 1) : 128 * m, :] = acc
    copy.wait()


LOWS = ((0, 1, 2, 3), (0, 1, 4, 5), (0, 2, 4, 6))
HIGHS = ((4, 5, 6, 7), (2, 3, 6, 7), (1, 3, 5, 7))


def ahead(v, d):
    if d == 0:
        return roll(v, -1, 0)
    return roll(v, -32 if d == 1 else -1, 1)


def behind(v, d):
    if d == 0:
        return roll(v, 1, 0)
    return roll(v, 32 if d == 1 else 1, 1)


def mid_setup(pos, scal, cfm, sel, faces, inv, diag):
    place = lanes((16, 1024))
    x_at = lax.broadcasted_iota(jnp.int32, (16, 1024), 0)
    y_at = pos[0] * 8 - 12 + place // 32
    z_at = pos[1] * 8 - 12 + place % 32
    domain = (y_at >= 0) & (y_at < NY) & (z_at >= 0) & (z_at < NZ)
    known = domain & (place >= 128) & (place < 896) & (place % 32 >= 4) & (place % 32 < 28)
    lasts = (x_at < NX - 1, y_at < NY - 1, z_at < NZ - 1)
    for d in range(3):
        is_open = domain & lasts[d] & (cfm[64 + 16 * d : 80 + 16 * d, :] == 0.0)
        sel[d] = jnp.where(is_open, cfm[16 + 16 * d : 32 + 16 * d, :], 4.0)
    coef = cfm[0:16, :]

    for d in range(3):
        for c in range(8):
            at = slice(128 * c, 128 * c + 128)
            kind = sel[d, :, at]
            ones = [kind == float(k) for k in range(KINDS)]
            for i in range(4):
                for j in range(i, 4):
                    value = jnp.zeros((16, 128), F32)
                    for k in range(KINDS):
                        value = jnp.where(ones[k], scal[64 + 16 * k + 4 * i + j], value)
                    faces[d, 4 * i + j, :, at] = value
    if inv is None:
        return known
    for i in range(8):
        total = coef * scal[9 * i]
        for d in range(3):
            if i in HIGHS[d]:
                total = total + faces[d, 5 * HIGHS[d].index(i)]
            else:
                total = total + behind(faces[d, 5 * LOWS[d].index(i)], d)
        if diag is not None:
            diag[i] = total
        inv[i] = jnp.where(known, 1.0 / total, 0.0)
    return known


def mid_apply(v, r, scal, cfm, faces, jump, flux):
    for d in range(3):
        for j in range(4):
            jump[j] = v[HIGHS[d][j]] - ahead(v[LOWS[d][j]], d)

        for c in range(8):
            at = slice(128 * c, 128 * c + 128)
            jumps = [jump[j, :, at] for j in range(4)]
            for i in range(4):
                total = faces[d, i, :, at] * jumps[0]
                for j in range(1, 4):
                    total = total + faces[d, 4 * min(i, j) + max(i, j), :, at] * jumps[j]
                flux[4 * d + i, :, at] = total

    for c in range(1, 7):
        at = slice(128 * c, 128 * c + 128)
        values = [v[j, :, at] for j in range(8)]
        coef = cfm[0:16, at]
        for i in range(8):
            total = scal[8 * i] * values[0]
            for j in range(1, 8):
                total = total + scal[8 * i + j] * values[j]
            r[i, :, at] = r[i, :, at] - coef * total
    for d in range(3):
        for j in range(4):
            value = flux[4 * d + j]
            r[HIGHS[d][j]] = r[HIGHS[d][j]] - value
            r[LOWS[d][j]] = r[LOWS[d][j]] + behind(value, d)


def mid_step(step, u, r, sol, inv):
    keep, gain = STEPS[step]
    for i in range(8):
        new = keep * u[i] + gain * (inv[i] * r[i])
        u[i] = new
        sol[i] = sol[i] + new


def mid_pre_body(
    pos, scal, slab, below, above, cfm, sol_out, r_out, coarse, send_up, send_down,
    sel, faces, inv, diag, u, sol, r, jump, flux, sems,
):
    for i in range(8):
        rows = slice(16 * i, 16 * i + 16)
        for m in range(3):
            u[i, :, 128 * m : 128 * m + 128] = below[128 * m + 16 * i : 128 * m + 16 * i + 16, :]
            u[i, :, 128 * (m + 5) : 128 * (m + 6)] = above[128 * m + 16 * i : 128 * m + 16 * i + 16, :]
        u[i, :, 384:640] = slab[rows, :]
    mid_setup(pos, scal, cfm, sel, faces, inv, diag)
    for i in range(8):
        r[i] = (MIDDLE * diag[i]) * u[i]
        sol[i] = u[i]
    mid_apply(u, r, scal, cfm, faces, jump, flux)
    mid_step(0, u, r, sol, inv)
    mid_apply(u, r, scal, cfm, faces, jump, flux)
    mid_step(1, u, r, sol, inv)
    copies = [
        pltpu.make_async_copy(sol, sol_out, sems.at[0]),
        pltpu.make_async_copy(r, r_out, sems.at[1]),
    ]
    copies[0].start()
    mid_apply(u, r, scal, cfm, faces, jump, flux)
    copies[1].start()
    total = r[0]
    for i in range(1, 8):
        total = total + r[i]
    coarse[0] = total
    center = cfm[0:16, :] * scal[128]
    for d in range(3):
        kind = sel[d]
        value = jnp.zeros((16, 1024), F32)
        for k in range(KINDS):
            value = jnp.where(kind == float(k), scal[129 + k], value)
        coarse[2 + d] = value
        center = center + value + behind(value, d)
    coarse[1] = center
    l32 = lanes((16, 768)) % 32
    for out, first in ((send_up, 6), (send_down, 18)):
        acc = jnp.zeros((16, 768), F32)
        for f in range(4):
            acc = jnp.where(l32 // 8 == f, roll(coarse[f, :, 128:896], 8 * f - first), acc)
        out[0] = acc
        out[1] = roll(coarse[4, :, 128:896], -first)
    for copy in copies:
        copy.wait()


def coarse_z_body(own, dn, up, slab, fwd, bwd):
    lane = lanes((16, 128))
    for f in range(5):
        part = 0 if f < 4 else 1
        shift = 8 * f if f < 4 else 0
        for m in range(10):
            acc = jnp.zeros((16, 128), F32)
            for n in range(2):
                y = 2 * m + n - 6
                tile, at = (y + 12) // 4, 32 * ((y + 12) % 4)
                to = 64 * n
                mine = own[f, :, 128 * tile : 128 * tile + 128]
                left = dn[part, :, 128 * (tile - 1) : 128 * tile]
                right = up[part, :, 128 * (tile - 1) : 128 * tile]
                acc = jnp.where(
                    (lane >= to + 22) & (lane < to + 42), roll(mine, to + 22 - (at + 6)), acc
                )
                acc = jnp.where(
                    (lane >= to + 14) & (lane < to + 22), roll(left, to + 14 - (at + shift)), acc
                )
                acc = jnp.where(
                    (lane >= to + 42) & (lane < to + 50), roll(right, to + 42 - (at + shift)), acc
                )
            slab[f, :, 128 * m : 128 * m + 128] = acc
            if m < 4:
                fwd[f, :, 128 * m : 128 * m + 128] = acc
            if m >= 6:
                bwd[f, :, 128 * (m - 6) : 128 * (m - 5)] = acc


def two_sum(a, b):
    s = a + b
    t = s - a
    return s, (a - (s - t)) + (b - t)


def halves(a):
    t = a * 4097.0
    high = t - (t - a)
    return high, a - high


def two_prod(a, b):
    ah, al = halves(a)
    bh, bl = halves(b)
    p = a * b
    return p, ((ah * bh - p) + ah * bl + al * bh) + al * bl


def pair_mul(a, b):
    p, e = two_prod(a[0], b[0])
    return two_sum(p, e + (a[0] * b[1] + a[1] * b[0]))


def pair_sub(a, b):
    s, e = two_sum(a[0], -b[0])
    return two_sum(s, e + (a[1] - b[1]))


def pair_div(a, b):
    first = a[0] / b[0]
    rest = pair_sub(a, pair_mul((first, jnp.zeros_like(first)), b))
    return two_sum(first, rest[0] / b[0])


START = (0, 9, 17, 24, 30, 35, 39, 42)
PAIRS = sum(9 - i for i in range(BASIS))


def krylov_body(scal, own, below, above, basis_out, gram, basis, field, hold, sem):
    for f in range(5):
        field[f, :, 0:512] = below[f]
        field[f, :, 512:1792] = own[f]
        field[f, :, 1792:2304] = above[f]
    center, half = scal[133], scal[134]
    lane8 = lanes((8, 128))

    def apply(v):
        total = field[1] * v
        for d in range(3):
            cond = field[2 + d]
            axis, step = ((0, 1), (1, 64), (1, 1))[d]
            total = total - cond * roll(v, -step, axis) - roll(cond * v, step, axis)
        return total

    def compact(v):
        acc = jnp.zeros((8, 128), F32)
        for t in range(2):
            for y in range(8):
                tile, at = (y + 14) // 2, 64 * ((y + 14) % 2) + 28
                to = 64 * t + 8 * y
                piece = v[8 * t : 8 * t + 8, 128 * tile : 128 * tile + 128]
                acc = jnp.where((lane8 >= to) & (lane8 < to + 8), roll(piece, to - at), acc)
        return acc

    before = None
    now = field[0]
    for j in range(BASIS):
        basis[j] = now[:, 384:1920]
        hold[j] = compact(now)
        image = apply(now)
        hold[BASIS + j] = compact(image)
        if j + 1 < BASIS:
            nxt = (image - center * now) * half
            if j > 0:
                nxt = 2.0 * nxt - before
            before, now = now, nxt
    copy = pltpu.make_async_copy(basis, basis_out, sem)
    copy.start()
    high_rows, low_rows = [], []
    for i in range(BASIS):
        for j in range(i, BASIS + 1):
            other = hold[BASIS + j] if j < BASIS else hold[0]
            p, e = two_prod(hold[i], other)
            high_rows.append(p)
            low_rows.append(e)
    high = jnp.stack(high_rows)
    low = jnp.stack(low_rows)
    for axis, shifts in ((1, (4, 2, 1)), (2, (64, 32, 16, 8, 4, 2, 1))):
        for s in shifts:
            high, e = two_sum(high, roll(high, s, axis))
            low = low + roll(low, s, axis) + e
    row = jnp.zeros((8, 128), F32)
    for n in range(PAIRS):
        row = jnp.where(lane8 == n, high[n], row)
        row = jnp.where(lane8 == 64 + n, low[n], row)
    for m in range(64):
        gram[8 * m : 8 * m + 8, :] = row
    copy.wait()


def mid_post(
    pos, scal, gram, basis, cfm, out, sel, faces, inv, u, r, sol, jump, flux, wait_basis, wait_level
):
    high = gram[...].reshape(64, 8, 128)
    low = jnp.zeros((64, 8, 128), F32)
    count = 64
    while count > 1:
        count //= 2
        high, e = two_sum(high[:count], high[count : 2 * count])
        low = low[:count] + low[count : 2 * count] + e
    high, low = high[0], low[0]
    for s in (4, 2, 1):
        high, e = two_sum(high, roll(high, s, 0))
        low = low + roll(low, s, 0) + e
    low = low + roll(high, 64)
    high, low = two_sum(high, low)
    lane = lanes((8, 128))
    sub = lax.broadcasted_iota(jnp.int32, (8, 128), 0)
    mat_h = jnp.zeros((8, 128), F32)
    mat_l = jnp.zeros((8, 128), F32)
    for i in range(BASIS):
        here = (sub == i) & (lane >= i) & (lane <= BASIS)
        mat_h = jnp.where(here, roll(high, i - START[i]), mat_h)
        mat_l = jnp.where(here, roll(low, i - START[i]), mat_l)
        for j in range(i + 1, BASIS):
            here = (sub == j) & (lane == i)
            shift = i - (START[i] + j - i)
            mat_h = jnp.where(here, roll(high, shift), mat_h)
            mat_l = jnp.where(here, roll(low, shift), mat_l)

    def spread_at(v, row, col):
        return jnp.broadcast_to(v[row : row + 1, col : col + 1], (8, 128))

    answers = []
    pivots = []
    for k in range(BASIS):
        start = spread_at(high, 0, START[k])
        piv = (spread_at(mat_h, k, k), spread_at(mat_l, k, k))
        good = jnp.abs(piv[0]) > 1e-12 * jnp.abs(start)
        safe = (jnp.where(good, piv[0], 1.0), jnp.where(good, piv[1], 0.0))
        pivots.append((safe, good))
        row = (
            jnp.broadcast_to(mat_h[k : k + 1, :], (8, 128)),
            jnp.broadcast_to(mat_l[k : k + 1, :], (8, 128)),
        )
        col = (
            jnp.broadcast_to(mat_h[:, k : k + 1], (8, 128)),
            jnp.broadcast_to(mat_l[:, k : k + 1], (8, 128)),
        )
        factor = pair_div(col, safe)
        use = good & (sub != k)
        factor = (jnp.where(use, factor[0], 0.0), jnp.where(use, factor[1], 0.0))
        mat_h, mat_l = pair_sub((mat_h, mat_l), pair_mul(factor, row))
    for k in range(BASIS):
        safe, good = pivots[k]
        value = pair_div((spread_at(mat_h, k, BASIS), spread_at(mat_l, k, BASIS)), safe)[0]
        answers.append(jnp.where(good, value, 0.0))
    wait_basis()
    weights = [jnp.concatenate([a, a], axis=0) for a in answers]
    lane16 = lanes((16, 128))
    tiles = []
    for m in range(12):
        total = weights[0] * basis[0, :, 128 * m : 128 * m + 128]
        for j in range(1, BASIS):
            total = total + weights[j] * basis[j, :, 128 * m : 128 * m + 128]
        tiles.append(total)
    for m in range(8):
        acc = jnp.zeros((16, 128), F32)
        if 1 <= m <= 6:
            for n in range(4):
                y = 4 * m + n - 12
                tile, at = (y + 14) // 2 - 3, 64 * ((y + 14) % 2)
                to = 32 * n
                acc = jnp.where(
                    (lane16 >= to + 5) & (lane16 < to + 27), roll(tiles[tile], to + 5 - (at + 21)), acc
                )
        for i in range(8):
            u[i, :, 128 * m : 128 * m + 128] = acc
    mid_setup(pos, scal, cfm, sel, faces, inv, None)
    wait_level()
    for i in range(8):
        sol[i] = sol[i] + u[i]
    mid_apply(u, r, scal, cfm, faces, jump, flux)
    for i in range(8):
        new = inv[i] * r[i] / MIDDLE
        u[i] = new
        sol[i] = sol[i] + new
    mid_apply(u, r, scal, cfm, faces, jump, flux)
    mid_step(0, u, r, sol, inv)
    mid_apply(u, r, scal, cfm, faces, jump, flux)
    mid_step(1, u, r, sol, inv)
    for i in range(8):
        for half in range(2):
            acc = jnp.zeros((16, 128), F32)
            for n in range(8):
                y = 8 * half + n - 4
                tile, at = (y + 12) // 4, 32 * ((y + 12) % 4) + 8
                acc = jnp.where(
                    lane16 // 16 == n,
                    roll(sol[i, :, 128 * tile : 128 * tile + 128], 16 * n - at),
                    acc,
                )
            out[128 * half + 16 * i : 128 * half + 16 * i + 16, :] = acc


def post_body(
    pos, scal, gram, basis_in, cfm, mid_pre, mid_res, pre, frz_in, below, above, w_in, coef_in,
    inv_in, wide, spread, lift, out,
    basis, sel, faces, mid_inv, mid_u, mid_r, mid_sol, jump, flux, mid,
    frz, w, coef, inv, u, r, sol, px, qx, sems,
):
    copies = [
        pltpu.make_async_copy(source, to, sems.at[n])
        for n, (source, to) in enumerate(
            (
                (basis_in, basis),
                (mid_pre, mid_sol),
                (mid_res, mid_r),
                (frz_in, frz),
                (pre, sol),
                (w_in, w),
                (coef_in, coef),
                (inv_in, inv),
            )
        )
    ]
    for copy in copies:
        copy.start()

    def wait_level():
        copies[1].wait()
        copies[2].wait()

    mid_post(
        pos, scal, gram, basis, cfm, mid, sel, faces, mid_inv, mid_u, mid_r, mid_sol, jump, flux,
        copies[0].wait, wait_level,
    )
    for copy in copies[3:]:
        copy.wait()
    low = lanes((64, 128)) < 64
    px[:, 0:256] = jnp.zeros((16, 256), F32)
    qx[:, NX * 256 :] = jnp.zeros((16, 256), F32)
    for x in range(NX):
        first, second = slice(256 * x, 256 * x + 128), slice(256 * x + 128, 256 * x + 256)
        turned = roll(frz[x], 64)
        at = 384 + 64 * (x % 8)
        down = below[at : at + 64, :]
        over = above[at : at + 64, :]
        if x >= 8:
            down = roll(down, 64)
        else:
            over = roll(over, 64)
        r[:, first] = jnp.where(low, down, turned)
        r[:, second] = jnp.where(low, turned, over)
    planes = CHUNK // 256
    for c in range(CHUNKS):
        at = slice(CHUNK * c, CHUNK * (c + 1))
        pieces = [
            mid[pl.ds(128 * half + planes * c + n, 8, stride=16), :]
            for n in range(planes)
            for half in range(2)
        ]
        high, rest = split3(jnp.concatenate(pieces, axis=1))
        stacked = jnp.concatenate([high, rest, high, jnp.zeros((8, CHUNK), F32)], axis=0)
        lifted = mm(lift[...], stacked.astype(BF16))
        u[:, at] = lifted
        sol[:, at] = sol[:, at] + lifted
    fine_apply(u, r, w, coef, wide, spread, px, qx, None, sol, inv)
    for c in range(CHUNKS):
        at = slice(CHUNK * c, CHUNK * (c + 1))
        new = inv[:, at] * r[:, at] / MIDDLE
        u[:, at] = new
        sol[:, at] = sol[:, at] + new
    fine_apply(u, r, w, coef, wide, spread, px, qx, 0, sol, inv)
    fine_apply(u, r, w, coef, wide, spread, px, qx, 1, sol, inv)
    fine_apply(u, r, w, coef, wide, spread, px, qx, None, sol, inv)
    lane = lanes((64, 128))
    for x in range(NX):
        acc = jnp.zeros((64, 128), F32)
        for part, ref in enumerate((sol, r)):
            for y in range(8):
                half, at = (y + 4) // 8, 16 * ((y + 4) % 8) + 4
                start = 256 * x + 128 * half
                acc = jnp.where(
                    lane // 8 == 8 * part + y,
                    roll(ref[:, start : start + 128], 64 * part + 8 * y - at),
                    acc,
                )
        out[x] = acc


def unpack_body(got, first, second):
    low = lanes((64, 128)) < 64
    for part, out in enumerate((first, second)):
        held = []
        for g in range(8):
            a, b = got[g], got[g + 8]
            if part == 0:
                held.append(jnp.where(low, a, roll(b, 64)))
            else:
                held.append(jnp.where(low, roll(a, 64), b))
        for y, rows in enumerate(exchange(held, 8)):
            out[pl.ds(y, 64, stride=8), :] = rows


def trace_tables():
    high = np.zeros((3, 16, 64), np.float32)
    low = np.zeros((3, 16, 64), np.float32)
    for p in range(4):
        for q in range(4):
            for d in range(3):
                for table, at in ((high, 3), (low, 0)):
                    index = [p, q]
                    index.insert(d, at)
                    table[d, 4 * p + q, 16 * index[0] + 4 * index[1] + index[2]] = 1.0
    return high, low


def mid_traces():
    high = np.zeros((3, 4, 8), np.float32)
    low = np.zeros((3, 4, 8), np.float32)
    for d in range(3):
        for n in range(4):
            high[d, n, HIGHS[d][n]] = 1.0
            low[d, n, LOWS[d][n]] = 1.0
    return high, low


def prolong_tables():
    node_points = jnp.array(
        [-1.0, -1.0 / math.sqrt(5.0), 1.0 / math.sqrt(5.0), 1.0], dtype=jnp.float32
    )
    basis_table = jnp.stack([(1.0 - node_points) * 0.5, (1.0 + node_points) * 0.5], axis=1)
    volume = (
        basis_table[:, None, None, :, None, None]
        * basis_table[None, :, None, None, :, None]
        * basis_table[None, None, :, None, None, :]
    ).reshape(64, 8)
    surface = (basis_table[:, None, :, None] * basis_table[None, :, None, :]).reshape(16, 4)
    return (volume, surface)


def cut(x):
    return lax.reduce_precision(x, 8, 7)


def two_parts(x):
    high = cut(x)
    return high, cut(x - high)


def three_parts(x):
    high = cut(x)
    rest = x - high
    mid = cut(rest)
    return high, mid, cut(rest - mid)


def tables(element, faces):
    volume, surface = prolong_tables()
    elem_mid = jnp.dot(volume.T, jnp.dot(element, volume, precision=HIGHEST), precision=HIGHEST)
    face_mid = jnp.einsum("kij,jb->kib", faces, surface, precision=HIGHEST)
    face_mid = jnp.einsum("ia,kib->kab", surface, face_mid, precision=HIGHEST)
    elem_coarse = jnp.sum(elem_mid)
    face_coarse = jnp.sum(face_mid, axis=(1, 2))
    high, low = trace_tables()
    both = np.concatenate([high, low], axis=0)
    rows = jnp.einsum("kij,djm->dkim", faces, both, precision=HIGHEST).reshape(384, 64)
    wide = jnp.concatenate([element, rows], axis=0)
    wh, wl = two_parts(wide)
    wide = jnp.concatenate([wh, wh, wl], axis=1).astype(BF16)
    spread = np.concatenate([high[1], -low[1], high[2], -low[2]], axis=0).T
    spread = np.concatenate([spread, spread], axis=1)
    face_diag = jnp.diagonal(faces, axis1=1, axis2=2)
    diag = jnp.einsum("dim,ki->mdk", both, face_diag, precision=HIGHEST).reshape(64, 24)
    diag_w = jnp.concatenate(three_parts(diag) + (jnp.zeros((64, 8), F32),), axis=1).astype(BF16)
    diag_e = jnp.diagonal(element)[:, None]
    mh, ml = mid_traces()
    both = np.concatenate([mh, ml], axis=0)
    diag = jnp.einsum(
        "dim,ki->mdk", both, jnp.diagonal(face_mid, axis1=1, axis2=2), precision=HIGHEST
    ).reshape(8, 24)
    mid_diag_w = jnp.concatenate(three_parts(diag) + (jnp.zeros((8, 8), F32),), axis=1).astype(BF16)
    mid_diag_e = jnp.diagonal(elem_mid)[:, None]
    vh, vl = two_parts(volume)
    down = jnp.concatenate([vh.T, vh.T, vl.T], axis=1).astype(BF16)
    lift = jnp.concatenate([vh, vh, vl, jnp.zeros((64, 8), F32)], axis=1).astype(BF16)
    least = 0.1 * elem_coarse
    most = 1.35 * elem_coarse + 9.0 * jnp.max(jnp.abs(face_coarse))
    half = 0.5 * (most - least)
    half = jnp.where(jnp.abs(half) > 0.0, half, 1.0)
    scal = jnp.concatenate(
        [
            elem_mid.reshape(-1),
            face_mid.reshape(-1),
            elem_coarse[None],
            face_coarse,
            (0.5 * (most + least))[None],
            (1.0 / half)[None],
            jnp.zeros((9,), F32),
        ]
    )
    return (
        wide,
        jnp.asarray(spread, BF16),
        diag_w,
        diag_e,
        down,
        mid_diag_w,
        mid_diag_e,
        lift,
        scal,
    )


def local(residual, coefficient, element, faces, kind, flag):
    shift_up = [(i, i + 1) for i in range(15)]
    shift_dn = [(i + 1, i) for i in range(15)]

    def z_index(zb):
        return (zb % 16) * 2 + zb // 16

    z_up = [(z_index(i), z_index(i + 1)) for i in range(31)]
    z_dn = [(z_index(i + 1), z_index(i)) for i in range(31)]
    z_axes = ("gx", "lvl")
    side = lax.axis_index("lvl")
    pos = jnp.stack(
        [
            lax.axis_index("yz"),
            side * 16 + lax.axis_index("gx"),
        ]
    ).astype(jnp.int32)
    res = residual.reshape(512, 128)
    none = jnp.zeros_like(coefficient)
    cf = jnp.concatenate(
        [coefficient]
        + [v[n].astype(F32) for v in (kind, flag) for n in (1, 3, 5)]
        + [none, none, none]
        + [kind[n].astype(F32) for n in (2, 4)]
        + [none]
        + [flag[n].astype(F32) for n in (2, 4)]
        + [none],
        axis=0,
    ).reshape(128, 128)
    slots = call(slots_body, "slots", [f32s(16, 40, 128)], (0, 0))(res, cf)[0]
    element, faces, slots = lax.optimization_barrier((element, faces, slots))
    wide, spread, diag_w, diag_e, down, mid_diag_w, mid_diag_e, lift, scal = tables(element, faces)
    own = lax.all_to_all(slots, "gx", 0, 0, tiled=True)
    dn = lax.ppermute(own, z_axes, z_up)
    up = lax.ppermute(own, z_axes, z_dn)
    place_values, place_kinds = place_tables()
    rows, own, bwd = call(
        join_body,
        "join",
        [f32s(NX, 64, 128), f32s(896, 128), f32s(768, 128)],
        (0,) * 5,
    )(own, dn, up, jnp.asarray(place_values, BF16), jnp.asarray(place_kinds, BF16))
    below = lax.ppermute(own, "yz", shift_up)
    above = lax.ppermute(bwd, "yz", shift_dn)
    plane = (64, NX * 256)
    strip = (16, NX * 256 + 256)
    pre, r, w, coef, inv, cfm, send_up, send_down = call(
        fine_pre_body,
        "fine_pre",
        [
            f32s(*plane),
            f32s(*plane),
            f32s(24, NX * 256),
            f32s(8, NX * 256),
            f32s(*plane),
            f32s(128, 1024),
            f32s(512, 128),
            f32s(512, 128),
        ],
        (1,) + (0,) * 11,
        [
            pltpu.VMEM(plane, F32),
            pltpu.VMEM((24, NX * 256), F32),
            pltpu.VMEM((8, NX * 256), F32),
            pltpu.VMEM(plane, F32),
            pltpu.VMEM(plane, F32),
            pltpu.VMEM(strip, F32),
            pltpu.VMEM(strip, F32),
            pltpu.VMEM((896, 128), F32),
            pltpu.SemaphoreType.DMA((4,)),
        ],
        (2, 0, 2, 2, 2, 0, 0, 0),
    )(pos, rows, own, below, above, wide, spread, diag_w, diag_e, down, mid_diag_w, mid_diag_e)
    dn = lax.ppermute(send_up, z_axes, z_up)
    up = lax.ppermute(send_down, z_axes, z_dn)
    slab, fwd, bwd, frz = call(
        mid_z_body,
        "mid_z",
        [f32s(128, 256), f32s(896, 128), f32s(896, 128), f32s(NX, 64, 128)],
        (0,) * 4,
        [pltpu.VMEM((NX, 64, 128), F32), pltpu.SemaphoreType.DMA],
        (0, 0, 0, 2),
    )(send_up, dn, up, r)
    below = lax.ppermute(fwd, "yz", shift_up)
    above = lax.ppermute(bwd, "yz", shift_dn)
    mid = (8, 16, 1024)
    mid_scratch = [
        pltpu.VMEM((3, 16, 1024), F32),
        pltpu.VMEM((3, 16, 16, 1024), F32),
        pltpu.VMEM(mid, F32),
    ]
    tail_scratch = [pltpu.VMEM((4, 16, 1024), F32), pltpu.VMEM((12, 16, 1024), F32)]
    mid_pre, mid_res, coarse, send_up, send_down = call(
        mid_pre_body,
        "mid_pre",
        [f32s(*mid), f32s(*mid), f32s(5, 16, 1024), f32s(2, 16, 768), f32s(2, 16, 768)],
        (1, 1, 0, 0, 0, 0),
        mid_scratch
        + [pltpu.VMEM(mid, F32)] * 4
        + tail_scratch
        + [pltpu.SemaphoreType.DMA((2,))],
        (2, 2, 0, 0, 0),
    )(pos, scal, slab, below, above, cfm)
    dn = lax.ppermute(send_up, z_axes, z_up)
    up = lax.ppermute(send_down, z_axes, z_dn)
    coarse_slab, fwd, bwd = call(
        coarse_z_body,
        "coarse_z",
        [f32s(5, 16, 1280), f32s(5, 16, 512), f32s(5, 16, 512)],
        (0, 0, 0),
    )(coarse, dn, up)
    coarse_below = lax.ppermute(fwd, "yz", shift_up)
    coarse_above = lax.ppermute(bwd, "yz", shift_dn)
    basis, gram = call(
        krylov_body,
        "krylov",
        [f32s(BASIS, 16, 1536), f32s(512, 128)],
        (1, 0, 0, 0),
        [
            pltpu.VMEM((BASIS, 16, 1536), F32),
            pltpu.VMEM((5, 16, 2304), F32),
            pltpu.VMEM((2 * BASIS, 8, 128), F32),
            pltpu.SemaphoreType.DMA,
        ],
        (2, 0),
    )(scal, coarse_slab, coarse_below, coarse_above)
    grams = lax.all_to_all(gram, ("gx", "yz", "lvl"), 0, 0, tiled=True)
    packed = call(
        post_body,
        "post",
        [f32s(16, 64, 128)],
        (1, 1, 0, 2, 0, 2, 2, 2, 2, 0, 0, 2, 2, 2, 0, 0, 0),
        [pltpu.VMEM((BASIS, 16, 1536), F32)]
        + mid_scratch
        + [pltpu.VMEM(mid, F32)] * 3
        + tail_scratch
        + [
            pltpu.VMEM((256, 128), F32),
            pltpu.VMEM((NX, 64, 128), F32),
            pltpu.VMEM((24, NX * 256), F32),
            pltpu.VMEM((8, NX * 256), F32),
            pltpu.VMEM(plane, F32),
            pltpu.VMEM(plane, F32),
            pltpu.VMEM(plane, F32),
            pltpu.VMEM(plane, F32),
            pltpu.VMEM(strip, F32),
            pltpu.VMEM(strip, F32),
            pltpu.SemaphoreType.DMA((8,)),
        ],
    )(
        pos, scal, grams, basis, cfm, mid_pre, mid_res, pre, frz, below, above, w, coef, inv,
        wide, spread, lift,
    )[0]
    got = lax.all_to_all(packed, "gx", 0, 0, tiled=True)
    correction, rest = call(unpack_body, "unpack", [f32s(512, 128), f32s(512, 128)], (0,))(got)
    return (correction.reshape(64, 1, 8, 128), rest.reshape(64, 1, 8, 128))


def solution(mesh):
    in_specs = (
        P(None, "gx", "yz", "lvl"),
        P("gx", "yz", "lvl"),
        P(),
        P(),
        P(None, "gx", "yz", "lvl"),
        P(None, "gx", "yz", "lvl"),
    )
    out_specs = (P(None, "gx", "yz", "lvl"), P(None, "gx", "yz", "lvl"))
    return jax.shard_map(local, mesh=mesh, in_specs=in_specs, out_specs=out_specs, check_vma=False)
```

```python
import functools
import math

import jax
import jax.numpy as jnp
import numpy as np
from jax import lax
from jax.experimental import pallas as pl
from jax.experimental.pallas import tpu as pltpu
from jax.sharding import PartitionSpec as P

NX = 16
NY = 128
NZ = 256
KINDS = 4
F32 = jnp.float32
BF16 = jnp.bfloat16
HIGHEST = lax.Precision.HIGHEST
LOW_EIG = 0.3
HIGH_EIG = 3.0
MIDDLE = 0.5 * (HIGH_EIG + LOW_EIG)
SPREAD = 0.5 * (HIGH_EIG - LOW_EIG)
SCALED = MIDDLE / SPREAD
RHO0 = 1.0 / SCALED
RHO1 = 1.0 / (2.0 * SCALED - RHO0)
RHO2 = 1.0 / (2.0 * SCALED - RHO1)
STEPS = ((RHO1 * RHO0, 2.0 * RHO1 / SPREAD), (RHO2 * RHO1, 2.0 * RHO2 / SPREAD))
BASIS = 8
VMEM_LIMIT = 24 * 2**20


def lanes(shape):
    return lax.broadcasted_iota(jnp.int32, shape, len(shape) - 1)


def roll(x, shift, axis=None):
    axis = x.ndim - 1 if axis is None else axis
    shift = shift % x.shape[axis]
    return x if shift == 0 else pltpu.roll(x, shift, axis)


SPACES = {
    0: pl.BlockSpec(memory_space=pltpu.VMEM),
    1: pl.BlockSpec(memory_space=pltpu.SMEM),
    2: pl.BlockSpec(memory_space=pltpu.HBM),
}


def call(body, name, out_shape, in_specs, scratch=(), out_specs=None):
    out_specs = out_specs or (0,) * len(out_shape)
    return pl.pallas_call(
        body,
        out_shape=list(out_shape),
        in_specs=[SPACES[i] for i in in_specs],
        out_specs=[SPACES[i] for i in out_specs],
        scratch_shapes=list(scratch),
        compiler_params=pltpu.CompilerParams(vmem_limit_bytes=VMEM_LIMIT),
        cost_estimate=pl.CostEstimate(flops=1000000, bytes_accessed=1000000, transcendentals=0),
        name=name,
    )


def f32s(*shape):
    return jax.ShapeDtypeStruct(shape, F32)


def split3(x):
    high = x.astype(BF16).astype(F32)
    low = x - high
    return high, low


def stack_hlh(x):
    high, low = split3(x)
    return jnp.concatenate([high, low, high], axis=0).astype(BF16)


def mm(a, b):
    return jnp.dot(a, b, preferred_element_type=F32)


def exchange(arrays, lane_block):
    arrays = list(arrays)
    group = lanes(arrays[0].shape) // lane_block
    for bit in (1, 2, 4):
        upper = (group // bit) % 2 == 1
        for n in range(8):
            if n & bit:
                continue
            a, b = arrays[n], arrays[n | bit]
            arrays[n] = jnp.where(upper, roll(b, lane_block * bit), a)
            arrays[n | bit] = jnp.where(upper, b, roll(a, -lane_block * bit))
    return arrays


def slots_body(res, coef, kind, flag, out, cf):
    for n in range(16):
        cf[8 * n : 8 * n + 8, :] = jnp.zeros((8, 128), F32)
    cf[0:8, :] = coef[...]
    for first, ref in ((8, kind), (32, flag)):
        for n in range(3):
            at = 8 * (2 * n + 1)
            cf[first + 8 * n : first + 8 * n + 8, :] = ref[at : at + 8, :].astype(F32)
    for first, ref in ((80, kind), (104, flag)):
        for n in range(2):
            at = 8 * (2 * n + 2)
            cf[first + 8 * n : first + 8 * n + 8, :] = ref[at : at + 8, :].astype(F32)
    low = lanes((32, 128)) < 64
    low8 = lanes((8, 128)) < 64
    values = exchange([res[pl.ds(y, 64, stride=8), :] for y in range(8)], 8)
    kinds = exchange([cf[pl.ds(y, 16, stride=8), :] for y in range(8)], 8)
    for j in range(8):
        a, b = values[j][0:32], values[j][32:64]
        out[j, 0:32, :] = jnp.where(low, a, roll(b, 64))
        out[j + 8, 0:32, :] = jnp.where(low, roll(a, 64), b)
        a, b = kinds[j][0:8], kinds[j][8:16]
        out[j, 32:40, :] = jnp.where(low8, a, roll(b, 64))
        out[j + 8, 32:40, :] = jnp.where(low8, roll(a, 64), b)


def place_tables():
    values = np.zeros((256, 256), np.float32)
    kinds = np.zeros((384, 512), np.float32)
    for half in range(2):
        for y in range(8):
            for z in range(8):
                lane = 64 * half + 8 * y + z
                values[lane, 128 * half + 16 * y + z + 4] = 1.0
                beside = z + 12 if z < 4 else z - 4
                values[128 + lane, 128 * half + 16 * y + beside] = 1.0
                for n, first in enumerate((12, 4, 20)):
                    kinds[128 * n + lane, 256 * half + 32 * y + first + z] = 1.0
    return values, kinds


def three_rows(x):
    high = x.astype(BF16).astype(F32)
    rest = x - high
    mid = rest.astype(BF16).astype(F32)
    return jnp.concatenate([high, mid, rest - mid], axis=0).astype(BF16)


def moved(x, table):
    count = x.shape[0]
    out = mm(three_rows(x), table)
    return out[0:count] + out[count : 2 * count] + out[2 * count :]


def join_body(own, dn, up, place_values, place_kinds, rows, fwd, bwd):
    near = lanes((512, 128)) % 8 < 4
    mine = own[:, 0:32, :].reshape(512, 128)
    beside = jnp.where(near, up[:, 0:32, :].reshape(512, 128), dn[:, 0:32, :].reshape(512, 128))
    out = moved(jnp.concatenate([mine, beside], axis=1), place_values[...])
    for x in range(NX):
        rows[x, 0:32, :] = out[32 * x : 32 * x + 32, 0:128]
        rows[x, 32:64, :] = out[32 * x : 32 * x + 32, 128:256]
    low = lanes((64, 128)) < 64
    for x in range(8):
        fwd[64 * x : 64 * x + 64, :] = jnp.where(low, roll(rows[x], 64), rows[x + 8])
        bwd[64 * x : 64 * x + 64, :] = jnp.where(low, rows[x], roll(rows[x + 8], 64))
    kinds = jnp.concatenate([v[:, 32:40, :].reshape(128, 128) for v in (own, dn, up)], axis=1)
    out = moved(kinds, place_kinds[...])
    array = lax.broadcasted_iota(jnp.int32, (128, 128), 0) % 8
    edge = (lanes((128, 128)) % 32 == 3) & ((array == 3) | (array == 6))
    for h in range(2):
        minus = out[:, 256 + 128 * h : 384 + 128 * h]
        plus = jnp.where(edge, roll(minus, -1), out[:, 128 * h : 128 * h + 128])
        fwd[512 + 128 * h : 640 + 128 * h, :] = plus
        bwd[512 + 128 * h : 640 + 128 * h, :] = plus
    fwd[768:896, :] = out[:, 256:384]


CHUNK = 4096
CHUNKS = NX * 256 // CHUNK


def fine_apply(u, r, w, coef, wide, spread, px, qx, step, sol, inv):
    for c in range(CHUNKS):
        at = slice(CHUNK * c, CHUNK * (c + 1))
        after = slice(CHUNK * c + 256, CHUNK * (c + 1) + 256)
        prod = mm(wide[...], stack_hlh(u[:, at]))

        def pick(base, row):
            total = w[row : row + 1, at] * prod[base : base + 16]
            for k in range(1, KINDS):
                total = total + w[row + k : row + k + 1, at] * prod[base + 16 * k : base + 16 * k + 16]
            return total

        px[:, after] = pick(64, 0)
        py = pick(128, 4)
        pz = pick(192, 8)
        qx[:, at] = pick(256, 12)
        qy = pick(320, 16)
        qz = pick(384, 20)
        flux = jnp.concatenate(
            [py - roll(qy, -16), roll(py, 16) - qy, pz - roll(qz, -1), roll(pz, 1) - qz], axis=0
        )
        high, low = split3(flux)
        faces = mm(spread[...], jnp.concatenate([high, low], axis=0).astype(BF16))
        r[:, at] = r[:, at] - (coef[0:1, at] * prod[0:64] + faces)

    for c in range(CHUNKS):
        at = slice(CHUNK * c, CHUNK * (c + 1))
        after = slice(CHUNK * c + 256, CHUNK * (c + 1) + 256)
        r[48:64, at] = r[48:64, at] - (px[:, after] - qx[:, after])
        r[0:16, at] = r[0:16, at] + (px[:, at] - qx[:, at])
        if step is not None:
            keep, gain = STEPS[step]
            new = keep * u[:, at] + gain * (inv[:, at] * r[:, at])
            u[:, at] = new
            sol[:, at] = sol[:, at] + new


def fine_places(pos):
    place = lanes((1, 256))
    y_at = pos[0] * 8 - 4 + place // 16
    z_at = pos[1] * 8 - 4 + place % 16
    inside = (y_at >= 0) & (y_at < NY) & (z_at >= 0) & (z_at < NZ)
    return inside, inside & (y_at < NY - 1), inside & (z_at < NZ - 1)


def fine_weights(pos, coef, w):
    inside, has_y, has_z = fine_places(pos)
    w[12:16, 0:256] = jnp.zeros((4, 256), F32)
    for x in range(NX):
        at = slice(256 * x, 256 * x + 256)
        rows = coef[:, at]
        opens = [
            inside & (rows[4:5] == 0.0) if x < NX - 1 else jnp.zeros((1, 256), jnp.bool_),
            has_y & (rows[5:6] == 0.0),
            has_z & (rows[6:7] == 0.0),
        ]
        plus = [
            [jnp.where(opens[d] & (rows[1 + d : 2 + d] == float(k)), 1.0, 0.0) for k in range(KINDS)]
            for d in range(3)
        ]
        plus_all = jnp.concatenate(plus[0] + plus[1] + plus[2], axis=0)
        w[0:12, at] = plus_all
        if x < NX - 1:
            w[12:16, 256 * x + 256 : 256 * x + 512] = plus_all[0:4]
        w[16:20, at] = roll(plus_all[4:8], 16)
        w[20:24, at] = roll(plus_all[8:12], 1)


def kinds_of(w, at):
    ws = w[:, at]
    return jnp.concatenate([ws, ws, ws, jnp.zeros((8, CHUNK), F32)], axis=0).astype(BF16)


def fine_inverse(coef, w, diag_w, diag_e, inside, at):
    diag = diag_e[...] * coef[0:1, at] + mm(diag_w[...], kinds_of(w, at))
    return jnp.where(inside, 1.0 / diag, 0.0)


def compacted(first, second, lane):
    v = roll(jnp.where(lane < 64, roll(first, 64), roll(second, 64)), -4)
    for size in (8, 16, 32):
        v = jnp.where(lane % (4 * size) < size, v, roll(v, -size))
    return v


def fine_pre_body(
    pos,
    rows_in,
    own,
    below,
    above,
    wide,
    spread,
    diag_w,
    diag_e,
    down,
    mid_diag_w,
    mid_diag_e,
    keep,
    r,
    coef,
    cfm,
    send_up,
    send_down,
    sol,
    w,
    inv,
    u,
    px,
    qx,
    gather,
):
    low = lanes((64, 128)) < 64
    lane8 = lanes((8, 128))
    inside = fine_places(pos)[0]
    px[:, 0:256] = jnp.zeros((16, 256), F32)
    qx[:, NX * 256 :] = jnp.zeros((16, 256), F32)
    cfm[:, 896:1024] = jnp.zeros((128, 128), F32)
    array = lax.broadcasted_iota(jnp.int32, (8, 128), 0)
    edge = (lane8 >= 96) & ((array == 2) | (array == 5))
    for x in range(NX):
        first, second = slice(256 * x, 256 * x + 128), slice(256 * x + 128, 256 * x + 256)
        turned = roll(rows_in[x], 64)
        at = 64 * (x % 8)
        under = below[at : at + 64, :]
        over = above[at : at + 64, :]
        if x >= 8:
            under = roll(under, 64)
        else:
            over = roll(over, 64)
        r[:, first] = jnp.where(low, under, turned)
        r[:, second] = jnp.where(low, turned, over)
        blocks = [
            ref[512 + 128 * h + 8 * x : 520 + 128 * h + 8 * x, :]
            for ref in (below, own, above)
            for h in range(2)
        ]
        minus = below[768 + 8 * x : 776 + 8 * x, :]
        gather[pl.ds(x, 8, stride=16), :] = jnp.where(edge, roll(minus, 96), 0.0)
        for m in range(6):
            gather[pl.ds(128 * (m + 1) + x, 8, stride=16), :] = blocks[m]
        for half, at in enumerate((first, second)):
            acc = jnp.zeros((8, 128), F32)
            for row in range(8):
                n = 8 * half + row
                acc = jnp.where(
                    lane8 // 16 == row,
                    roll(blocks[1 + n // 4], 16 * row - (n % 4) * 32 - 8),
                    acc,
                )
            coef[:, at] = acc
    for m in range(7):
        cfm[:, 128 * m : 128 * m + 128] = gather[128 * m : 128 * m + 128, :]
    fine_weights(pos, coef, w)
    wide_inside = jnp.concatenate([inside] * (CHUNK // 256), axis=1)
    for c in range(CHUNKS):
        at = slice(CHUNK * c, CHUNK * (c + 1))
        inverse = fine_inverse(coef, w, diag_w, diag_e, wide_inside, at)
        inv[:, at] = inverse
        update = inverse * r[:, at] / MIDDLE
        u[:, at] = update
        sol[:, at] = update
    fine_apply(u, r, w, coef, wide, spread, px, qx, 0, sol, inv)
    fine_apply(u, r, w, coef, wide, spread, px, qx, 1, sol, inv)
    fine_apply(u, r, w, coef, wide, spread, px, qx, None, sol, inv)
    lane16 = lanes((16, 128)) % 16 // 4
    for c in range(CHUNKS):
        at = slice(CHUNK * c, CHUNK * (c + 1))
        rhs = mm(down[...], stack_hlh(r[:, at]))
        diag = mid_diag_e[...] * coef[0:1, at] + mm(mid_diag_w[...], kinds_of(w, at))
        update = jnp.where(wide_inside, 1.0 / diag, 0.0) * rhs / MIDDLE
        for n in range(CHUNK // 256):
            x = (CHUNK // 256) * c + n
            for half in range(2):
                piece = update[:, 256 * n + 128 * half : 256 * n + 128 * half + 128]
                send_up[pl.ds(128 * half + x, 8, stride=16), :] = piece
                send_down[pl.ds(128 * half + x, 8, stride=16), :] = piece
    for x in range(NX):
        first, second = slice(256 * x, 256 * x + 128), slice(256 * x + 128, 256 * x + 256)
        mine = jnp.where(low, roll(r[:, first], 64), roll(r[:, second], 64))
        up = jnp.zeros((16, 128), F32)
        dn = jnp.zeros((16, 128), F32)
        for j in range(4):
            part = mine[16 * j : 16 * j + 16]
            up = jnp.where(lane16 == j, roll(part, 4 * j - 8), up)
            dn = jnp.where(lane16 == j, roll(part, 4 * j - 4), dn)
        send_up[256 + 16 * x : 272 + 16 * x, :] = up
        send_down[256 + 16 * x : 272 + 16 * x, :] = dn
    lane = lanes((64, 128))
    for x in range(8):
        a, b = [
            compacted(sol[:, 256 * n : 256 * n + 128], sol[:, 256 * n + 128 : 256 * n + 256], lane)
            for n in (x, x + 8)
        ]
        keep[x] = jnp.where(low, a, roll(b, 64))


def mid_z_body(own, dn, up, r, slab, fwd, bwd, frz):
    low = lanes((64, 128)) < 64
    l16 = lanes((16, 128)) % 16
    for x in range(NX):
        at = 256 * x
        mine = jnp.where(low, roll(r[:, at : at + 128], 64), roll(r[:, at + 128 : at + 256], 64))
        pack_dn = dn[256 + 16 * x : 272 + 16 * x, :]
        pack_up = up[256 + 16 * x : 272 + 16 * x, :]
        for j in range(4):
            rows = slice(16 * j, 16 * j + 16)
            part = jnp.where(l16 < 4, roll(pack_dn, -4 * j), mine[rows])
            part = jnp.where(l16 >= 12, roll(pack_up, 12 - 4 * j), part)
            frz[x, rows, :] = part
    for x in range(8):
        fwd[384 + 64 * x : 448 + 64 * x, :] = jnp.where(low, roll(frz[x], 64), frz[x + 8])
        bwd[384 + 64 * x : 448 + 64 * x, :] = jnp.where(low, frz[x], roll(frz[x + 8], 64))
    lane = lanes((128, 128))
    for m in range(4):
        acc = jnp.zeros((128, 128), F32)
        for n in range(4):
            y = 4 * (m - 1) + n
            if y < -1 or y > 8:
                continue
            to = 32 * n
            half, at = (y + 4) // 8, 16 * ((y + 4) % 8)
            rows = slice(128 * half, 128 * half + 128)
            acc = jnp.where((lane >= to + 12) & (lane < to + 20), roll(own[rows, :], to + 8 - at), acc)
            acc = jnp.where((lane >= to + 3) & (lane < to + 12), roll(dn[rows, :], to - at), acc)
            acc = jnp.where((lane >= to + 20) & (lane < to + 29), roll(up[rows, :], to + 16 - at), acc)
        if 1 <= m <= 2:
            slab[:, 128 * (m - 1) : 128 * m] = acc
        if m <= 2:
            fwd[128 * m : 128 * m + 128, :] = acc
        if m >= 1:
            bwd[128 * (m - 1) : 128 * m, :] = acc


LOWS = ((0, 1, 2, 3), (0, 1, 4, 5), (0, 2, 4, 6))
HIGHS = ((4, 5, 6, 7), (2, 3, 6, 7), (1, 3, 5, 7))


def ahead(v, d):
    if d == 0:
        return roll(v, -1, 0)
    return roll(v, -32 if d == 1 else -1, 1)


def behind(v, d):
    if d == 0:
        return roll(v, 1, 0)
    return roll(v, 32 if d == 1 else 1, 1)


def mid_setup(pos, scal, cfm, sel, faces, inv, diag):
    place = lanes((16, 1024))
    x_at = lax.broadcasted_iota(jnp.int32, (16, 1024), 0)
    y_at = pos[0] * 8 - 12 + place // 32
    z_at = pos[1] * 8 - 12 + place % 32
    domain = (y_at >= 0) & (y_at < NY) & (z_at >= 0) & (z_at < NZ)
    known = domain & (place >= 128) & (place < 896) & (place % 32 >= 4) & (place % 32 < 28)
    lasts = (x_at < NX - 1, y_at < NY - 1, z_at < NZ - 1)
    for d in range(3):
        is_open = domain & lasts[d] & (cfm[64 + 16 * d : 80 + 16 * d, :] == 0.0)
        sel[d] = jnp.where(is_open, cfm[16 + 16 * d : 32 + 16 * d, :], 4.0)
    coef = cfm[0:16, :]

    for d in range(3):
        for c in range(8):
            at = slice(128 * c, 128 * c + 128)
            kind = sel[d, :, at]
            ones = [kind == float(k) for k in range(KINDS)]
            for i in range(4):
                for j in range(i, 4):
                    value = jnp.zeros((16, 128), F32)
                    for k in range(KINDS):
                        value = jnp.where(ones[k], scal[64 + 16 * k + 4 * i + j], value)
                    faces[d, 4 * i + j, :, at] = value
    if inv is None:
        return known
    for i in range(8):
        total = coef * scal[9 * i]
        for d in range(3):
            if i in HIGHS[d]:
                total = total + faces[d, 5 * HIGHS[d].index(i)]
            else:
                total = total + behind(faces[d, 5 * LOWS[d].index(i)], d)
        if diag is not None:
            diag[i] = total
        inv[i] = jnp.where(known, 1.0 / total, 0.0)
    return known


def mid_apply(v, r, scal, cfm, faces, jump, flux):
    for d in range(3):
        for j in range(4):
            jump[j] = v[HIGHS[d][j]] - ahead(v[LOWS[d][j]], d)

        for c in range(8):
            at = slice(128 * c, 128 * c + 128)
            jumps = [jump[j, :, at] for j in range(4)]
            for i in range(4):
                total = faces[d, i, :, at] * jumps[0]
                for j in range(1, 4):
                    total = total + faces[d, 4 * min(i, j) + max(i, j), :, at] * jumps[j]
                flux[4 * d + i, :, at] = total

    for c in range(1, 7):
        at = slice(128 * c, 128 * c + 128)
        values = [v[j, :, at] for j in range(8)]
        coef = cfm[0:16, at]
        for i in range(8):
            total = scal[8 * i] * values[0]
            for j in range(1, 8):
                total = total + scal[8 * i + j] * values[j]
            r[i, :, at] = r[i, :, at] - coef * total
    for d in range(3):
        for j in range(4):
            value = flux[4 * d + j]
            r[HIGHS[d][j]] = r[HIGHS[d][j]] - value
            r[LOWS[d][j]] = r[LOWS[d][j]] + behind(value, d)


def mid_step(step, u, r, sol, inv):
    keep, gain = STEPS[step]
    for i in range(8):
        new = keep * u[i] + gain * (inv[i] * r[i])
        u[i] = new
        sol[i] = sol[i] + new


def mid_pre_body(
    pos, scal, slab, below, above, cfm, sol_out, r_out, coarse, send_up, send_down,
    sel, faces, inv, diag, u, sol, r, jump, flux,
):
    for i in range(8):
        rows = slice(16 * i, 16 * i + 16)
        for m in range(3):
            u[i, :, 128 * m : 128 * m + 128] = below[128 * m + 16 * i : 128 * m + 16 * i + 16, :]
            u[i, :, 128 * (m + 5) : 128 * (m + 6)] = above[128 * m + 16 * i : 128 * m + 16 * i + 16, :]
        u[i, :, 384:640] = slab[rows, :]
    mid_setup(pos, scal, cfm, sel, faces, inv, diag)
    for i in range(8):
        r[i] = (MIDDLE * diag[i]) * u[i]
        sol[i] = u[i]
    mid_apply(u, r, scal, cfm, faces, jump, flux)
    mid_step(0, u, r, sol, inv)
    mid_apply(u, r, scal, cfm, faces, jump, flux)
    mid_step(1, u, r, sol, inv)
    mid_apply(u, r, scal, cfm, faces, jump, flux)
    sol_out[...] = sol[:, :, 128:896]
    r_out[...] = r[:, :, 128:896]
    total = r[0]
    for i in range(1, 8):
        total = total + r[i]
    coarse[0] = total
    center = cfm[0:16, :] * scal[128]
    for d in range(3):
        kind = sel[d]
        value = jnp.zeros((16, 1024), F32)
        for k in range(KINDS):
            value = jnp.where(kind == float(k), scal[129 + k], value)
        coarse[2 + d] = value
        center = center + value + behind(value, d)
    coarse[1] = center
    l32 = lanes((16, 768)) % 32
    for out, first in ((send_up, 6), (send_down, 18)):
        acc = jnp.zeros((16, 768), F32)
        for f in range(4):
            acc = jnp.where(l32 // 8 == f, roll(coarse[f, :, 128:896], 8 * f - first), acc)
        out[0] = acc
        out[1] = roll(coarse[4, :, 128:896], -first)


def coarse_z_body(own, dn, up, slab, fwd, bwd):
    lane = lanes((16, 128))
    for f in range(5):
        part = 0 if f < 4 else 1
        shift = 8 * f if f < 4 else 0
        for m in range(10):
            acc = jnp.zeros((16, 128), F32)
            for n in range(2):
                y = 2 * m + n - 6
                tile, at = (y + 12) // 4, 32 * ((y + 12) % 4)
                to = 64 * n
                mine = own[f, :, 128 * tile : 128 * tile + 128]
                left = dn[part, :, 128 * (tile - 1) : 128 * tile]
                right = up[part, :, 128 * (tile - 1) : 128 * tile]
                acc = jnp.where(
                    (lane >= to + 22) & (lane < to + 42), roll(mine, to + 22 - (at + 6)), acc
                )
                acc = jnp.where(
                    (lane >= to + 14) & (lane < to + 22), roll(left, to + 14 - (at + shift)), acc
                )
                acc = jnp.where(
                    (lane >= to + 42) & (lane < to + 50), roll(right, to + 42 - (at + shift)), acc
                )
            slab[f, :, 128 * m : 128 * m + 128] = acc
            if m < 4:
                fwd[f, :, 128 * m : 128 * m + 128] = acc
            if m >= 6:
                bwd[f, :, 128 * (m - 6) : 128 * (m - 5)] = acc


def settle(v, basis, j):
    lane = lanes((16, 128))
    for m in range(6):
        acc = jnp.zeros((16, 128), F32)
        for n in range(4):
            y = 4 * m + n - 8
            tile, at = (y + 14) // 2, 64 * ((y + 14) % 2)
            to = 32 * n
            piece = roll(v[:, 128 * tile : 128 * tile + 128], to + 5 - (at + 21))
            acc = jnp.where((lane >= to + 5) & (lane < to + 27), piece, acc)
        basis[j, :, 128 * m : 128 * m + 128] = acc


def two_sum(a, b):
    s = a + b
    t = s - a
    return s, (a - (s - t)) + (b - t)


def halves(a):
    t = a * 4097.0
    high = t - (t - a)
    return high, a - high


def two_prod(a, b):
    ah, al = halves(a)
    bh, bl = halves(b)
    p = a * b
    return p, ((ah * bh - p) + ah * bl + al * bh) + al * bl


def pair_mul(a, b):
    p, e = two_prod(a[0], b[0])
    return two_sum(p, e + (a[0] * b[1] + a[1] * b[0]))


def pair_sub(a, b):
    s, e = two_sum(a[0], -b[0])
    return two_sum(s, e + (a[1] - b[1]))


def pair_div(a, b):
    first = a[0] / b[0]
    rest = pair_sub(a, pair_mul((first, jnp.zeros_like(first)), b))
    return two_sum(first, rest[0] / b[0])


START = (0, 9, 17, 24, 30, 35, 39, 42)
PAIRS = sum(9 - i for i in range(BASIS))


def krylov_body(scal, own, below, above, basis, gram, field, hold):
    for f in range(5):
        field[f, :, 0:512] = below[f]
        field[f, :, 512:1792] = own[f]
        field[f, :, 1792:2304] = above[f]
    center, half = scal[133], scal[134]
    lane8 = lanes((8, 128))

    def apply(v):
        total = field[1] * v
        for d in range(3):
            cond = field[2 + d]
            axis, step = ((0, 1), (1, 64), (1, 1))[d]
            total = total - cond * roll(v, -step, axis) - roll(cond * v, step, axis)
        return total

    def compact(v):
        acc = jnp.zeros((8, 128), F32)
        for t in range(2):
            for y in range(8):
                tile, at = (y + 14) // 2, 64 * ((y + 14) % 2) + 28
                to = 64 * t + 8 * y
                piece = v[8 * t : 8 * t + 8, 128 * tile : 128 * tile + 128]
                acc = jnp.where((lane8 >= to) & (lane8 < to + 8), roll(piece, to - at), acc)
        return acc

    before = None
    now = field[0]
    for j in range(BASIS):
        settle(now, basis, j)
        hold[j] = compact(now)
        image = apply(now)
        hold[BASIS + j] = compact(image)
        if j + 1 < BASIS:
            nxt = (image - center * now) * half
            if j > 0:
                nxt = 2.0 * nxt - before
            before, now = now, nxt
    high_rows, low_rows = [], []
    for i in range(BASIS):
        for j in range(i, BASIS + 1):
            other = hold[BASIS + j] if j < BASIS else hold[0]
            p, e = two_prod(hold[i], other)
            high_rows.append(p)
            low_rows.append(e)
    high = jnp.stack(high_rows)
    low = jnp.stack(low_rows)
    for axis, shifts in ((1, (4, 2, 1)), (2, (64, 32, 16, 8, 4, 2, 1))):
        for s in shifts:
            high, e = two_sum(high, roll(high, s, axis))
            low = low + roll(low, s, axis) + e
    row = jnp.zeros((8, 128), F32)
    for n in range(PAIRS):
        row = jnp.where(lane8 == n, high[n], row)
        row = jnp.where(lane8 == 64 + n, low[n], row)
    for m in range(2):
        gram[8 * m : 8 * m + 8, :] = row


def summed(gram):
    count = gram.shape[0] // 8
    high = gram[...].reshape(count, 8, 128)
    low = jnp.zeros((count, 8, 128), F32)
    while count > 1:
        count //= 2
        high, e = two_sum(high[:count], high[count : 2 * count])
        low = low[:count] + low[count : 2 * count] + e
    high, low = high[0], low[0]
    for s in (4, 2, 1):
        high, e = two_sum(high, roll(high, s, 0))
        low = low + roll(low, s, 0) + e
    return two_sum(high, low + roll(high, 64))


def gram_body(gram, out):
    high, low = summed(gram)
    row = jnp.where(lanes((8, 128)) < 64, high, roll(low, 64))
    for m in range(4):
        out[8 * m : 8 * m + 8, :] = row


def mid_post(pos, scal, gram, basis, cfm, pre, res, out, sel, faces, inv, u, r, sol, jump, flux):
    high, low = summed(gram)
    lane = lanes((8, 128))
    sub = lax.broadcasted_iota(jnp.int32, (8, 128), 0)
    mat_h = jnp.zeros((8, 128), F32)
    mat_l = jnp.zeros((8, 128), F32)
    for i in range(BASIS):
        here = (sub == i) & (lane >= i) & (lane <= BASIS)
        mat_h = jnp.where(here, roll(high, i - START[i]), mat_h)
        mat_l = jnp.where(here, roll(low, i - START[i]), mat_l)
        for j in range(i + 1, BASIS):
            here = (sub == j) & (lane == i)
            shift = i - (START[i] + j - i)
            mat_h = jnp.where(here, roll(high, shift), mat_h)
            mat_l = jnp.where(here, roll(low, shift), mat_l)

    def spread_at(v, row, col):
        return jnp.broadcast_to(v[row : row + 1, col : col + 1], (8, 128))

    answers = []
    pivots = []
    for k in range(BASIS):
        start = spread_at(high, 0, START[k])
        piv = (spread_at(mat_h, k, k), spread_at(mat_l, k, k))
        good = jnp.abs(piv[0]) > 1e-12 * jnp.abs(start)
        safe = (jnp.where(good, piv[0], 1.0), jnp.where(good, piv[1], 0.0))
        pivots.append((safe, good))
        row = (
            jnp.broadcast_to(mat_h[k : k + 1, :], (8, 128)),
            jnp.broadcast_to(mat_l[k : k + 1, :], (8, 128)),
        )
        col = (
            jnp.broadcast_to(mat_h[:, k : k + 1], (8, 128)),
            jnp.broadcast_to(mat_l[:, k : k + 1], (8, 128)),
        )
        factor = pair_div(col, safe)
        use = good & (sub != k)
        factor = (jnp.where(use, factor[0], 0.0), jnp.where(use, factor[1], 0.0))
        mat_h, mat_l = pair_sub((mat_h, mat_l), pair_mul(factor, row))
    for k in range(BASIS):
        safe, good = pivots[k]
        value = pair_div((spread_at(mat_h, k, BASIS), spread_at(mat_l, k, BASIS)), safe)[0]
        answers.append(jnp.where(good, value, 0.0))
    weights = [jnp.concatenate([a, a], axis=0) for a in answers]
    lane16 = lanes((16, 128))
    for m in range(8):
        total = jnp.zeros((16, 128), F32)
        if 1 <= m <= 6:
            at = slice(128 * (m - 1), 128 * m)
            for j in range(BASIS):
                total = total + weights[j] * basis[j, :, at]
        for i in range(8):
            u[i, :, 128 * m : 128 * m + 128] = total
    mid_setup(pos, scal, cfm, sel, faces, inv, None)
    ends = jnp.zeros((16, 128), F32)
    for i in range(8):
        for ref in (r, sol):
            ref[i, :, 0:128] = ends
            ref[i, :, 896:1024] = ends
        r[i, :, 128:896] = res[i]
        sol[i, :, 128:896] = pre[i] + u[i, :, 128:896]
    mid_apply(u, r, scal, cfm, faces, jump, flux)
    for i in range(8):
        new = inv[i] * r[i] / MIDDLE
        u[i] = new
        sol[i] = sol[i] + new
    mid_apply(u, r, scal, cfm, faces, jump, flux)
    mid_step(0, u, r, sol, inv)
    mid_apply(u, r, scal, cfm, faces, jump, flux)
    mid_step(1, u, r, sol, inv)
    for i in range(8):
        for half in range(2):
            acc = jnp.zeros((16, 128), F32)
            for n in range(8):
                y = 8 * half + n - 4
                tile, at = (y + 12) // 4, 32 * ((y + 12) % 4) + 8
                acc = jnp.where(
                    lane16 // 16 == n,
                    roll(sol[i, :, 128 * tile : 128 * tile + 128], 16 * n - at),
                    acc,
                )
            out[128 * half + 16 * i : 128 * half + 16 * i + 16, :] = acc


def post_body(
    pos, scal, gram, basis, cfm, mid_pre, mid_res, keep, frz, below, above, coef, wide, spread,
    lift, diag_w, diag_e, out,
    sel, faces, mid_inv, mid_u, mid_r, mid_sol, jump, flux, mid, w, inv, u, r, sol, px, qx,
):
    fine_weights(pos, coef, w)
    wide_inside = jnp.concatenate([fine_places(pos)[0]] * (CHUNK // 256), axis=1)
    for c in range(CHUNKS):
        at = slice(CHUNK * c, CHUNK * (c + 1))
        inv[:, at] = fine_inverse(coef, w, diag_w, diag_e, wide_inside, at)
    mid_post(
        pos, scal, gram, basis, cfm, mid_pre, mid_res, mid, sel, faces, mid_inv, mid_u, mid_r,
        mid_sol, jump, flux,
    )
    low = lanes((64, 128)) < 64
    px[:, 0:256] = jnp.zeros((16, 256), F32)
    qx[:, NX * 256 :] = jnp.zeros((16, 256), F32)
    for x in range(NX):
        first, second = slice(256 * x, 256 * x + 128), slice(256 * x + 128, 256 * x + 256)
        turned = roll(frz[x], 64)
        at = 384 + 64 * (x % 8)
        down = below[at : at + 64, :]
        over = above[at : at + 64, :]
        if x >= 8:
            down = roll(down, 64)
        else:
            over = roll(over, 64)
        r[:, first] = jnp.where(low, down, turned)
        r[:, second] = jnp.where(low, turned, over)
    planes = CHUNK // 256
    for c in range(CHUNKS):
        at = slice(CHUNK * c, CHUNK * (c + 1))
        pieces = [
            mid[pl.ds(128 * half + planes * c + n, 8, stride=16), :]
            for n in range(planes)
            for half in range(2)
        ]
        high, rest = split3(jnp.concatenate(pieces, axis=1))
        stacked = jnp.concatenate([high, rest, high, jnp.zeros((8, CHUNK), F32)], axis=0)
        lifted = mm(lift[...], stacked.astype(BF16))
        u[:, at] = lifted
        sol[:, at] = lifted
    fine_apply(u, r, w, coef, wide, spread, px, qx, None, sol, inv)
    for c in range(CHUNKS):
        at = slice(CHUNK * c, CHUNK * (c + 1))
        new = inv[:, at] * r[:, at] / MIDDLE
        u[:, at] = new
        sol[:, at] = sol[:, at] + new
    fine_apply(u, r, w, coef, wide, spread, px, qx, 0, sol, inv)
    fine_apply(u, r, w, coef, wide, spread, px, qx, 1, sol, inv)
    fine_apply(u, r, w, coef, wide, spread, px, qx, None, sol, inv)
    lane = lanes((64, 128))
    for x in range(NX):
        acc = jnp.zeros((64, 128), F32)
        for part, ref in enumerate((sol, r)):
            for y in range(8):
                half, at = (y + 4) // 8, 16 * ((y + 4) % 8) + 4
                start = 256 * x + 128 * half
                acc = jnp.where(
                    lane // 8 == 8 * part + y,
                    roll(ref[:, start : start + 128], 64 * part + 8 * y - at),
                    acc,
                )
        kept = keep[x % 8] if x < 8 else roll(keep[x % 8], 64)
        out[x] = acc + jnp.where(low, kept, 0.0)


def unpack_body(got, first, second):
    low = lanes((64, 128)) < 64
    for part, out in enumerate((first, second)):
        held = []
        for g in range(8):
            a, b = got[g], got[g + 8]
            if part == 0:
                held.append(jnp.where(low, a, roll(b, 64)))
            else:
                held.append(jnp.where(low, roll(a, 64), b))
        for y, rows in enumerate(exchange(held, 8)):
            out[pl.ds(y, 64, stride=8), :] = rows


def trace_tables():
    high = np.zeros((3, 16, 64), np.float32)
    low = np.zeros((3, 16, 64), np.float32)
    for p in range(4):
        for q in range(4):
            for d in range(3):
                for table, at in ((high, 3), (low, 0)):
                    index = [p, q]
                    index.insert(d, at)
                    table[d, 4 * p + q, 16 * index[0] + 4 * index[1] + index[2]] = 1.0
    return high, low


def mid_traces():
    high = np.zeros((3, 4, 8), np.float32)
    low = np.zeros((3, 4, 8), np.float32)
    for d in range(3):
        for n in range(4):
            high[d, n, HIGHS[d][n]] = 1.0
            low[d, n, LOWS[d][n]] = 1.0
    return high, low


def prolong_tables():
    node_points = jnp.array(
        [-1.0, -1.0 / math.sqrt(5.0), 1.0 / math.sqrt(5.0), 1.0], dtype=jnp.float32
    )
    basis_table = jnp.stack([(1.0 - node_points) * 0.5, (1.0 + node_points) * 0.5], axis=1)
    volume = (
        basis_table[:, None, None, :, None, None]
        * basis_table[None, :, None, None, :, None]
        * basis_table[None, None, :, None, None, :]
    ).reshape(64, 8)
    surface = (basis_table[:, None, :, None] * basis_table[None, :, None, :]).reshape(16, 4)
    return (volume, surface)


def cut(x):
    return lax.reduce_precision(x, 8, 7)


def two_parts(x):
    high = cut(x)
    return high, cut(x - high)


def three_parts(x):
    high = cut(x)
    rest = x - high
    mid = cut(rest)
    return high, mid, cut(rest - mid)


def tables(element, faces):
    volume, surface = prolong_tables()
    elem_mid = jnp.dot(volume.T, jnp.dot(element, volume, precision=HIGHEST), precision=HIGHEST)
    face_mid = jnp.einsum("kij,jb->kib", faces, surface, precision=HIGHEST)
    face_mid = jnp.einsum("ia,kib->kab", surface, face_mid, precision=HIGHEST)
    elem_coarse = jnp.sum(elem_mid)
    face_coarse = jnp.sum(face_mid, axis=(1, 2))
    high, low = trace_tables()
    both = np.concatenate([high, low], axis=0)
    rows = jnp.einsum("kij,djm->dkim", faces, both, precision=HIGHEST).reshape(384, 64)
    wide = jnp.concatenate([element, rows], axis=0)
    wh, wl = two_parts(wide)
    wide = jnp.concatenate([wh, wh, wl], axis=1).astype(BF16)
    spread = np.concatenate([high[1], -low[1], high[2], -low[2]], axis=0).T
    spread = np.concatenate([spread, spread], axis=1)
    face_diag = jnp.diagonal(faces, axis1=1, axis2=2)
    diag = jnp.einsum("dim,ki->mdk", both, face_diag, precision=HIGHEST).reshape(64, 24)
    diag_w = jnp.concatenate(three_parts(diag) + (jnp.zeros((64, 8), F32),), axis=1).astype(BF16)
    diag_e = jnp.diagonal(element)[:, None]
    mh, ml = mid_traces()
    both = np.concatenate([mh, ml], axis=0)
    diag = jnp.einsum(
        "dim,ki->mdk", both, jnp.diagonal(face_mid, axis1=1, axis2=2), precision=HIGHEST
    ).reshape(8, 24)
    mid_diag_w = jnp.concatenate(three_parts(diag) + (jnp.zeros((8, 8), F32),), axis=1).astype(BF16)
    mid_diag_e = jnp.diagonal(elem_mid)[:, None]
    vh, vl = two_parts(volume)
    down = jnp.concatenate([vh.T, vh.T, vl.T], axis=1).astype(BF16)
    lift = jnp.concatenate([vh, vh, vl, jnp.zeros((64, 8), F32)], axis=1).astype(BF16)
    least = 0.1 * elem_coarse
    most = 1.35 * elem_coarse + 9.0 * jnp.max(jnp.abs(face_coarse))
    half = 0.5 * (most - least)
    half = jnp.where(jnp.abs(half) > 0.0, half, 1.0)
    scal = jnp.concatenate(
        [
            elem_mid.reshape(-1),
            face_mid.reshape(-1),
            elem_coarse[None],
            face_coarse,
            (0.5 * (most + least))[None],
            (1.0 / half)[None],
            jnp.zeros((9,), F32),
        ]
    )
    return (
        wide,
        jnp.asarray(spread, BF16),
        diag_w,
        diag_e,
        down,
        mid_diag_w,
        mid_diag_e,
        lift,
        scal,
    )


def local(residual, coefficient, element, faces, kind, flag):
    shift_up = [(i, i + 1) for i in range(15)]
    shift_dn = [(i + 1, i) for i in range(15)]

    def z_index(zb):
        return (zb % 16) * 2 + zb // 16

    z_up = [(z_index(i), z_index(i + 1)) for i in range(31)]
    z_dn = [(z_index(i + 1), z_index(i)) for i in range(31)]
    z_axes = ("gx", "lvl")
    side = lax.axis_index("lvl")
    pos = jnp.stack(
        [
            lax.axis_index("yz"),
            side * 16 + lax.axis_index("gx"),
        ]
    ).astype(jnp.int32)
    res = residual.reshape(512, 128)
    slots = call(
        slots_body, "slots", [f32s(16, 40, 128)], (0,) * 4, [pltpu.VMEM((128, 128), F32)]
    )(res, coefficient.reshape(8, 128), kind.reshape(48, 128), flag.reshape(48, 128))[0]
    element, faces, slots = lax.optimization_barrier((element, faces, slots))
    wide, spread, diag_w, diag_e, down, mid_diag_w, mid_diag_e, lift, scal = tables(element, faces)
    own = lax.all_to_all(slots, "gx", 0, 0, tiled=True)
    dn = lax.ppermute(own, z_axes, z_up)
    up = lax.ppermute(own, z_axes, z_dn)
    place_values, place_kinds = place_tables()
    rows, own, bwd = call(
        join_body,
        "join",
        [f32s(NX, 64, 128), f32s(896, 128), f32s(768, 128)],
        (0,) * 5,
    )(own, dn, up, jnp.asarray(place_values, BF16), jnp.asarray(place_kinds, BF16))
    below = lax.ppermute(own, "yz", shift_up)
    above = lax.ppermute(bwd, "yz", shift_dn)
    plane = (64, NX * 256)
    strip = (16, NX * 256 + 256)
    keep, r, coef, cfm, send_up, send_down = call(
        fine_pre_body,
        "fine_pre",
        [
            f32s(8, 64, 128),
            f32s(*plane),
            f32s(8, NX * 256),
            f32s(128, 1024),
            f32s(512, 128),
            f32s(512, 128),
        ],
        (1,) + (0,) * 11,
        [
            pltpu.VMEM(plane, F32),
            pltpu.VMEM((24, NX * 256), F32),
            pltpu.VMEM(plane, F32),
            pltpu.VMEM(plane, F32),
            pltpu.VMEM(strip, F32),
            pltpu.VMEM(strip, F32),
            pltpu.VMEM((896, 128), F32),
        ],
    )(pos, rows, own, below, above, wide, spread, diag_w, diag_e, down, mid_diag_w, mid_diag_e)
    dn = lax.ppermute(send_up, z_axes, z_up)
    up = lax.ppermute(send_down, z_axes, z_dn)
    slab, fwd, bwd, frz = call(
        mid_z_body,
        "mid_z",
        [f32s(128, 256), f32s(896, 128), f32s(896, 128), f32s(NX, 64, 128)],
        (0,) * 4,
    )(send_up, dn, up, r)
    below = lax.ppermute(fwd, "yz", shift_up)
    above = lax.ppermute(bwd, "yz", shift_dn)
    mid = (8, 16, 1024)
    mid_scratch = [
        pltpu.VMEM((3, 16, 1024), F32),
        pltpu.VMEM((3, 16, 16, 1024), F32),
        pltpu.VMEM(mid, F32),
    ]
    tail_scratch = [pltpu.VMEM((4, 16, 1024), F32), pltpu.VMEM((12, 16, 1024), F32)]
    mid_pre, mid_res, coarse, send_up, send_down = call(
        mid_pre_body,
        "mid_pre",
        [f32s(8, 16, 768), f32s(8, 16, 768), f32s(5, 16, 1024), f32s(2, 16, 768), f32s(2, 16, 768)],
        (1, 1, 0, 0, 0, 0),
        mid_scratch
        + [pltpu.VMEM(mid, F32)] * 4
        + tail_scratch,
    )(pos, scal, slab, below, above, cfm)
    dn = lax.ppermute(send_up, z_axes, z_up)
    up = lax.ppermute(send_down, z_axes, z_dn)
    coarse_slab, fwd, bwd = call(
        coarse_z_body,
        "coarse_z",
        [f32s(5, 16, 1280), f32s(5, 16, 512), f32s(5, 16, 512)],
        (0, 0, 0),
    )(coarse, dn, up)
    coarse_below = lax.ppermute(fwd, "yz", shift_up)
    coarse_above = lax.ppermute(bwd, "yz", shift_dn)
    basis, gram = call(
        krylov_body,
        "krylov",
        [f32s(BASIS, 16, 768), f32s(16, 128)],
        (1, 0, 0, 0),
        [
            pltpu.VMEM((5, 16, 2304), F32),
            pltpu.VMEM((2 * BASIS, 8, 128), F32),
        ],
    )(scal, coarse_slab, coarse_below, coarse_above)
    gram = lax.all_to_all(gram, "yz", 0, 0, tiled=True)
    gram = call(gram_body, "gram", [f32s(32, 128)], (0,))(gram)[0]
    gram = lax.all_to_all(gram, z_axes, 0, 0, tiled=True)
    packed = call(
        post_body,
        "post",
        [f32s(16, 64, 128)],
        (1, 1) + (0,) * 15,
        mid_scratch
        + [pltpu.VMEM(mid, F32)] * 3
        + tail_scratch
        + [
            pltpu.VMEM((256, 128), F32),
            pltpu.VMEM((24, NX * 256), F32),
            pltpu.VMEM(plane, F32),
            pltpu.VMEM(plane, F32),
            pltpu.VMEM(plane, F32),
            pltpu.VMEM(plane, F32),
            pltpu.VMEM(strip, F32),
            pltpu.VMEM(strip, F32),
        ],
    )(
        pos, scal, gram, basis, cfm, mid_pre, mid_res, keep, frz, below, above, coef, wide, spread,
        lift, diag_w, diag_e,
    )[0]
    got = lax.all_to_all(packed, "gx", 0, 0, tiled=True)
    correction, rest = call(unpack_body, "unpack", [f32s(512, 128), f32s(512, 128)], (0,))(got)
    return (correction.reshape(64, 1, 8, 128), rest.reshape(64, 1, 8, 128))


def solution(mesh):
    in_specs = (
        P(None, "gx", "yz", "lvl"),
        P("gx", "yz", "lvl"),
        P(),
        P(),
        P(None, "gx", "yz", "lvl"),
        P(None, "gx", "yz", "lvl"),
    )
    out_specs = (P(None, "gx", "yz", "lvl"), P(None, "gx", "yz", "lvl"))
    return jax.shard_map(local, mesh=mesh, in_specs=in_specs, out_specs=out_specs, check_vma=False)
```

```python
import functools
import math

import jax
import jax.numpy as jnp
import numpy as np
from jax import lax
from jax.experimental import pallas as pl
from jax.experimental.pallas import tpu as pltpu
from jax.sharding import PartitionSpec as P

NX = 16
NY = 128
NZ = 256
KINDS = 4
F32 = jnp.float32
BF16 = jnp.bfloat16
HIGHEST = lax.Precision.HIGHEST
LOW_EIG = 0.3
HIGH_EIG = 3.0
MIDDLE = 0.5 * (HIGH_EIG + LOW_EIG)
SPREAD = 0.5 * (HIGH_EIG - LOW_EIG)
SCALED = MIDDLE / SPREAD
RHO0 = 1.0 / SCALED
RHO1 = 1.0 / (2.0 * SCALED - RHO0)
RHO2 = 1.0 / (2.0 * SCALED - RHO1)
STEPS = ((RHO1 * RHO0, 2.0 * RHO1 / SPREAD), (RHO2 * RHO1, 2.0 * RHO2 / SPREAD))
BASIS = 8
ORDER = tuple(2 * n if n < 8 else 2 * (15 - n) + 1 for n in range(16))
VMEM_LIMIT = 24 * 2**20
LARGE_LIMIT = 60 * 2**20


def lanes(shape):
    return lax.broadcasted_iota(jnp.int32, shape, len(shape) - 1)


def roll(x, shift, axis=None):
    axis = x.ndim - 1 if axis is None else axis
    shift = shift % x.shape[axis]
    return x if shift == 0 else pltpu.roll(x, shift, axis)


SPACES = {
    0: pl.BlockSpec(memory_space=pltpu.VMEM),
    1: pl.BlockSpec(memory_space=pltpu.SMEM),
}


def call(body, name, out_shape, in_specs, scratch=(), out_specs=None, limit=VMEM_LIMIT):
    out_specs = out_specs or (0,) * len(out_shape)
    return pl.pallas_call(
        body,
        out_shape=list(out_shape),
        in_specs=[SPACES[i] for i in in_specs],
        out_specs=[SPACES[i] for i in out_specs],
        scratch_shapes=list(scratch),
        compiler_params=pltpu.CompilerParams(vmem_limit_bytes=limit),
        cost_estimate=pl.CostEstimate(flops=1000000, bytes_accessed=1000000, transcendentals=0),
        name=name,
    )


def f32s(*shape):
    return jax.ShapeDtypeStruct(shape, F32)


def split3(x):
    high = x.astype(BF16).astype(F32)
    low = x - high
    return high, low


def stack_hlh(x):
    high, low = split3(x)
    return jnp.concatenate([high, low, high], axis=0).astype(BF16)


def mm(a, b):
    return jnp.dot(a, b, preferred_element_type=F32)


def exchange(arrays, lane_block):
    arrays = list(arrays)
    group = lanes(arrays[0].shape) // lane_block
    for bit in (1, 2, 4):
        upper = (group // bit) % 2 == 1
        for n in range(8):
            if n & bit:
                continue
            a, b = arrays[n], arrays[n | bit]
            arrays[n] = jnp.where(upper, roll(b, lane_block * bit), a)
            arrays[n | bit] = jnp.where(upper, b, roll(a, -lane_block * bit))
    return arrays


def slots_body(res, coef, kind, flag, out, cf):
    for n in range(16):
        cf[8 * n : 8 * n + 8, :] = jnp.zeros((8, 128), F32)
    cf[0:8, :] = coef[...]
    for first, ref in ((8, kind), (32, flag)):
        for n in range(3):
            at = 8 * (2 * n + 1)
            cf[first + 8 * n : first + 8 * n + 8, :] = ref[at : at + 8, :].astype(F32)
    for first, ref in ((80, kind), (104, flag)):
        for n in range(2):
            at = 8 * (2 * n + 2)
            cf[first + 8 * n : first + 8 * n + 8, :] = ref[at : at + 8, :].astype(F32)
    low = lanes((16, 128)) < 64
    low8 = lanes((8, 128)) < 64
    near = lanes((32, 128)) % 8 < 4
    values = exchange([res[pl.ds(y, 64, stride=8), :] for y in range(8)], 8)
    kinds = exchange([cf[pl.ds(y, 16, stride=8), :] for y in range(8)], 8)
    for j in range(8):
        first, second = ORDER[j], ORDER[j + 8]
        a, b = values[j][0:32], values[j][32:64]
        for at, v in (
            (0, jnp.where(near, a, roll(b, 4))),
            (24, jnp.where(near, roll(a, -4), b)),
        ):
            out[first, at : at + 16, :] = jnp.where(low, v[0:16], roll(v[16:32], 64))
            out[second, at : at + 16, :] = jnp.where(low, roll(v[0:16], 64), v[16:32])
        a, b = kinds[j][0:8], kinds[j][8:16]
        out[first, 16:24, :] = jnp.where(low8, a, roll(b, 64))
        out[second, 16:24, :] = jnp.where(low8, roll(a, 64), b)


def place_tables():
    values = np.zeros((512, 512), np.float32)
    kinds = np.zeros((384, 512), np.float32)
    pack = np.zeros((256, 128), np.float32)
    for half in range(2):
        for y in range(8):
            for z in range(8):
                lane = 64 * half + 8 * y + z
                to = 128 * (2 * (z // 4) + half) + 16 * y + z % 4
                for n, first in enumerate((4, 8, 12, 0)):
                    values[128 * n + lane, to + first] = 1.0
                for n, first in enumerate((12, 4, 20)):
                    kinds[128 * n + lane, 256 * half + 32 * y + first + z] = 1.0
    for y in range(-1, 9):
        for z in range(-1, 9):
            pack[16 * (y + 4) + z + 4, 12 * (y + 1) + z + 1] = 1.0
    return [jnp.asarray(v, BF16) for v in (values, kinds, pack)]


def three_rows(x):
    high = x.astype(BF16).astype(F32)
    rest = x - high
    mid = rest.astype(BF16).astype(F32)
    return jnp.concatenate([high, mid, rest - mid], axis=0).astype(BF16)


def moved(x, table):
    count = x.shape[0]
    out = mm(three_rows(x), table)
    return out[0:count] + out[count : 2 * count] + out[2 * count :]


def join_body(own, dn, up, place_values, place_kinds, rows, fwd, bwd):
    parts = (own[:, 0:16, :], own[:, 24:40, :], up[:, 0:16, :], dn[:, 8:24, :])
    values = jnp.concatenate([v.reshape(256, 128) for v in parts], axis=1)
    out = moved(values, place_values[...])
    for x in range(NX):
        for n in range(4):
            rows[x, 16 * n : 16 * n + 16, :] = out[16 * x : 16 * x + 16, 128 * n : 128 * n + 128]
    low = lanes((64, 128)) < 64
    for x in range(8):
        fwd[64 * x : 64 * x + 64, :] = jnp.where(low, roll(rows[x], 64), rows[x + 8])
        bwd[64 * x : 64 * x + 64, :] = jnp.where(low, rows[x], roll(rows[x + 8], 64))
    parts = (own[:, 16:24, :], dn[:, 0:8, :], up[:, 16:24, :])
    kinds = jnp.concatenate([v.reshape(128, 128) for v in parts], axis=1)
    out = moved(kinds, place_kinds[...])
    array = lax.broadcasted_iota(jnp.int32, (128, 128), 0) % 8
    edge = (lanes((128, 128)) % 32 == 3) & ((array == 3) | (array == 6))
    for h in range(2):
        minus = out[:, 256 + 128 * h : 384 + 128 * h]
        plus = jnp.where(edge, roll(minus, -1), out[:, 128 * h : 128 * h + 128])
        fwd[512 + 128 * h : 640 + 128 * h, :] = plus
        bwd[512 + 128 * h : 640 + 128 * h, :] = plus
    fwd[768:896, :] = out[:, 256:384]


CHUNK = 4096
CHUNKS = NX * 256 // CHUNK


def fine_apply(u, r, w, coef, wide, spread, px, qx, step, sol, inv):
    for c in range(CHUNKS):
        at = slice(CHUNK * c, CHUNK * (c + 1))
        after = slice(CHUNK * c + 256, CHUNK * (c + 1) + 256)
        prod = mm(wide[...], stack_hlh(u[:, at]))

        def pick(base, row):
            total = w[row : row + 1, at] * prod[base : base + 16]
            for k in range(1, KINDS):
                total = total + w[row + k : row + k + 1, at] * prod[base + 16 * k : base + 16 * k + 16]
            return total

        px[:, after] = pick(64, 0)
        py = pick(128, 4)
        pz = pick(192, 8)
        qx[:, at] = pick(256, 12)
        qy = pick(320, 16)
        qz = pick(384, 20)
        flux = jnp.concatenate(
            [py - roll(qy, -16), roll(py, 16) - qy, pz - roll(qz, -1), roll(pz, 1) - qz], axis=0
        )
        high, low = split3(flux)
        faces = mm(spread[...], jnp.concatenate([high, low], axis=0).astype(BF16))
        r[:, at] = r[:, at] - (coef[0:1, at] * prod[0:64] + faces)

    for c in range(CHUNKS):
        at = slice(CHUNK * c, CHUNK * (c + 1))
        after = slice(CHUNK * c + 256, CHUNK * (c + 1) + 256)
        r[48:64, at] = r[48:64, at] - (px[:, after] - qx[:, after])
        r[0:16, at] = r[0:16, at] + (px[:, at] - qx[:, at])
        if step is not None:
            keep, gain = STEPS[step]
            new = keep * u[:, at] + gain * (inv[:, at] * r[:, at])
            u[:, at] = new
            sol[:, at] = sol[:, at] + new


def fine_places(pos):
    place = lanes((1, 256))
    y_at = pos[0] * 8 - 4 + place // 16
    z_at = pos[1] * 8 - 4 + place % 16
    inside = (y_at >= 0) & (y_at < NY) & (z_at >= 0) & (z_at < NZ)
    return inside, inside & (y_at < NY - 1), inside & (z_at < NZ - 1)


def fine_weights(pos, coef, w):
    inside, has_y, has_z = fine_places(pos)
    w[12:16, 0:256] = jnp.zeros((4, 256), F32)
    for x in range(NX):
        at = slice(256 * x, 256 * x + 256)
        rows = coef[:, at]
        opens = [
            inside & (rows[4:5] == 0.0) if x < NX - 1 else jnp.zeros((1, 256), jnp.bool_),
            has_y & (rows[5:6] == 0.0),
            has_z & (rows[6:7] == 0.0),
        ]
        plus = [
            [jnp.where(opens[d] & (rows[1 + d : 2 + d] == float(k)), 1.0, 0.0) for k in range(KINDS)]
            for d in range(3)
        ]
        plus_all = jnp.concatenate(plus[0] + plus[1] + plus[2], axis=0)
        w[0:12, at] = plus_all
        if x < NX - 1:
            w[12:16, 256 * x + 256 : 256 * x + 512] = plus_all[0:4]
        w[16:20, at] = roll(plus_all[4:8], 16)
        w[20:24, at] = roll(plus_all[8:12], 1)


def kinds_of(w, at):
    ws = w[:, at]
    return jnp.concatenate([ws, ws, ws, jnp.zeros((8, CHUNK), F32)], axis=0).astype(BF16)


def fine_inverse(coef, w, diag_w, diag_e, inside, at):
    diag = diag_e[...] * coef[0:1, at] + mm(diag_w[...], kinds_of(w, at))
    return jnp.where(inside, 1.0 / diag, 0.0)


def compacted(first, second, lane):
    v = roll(jnp.where(lane < 64, roll(first, 64), roll(second, 64)), -4)
    for size in (8, 16, 32):
        v = jnp.where(lane % (4 * size) < size, v, roll(v, -size))
    return v


def fine_pre_body(
    pos,
    rows_in,
    own,
    below,
    above,
    wide,
    spread,
    diag_w,
    diag_e,
    down,
    mid_diag_w,
    mid_diag_e,
    pack,
    keep,
    r,
    coef,
    cfm,
    send_up,
    send_down,
    sol,
    w,
    inv,
    u,
    px,
    qx,
    gather,
    held,
):
    low = lanes((64, 128)) < 64
    lane8 = lanes((8, 128))
    inside = fine_places(pos)[0]
    px[:, 0:256] = jnp.zeros((16, 256), F32)
    qx[:, NX * 256 :] = jnp.zeros((16, 256), F32)
    cfm[:, 896:1024] = jnp.zeros((128, 128), F32)
    array = lax.broadcasted_iota(jnp.int32, (8, 128), 0)
    edge = (lane8 >= 96) & ((array == 2) | (array == 5))
    for x in range(NX):
        first, second = slice(256 * x, 256 * x + 128), slice(256 * x + 128, 256 * x + 256)
        turned = roll(rows_in[x], 64)
        at = 64 * (x % 8)
        under = below[at : at + 64, :]
        over = above[at : at + 64, :]
        if x >= 8:
            under = roll(under, 64)
        else:
            over = roll(over, 64)
        r[:, first] = jnp.where(low, under, turned)
        r[:, second] = jnp.where(low, turned, over)
        blocks = [
            ref[512 + 128 * h + 8 * x : 520 + 128 * h + 8 * x, :]
            for ref in (below, own, above)
            for h in range(2)
        ]
        minus = below[768 + 8 * x : 776 + 8 * x, :]
        gather[pl.ds(x, 8, stride=16), :] = jnp.where(edge, roll(minus, 96), 0.0)
        for m in range(6):
            gather[pl.ds(128 * (m + 1) + x, 8, stride=16), :] = blocks[m]
        for half, at in enumerate((first, second)):
            acc = jnp.zeros((8, 128), F32)
            for row in range(8):
                n = 8 * half + row
                acc = jnp.where(
                    lane8 // 16 == row,
                    roll(blocks[1 + n // 4], 16 * row - (n % 4) * 32 - 8),
                    acc,
                )
            coef[:, at] = acc
    for m in range(7):
        cfm[:, 128 * m : 128 * m + 128] = gather[128 * m : 128 * m + 128, :]
    fine_weights(pos, coef, w)
    wide_inside = jnp.concatenate([inside] * (CHUNK // 256), axis=1)
    for c in range(CHUNKS):
        at = slice(CHUNK * c, CHUNK * (c + 1))
        inverse = fine_inverse(coef, w, diag_w, diag_e, wide_inside, at)
        inv[:, at] = inverse
        update = inverse * r[:, at] / MIDDLE
        u[:, at] = update
        sol[:, at] = update
    fine_apply(u, r, w, coef, wide, spread, px, qx, 0, sol, inv)
    fine_apply(u, r, w, coef, wide, spread, px, qx, 1, sol, inv)
    fine_apply(u, r, w, coef, wide, spread, px, qx, None, sol, inv)
    lane16 = lanes((16, 128)) % 16 // 4
    for c in range(CHUNKS):
        at = slice(CHUNK * c, CHUNK * (c + 1))
        rhs = mm(down[...], stack_hlh(r[:, at]))
        diag = mid_diag_e[...] * coef[0:1, at] + mm(mid_diag_w[...], kinds_of(w, at))
        update = jnp.where(wide_inside, 1.0 / diag, 0.0) * rhs / MIDDLE
        for n in range(CHUNK // 256):
            x = (CHUNK // 256) * c + n
            for half in range(2):
                piece = update[:, 256 * n + 128 * half : 256 * n + 128 * half + 128]
                held[pl.ds(128 * half + x, 8, stride=16), :] = piece
    packed = moved(jnp.concatenate([held[0:128, :], held[128:256, :]], axis=1), pack[...])
    send_up[0:128, :] = packed
    send_down[0:128, :] = packed
    for x in range(NX):
        first, second = slice(256 * x, 256 * x + 128), slice(256 * x + 128, 256 * x + 256)
        mine = jnp.where(low, roll(r[:, first], 64), roll(r[:, second], 64))
        up = jnp.zeros((16, 128), F32)
        dn = jnp.zeros((16, 128), F32)
        for j in range(4):
            part = mine[16 * j : 16 * j + 16]
            up = jnp.where(lane16 == j, roll(part, 4 * j - 8), up)
            dn = jnp.where(lane16 == j, roll(part, 4 * j - 4), dn)
        send_up[128 + 16 * x : 144 + 16 * x, :] = up
        send_down[128 + 16 * x : 144 + 16 * x, :] = dn
    lane = lanes((64, 128))
    for x in range(8):
        a, b = [
            compacted(sol[:, 256 * n : 256 * n + 128], sol[:, 256 * n + 128 : 256 * n + 256], lane)
            for n in (x, x + 8)
        ]
        keep[x] = jnp.where(low, a, roll(b, 64))


def mid_z_body(own, dn, up, r, slab, fwd, bwd, frz):
    low = lanes((64, 128)) < 64
    l16 = lanes((16, 128)) % 16
    for x in range(NX):
        at = 256 * x
        mine = jnp.where(low, roll(r[:, at : at + 128], 64), roll(r[:, at + 128 : at + 256], 64))
        pack_dn = dn[128 + 16 * x : 144 + 16 * x, :]
        pack_up = up[128 + 16 * x : 144 + 16 * x, :]
        for j in range(4):
            rows = slice(16 * j, 16 * j + 16)
            part = jnp.where(l16 < 4, roll(pack_dn, -4 * j), mine[rows])
            part = jnp.where(l16 >= 12, roll(pack_up, 12 - 4 * j), part)
            frz[x, rows, :] = part
    for x in range(8):
        fwd[384 + 64 * x : 448 + 64 * x, :] = jnp.where(low, roll(frz[x], 64), frz[x + 8])
        bwd[384 + 64 * x : 448 + 64 * x, :] = jnp.where(low, frz[x], roll(frz[x + 8], 64))
    lane = lanes((128, 128))
    for m in range(4):
        acc = jnp.zeros((128, 128), F32)
        for n in range(4):
            y = 4 * (m - 1) + n
            if y < -1 or y > 8:
                continue
            to = 32 * n
            at = 12 * (y + 1)
            rows = slice(0, 128)
            acc = jnp.where((lane >= to + 12) & (lane < to + 20), roll(own[rows, :], to + 11 - at), acc)
            acc = jnp.where((lane >= to + 3) & (lane < to + 12), roll(dn[rows, :], to + 3 - at), acc)
            acc = jnp.where((lane >= to + 20) & (lane < to + 29), roll(up[rows, :], to + 19 - at), acc)
        if 1 <= m <= 2:
            slab[:, 128 * (m - 1) : 128 * m] = acc
        if m <= 2:
            fwd[128 * m : 128 * m + 128, :] = acc
        if m >= 1:
            bwd[128 * (m - 1) : 128 * m, :] = acc


LOWS = ((0, 1, 2, 3), (0, 1, 4, 5), (0, 2, 4, 6))
HIGHS = ((4, 5, 6, 7), (2, 3, 6, 7), (1, 3, 5, 7))


def ahead(v, d):
    if d == 0:
        return roll(v, -1, 0)
    return roll(v, -32 if d == 1 else -1, 1)


def behind(v, d):
    if d == 0:
        return roll(v, 1, 0)
    return roll(v, 32 if d == 1 else 1, 1)


def mid_setup(pos, scal, cfm, sel, faces, inv, diag):
    place = lanes((16, 1024))
    x_at = lax.broadcasted_iota(jnp.int32, (16, 1024), 0)
    y_at = pos[0] * 8 - 12 + place // 32
    z_at = pos[1] * 8 - 12 + place % 32
    domain = (y_at >= 0) & (y_at < NY) & (z_at >= 0) & (z_at < NZ)
    known = domain & (place >= 128) & (place < 896) & (place % 32 >= 4) & (place % 32 < 28)
    lasts = (x_at < NX - 1, y_at < NY - 1, z_at < NZ - 1)
    for d in range(3):
        is_open = domain & lasts[d] & (cfm[64 + 16 * d : 80 + 16 * d, :] == 0.0)
        sel[d] = jnp.where(is_open, cfm[16 + 16 * d : 32 + 16 * d, :], 4.0)
    coef = cfm[0:16, :]

    for d in range(3):
        for c in range(8):
            at = slice(128 * c, 128 * c + 128)
            kind = sel[d, :, at]
            ones = [kind == float(k) for k in range(KINDS)]
            for i in range(4):
                for j in range(i, 4):
                    value = jnp.zeros((16, 128), F32)
                    for k in range(KINDS):
                        value = jnp.where(ones[k], scal[64 + 16 * k + 4 * i + j], value)
                    faces[d, 4 * i + j, :, at] = value
    if inv is None:
        return known
    for i in range(8):
        total = coef * scal[9 * i]
        for d in range(3):
            if i in HIGHS[d]:
                total = total + faces[d, 5 * HIGHS[d].index(i)]
            else:
                total = total + behind(faces[d, 5 * LOWS[d].index(i)], d)
        if diag is not None:
            diag[i] = total
        inv[i] = jnp.where(known, 1.0 / total, 0.0)
    return known


def mid_apply(v, r, scal, cfm, faces, jump, flux):
    for d in range(3):
        for j in range(4):
            jump[j] = v[HIGHS[d][j]] - ahead(v[LOWS[d][j]], d)

        for c in range(8):
            at = slice(128 * c, 128 * c + 128)
            jumps = [jump[j, :, at] for j in range(4)]
            for i in range(4):
                total = faces[d, i, :, at] * jumps[0]
                for j in range(1, 4):
                    total = total + faces[d, 4 * min(i, j) + max(i, j), :, at] * jumps[j]
                flux[4 * d + i, :, at] = total

    for c in range(1, 7):
        at = slice(128 * c, 128 * c + 128)
        values = [v[j, :, at] for j in range(8)]
        coef = cfm[0:16, at]
        for i in range(8):
            total = scal[8 * i] * values[0]
            for j in range(1, 8):
                total = total + scal[8 * i + j] * values[j]
            r[i, :, at] = r[i, :, at] - coef * total
    for d in range(3):
        for j in range(4):
            value = flux[4 * d + j]
            r[HIGHS[d][j]] = r[HIGHS[d][j]] - value
            r[LOWS[d][j]] = r[LOWS[d][j]] + behind(value, d)


def mid_step(step, u, r, sol, inv):
    keep, gain = STEPS[step]
    for i in range(8):
        new = keep * u[i] + gain * (inv[i] * r[i])
        u[i] = new
        sol[i] = sol[i] + new


def mid_pre_body(
    pos, scal, slab, below, above, cfm, sol_out, r_out, coarse, send_up, send_down,
    sel, faces, inv, diag, u, sol, r, jump, flux,
):
    for i in range(8):
        rows = slice(16 * i, 16 * i + 16)
        for m in range(3):
            u[i, :, 128 * m : 128 * m + 128] = below[128 * m + 16 * i : 128 * m + 16 * i + 16, :]
            u[i, :, 128 * (m + 5) : 128 * (m + 6)] = above[128 * m + 16 * i : 128 * m + 16 * i + 16, :]
        u[i, :, 384:640] = slab[rows, :]
    mid_setup(pos, scal, cfm, sel, faces, inv, diag)
    for i in range(8):
        r[i] = (MIDDLE * diag[i]) * u[i]
        sol[i] = u[i]
    mid_apply(u, r, scal, cfm, faces, jump, flux)
    mid_step(0, u, r, sol, inv)
    mid_apply(u, r, scal, cfm, faces, jump, flux)
    mid_step(1, u, r, sol, inv)
    mid_apply(u, r, scal, cfm, faces, jump, flux)
    sol_out[...] = sol[:, :, 128:896]
    r_out[...] = r[:, :, 128:896]
    total = r[0]
    for i in range(1, 8):
        total = total + r[i]
    coarse[0] = total
    center = cfm[0:16, :] * scal[128]
    for d in range(3):
        kind = sel[d]
        value = jnp.zeros((16, 1024), F32)
        for k in range(KINDS):
            value = jnp.where(kind == float(k), scal[129 + k], value)
        coarse[2 + d] = value
        center = center + value + behind(value, d)
    coarse[1] = center
    l32 = lanes((16, 768)) % 32
    for out, first in ((send_up, 6), (send_down, 18)):
        acc = jnp.zeros((16, 768), F32)
        for f in range(4):
            acc = jnp.where(l32 // 8 == f, roll(coarse[f, :, 128:896], 8 * f - first), acc)
        out[0] = acc
        out[1] = roll(coarse[4, :, 128:896], -first)


def coarse_z_body(own, dn, up, slab, fwd, bwd):
    lane = lanes((16, 128))
    for f in range(5):
        part = 0 if f < 4 else 1
        shift = 8 * f if f < 4 else 0
        for m in range(10):
            acc = jnp.zeros((16, 128), F32)
            for n in range(2):
                y = 2 * m + n - 6
                tile, at = (y + 12) // 4, 32 * ((y + 12) % 4)
                to = 64 * n
                mine = own[f, :, 128 * tile : 128 * tile + 128]
                left = dn[part, :, 128 * (tile - 1) : 128 * tile]
                right = up[part, :, 128 * (tile - 1) : 128 * tile]
                acc = jnp.where(
                    (lane >= to + 22) & (lane < to + 42), roll(mine, to + 22 - (at + 6)), acc
                )
                acc = jnp.where(
                    (lane >= to + 14) & (lane < to + 22), roll(left, to + 14 - (at + shift)), acc
                )
                acc = jnp.where(
                    (lane >= to + 42) & (lane < to + 50), roll(right, to + 42 - (at + shift)), acc
                )
            slab[f, :, 128 * m : 128 * m + 128] = acc
            if m < 4:
                fwd[f, :, 128 * m : 128 * m + 128] = acc
            if m >= 6:
                bwd[f, :, 128 * (m - 6) : 128 * (m - 5)] = acc


def settle(v, basis, j):
    lane = lanes((16, 128))
    for m in range(6):
        acc = jnp.zeros((16, 128), F32)
        for n in range(4):
            y = 4 * m + n - 8
            tile, at = (y + 14) // 2, 64 * ((y + 14) % 2)
            to = 32 * n
            piece = roll(v[:, 128 * tile : 128 * tile + 128], to + 5 - (at + 21))
            acc = jnp.where((lane >= to + 5) & (lane < to + 27), piece, acc)
        basis[j, :, 128 * m : 128 * m + 128] = acc


def two_sum(a, b):
    s = a + b
    t = s - a
    return s, (a - (s - t)) + (b - t)


def halves(a):
    t = a * 4097.0
    high = t - (t - a)
    return high, a - high


def two_prod(a, b):
    ah, al = halves(a)
    bh, bl = halves(b)
    p = a * b
    return p, ((ah * bh - p) + ah * bl + al * bh) + al * bl


def pair_mul(a, b):
    p, e = two_prod(a[0], b[0])
    return two_sum(p, e + (a[0] * b[1] + a[1] * b[0]))


def pair_sub(a, b):
    s, e = two_sum(a[0], -b[0])
    return two_sum(s, e + (a[1] - b[1]))


def pair_div(a, b):
    first = a[0] / b[0]
    rest = pair_sub(a, pair_mul((first, jnp.zeros_like(first)), b))
    return two_sum(first, rest[0] / b[0])


START = (0, 9, 17, 24, 30, 35, 39, 42)
PAIRS = sum(9 - i for i in range(BASIS))


def krylov_body(scal, own, below, above, basis, gram, field, hold):
    for f in range(5):
        field[f, :, 0:512] = below[f]
        field[f, :, 512:1792] = own[f]
        field[f, :, 1792:2304] = above[f]
    center, half = scal[133], scal[134]
    lane8 = lanes((8, 128))

    def apply(v):
        total = field[1] * v
        for d in range(3):
            cond = field[2 + d]
            axis, step = ((0, 1), (1, 64), (1, 1))[d]
            total = total - cond * roll(v, -step, axis) - roll(cond * v, step, axis)
        return total

    def compact(v):
        acc = jnp.zeros((8, 128), F32)
        for t in range(2):
            for y in range(8):
                tile, at = (y + 14) // 2, 64 * ((y + 14) % 2) + 28
                to = 64 * t + 8 * y
                piece = v[8 * t : 8 * t + 8, 128 * tile : 128 * tile + 128]
                acc = jnp.where((lane8 >= to) & (lane8 < to + 8), roll(piece, to - at), acc)
        return acc

    before = None
    now = field[0]
    for j in range(BASIS):
        settle(now, basis, j)
        hold[j] = compact(now)
        image = apply(now)
        hold[BASIS + j] = compact(image)
        if j + 1 < BASIS:
            nxt = (image - center * now) * half
            if j > 0:
                nxt = 2.0 * nxt - before
            before, now = now, nxt
    high_rows, low_rows = [], []
    for i in range(BASIS):
        for j in range(i, BASIS + 1):
            other = hold[BASIS + j] if j < BASIS else hold[0]
            p, e = two_prod(hold[i], other)
            high_rows.append(p)
            low_rows.append(e)
    high = jnp.stack(high_rows)
    low = jnp.stack(low_rows)
    for axis, shifts in ((1, (4, 2, 1)), (2, (64, 32, 16, 8, 4, 2, 1))):
        for s in shifts:
            high, e = two_sum(high, roll(high, s, axis))
            low = low + roll(low, s, axis) + e
    row = jnp.zeros((8, 128), F32)
    for n in range(PAIRS):
        row = jnp.where(lane8 == n, high[n], row)
        row = jnp.where(lane8 == 64 + n, low[n], row)
    for m in range(2):
        gram[8 * m : 8 * m + 8, :] = row


def summed(gram):
    count = gram.shape[0] // 8
    high = gram[...].reshape(count, 8, 128)
    low = jnp.zeros((count, 8, 128), F32)
    while count > 1:
        count //= 2
        high, e = two_sum(high[:count], high[count : 2 * count])
        low = low[:count] + low[count : 2 * count] + e
    high, low = high[0], low[0]
    for s in (4, 2, 1):
        high, e = two_sum(high, roll(high, s, 0))
        low = low + roll(low, s, 0) + e
    return two_sum(high, low + roll(high, 64))


def gram_body(gram, out):
    high, low = summed(gram)
    row = jnp.where(lanes((8, 128)) < 64, high, roll(low, 64))
    for m in range(4):
        out[8 * m : 8 * m + 8, :] = row


def mid_post(pos, scal, gram, basis, cfm, pre, res, out, sel, faces, inv, u, r, sol, jump, flux):
    high, low = summed(gram)
    lane = lanes((8, 128))
    sub = lax.broadcasted_iota(jnp.int32, (8, 128), 0)
    mat_h = jnp.zeros((8, 128), F32)
    mat_l = jnp.zeros((8, 128), F32)
    for i in range(BASIS):
        here = (sub == i) & (lane >= i) & (lane <= BASIS)
        mat_h = jnp.where(here, roll(high, i - START[i]), mat_h)
        mat_l = jnp.where(here, roll(low, i - START[i]), mat_l)
        for j in range(i + 1, BASIS):
            here = (sub == j) & (lane == i)
            shift = i - (START[i] + j - i)
            mat_h = jnp.where(here, roll(high, shift), mat_h)
            mat_l = jnp.where(here, roll(low, shift), mat_l)

    def spread_at(v, row, col):
        return jnp.broadcast_to(v[row : row + 1, col : col + 1], (8, 128))

    answers = []
    pivots = []
    for k in range(BASIS):
        start = spread_at(high, 0, START[k])
        piv = (spread_at(mat_h, k, k), spread_at(mat_l, k, k))
        good = jnp.abs(piv[0]) > 1e-12 * jnp.abs(start)
        safe = (jnp.where(good, piv[0], 1.0), jnp.where(good, piv[1], 0.0))
        pivots.append((safe, good))
        row = (
            jnp.broadcast_to(mat_h[k : k + 1, :], (8, 128)),
            jnp.broadcast_to(mat_l[k : k + 1, :], (8, 128)),
        )
        col = (
            jnp.broadcast_to(mat_h[:, k : k + 1], (8, 128)),
            jnp.broadcast_to(mat_l[:, k : k + 1], (8, 128)),
        )
        factor = pair_div(col, safe)
        use = good & (sub != k)
        factor = (jnp.where(use, factor[0], 0.0), jnp.where(use, factor[1], 0.0))
        mat_h, mat_l = pair_sub((mat_h, mat_l), pair_mul(factor, row))
    for k in range(BASIS):
        safe, good = pivots[k]
        value = pair_div((spread_at(mat_h, k, BASIS), spread_at(mat_l, k, BASIS)), safe)[0]
        answers.append(jnp.where(good, value, 0.0))
    weights = [jnp.concatenate([a, a], axis=0) for a in answers]
    lane16 = lanes((16, 128))
    for m in range(8):
        total = jnp.zeros((16, 128), F32)
        if 1 <= m <= 6:
            at = slice(128 * (m - 1), 128 * m)
            for j in range(BASIS):
                total = total + weights[j] * basis[j, :, at]
        for i in range(8):
            u[i, :, 128 * m : 128 * m + 128] = total
    mid_setup(pos, scal, cfm, sel, faces, inv, None)
    ends = jnp.zeros((16, 128), F32)
    for i in range(8):
        for ref in (r, sol):
            ref[i, :, 0:128] = ends
            ref[i, :, 896:1024] = ends
        r[i, :, 128:896] = res[i]
        sol[i, :, 128:896] = pre[i] + u[i, :, 128:896]
    mid_apply(u, r, scal, cfm, faces, jump, flux)
    for i in range(8):
        new = inv[i] * r[i] / MIDDLE
        u[i] = new
        sol[i] = sol[i] + new
    mid_apply(u, r, scal, cfm, faces, jump, flux)
    mid_step(0, u, r, sol, inv)
    mid_apply(u, r, scal, cfm, faces, jump, flux)
    mid_step(1, u, r, sol, inv)
    for i in range(8):
        for half in range(2):
            acc = jnp.zeros((16, 128), F32)
            for n in range(8):
                y = 8 * half + n - 4
                tile, at = (y + 12) // 4, 32 * ((y + 12) % 4) + 8
                acc = jnp.where(
                    lane16 // 16 == n,
                    roll(sol[i, :, 128 * tile : 128 * tile + 128], 16 * n - at),
                    acc,
                )
            out[128 * half + 16 * i : 128 * half + 16 * i + 16, :] = acc


def post_body(
    pos, scal, gram, basis, cfm, mid_pre, mid_res, keep, frz, below, above, coef, wide, spread,
    lift, diag_w, diag_e, out,
    sel, faces, mid_inv, mid_u, mid_r, mid_sol, jump, flux, mid, w, inv, u, r, sol, px, qx,
):
    fine_weights(pos, coef, w)
    wide_inside = jnp.concatenate([fine_places(pos)[0]] * (CHUNK // 256), axis=1)
    for c in range(CHUNKS):
        at = slice(CHUNK * c, CHUNK * (c + 1))
        inv[:, at] = fine_inverse(coef, w, diag_w, diag_e, wide_inside, at)
    mid_post(
        pos, scal, gram, basis, cfm, mid_pre, mid_res, mid, sel, faces, mid_inv, mid_u, mid_r,
        mid_sol, jump, flux,
    )
    low = lanes((64, 128)) < 64
    px[:, 0:256] = jnp.zeros((16, 256), F32)
    qx[:, NX * 256 :] = jnp.zeros((16, 256), F32)
    for x in range(NX):
        first, second = slice(256 * x, 256 * x + 128), slice(256 * x + 128, 256 * x + 256)
        turned = roll(frz[x], 64)
        at = 384 + 64 * (x % 8)
        down = below[at : at + 64, :]
        over = above[at : at + 64, :]
        if x >= 8:
            down = roll(down, 64)
        else:
            over = roll(over, 64)
        r[:, first] = jnp.where(low, down, turned)
        r[:, second] = jnp.where(low, turned, over)
    planes = CHUNK // 256
    for c in range(CHUNKS):
        at = slice(CHUNK * c, CHUNK * (c + 1))
        pieces = [
            mid[pl.ds(128 * half + planes * c + n, 8, stride=16), :]
            for n in range(planes)
            for half in range(2)
        ]
        high, rest = split3(jnp.concatenate(pieces, axis=1))
        stacked = jnp.concatenate([high, rest, high, jnp.zeros((8, CHUNK), F32)], axis=0)
        lifted = mm(lift[...], stacked.astype(BF16))
        u[:, at] = lifted
        sol[:, at] = lifted
    fine_apply(u, r, w, coef, wide, spread, px, qx, None, sol, inv)
    for c in range(CHUNKS):
        at = slice(CHUNK * c, CHUNK * (c + 1))
        new = inv[:, at] * r[:, at] / MIDDLE
        u[:, at] = new
        sol[:, at] = sol[:, at] + new
    fine_apply(u, r, w, coef, wide, spread, px, qx, 0, sol, inv)
    fine_apply(u, r, w, coef, wide, spread, px, qx, 1, sol, inv)
    fine_apply(u, r, w, coef, wide, spread, px, qx, None, sol, inv)
    lane = lanes((64, 128))
    for x in range(NX):
        acc = jnp.zeros((64, 128), F32)
        for part, ref in enumerate((sol, r)):
            for y in range(8):
                half, at = (y + 4) // 8, 16 * ((y + 4) % 8) + 4
                start = 256 * x + 128 * half
                acc = jnp.where(
                    lane // 8 == 8 * part + y,
                    roll(ref[:, start : start + 128], 64 * part + 8 * y - at),
                    acc,
                )
        kept = keep[x % 8] if x < 8 else roll(keep[x % 8], 64)
        out[x] = acc + jnp.where(low, kept, 0.0)


def unpack_body(got, first, second):
    low = lanes((64, 128)) < 64
    for part, out in enumerate((first, second)):
        held = []
        for g in range(8):
            a, b = got[ORDER[g]], got[ORDER[g + 8]]
            if part == 0:
                held.append(jnp.where(low, a, roll(b, 64)))
            else:
                held.append(jnp.where(low, roll(a, 64), b))
        for y, rows in enumerate(exchange(held, 8)):
            out[pl.ds(y, 64, stride=8), :] = rows


def trace_tables():
    high = np.zeros((3, 16, 64), np.float32)
    low = np.zeros((3, 16, 64), np.float32)
    for p in range(4):
        for q in range(4):
            for d in range(3):
                for table, at in ((high, 3), (low, 0)):
                    index = [p, q]
                    index.insert(d, at)
                    table[d, 4 * p + q, 16 * index[0] + 4 * index[1] + index[2]] = 1.0
    return high, low


def mid_traces():
    high = np.zeros((3, 4, 8), np.float32)
    low = np.zeros((3, 4, 8), np.float32)
    for d in range(3):
        for n in range(4):
            high[d, n, HIGHS[d][n]] = 1.0
            low[d, n, LOWS[d][n]] = 1.0
    return high, low


def prolong_tables():
    node_points = jnp.array(
        [-1.0, -1.0 / math.sqrt(5.0), 1.0 / math.sqrt(5.0), 1.0], dtype=jnp.float32
    )
    basis_table = jnp.stack([(1.0 - node_points) * 0.5, (1.0 + node_points) * 0.5], axis=1)
    volume = (
        basis_table[:, None, None, :, None, None]
        * basis_table[None, :, None, None, :, None]
        * basis_table[None, None, :, None, None, :]
    ).reshape(64, 8)
    surface = (basis_table[:, None, :, None] * basis_table[None, :, None, :]).reshape(16, 4)
    return (volume, surface)


def cut(x):
    return lax.reduce_precision(x, 8, 7)


def two_parts(x):
    high = cut(x)
    return high, cut(x - high)


def three_parts(x):
    high = cut(x)
    rest = x - high
    mid = cut(rest)
    return high, mid, cut(rest - mid)


def tables(element, faces):
    volume, surface = prolong_tables()
    elem_mid = jnp.dot(volume.T, jnp.dot(element, volume, precision=HIGHEST), precision=HIGHEST)
    face_mid = jnp.einsum("kij,jb->kib", faces, surface, precision=HIGHEST)
    face_mid = jnp.einsum("ia,kib->kab", surface, face_mid, precision=HIGHEST)
    elem_coarse = jnp.sum(elem_mid)
    face_coarse = jnp.sum(face_mid, axis=(1, 2))
    high, low = trace_tables()
    both = np.concatenate([high, low], axis=0)
    rows = jnp.einsum("kij,djm->dkim", faces, both, precision=HIGHEST).reshape(384, 64)
    wide = jnp.concatenate([element, rows], axis=0)
    wh, wl = two_parts(wide)
    wide = jnp.concatenate([wh, wh, wl], axis=1).astype(BF16)
    spread = np.concatenate([high[1], -low[1], high[2], -low[2]], axis=0).T
    spread = np.concatenate([spread, spread], axis=1)
    face_diag = jnp.diagonal(faces, axis1=1, axis2=2)
    diag = jnp.einsum("dim,ki->mdk", both, face_diag, precision=HIGHEST).reshape(64, 24)
    diag_w = jnp.concatenate(three_parts(diag) + (jnp.zeros((64, 8), F32),), axis=1).astype(BF16)
    diag_e = jnp.diagonal(element)[:, None]
    mh, ml = mid_traces()
    both = np.concatenate([mh, ml], axis=0)
    diag = jnp.einsum(
        "dim,ki->mdk", both, jnp.diagonal(face_mid, axis1=1, axis2=2), precision=HIGHEST
    ).reshape(8, 24)
    mid_diag_w = jnp.concatenate(three_parts(diag) + (jnp.zeros((8, 8), F32),), axis=1).astype(BF16)
    mid_diag_e = jnp.diagonal(elem_mid)[:, None]
    vh, vl = two_parts(volume)
    down = jnp.concatenate([vh.T, vh.T, vl.T], axis=1).astype(BF16)
    lift = jnp.concatenate([vh, vh, vl, jnp.zeros((64, 8), F32)], axis=1).astype(BF16)
    least = 0.1 * elem_coarse
    most = 1.35 * elem_coarse + 9.0 * jnp.max(jnp.abs(face_coarse))
    half = 0.5 * (most - least)
    half = jnp.where(jnp.abs(half) > 0.0, half, 1.0)
    scal = jnp.concatenate(
        [
            elem_mid.reshape(-1),
            face_mid.reshape(-1),
            elem_coarse[None],
            face_coarse,
            (0.5 * (most + least))[None],
            (1.0 / half)[None],
            jnp.zeros((9,), F32),
        ]
    )
    return (
        wide,
        jnp.asarray(spread, BF16),
        diag_w,
        diag_e,
        down,
        mid_diag_w,
        mid_diag_e,
        lift,
        scal,
    )


def local(residual, coefficient, element, faces, kind, flag):
    shift_up = [(i, i + 1) for i in range(15)]
    shift_dn = [(i + 1, i) for i in range(15)]

    def z_index(zb):
        return ORDER[zb % 16] * 2 + zb // 16

    z_up = [(z_index(i), z_index(i + 1)) for i in range(31)]
    z_dn = [(z_index(i + 1), z_index(i)) for i in range(31)]
    z_axes = ("gx", "lvl")
    side = lax.axis_index("lvl")
    chip = lax.axis_index("gx")
    pos = jnp.stack(
        [
            lax.axis_index("yz"),
            side * 16 + jnp.where(chip % 2 == 0, chip // 2, 15 - chip // 2),
        ]
    ).astype(jnp.int32)
    res = residual.reshape(512, 128)
    slots = call(
        slots_body,
        "slots",
        [f32s(16, 40, 128)],
        (0,) * 4,
        [pltpu.VMEM((128, 128), F32)],
        limit=LARGE_LIMIT,
    )(res, coefficient.reshape(8, 128), kind.reshape(48, 128), flag.reshape(48, 128))[0]
    element, faces, slots = lax.optimization_barrier((element, faces, slots))
    wide, spread, diag_w, diag_e, down, mid_diag_w, mid_diag_e, lift, scal = tables(element, faces)
    own = lax.all_to_all(slots, "gx", 0, 0, tiled=True)
    dn = lax.ppermute(own[:, 16:40], z_axes, z_up)
    up = lax.ppermute(own[:, 0:24], z_axes, z_dn)
    place_values, place_kinds, pack = place_tables()
    rows, own, bwd = call(
        join_body,
        "join",
        [f32s(NX, 64, 128), f32s(896, 128), f32s(768, 128)],
        (0,) * 5,
    )(own, dn, up, place_values, place_kinds)
    below = lax.ppermute(own, "yz", shift_up)
    above = lax.ppermute(bwd, "yz", shift_dn)
    plane = (64, NX * 256)
    strip = (16, NX * 256 + 256)
    keep, r, coef, cfm, send_up, send_down = call(
        fine_pre_body,
        "fine_pre",
        [
            f32s(8, 64, 128),
            f32s(*plane),
            f32s(8, NX * 256),
            f32s(128, 1024),
            f32s(384, 128),
            f32s(384, 128),
        ],
        (1,) + (0,) * 12,
        [
            pltpu.VMEM(plane, F32),
            pltpu.VMEM((24, NX * 256), F32),
            pltpu.VMEM(plane, F32),
            pltpu.VMEM(plane, F32),
            pltpu.VMEM(strip, F32),
            pltpu.VMEM(strip, F32),
            pltpu.VMEM((896, 128), F32),
            pltpu.VMEM((256, 128), F32),
        ],
    )(
        pos, rows, own, below, above, wide, spread, diag_w, diag_e, down, mid_diag_w, mid_diag_e, pack
    )
    dn = lax.ppermute(send_up, z_axes, z_up)
    up = lax.ppermute(send_down, z_axes, z_dn)
    slab, fwd, bwd, frz = call(
        mid_z_body,
        "mid_z",
        [f32s(128, 256), f32s(896, 128), f32s(896, 128), f32s(NX, 64, 128)],
        (0,) * 4,
    )(send_up, dn, up, r)
    below = lax.ppermute(fwd, "yz", shift_up)
    above = lax.ppermute(bwd, "yz", shift_dn)
    mid = (8, 16, 1024)
    mid_scratch = [
        pltpu.VMEM((3, 16, 1024), F32),
        pltpu.VMEM((3, 16, 16, 1024), F32),
        pltpu.VMEM(mid, F32),
    ]
    tail_scratch = [pltpu.VMEM((4, 16, 1024), F32), pltpu.VMEM((12, 16, 1024), F32)]
    mid_pre, mid_res, coarse, send_up, send_down = call(
        mid_pre_body,
        "mid_pre",
        [f32s(8, 16, 768), f32s(8, 16, 768), f32s(5, 16, 1024), f32s(2, 16, 768), f32s(2, 16, 768)],
        (1, 1, 0, 0, 0, 0),
        mid_scratch
        + [pltpu.VMEM(mid, F32)] * 4
        + tail_scratch,
    )(pos, scal, slab, below, above, cfm)
    dn = lax.ppermute(send_up, z_axes, z_up)
    up = lax.ppermute(send_down, z_axes, z_dn)
    coarse_slab, fwd, bwd = call(
        coarse_z_body,
        "coarse_z",
        [f32s(5, 16, 1280), f32s(5, 16, 512), f32s(5, 16, 512)],
        (0, 0, 0),
    )(coarse, dn, up)
    coarse_below = lax.ppermute(fwd, "yz", shift_up)
    coarse_above = lax.ppermute(bwd, "yz", shift_dn)
    basis, gram = call(
        krylov_body,
        "krylov",
        [f32s(BASIS, 16, 768), f32s(16, 128)],
        (1, 0, 0, 0),
        [
            pltpu.VMEM((5, 16, 2304), F32),
            pltpu.VMEM((2 * BASIS, 8, 128), F32),
        ],
    )(scal, coarse_slab, coarse_below, coarse_above)
    gram = lax.all_to_all(gram, "yz", 0, 0, tiled=True)
    gram = call(gram_body, "gram", [f32s(32, 128)], (0,))(gram)[0]
    gram = lax.all_to_all(gram, z_axes, 0, 0, tiled=True)
    packed = call(
        post_body,
        "post",
        [f32s(16, 64, 128)],
        (1, 1) + (0,) * 15,
        mid_scratch
        + [pltpu.VMEM(mid, F32)] * 3
        + tail_scratch
        + [
            pltpu.VMEM((256, 128), F32),
            pltpu.VMEM((24, NX * 256), F32),
            pltpu.VMEM(plane, F32),
            pltpu.VMEM(plane, F32),
            pltpu.VMEM(plane, F32),
            pltpu.VMEM(plane, F32),
            pltpu.VMEM(strip, F32),
            pltpu.VMEM(strip, F32),
        ],
        limit=LARGE_LIMIT,
    )(
        pos, scal, gram, basis, cfm, mid_pre, mid_res, keep, frz, below, above, coef, wide, spread,
        lift, diag_w, diag_e,
    )[0]
    got = lax.all_to_all(packed, "gx", 0, 0, tiled=True)
    correction, rest = call(unpack_body, "unpack", [f32s(512, 128), f32s(512, 128)], (0,))(got)
    return (correction.reshape(64, 1, 8, 128), rest.reshape(64, 1, 8, 128))


def solution(mesh):
    in_specs = (
        P(None, "gx", "yz", "lvl"),
        P("gx", "yz", "lvl"),
        P(),
        P(),
        P(None, "gx", "yz", "lvl"),
        P(None, "gx", "yz", "lvl"),
    )
    out_specs = (P(None, "gx", "yz", "lvl"), P(None, "gx", "yz", "lvl"))
    return jax.shard_map(local, mesh=mesh, in_specs=in_specs, out_specs=out_specs, check_vma=False)
```

```python
import functools
import math

import jax
import jax.numpy as jnp
import numpy as np
from jax import lax
from jax.experimental import pallas as pl
from jax.experimental.pallas import tpu as pltpu
from jax.sharding import PartitionSpec as P

NX = 16
NY = 128
NZ = 256
KINDS = 4
F32 = jnp.float32
BF16 = jnp.bfloat16
HIGHEST = lax.Precision.HIGHEST
LOW_EIG = 0.3
HIGH_EIG = 3.0
MIDDLE = 0.5 * (HIGH_EIG + LOW_EIG)
SPREAD = 0.5 * (HIGH_EIG - LOW_EIG)
SCALED = MIDDLE / SPREAD
RHO0 = 1.0 / SCALED
RHO1 = 1.0 / (2.0 * SCALED - RHO0)
RHO2 = 1.0 / (2.0 * SCALED - RHO1)
STEPS = ((RHO1 * RHO0, 2.0 * RHO1 / SPREAD), (RHO2 * RHO1, 2.0 * RHO2 / SPREAD))
BASIS = 8
ORDER = tuple(2 * n if n < 8 else 2 * (15 - n) + 1 for n in range(16))
VMEM_LIMIT = 24 * 2**20
LARGE_LIMIT = 60 * 2**20


def lanes(shape):
    return lax.broadcasted_iota(jnp.int32, shape, len(shape) - 1)


def roll(x, shift, axis=None):
    axis = x.ndim - 1 if axis is None else axis
    shift = shift % x.shape[axis]
    return x if shift == 0 else pltpu.roll(x, shift, axis)


SPACES = {
    0: pl.BlockSpec(memory_space=pltpu.VMEM),
    1: pl.BlockSpec(memory_space=pltpu.SMEM),
}


def call(body, name, out_shape, in_specs, scratch=(), out_specs=None, limit=VMEM_LIMIT):
    out_specs = out_specs or (0,) * len(out_shape)
    return pl.pallas_call(
        body,
        out_shape=list(out_shape),
        in_specs=[SPACES[i] for i in in_specs],
        out_specs=[SPACES[i] for i in out_specs],
        scratch_shapes=list(scratch),
        compiler_params=pltpu.CompilerParams(vmem_limit_bytes=limit),
        cost_estimate=pl.CostEstimate(flops=1000000, bytes_accessed=1000000, transcendentals=0),
        name=name,
    )


def even(pos):
    return pos[0] % 2 == 0


def put(pos, first, second, at, fwd, bwd):
    if fwd is None:
        fwd = bwd
    if bwd is None:
        bwd = fwd
    first[at] = jnp.where(even(pos), fwd, bwd)
    second[at] = jnp.where(even(pos), bwd, fwd)


def from_below(pos, first, second, at):
    return jnp.where(even(pos), second[at], first[at])


def from_above(pos, first, second, at):
    return jnp.where(even(pos), first[at], second[at])


def f32s(*shape):
    return jax.ShapeDtypeStruct(shape, F32)


def split3(x):
    high = x.astype(BF16).astype(F32)
    low = x - high
    return high, low


def stack_hlh(x):
    high, low = split3(x)
    return jnp.concatenate([high, low, high], axis=0).astype(BF16)


def mm(a, b):
    return jnp.dot(a, b, preferred_element_type=F32)


def exchange(arrays, lane_block):
    arrays = list(arrays)
    group = lanes(arrays[0].shape) // lane_block
    for bit in (1, 2, 4):
        upper = (group // bit) % 2 == 1
        for n in range(8):
            if n & bit:
                continue
            a, b = arrays[n], arrays[n | bit]
            arrays[n] = jnp.where(upper, roll(b, lane_block * bit), a)
            arrays[n | bit] = jnp.where(upper, b, roll(a, -lane_block * bit))
    return arrays


def slots_body(res, coef, kind, flag, out, cf):
    for n in range(16):
        cf[8 * n : 8 * n + 8, :] = jnp.zeros((8, 128), F32)
    cf[0:8, :] = coef[...]
    for first, ref in ((8, kind), (32, flag)):
        for n in range(3):
            at = 8 * (2 * n + 1)
            cf[first + 8 * n : first + 8 * n + 8, :] = ref[at : at + 8, :].astype(F32)
    for first, ref in ((80, kind), (104, flag)):
        for n in range(2):
            at = 8 * (2 * n + 2)
            cf[first + 8 * n : first + 8 * n + 8, :] = ref[at : at + 8, :].astype(F32)
    low = lanes((16, 128)) < 64
    low8 = lanes((8, 128)) < 64
    near = lanes((32, 128)) % 8 < 4
    values = exchange([res[pl.ds(y, 64, stride=8), :] for y in range(8)], 8)
    kinds = exchange([cf[pl.ds(y, 16, stride=8), :] for y in range(8)], 8)
    for j in range(8):
        first, second = ORDER[j], ORDER[j + 8]
        a, b = values[j][0:32], values[j][32:64]
        for at, v in (
            (0, jnp.where(near, a, roll(b, 4))),
            (24, jnp.where(near, roll(a, -4), b)),
        ):
            out[first, at : at + 16, :] = jnp.where(low, v[0:16], roll(v[16:32], 64))
            out[second, at : at + 16, :] = jnp.where(low, roll(v[0:16], 64), v[16:32])
        a, b = kinds[j][0:8], kinds[j][8:16]
        out[first, 16:24, :] = jnp.where(low8, a, roll(b, 64))
        out[second, 16:24, :] = jnp.where(low8, roll(a, 64), b)


def place_tables():
    values = np.zeros((512, 512), np.float32)
    kinds = np.zeros((384, 512), np.float32)
    pack = np.zeros((256, 128), np.float32)
    for half in range(2):
        for y in range(8):
            for z in range(8):
                lane = 64 * half + 8 * y + z
                to = 128 * (2 * (z // 4) + half) + 16 * y + z % 4
                for n, first in enumerate((4, 8, 12, 0)):
                    values[128 * n + lane, to + first] = 1.0
                for n, first in enumerate((12, 4, 20)):
                    kinds[128 * n + lane, 256 * half + 32 * y + first + z] = 1.0
    for y in range(-1, 9):
        for z in range(-1, 9):
            pack[16 * (y + 4) + z + 4, 12 * (y + 1) + z + 1] = 1.0
    return [jnp.asarray(v, BF16) for v in (values, kinds, pack)]


def three_rows(x):
    high = x.astype(BF16).astype(F32)
    rest = x - high
    mid = rest.astype(BF16).astype(F32)
    return jnp.concatenate([high, mid, rest - mid], axis=0).astype(BF16)


def moved(x, table):
    count = x.shape[0]
    out = mm(three_rows(x), table)
    return out[0:count] + out[count : 2 * count] + out[2 * count :]


def join_body(pos, own, dn, up, place_values, place_kinds, rows, first, second):
    parts = (own[:, 0:16, :], own[:, 24:40, :], up[:, 0:16, :], dn[:, 8:24, :])
    values = jnp.concatenate([v.reshape(256, 128) for v in parts], axis=1)
    out = moved(values, place_values[...])
    for x in range(NX):
        for n in range(4):
            rows[x, 16 * n : 16 * n + 16, :] = out[16 * x : 16 * x + 16, 128 * n : 128 * n + 128]
    low = lanes((64, 128)) < 64
    for x in range(8):
        fwd = jnp.where(low, roll(rows[x], 64), rows[x + 8])
        bwd = jnp.where(low, rows[x], roll(rows[x + 8], 64))
        put(pos, first, second, slice(64 * x, 64 * x + 64), fwd, bwd)
    parts = (own[:, 16:24, :], dn[:, 0:8, :], up[:, 16:24, :])
    kinds = jnp.concatenate([v.reshape(128, 128) for v in parts], axis=1)
    out = moved(kinds, place_kinds[...])
    array = lax.broadcasted_iota(jnp.int32, (128, 128), 0) % 8
    edge = (lanes((128, 128)) % 32 == 3) & ((array == 3) | (array == 6))
    lane = lanes((128, 128))
    for h in range(2):
        minus = out[:, 256 + 128 * h : 384 + 128 * h]
        plus = jnp.where(edge, roll(minus, -1), out[:, 128 * h : 128 * h + 128])
        if h == 0:
            plus = jnp.where((array == 7) & (lane < 32), roll(minus, 5, 0), plus)
            plus = jnp.where(
                (array == 7) & (lane >= 32) & (lane < 64), roll(roll(minus, 2, 0), 32), plus
            )
        first[512 + 128 * h : 640 + 128 * h, :] = plus
        second[512 + 128 * h : 640 + 128 * h, :] = plus


CHUNK = 4096
CHUNKS = NX * 256 // CHUNK


def fine_apply(u, r, w, coef, wide, spread, px, qx, step, sol, inv):
    for c in range(CHUNKS):
        at = slice(CHUNK * c, CHUNK * (c + 1))
        after = slice(CHUNK * c + 256, CHUNK * (c + 1) + 256)
        prod = mm(wide[...], stack_hlh(u[:, at]))

        def pick(base, row):
            total = w[row : row + 1, at] * prod[base : base + 16]
            for k in range(1, KINDS):
                total = total + w[row + k : row + k + 1, at] * prod[base + 16 * k : base + 16 * k + 16]
            return total

        px[:, after] = pick(64, 0)
        py = pick(128, 4)
        pz = pick(192, 8)
        qx[:, at] = pick(256, 12)
        qy = pick(320, 16)
        qz = pick(384, 20)
        flux = jnp.concatenate(
            [py - roll(qy, -16), roll(py, 16) - qy, pz - roll(qz, -1), roll(pz, 1) - qz], axis=0
        )
        high, low = split3(flux)
        faces = mm(spread[...], jnp.concatenate([high, low], axis=0).astype(BF16))
        r[:, at] = r[:, at] - (coef[0:1, at] * prod[0:64] + faces)

    for c in range(CHUNKS):
        at = slice(CHUNK * c, CHUNK * (c + 1))
        after = slice(CHUNK * c + 256, CHUNK * (c + 1) + 256)
        r[48:64, at] = r[48:64, at] - (px[:, after] - qx[:, after])
        r[0:16, at] = r[0:16, at] + (px[:, at] - qx[:, at])
        if step is not None:
            keep, gain = STEPS[step]
            new = keep * u[:, at] + gain * (inv[:, at] * r[:, at])
            u[:, at] = new
            sol[:, at] = sol[:, at] + new


def fine_places(pos):
    place = lanes((1, 256))
    y_at = pos[0] * 8 - 4 + place // 16
    z_at = pos[1] * 8 - 4 + place % 16
    inside = (y_at >= 0) & (y_at < NY) & (z_at >= 0) & (z_at < NZ)
    return inside, inside & (y_at < NY - 1), inside & (z_at < NZ - 1)


def fine_weights(pos, coef, w):
    inside, has_y, has_z = fine_places(pos)
    w[12:16, 0:256] = jnp.zeros((4, 256), F32)
    for x in range(NX):
        at = slice(256 * x, 256 * x + 256)
        rows = coef[:, at]
        opens = [
            inside & (rows[4:5] == 0.0) if x < NX - 1 else jnp.zeros((1, 256), jnp.bool_),
            has_y & (rows[5:6] == 0.0),
            has_z & (rows[6:7] == 0.0),
        ]
        plus = [
            [jnp.where(opens[d] & (rows[1 + d : 2 + d] == float(k)), 1.0, 0.0) for k in range(KINDS)]
            for d in range(3)
        ]
        plus_all = jnp.concatenate(plus[0] + plus[1] + plus[2], axis=0)
        w[0:12, at] = plus_all
        if x < NX - 1:
            w[12:16, 256 * x + 256 : 256 * x + 512] = plus_all[0:4]
        w[16:20, at] = roll(plus_all[4:8], 16)
        w[20:24, at] = roll(plus_all[8:12], 1)


def kinds_of(w, at):
    ws = w[:, at]
    return jnp.concatenate([ws, ws, ws, jnp.zeros((8, CHUNK), F32)], axis=0).astype(BF16)


def fine_inverse(coef, w, diag_w, diag_e, inside, at):
    diag = diag_e[...] * coef[0:1, at] + mm(diag_w[...], kinds_of(w, at))
    return jnp.where(inside, 1.0 / diag, 0.0)


def compacted(first, second, lane):
    v = roll(jnp.where(lane < 64, roll(first, 64), roll(second, 64)), -4)
    for size in (8, 16, 32):
        v = jnp.where(lane % (4 * size) < size, v, roll(v, -size))
    return v


def fine_pre_body(
    pos,
    rows_in,
    own,
    got_first,
    got_second,
    wide,
    spread,
    diag_w,
    diag_e,
    down,
    mid_diag_w,
    mid_diag_e,
    pack,
    keep,
    r,
    coef,
    cfm,
    send_up,
    send_down,
    sol,
    w,
    inv,
    u,
    px,
    qx,
    gather,
    held,
):
    low = lanes((64, 128)) < 64
    lane8 = lanes((8, 128))
    inside = fine_places(pos)[0]
    px[:, 0:256] = jnp.zeros((16, 256), F32)
    qx[:, NX * 256 :] = jnp.zeros((16, 256), F32)
    cfm[:, 896:1024] = jnp.zeros((128, 128), F32)
    array = lax.broadcasted_iota(jnp.int32, (8, 128), 0)
    edge = (lane8 >= 96) & ((array == 2) | (array == 5))
    for x in range(NX):
        first, second = slice(256 * x, 256 * x + 128), slice(256 * x + 128, 256 * x + 256)
        turned = roll(rows_in[x], 64)
        at = 64 * (x % 8)
        under = from_below(pos, got_first, got_second, slice(at, at + 64))
        over = from_above(pos, got_first, got_second, slice(at, at + 64))
        if x >= 8:
            under = roll(under, 64)
        else:
            over = roll(over, 64)
        r[:, first] = jnp.where(low, under, turned)
        r[:, second] = jnp.where(low, turned, over)
        places = [slice(512 + 128 * h + 8 * x, 520 + 128 * h + 8 * x) for h in range(2)]
        blocks = (
            [from_below(pos, got_first, got_second, p) for p in places]
            + [own[p] for p in places]
            + [from_above(pos, got_first, got_second, p) for p in places]
        )
        minus = jnp.where(array == 2, roll(roll(blocks[0], 3, 0), 96), roll(roll(blocks[0], 6, 0), 64))
        gather[pl.ds(x, 8, stride=16), :] = jnp.where(edge, minus, 0.0)
        for m in range(6):
            gather[pl.ds(128 * (m + 1) + x, 8, stride=16), :] = blocks[m]
        for half, at in enumerate((first, second)):
            acc = jnp.zeros((8, 128), F32)
            for row in range(8):
                n = 8 * half + row
                acc = jnp.where(
                    lane8 // 16 == row,
                    roll(blocks[1 + n // 4], 16 * row - (n % 4) * 32 - 8),
                    acc,
                )
            coef[:, at] = acc
    for m in range(7):
        cfm[:, 128 * m : 128 * m + 128] = gather[128 * m : 128 * m + 128, :]
    fine_weights(pos, coef, w)
    wide_inside = jnp.concatenate([inside] * (CHUNK // 256), axis=1)
    for c in range(CHUNKS):
        at = slice(CHUNK * c, CHUNK * (c + 1))
        inverse = fine_inverse(coef, w, diag_w, diag_e, wide_inside, at)
        inv[:, at] = inverse
        update = inverse * r[:, at] / MIDDLE
        u[:, at] = update
        sol[:, at] = update
    fine_apply(u, r, w, coef, wide, spread, px, qx, 0, sol, inv)
    fine_apply(u, r, w, coef, wide, spread, px, qx, 1, sol, inv)
    fine_apply(u, r, w, coef, wide, spread, px, qx, None, sol, inv)
    lane16 = lanes((16, 128)) % 16 // 4
    for c in range(CHUNKS):
        at = slice(CHUNK * c, CHUNK * (c + 1))
        rhs = mm(down[...], stack_hlh(r[:, at]))
        diag = mid_diag_e[...] * coef[0:1, at] + mm(mid_diag_w[...], kinds_of(w, at))
        update = jnp.where(wide_inside, 1.0 / diag, 0.0) * rhs / MIDDLE
        for n in range(CHUNK // 256):
            x = (CHUNK // 256) * c + n
            for half in range(2):
                piece = update[:, 256 * n + 128 * half : 256 * n + 128 * half + 128]
                held[pl.ds(128 * half + x, 8, stride=16), :] = piece
    packed = moved(jnp.concatenate([held[0:128, :], held[128:256, :]], axis=1), pack[...])
    send_up[0:128, :] = packed
    send_down[0:128, :] = packed
    for x in range(NX):
        first, second = slice(256 * x, 256 * x + 128), slice(256 * x + 128, 256 * x + 256)
        mine = jnp.where(low, roll(r[:, first], 64), roll(r[:, second], 64))
        up = jnp.zeros((16, 128), F32)
        dn = jnp.zeros((16, 128), F32)
        for j in range(4):
            part = mine[16 * j : 16 * j + 16]
            up = jnp.where(lane16 == j, roll(part, 4 * j - 8), up)
            dn = jnp.where(lane16 == j, roll(part, 4 * j - 4), dn)
        send_up[128 + 16 * x : 144 + 16 * x, :] = up
        send_down[128 + 16 * x : 144 + 16 * x, :] = dn
    lane = lanes((64, 128))
    for x in range(8):
        a, b = [
            compacted(sol[:, 256 * n : 256 * n + 128], sol[:, 256 * n + 128 : 256 * n + 256], lane)
            for n in (x, x + 8)
        ]
        keep[x] = jnp.where(low, a, roll(b, 64))


def mid_z_body(pos, own, dn, up, r, slab, first, second, frz):
    low = lanes((64, 128)) < 64
    l16 = lanes((16, 128)) % 16
    for x in range(NX):
        at = 256 * x
        mine = jnp.where(low, roll(r[:, at : at + 128], 64), roll(r[:, at + 128 : at + 256], 64))
        pack_dn = dn[128 + 16 * x : 144 + 16 * x, :]
        pack_up = up[128 + 16 * x : 144 + 16 * x, :]
        for j in range(4):
            rows = slice(16 * j, 16 * j + 16)
            part = jnp.where(l16 < 4, roll(pack_dn, -4 * j), mine[rows])
            part = jnp.where(l16 >= 12, roll(pack_up, 12 - 4 * j), part)
            frz[x, rows, :] = part
    for x in range(8):
        fwd = jnp.where(low, roll(frz[x], 64), frz[x + 8])
        bwd = jnp.where(low, frz[x], roll(frz[x + 8], 64))
        put(pos, first, second, slice(384 + 64 * x, 448 + 64 * x), fwd, bwd)
    lane = lanes((128, 128))
    tiles = []
    for m in range(4):
        acc = jnp.zeros((128, 128), F32)
        for n in range(4):
            y = 4 * (m - 1) + n
            if y < -1 or y > 8:
                continue
            to = 32 * n
            at = 12 * (y + 1)
            rows = slice(0, 128)
            acc = jnp.where((lane >= to + 12) & (lane < to + 20), roll(own[rows, :], to + 11 - at), acc)
            acc = jnp.where((lane >= to + 3) & (lane < to + 12), roll(dn[rows, :], to + 3 - at), acc)
            acc = jnp.where((lane >= to + 20) & (lane < to + 29), roll(up[rows, :], to + 19 - at), acc)
        if 1 <= m <= 2:
            slab[:, 128 * (m - 1) : 128 * m] = acc
        tiles.append(acc)
    for m in range(3):
        put(pos, first, second, slice(128 * m, 128 * m + 128), tiles[m], tiles[m + 1])


LOWS = ((0, 1, 2, 3), (0, 1, 4, 5), (0, 2, 4, 6))
HIGHS = ((4, 5, 6, 7), (2, 3, 6, 7), (1, 3, 5, 7))


def ahead(v, d):
    if d == 0:
        return roll(v, -1, 0)
    return roll(v, -32 if d == 1 else -1, 1)


def behind(v, d):
    if d == 0:
        return roll(v, 1, 0)
    return roll(v, 32 if d == 1 else 1, 1)


def mid_setup(pos, scal, cfm, sel, faces, inv, diag):
    place = lanes((16, 1024))
    x_at = lax.broadcasted_iota(jnp.int32, (16, 1024), 0)
    y_at = pos[0] * 8 - 12 + place // 32
    z_at = pos[1] * 8 - 12 + place % 32
    domain = (y_at >= 0) & (y_at < NY) & (z_at >= 0) & (z_at < NZ)
    known = domain & (place >= 128) & (place < 896) & (place % 32 >= 4) & (place % 32 < 28)
    lasts = (x_at < NX - 1, y_at < NY - 1, z_at < NZ - 1)
    for d in range(3):
        is_open = domain & lasts[d] & (cfm[64 + 16 * d : 80 + 16 * d, :] == 0.0)
        sel[d] = jnp.where(is_open, cfm[16 + 16 * d : 32 + 16 * d, :], 4.0)
    coef = cfm[0:16, :]

    for d in range(3):
        for c in range(8):
            at = slice(128 * c, 128 * c + 128)
            kind = sel[d, :, at]
            ones = [kind == float(k) for k in range(KINDS)]
            for i in range(4):
                for j in range(i, 4):
                    value = jnp.zeros((16, 128), F32)
                    for k in range(KINDS):
                        value = jnp.where(ones[k], scal[64 + 16 * k + 4 * i + j], value)
                    faces[d, 4 * i + j, :, at] = value
    if inv is None:
        return known
    for i in range(8):
        total = coef * scal[9 * i]
        for d in range(3):
            if i in HIGHS[d]:
                total = total + faces[d, 5 * HIGHS[d].index(i)]
            else:
                total = total + behind(faces[d, 5 * LOWS[d].index(i)], d)
        if diag is not None:
            diag[i] = total
        inv[i] = jnp.where(known, 1.0 / total, 0.0)
    return known


def mid_apply(v, r, scal, cfm, faces, jump, flux):
    for d in range(3):
        for j in range(4):
            jump[j] = v[HIGHS[d][j]] - ahead(v[LOWS[d][j]], d)

        for c in range(8):
            at = slice(128 * c, 128 * c + 128)
            jumps = [jump[j, :, at] for j in range(4)]
            for i in range(4):
                total = faces[d, i, :, at] * jumps[0]
                for j in range(1, 4):
                    total = total + faces[d, 4 * min(i, j) + max(i, j), :, at] * jumps[j]
                flux[4 * d + i, :, at] = total

    for c in range(1, 7):
        at = slice(128 * c, 128 * c + 128)
        values = [v[j, :, at] for j in range(8)]
        coef = cfm[0:16, at]
        for i in range(8):
            total = scal[8 * i] * values[0]
            for j in range(1, 8):
                total = total + scal[8 * i + j] * values[j]
            r[i, :, at] = r[i, :, at] - coef * total
    for d in range(3):
        for j in range(4):
            value = flux[4 * d + j]
            r[HIGHS[d][j]] = r[HIGHS[d][j]] - value
            r[LOWS[d][j]] = r[LOWS[d][j]] + behind(value, d)


def mid_step(step, u, r, sol, inv):
    keep, gain = STEPS[step]
    for i in range(8):
        new = keep * u[i] + gain * (inv[i] * r[i])
        u[i] = new
        sol[i] = sol[i] + new


def mid_pre_body(
    pos, scal, slab, got_first, got_second, cfm, level, coarse, send_up, send_down,
    sel, faces, inv, diag, u, sol, r, jump, flux,
):
    for i in range(8):
        rows = slice(16 * i, 16 * i + 16)
        for m in range(3):
            at = slice(128 * m + 16 * i, 128 * m + 16 * i + 16)
            u[i, :, 128 * m : 128 * m + 128] = from_below(pos, got_first, got_second, at)
            u[i, :, 128 * (m + 5) : 128 * (m + 6)] = from_above(pos, got_first, got_second, at)
        u[i, :, 384:640] = slab[rows, :]
    mid_setup(pos, scal, cfm, sel, faces, inv, diag)
    for i in range(8):
        r[i] = (MIDDLE * diag[i]) * u[i]
        sol[i] = u[i]
    mid_apply(u, r, scal, cfm, faces, jump, flux)
    mid_step(0, u, r, sol, inv)
    mid_apply(u, r, scal, cfm, faces, jump, flux)
    mid_step(1, u, r, sol, inv)
    mid_apply(u, r, scal, cfm, faces, jump, flux)
    level[0] = sol[:, :, 128:896]
    level[1] = r[:, :, 128:896]
    total = r[0]
    for i in range(1, 8):
        total = total + r[i]
    coarse[0] = total
    center = cfm[0:16, :] * scal[128]
    for d in range(3):
        kind = sel[d]
        value = jnp.zeros((16, 1024), F32)
        for k in range(KINDS):
            value = jnp.where(kind == float(k), scal[129 + k], value)
        coarse[2 + d] = value
        center = center + value + behind(value, d)
    coarse[1] = center
    l32 = lanes((16, 768)) % 32
    for out, first in ((send_up, 6), (send_down, 18)):
        acc = jnp.zeros((16, 768), F32)
        for f in range(4):
            acc = jnp.where(l32 // 8 == f, roll(coarse[f, :, 128:896], 8 * f - first), acc)
        out[0] = acc
        out[1] = roll(coarse[4, :, 128:896], -first)


def coarse_z_body(pos, own, dn, up, slab, first, second):
    lane = lanes((16, 128))
    for f in range(5):
        part = 0 if f < 4 else 1
        shift = 8 * f if f < 4 else 0
        for m in range(10):
            acc = jnp.zeros((16, 128), F32)
            for n in range(2):
                y = 2 * m + n - 6
                tile, at = (y + 12) // 4, 32 * ((y + 12) % 4)
                to = 64 * n
                mine = own[f, :, 128 * tile : 128 * tile + 128]
                left = dn[part, :, 128 * (tile - 1) : 128 * tile]
                right = up[part, :, 128 * (tile - 1) : 128 * tile]
                acc = jnp.where(
                    (lane >= to + 22) & (lane < to + 42), roll(mine, to + 22 - (at + 6)), acc
                )
                acc = jnp.where(
                    (lane >= to + 14) & (lane < to + 22), roll(left, to + 14 - (at + shift)), acc
                )
                acc = jnp.where(
                    (lane >= to + 42) & (lane < to + 50), roll(right, to + 42 - (at + shift)), acc
                )
            slab[f, :, 128 * m : 128 * m + 128] = acc
        for m in range(4):
            at = (f, slice(None), slice(128 * m, 128 * m + 128))
            after = (f, slice(None), slice(128 * (m + 6), 128 * (m + 7)))
            put(pos, first, second, at, slab[at], slab[after])


def settle(v, basis, j):
    lane = lanes((16, 128))
    for m in range(6):
        acc = jnp.zeros((16, 128), F32)
        for n in range(4):
            y = 4 * m + n - 8
            tile, at = (y + 14) // 2, 64 * ((y + 14) % 2)
            to = 32 * n
            piece = roll(v[:, 128 * tile : 128 * tile + 128], to + 5 - (at + 21))
            acc = jnp.where((lane >= to + 5) & (lane < to + 27), piece, acc)
        basis[j, :, 128 * m : 128 * m + 128] = acc


def two_sum(a, b):
    s = a + b
    t = s - a
    return s, (a - (s - t)) + (b - t)


def halves(a):
    t = a * 4097.0
    high = t - (t - a)
    return high, a - high


def two_prod(a, b):
    ah, al = halves(a)
    bh, bl = halves(b)
    p = a * b
    return p, ((ah * bh - p) + ah * bl + al * bh) + al * bl


def pair_mul(a, b):
    p, e = two_prod(a[0], b[0])
    return two_sum(p, e + (a[0] * b[1] + a[1] * b[0]))


def pair_sub(a, b):
    s, e = two_sum(a[0], -b[0])
    return two_sum(s, e + (a[1] - b[1]))


def pair_div(a, b):
    first = a[0] / b[0]
    rest = pair_sub(a, pair_mul((first, jnp.zeros_like(first)), b))
    return two_sum(first, rest[0] / b[0])


START = (0, 9, 17, 24, 30, 35, 39, 42)
PAIRS = sum(9 - i for i in range(BASIS))


def krylov_body(pos, scal, own, got_first, got_second, basis, gram, field, hold):
    for f in range(5):
        field[f, :, 0:512] = from_below(pos, got_first, got_second, f)
        field[f, :, 512:1792] = own[f]
        field[f, :, 1792:2304] = from_above(pos, got_first, got_second, f)
    center, half = scal[133], scal[134]
    lane8 = lanes((8, 128))

    def apply(v):
        total = field[1] * v
        for d in range(3):
            cond = field[2 + d]
            axis, step = ((0, 1), (1, 64), (1, 1))[d]
            total = total - cond * roll(v, -step, axis) - roll(cond * v, step, axis)
        return total

    def compact(v):
        acc = jnp.zeros((8, 128), F32)
        for t in range(2):
            for y in range(8):
                tile, at = (y + 14) // 2, 64 * ((y + 14) % 2) + 28
                to = 64 * t + 8 * y
                piece = v[8 * t : 8 * t + 8, 128 * tile : 128 * tile + 128]
                acc = jnp.where((lane8 >= to) & (lane8 < to + 8), roll(piece, to - at), acc)
        return acc

    before = None
    now = field[0]
    for j in range(BASIS):
        settle(now, basis, j)
        hold[j] = compact(now)
        image = apply(now)
        hold[BASIS + j] = compact(image)
        if j + 1 < BASIS:
            nxt = (image - center * now) * half
            if j > 0:
                nxt = 2.0 * nxt - before
            before, now = now, nxt
    high_rows, low_rows = [], []
    for i in range(BASIS):
        for j in range(i, BASIS + 1):
            other = hold[BASIS + j] if j < BASIS else hold[0]
            p, e = two_prod(hold[i], other)
            high_rows.append(p)
            low_rows.append(e)
    high = jnp.stack(high_rows)
    low = jnp.stack(low_rows)
    for axis, shifts in ((1, (4, 2, 1)), (2, (64, 32, 16, 8, 4, 2, 1))):
        for s in shifts:
            high, e = two_sum(high, roll(high, s, axis))
            low = low + roll(low, s, axis) + e
    row = jnp.zeros((8, 128), F32)
    for n in range(PAIRS):
        row = jnp.where(lane8 == n, high[n], row)
        row = jnp.where(lane8 == 64 + n, low[n], row)
    for m in range(2):
        gram[8 * m : 8 * m + 8, :] = row


def summed(gram):
    count = gram.shape[0] // 8
    high = gram[...].reshape(count, 8, 128)
    low = jnp.zeros((count, 8, 128), F32)
    while count > 1:
        count //= 2
        high, e = two_sum(high[:count], high[count : 2 * count])
        low = low[:count] + low[count : 2 * count] + e
    high, low = high[0], low[0]
    for s in (4, 2, 1):
        high, e = two_sum(high, roll(high, s, 0))
        low = low + roll(low, s, 0) + e
    return two_sum(high, low + roll(high, 64))


def gram_body(gram, out):
    high, low = summed(gram)
    row = jnp.where(lanes((8, 128)) < 64, high, roll(low, 64))
    for m in range(4):
        out[8 * m : 8 * m + 8, :] = row


def mid_post(pos, scal, gram, basis, cfm, level, out, sel, faces, inv, u, r, sol, jump, flux):
    high, low = summed(gram)
    lane = lanes((8, 128))
    sub = lax.broadcasted_iota(jnp.int32, (8, 128), 0)
    mat_h = jnp.zeros((8, 128), F32)
    mat_l = jnp.zeros((8, 128), F32)
    for i in range(BASIS):
        here = (sub == i) & (lane >= i) & (lane <= BASIS)
        mat_h = jnp.where(here, roll(high, i - START[i]), mat_h)
        mat_l = jnp.where(here, roll(low, i - START[i]), mat_l)
        for j in range(i + 1, BASIS):
            here = (sub == j) & (lane == i)
            shift = i - (START[i] + j - i)
            mat_h = jnp.where(here, roll(high, shift), mat_h)
            mat_l = jnp.where(here, roll(low, shift), mat_l)

    def spread_at(v, row, col):
        return jnp.broadcast_to(v[row : row + 1, col : col + 1], (8, 128))

    answers = []
    pivots = []
    for k in range(BASIS):
        start = spread_at(high, 0, START[k])
        piv = (spread_at(mat_h, k, k), spread_at(mat_l, k, k))
        good = jnp.abs(piv[0]) > 1e-12 * jnp.abs(start)
        safe = (jnp.where(good, piv[0], 1.0), jnp.where(good, piv[1], 0.0))
        pivots.append((safe, good))
        row = (
            jnp.broadcast_to(mat_h[k : k + 1, :], (8, 128)),
            jnp.broadcast_to(mat_l[k : k + 1, :], (8, 128)),
        )
        col = (
            jnp.broadcast_to(mat_h[:, k : k + 1], (8, 128)),
            jnp.broadcast_to(mat_l[:, k : k + 1], (8, 128)),
        )
        factor = pair_div(col, safe)
        use = good & (sub != k)
        factor = (jnp.where(use, factor[0], 0.0), jnp.where(use, factor[1], 0.0))
        mat_h, mat_l = pair_sub((mat_h, mat_l), pair_mul(factor, row))
    for k in range(BASIS):
        safe, good = pivots[k]
        value = pair_div((spread_at(mat_h, k, BASIS), spread_at(mat_l, k, BASIS)), safe)[0]
        answers.append(jnp.where(good, value, 0.0))
    weights = [jnp.concatenate([a, a], axis=0) for a in answers]
    lane16 = lanes((16, 128))
    for m in range(8):
        total = jnp.zeros((16, 128), F32)
        if 1 <= m <= 6:
            at = slice(128 * (m - 1), 128 * m)
            for j in range(BASIS):
                total = total + weights[j] * basis[j, :, at]
        for i in range(8):
            u[i, :, 128 * m : 128 * m + 128] = total
    mid_setup(pos, scal, cfm, sel, faces, inv, None)
    ends = jnp.zeros((16, 128), F32)
    for i in range(8):
        for ref in (r, sol):
            ref[i, :, 0:128] = ends
            ref[i, :, 896:1024] = ends
        r[i, :, 128:896] = level[1, i]
        sol[i, :, 128:896] = level[0, i] + u[i, :, 128:896]
    mid_apply(u, r, scal, cfm, faces, jump, flux)
    for i in range(8):
        new = inv[i] * r[i] / MIDDLE
        u[i] = new
        sol[i] = sol[i] + new
    mid_apply(u, r, scal, cfm, faces, jump, flux)
    mid_step(0, u, r, sol, inv)
    mid_apply(u, r, scal, cfm, faces, jump, flux)
    mid_step(1, u, r, sol, inv)
    for i in range(8):
        for half in range(2):
            acc = jnp.zeros((16, 128), F32)
            for n in range(8):
                y = 8 * half + n - 4
                tile, at = (y + 12) // 4, 32 * ((y + 12) % 4) + 8
                acc = jnp.where(
                    lane16 // 16 == n,
                    roll(sol[i, :, 128 * tile : 128 * tile + 128], 16 * n - at),
                    acc,
                )
            out[128 * half + 16 * i : 128 * half + 16 * i + 16, :] = acc


def post_body(
    pos, scal, gram, basis, cfm, level, keep, frz, got_first, got_second, coef, wide, spread,
    lift, diag_w, diag_e, out,
    sel, faces, mid_inv, mid_u, mid_r, mid_sol, jump, flux, mid, w, inv, u, r, sol, px, qx,
):
    fine_weights(pos, coef, w)
    wide_inside = jnp.concatenate([fine_places(pos)[0]] * (CHUNK // 256), axis=1)
    for c in range(CHUNKS):
        at = slice(CHUNK * c, CHUNK * (c + 1))
        inv[:, at] = fine_inverse(coef, w, diag_w, diag_e, wide_inside, at)
    mid_post(
        pos, scal, gram, basis, cfm, level, mid, sel, faces, mid_inv, mid_u, mid_r,
        mid_sol, jump, flux,
    )
    low = lanes((64, 128)) < 64
    px[:, 0:256] = jnp.zeros((16, 256), F32)
    qx[:, NX * 256 :] = jnp.zeros((16, 256), F32)
    for x in range(NX):
        first, second = slice(256 * x, 256 * x + 128), slice(256 * x + 128, 256 * x + 256)
        turned = roll(frz[x], 64)
        at = 384 + 64 * (x % 8)
        down = from_below(pos, got_first, got_second, slice(at, at + 64))
        over = from_above(pos, got_first, got_second, slice(at, at + 64))
        if x >= 8:
            down = roll(down, 64)
        else:
            over = roll(over, 64)
        r[:, first] = jnp.where(low, down, turned)
        r[:, second] = jnp.where(low, turned, over)
    planes = CHUNK // 256
    for c in range(CHUNKS):
        at = slice(CHUNK * c, CHUNK * (c + 1))
        pieces = [
            mid[pl.ds(128 * half + planes * c + n, 8, stride=16), :]
            for n in range(planes)
            for half in range(2)
        ]
        high, rest = split3(jnp.concatenate(pieces, axis=1))
        stacked = jnp.concatenate([high, rest, high, jnp.zeros((8, CHUNK), F32)], axis=0)
        lifted = mm(lift[...], stacked.astype(BF16))
        u[:, at] = lifted
        sol[:, at] = lifted
    fine_apply(u, r, w, coef, wide, spread, px, qx, None, sol, inv)
    for c in range(CHUNKS):
        at = slice(CHUNK * c, CHUNK * (c + 1))
        new = inv[:, at] * r[:, at] / MIDDLE
        u[:, at] = new
        sol[:, at] = sol[:, at] + new
    fine_apply(u, r, w, coef, wide, spread, px, qx, 0, sol, inv)
    fine_apply(u, r, w, coef, wide, spread, px, qx, 1, sol, inv)
    fine_apply(u, r, w, coef, wide, spread, px, qx, None, sol, inv)
    lane = lanes((64, 128))
    for x in range(NX):
        acc = jnp.zeros((64, 128), F32)
        for part, ref in enumerate((sol, r)):
            for y in range(8):
                half, at = (y + 4) // 8, 16 * ((y + 4) % 8) + 4
                start = 256 * x + 128 * half
                acc = jnp.where(
                    lane // 8 == 8 * part + y,
                    roll(ref[:, start : start + 128], 64 * part + 8 * y - at),
                    acc,
                )
        kept = keep[x % 8] if x < 8 else roll(keep[x % 8], 64)
        out[x] = acc + jnp.where(low, kept, 0.0)


def unpack_body(got, first, second):
    low = lanes((64, 128)) < 64
    for part, out in enumerate((first, second)):
        held = []
        for g in range(8):
            a, b = got[ORDER[g]], got[ORDER[g + 8]]
            if part == 0:
                held.append(jnp.where(low, a, roll(b, 64)))
            else:
                held.append(jnp.where(low, roll(a, 64), b))
        for y, rows in enumerate(exchange(held, 8)):
            out[pl.ds(y, 64, stride=8), :] = rows


def trace_tables():
    high = np.zeros((3, 16, 64), np.float32)
    low = np.zeros((3, 16, 64), np.float32)
    for p in range(4):
        for q in range(4):
            for d in range(3):
                for table, at in ((high, 3), (low, 0)):
                    index = [p, q]
                    index.insert(d, at)
                    table[d, 4 * p + q, 16 * index[0] + 4 * index[1] + index[2]] = 1.0
    return high, low


def mid_traces():
    high = np.zeros((3, 4, 8), np.float32)
    low = np.zeros((3, 4, 8), np.float32)
    for d in range(3):
        for n in range(4):
            high[d, n, HIGHS[d][n]] = 1.0
            low[d, n, LOWS[d][n]] = 1.0
    return high, low


def prolong_tables():
    node_points = jnp.array(
        [-1.0, -1.0 / math.sqrt(5.0), 1.0 / math.sqrt(5.0), 1.0], dtype=jnp.float32
    )
    basis_table = jnp.stack([(1.0 - node_points) * 0.5, (1.0 + node_points) * 0.5], axis=1)
    volume = (
        basis_table[:, None, None, :, None, None]
        * basis_table[None, :, None, None, :, None]
        * basis_table[None, None, :, None, None, :]
    ).reshape(64, 8)
    surface = (basis_table[:, None, :, None] * basis_table[None, :, None, :]).reshape(16, 4)
    return (volume, surface)


def cut(x):
    return lax.reduce_precision(x, 8, 7)


def two_parts(x):
    high = cut(x)
    return high, cut(x - high)


def three_parts(x):
    high = cut(x)
    rest = x - high
    mid = cut(rest)
    return high, mid, cut(rest - mid)


def tables(element, faces):
    volume, surface = prolong_tables()
    elem_mid = jnp.dot(volume.T, jnp.dot(element, volume, precision=HIGHEST), precision=HIGHEST)
    face_mid = jnp.einsum("kij,jb->kib", faces, surface, precision=HIGHEST)
    face_mid = jnp.einsum("ia,kib->kab", surface, face_mid, precision=HIGHEST)
    elem_coarse = jnp.sum(elem_mid)
    face_coarse = jnp.sum(face_mid, axis=(1, 2))
    high, low = trace_tables()
    both = np.concatenate([high, low], axis=0)
    rows = jnp.einsum("kij,djm->dkim", faces, both, precision=HIGHEST).reshape(384, 64)
    wide = jnp.concatenate([element, rows], axis=0)
    wh, wl = two_parts(wide)
    wide = jnp.concatenate([wh, wh, wl], axis=1).astype(BF16)
    spread = np.concatenate([high[1], -low[1], high[2], -low[2]], axis=0).T
    spread = np.concatenate([spread, spread], axis=1)
    face_diag = jnp.diagonal(faces, axis1=1, axis2=2)
    diag = jnp.einsum("dim,ki->mdk", both, face_diag, precision=HIGHEST).reshape(64, 24)
    diag_w = jnp.concatenate(three_parts(diag) + (jnp.zeros((64, 8), F32),), axis=1).astype(BF16)
    diag_e = jnp.diagonal(element)[:, None]
    mh, ml = mid_traces()
    both = np.concatenate([mh, ml], axis=0)
    diag = jnp.einsum(
        "dim,ki->mdk", both, jnp.diagonal(face_mid, axis1=1, axis2=2), precision=HIGHEST
    ).reshape(8, 24)
    mid_diag_w = jnp.concatenate(three_parts(diag) + (jnp.zeros((8, 8), F32),), axis=1).astype(BF16)
    mid_diag_e = jnp.diagonal(elem_mid)[:, None]
    vh, vl = two_parts(volume)
    down = jnp.concatenate([vh.T, vh.T, vl.T], axis=1).astype(BF16)
    lift = jnp.concatenate([vh, vh, vl, jnp.zeros((64, 8), F32)], axis=1).astype(BF16)
    least = 0.1 * elem_coarse
    most = 1.35 * elem_coarse + 9.0 * jnp.max(jnp.abs(face_coarse))
    half = 0.5 * (most - least)
    half = jnp.where(jnp.abs(half) > 0.0, half, 1.0)
    scal = jnp.concatenate(
        [
            elem_mid.reshape(-1),
            face_mid.reshape(-1),
            elem_coarse[None],
            face_coarse,
            (0.5 * (most + least))[None],
            (1.0 / half)[None],
            jnp.zeros((9,), F32),
        ]
    )
    return (
        wide,
        jnp.asarray(spread, BF16),
        diag_w,
        diag_e,
        down,
        mid_diag_w,
        mid_diag_e,
        lift,
        scal,
    )


def local(residual, coefficient, element, faces, kind, flag):
    y_first = [(i, i ^ 1) for i in range(16)]
    y_second = [p for i in range(1, 15, 2) for p in ((i, i + 1), (i + 1, i))]

    def z_index(zb):
        return ORDER[zb % 16] * 2 + zb // 16

    z_up = [(z_index(i), z_index(i + 1)) for i in range(31)]
    z_dn = [(z_index(i + 1), z_index(i)) for i in range(31)]
    z_axes = ("gx", "lvl")
    side = lax.axis_index("lvl")
    chip = lax.axis_index("gx")
    pos = jnp.stack(
        [
            lax.axis_index("yz"),
            side * 16 + jnp.where(chip % 2 == 0, chip // 2, 15 - chip // 2),
        ]
    ).astype(jnp.int32)
    res = residual.reshape(512, 128)
    slots = call(
        slots_body,
        "slots",
        [f32s(16, 40, 128)],
        (0,) * 4,
        [pltpu.VMEM((128, 128), F32)],
        limit=LARGE_LIMIT,
    )(res, coefficient.reshape(8, 128), kind.reshape(48, 128), flag.reshape(48, 128))[0]
    element, faces, slots = lax.optimization_barrier((element, faces, slots))
    wide, spread, diag_w, diag_e, down, mid_diag_w, mid_diag_e, lift, scal = tables(element, faces)
    own = lax.all_to_all(slots, "gx", 0, 0, tiled=True)
    dn = lax.ppermute(own[:, 16:40], z_axes, z_up)
    up = lax.ppermute(own[:, 0:24], z_axes, z_dn)
    place_values, place_kinds, pack = place_tables()
    rows, own, other = call(
        join_body,
        "join",
        [f32s(NX, 64, 128), f32s(768, 128), f32s(768, 128)],
        (1,) + (0,) * 5,
    )(pos, own, dn, up, place_values, place_kinds)
    got_first = lax.ppermute(own, "yz", y_first)
    got_second = lax.ppermute(other, "yz", y_second)
    plane = (64, NX * 256)
    strip = (16, NX * 256 + 256)
    keep, r, coef, cfm, send_up, send_down = call(
        fine_pre_body,
        "fine_pre",
        [
            f32s(8, 64, 128),
            f32s(*plane),
            f32s(8, NX * 256),
            f32s(128, 1024),
            f32s(384, 128),
            f32s(384, 128),
        ],
        (1,) + (0,) * 12,
        [
            pltpu.VMEM(plane, F32),
            pltpu.VMEM((24, NX * 256), F32),
            pltpu.VMEM(plane, F32),
            pltpu.VMEM(plane, F32),
            pltpu.VMEM(strip, F32),
            pltpu.VMEM(strip, F32),
            pltpu.VMEM((896, 128), F32),
            pltpu.VMEM((256, 128), F32),
        ],
    )(
        pos, rows, own, got_first, got_second, wide, spread, diag_w, diag_e, down, mid_diag_w, mid_diag_e, pack
    )
    dn = lax.ppermute(send_up, z_axes, z_up)
    up = lax.ppermute(send_down, z_axes, z_dn)
    slab, first, second, frz = call(
        mid_z_body,
        "mid_z",
        [f32s(128, 256), f32s(896, 128), f32s(896, 128), f32s(NX, 64, 128)],
        (1,) + (0,) * 4,
    )(pos, send_up, dn, up, r)
    got_first = lax.ppermute(first, "yz", y_first)
    got_second = lax.ppermute(second, "yz", y_second)
    mid = (8, 16, 1024)
    mid_scratch = [
        pltpu.VMEM((3, 16, 1024), F32),
        pltpu.VMEM((3, 16, 16, 1024), F32),
        pltpu.VMEM(mid, F32),
    ]
    tail_scratch = [pltpu.VMEM((4, 16, 1024), F32), pltpu.VMEM((12, 16, 1024), F32)]
    level, coarse, send_up, send_down = call(
        mid_pre_body,
        "mid_pre",
        [f32s(2, 8, 16, 768), f32s(5, 16, 1024), f32s(2, 16, 768), f32s(2, 16, 768)],
        (1, 1, 0, 0, 0, 0),
        mid_scratch
        + [pltpu.VMEM(mid, F32)] * 4
        + tail_scratch,
    )(pos, scal, slab, got_first, got_second, cfm)
    dn = lax.ppermute(send_up, z_axes, z_up)
    up = lax.ppermute(send_down, z_axes, z_dn)
    coarse_slab, first, second = call(
        coarse_z_body,
        "coarse_z",
        [f32s(5, 16, 1280), f32s(5, 16, 512), f32s(5, 16, 512)],
        (1, 0, 0, 0),
    )(pos, coarse, dn, up)
    coarse_first = lax.ppermute(first, "yz", y_first)
    coarse_second = lax.ppermute(second, "yz", y_second)
    basis, gram = call(
        krylov_body,
        "krylov",
        [f32s(BASIS, 16, 768), f32s(16, 128)],
        (1, 1, 0, 0, 0),
        [
            pltpu.VMEM((5, 16, 2304), F32),
            pltpu.VMEM((2 * BASIS, 8, 128), F32),
        ],
    )(pos, scal, coarse_slab, coarse_first, coarse_second)
    gram = lax.all_to_all(gram, "yz", 0, 0, tiled=True)
    gram = call(gram_body, "gram", [f32s(32, 128)], (0,))(gram)[0]
    gram = lax.all_to_all(gram, z_axes, 0, 0, tiled=True)
    packed = call(
        post_body,
        "post",
        [f32s(16, 64, 128)],
        (1, 1) + (0,) * 14,
        mid_scratch
        + [pltpu.VMEM(mid, F32)] * 3
        + tail_scratch
        + [
            pltpu.VMEM((256, 128), F32),
            pltpu.VMEM((24, NX * 256), F32),
            pltpu.VMEM(plane, F32),
            pltpu.VMEM(plane, F32),
            pltpu.VMEM(plane, F32),
            pltpu.VMEM(plane, F32),
            pltpu.VMEM(strip, F32),
            pltpu.VMEM(strip, F32),
        ],
        limit=LARGE_LIMIT,
    )(
        pos, scal, gram, basis, cfm, level, keep, frz, got_first, got_second, coef, wide, spread,
        lift, diag_w, diag_e,
    )[0]
    got = lax.all_to_all(packed, "gx", 0, 0, tiled=True)
    correction, rest = call(unpack_body, "unpack", [f32s(512, 128), f32s(512, 128)], (0,))(got)
    return (correction.reshape(64, 1, 8, 128), rest.reshape(64, 1, 8, 128))


def solution(mesh):
    in_specs = (
        P(None, "gx", "yz", "lvl"),
        P("gx", "yz", "lvl"),
        P(),
        P(),
        P(None, "gx", "yz", "lvl"),
        P(None, "gx", "yz", "lvl"),
    )
    out_specs = (P(None, "gx", "yz", "lvl"), P(None, "gx", "yz", "lvl"))
    return jax.shard_map(local, mesh=mesh, in_specs=in_specs, out_specs=out_specs, check_vma=False)
```

```python
import functools
import math

import jax
import jax.numpy as jnp
import numpy as np
from jax import lax
from jax.experimental import pallas as pl
from jax.experimental.pallas import tpu as pltpu
from jax.sharding import PartitionSpec as P

NX = 16
NY = 128
NZ = 256
KINDS = 4
F32 = jnp.float32
BF16 = jnp.bfloat16
HIGHEST = lax.Precision.HIGHEST
LOW_EIG = 0.3
HIGH_EIG = 3.0
MIDDLE = 0.5 * (HIGH_EIG + LOW_EIG)
SPREAD = 0.5 * (HIGH_EIG - LOW_EIG)
SCALED = MIDDLE / SPREAD
RHO0 = 1.0 / SCALED
RHO1 = 1.0 / (2.0 * SCALED - RHO0)
RHO2 = 1.0 / (2.0 * SCALED - RHO1)
STEPS = ((RHO1 * RHO0, 2.0 * RHO1 / SPREAD), (RHO2 * RHO1, 2.0 * RHO2 / SPREAD))
BASIS = 8
ORDER = tuple(2 * n if n < 8 else 2 * (15 - n) + 1 for n in range(16))
VMEM_LIMIT = 24 * 2**20
LARGE_LIMIT = 60 * 2**20


def lanes(shape):
    return lax.broadcasted_iota(jnp.int32, shape, len(shape) - 1)


def roll(x, shift, axis=None):
    axis = x.ndim - 1 if axis is None else axis
    shift = shift % x.shape[axis]
    return x if shift == 0 else pltpu.roll(x, shift, axis)


SPACES = {
    0: pl.BlockSpec(memory_space=pltpu.VMEM),
    1: pl.BlockSpec(memory_space=pltpu.SMEM),
}


def call(body, name, out_shape, in_specs, scratch=(), out_specs=None, limit=VMEM_LIMIT):
    out_specs = out_specs or (0,) * len(out_shape)
    return pl.pallas_call(
        body,
        out_shape=list(out_shape),
        in_specs=[SPACES[i] for i in in_specs],
        out_specs=[SPACES[i] for i in out_specs],
        scratch_shapes=list(scratch),
        compiler_params=pltpu.CompilerParams(vmem_limit_bytes=limit),
        cost_estimate=pl.CostEstimate(flops=1000000, bytes_accessed=1000000, transcendentals=0),
        name=name,
    )


def even(pos):
    return pos[0] % 2 == 0


def put(parity, first, second, at, fwd, bwd):
    is_even = jnp.broadcast_to(parity[0:1, :], fwd.shape) == 0.0
    first[at] = jnp.where(is_even, fwd, bwd)
    second[at] = jnp.where(is_even, bwd, fwd)


def from_below(pos, first, second, at):
    return jnp.where(even(pos), second[at], first[at])


def from_above(pos, first, second, at):
    return jnp.where(even(pos), first[at], second[at])


def f32s(*shape):
    return jax.ShapeDtypeStruct(shape, F32)


def split3(x):
    high = x.astype(BF16).astype(F32)
    low = x - high
    return high, low


def stack_hlh(x):
    high, low = split3(x)
    return jnp.concatenate([high, low, high], axis=0).astype(BF16)


def mm(a, b):
    return jnp.dot(a, b, preferred_element_type=F32)


def exchange(arrays, lane_block):
    arrays = list(arrays)
    group = lanes(arrays[0].shape) // lane_block
    for bit in (1, 2, 4):
        upper = (group // bit) % 2 == 1
        for n in range(8):
            if n & bit:
                continue
            a, b = arrays[n], arrays[n | bit]
            arrays[n] = jnp.where(upper, roll(b, lane_block * bit), a)
            arrays[n | bit] = jnp.where(upper, b, roll(a, -lane_block * bit))
    return arrays


def slots_body(res, coef, kind, flag, out, cf):
    for n in range(16):
        cf[8 * n : 8 * n + 8, :] = jnp.zeros((8, 128), F32)
    cf[0:8, :] = coef[...]
    for first, ref in ((8, kind), (32, flag)):
        for n in range(3):
            at = 8 * (2 * n + 1)
            cf[first + 8 * n : first + 8 * n + 8, :] = ref[at : at + 8, :].astype(F32)
    for first, ref in ((80, kind), (104, flag)):
        for n in range(2):
            at = 8 * (2 * n + 2)
            cf[first + 8 * n : first + 8 * n + 8, :] = ref[at : at + 8, :].astype(F32)
    low = lanes((16, 128)) < 64
    low8 = lanes((8, 128)) < 64
    near = lanes((32, 128)) % 8 < 4
    values = exchange([res[pl.ds(y, 64, stride=8), :] for y in range(8)], 8)
    kinds = exchange([cf[pl.ds(y, 16, stride=8), :] for y in range(8)], 8)
    for j in range(8):
        first, second = ORDER[j], ORDER[j + 8]
        a, b = values[j][0:32], values[j][32:64]
        for at, v in (
            (0, jnp.where(near, a, roll(b, 4))),
            (24, jnp.where(near, roll(a, -4), b)),
        ):
            out[first, at : at + 16, :] = jnp.where(low, v[0:16], roll(v[16:32], 64))
            out[second, at : at + 16, :] = jnp.where(low, roll(v[0:16], 64), v[16:32])
        a, b = kinds[j][0:8], kinds[j][8:16]
        out[first, 16:24, :] = jnp.where(low8, a, roll(b, 64))
        out[second, 16:24, :] = jnp.where(low8, roll(a, 64), b)


def place_tables():
    values = np.zeros((512, 512), np.float32)
    kinds = np.zeros((384, 512), np.float32)
    pack = np.zeros((256, 128), np.float32)
    for half in range(2):
        for y in range(8):
            for z in range(8):
                lane = 64 * half + 8 * y + z
                to = 128 * (2 * (z // 4) + half) + 16 * y + z % 4
                for n, first in enumerate((4, 8, 12, 0)):
                    values[128 * n + lane, to + first] = 1.0
                for n, first in enumerate((12, 4, 20)):
                    kinds[128 * n + lane, 256 * half + 32 * y + first + z] = 1.0
    for y in range(-1, 9):
        for z in range(-1, 9):
            pack[16 * (y + 4) + z + 4, 12 * (y + 1) + z + 1] = 1.0
    return [jnp.asarray(v, BF16) for v in (values, kinds, pack)]


def three_rows(x):
    high = x.astype(BF16).astype(F32)
    rest = x - high
    mid = rest.astype(BF16).astype(F32)
    return jnp.concatenate([high, mid, rest - mid], axis=0).astype(BF16)


def moved(x, table):
    count = x.shape[0]
    out = mm(three_rows(x), table)
    return out[0:count] + out[count : 2 * count] + out[2 * count :]


def join_body(parity, own, dn, up, place_values, place_kinds, rows, first, second):
    parts = (own[:, 0:16, :], own[:, 24:40, :], up[:, 0:16, :], dn[:, 8:24, :])
    values = jnp.concatenate([v.reshape(256, 128) for v in parts], axis=1)
    out = moved(values, place_values[...])
    for x in range(NX):
        for n in range(4):
            rows[x, 16 * n : 16 * n + 16, :] = out[16 * x : 16 * x + 16, 128 * n : 128 * n + 128]
    low = lanes((64, 128)) < 64
    for x in range(8):
        fwd = jnp.where(low, roll(rows[x], 64), rows[x + 8])
        bwd = jnp.where(low, rows[x], roll(rows[x + 8], 64))
        put(parity, first, second, slice(64 * x, 64 * x + 64), fwd, bwd)
    parts = (own[:, 16:24, :], dn[:, 0:8, :], up[:, 16:24, :])
    kinds = jnp.concatenate([v.reshape(128, 128) for v in parts], axis=1)
    out = moved(kinds, place_kinds[...])
    array = lax.broadcasted_iota(jnp.int32, (128, 128), 0) % 8
    edge = (lanes((128, 128)) % 32 == 3) & ((array == 3) | (array == 6))
    lane = lanes((128, 128))
    for h in range(2):
        minus = out[:, 256 + 128 * h : 384 + 128 * h]
        plus = jnp.where(edge, roll(minus, -1), out[:, 128 * h : 128 * h + 128])
        if h == 0:
            plus = jnp.where((array == 7) & (lane < 32), roll(minus, 5, 0), plus)
            plus = jnp.where(
                (array == 7) & (lane >= 32) & (lane < 64), roll(roll(minus, 2, 0), 32), plus
            )
        first[512 + 128 * h : 640 + 128 * h, :] = plus
        second[512 + 128 * h : 640 + 128 * h, :] = plus


CHUNK = 4096
CHUNKS = NX * 256 // CHUNK


def fine_apply(u, r, w, coef, wide, spread, px, qx, step, sol, inv):
    for c in range(CHUNKS):
        at = slice(CHUNK * c, CHUNK * (c + 1))
        after = slice(CHUNK * c + 256, CHUNK * (c + 1) + 256)
        prod = mm(wide[...], stack_hlh(u[:, at]))

        def pick(base, row):
            total = w[row : row + 1, at] * prod[base : base + 16]
            for k in range(1, KINDS):
                total = total + w[row + k : row + k + 1, at] * prod[base + 16 * k : base + 16 * k + 16]
            return total

        px[:, after] = pick(64, 0)
        py = pick(128, 4)
        pz = pick(192, 8)
        qx[:, at] = pick(256, 12)
        qy = pick(320, 16)
        qz = pick(384, 20)
        flux = jnp.concatenate(
            [py - roll(qy, -16), roll(py, 16) - qy, pz - roll(qz, -1), roll(pz, 1) - qz], axis=0
        )
        high, low = split3(flux)
        faces = mm(spread[...], jnp.concatenate([high, low], axis=0).astype(BF16))
        r[:, at] = r[:, at] - (coef[0:1, at] * prod[0:64] + faces)

    for c in range(CHUNKS):
        at = slice(CHUNK * c, CHUNK * (c + 1))
        after = slice(CHUNK * c + 256, CHUNK * (c + 1) + 256)
        r[48:64, at] = r[48:64, at] - (px[:, after] - qx[:, after])
        r[0:16, at] = r[0:16, at] + (px[:, at] - qx[:, at])
        if step is not None:
            keep, gain = STEPS[step]
            new = keep * u[:, at] + gain * (inv[:, at] * r[:, at])
            u[:, at] = new
            sol[:, at] = sol[:, at] + new


def fine_places(pos):
    place = lanes((1, 256))
    y_at = pos[0] * 8 - 4 + place // 16
    z_at = pos[1] * 8 - 4 + place % 16
    inside = (y_at >= 0) & (y_at < NY) & (z_at >= 0) & (z_at < NZ)
    return inside, inside & (y_at < NY - 1), inside & (z_at < NZ - 1)


def fine_weights(pos, coef, w):
    inside, has_y, has_z = fine_places(pos)
    w[12:16, 0:256] = jnp.zeros((4, 256), F32)
    for x in range(NX):
        at = slice(256 * x, 256 * x + 256)
        rows = coef[:, at]
        opens = [
            inside & (rows[4:5] == 0.0) if x < NX - 1 else jnp.zeros((1, 256), jnp.bool_),
            has_y & (rows[5:6] == 0.0),
            has_z & (rows[6:7] == 0.0),
        ]
        plus = [
            [jnp.where(opens[d] & (rows[1 + d : 2 + d] == float(k)), 1.0, 0.0) for k in range(KINDS)]
            for d in range(3)
        ]
        plus_all = jnp.concatenate(plus[0] + plus[1] + plus[2], axis=0)
        w[0:12, at] = plus_all
        if x < NX - 1:
            w[12:16, 256 * x + 256 : 256 * x + 512] = plus_all[0:4]
        w[16:20, at] = roll(plus_all[4:8], 16)
        w[20:24, at] = roll(plus_all[8:12], 1)


def kinds_of(w, at):
    ws = w[:, at]
    return jnp.concatenate([ws, ws, ws, jnp.zeros((8, CHUNK), F32)], axis=0).astype(BF16)


def fine_inverse(coef, w, diag_w, diag_e, inside, at):
    diag = diag_e[...] * coef[0:1, at] + mm(diag_w[...], kinds_of(w, at))
    return jnp.where(inside, 1.0 / diag, 0.0)


def compacted(first, second, lane):
    v = roll(jnp.where(lane < 64, roll(first, 64), roll(second, 64)), -4)
    for size in (8, 16, 32):
        v = jnp.where(lane % (4 * size) < size, v, roll(v, -size))
    return v


def fine_pre_body(
    pos,
    rows_in,
    own,
    got_first,
    got_second,
    wide,
    spread,
    diag_w,
    diag_e,
    down,
    mid_diag_w,
    mid_diag_e,
    pack,
    keep,
    r,
    coef,
    cfm,
    send_up,
    send_down,
    sol,
    w,
    inv,
    u,
    px,
    qx,
    gather,
    held,
):
    low = lanes((64, 128)) < 64
    lane8 = lanes((8, 128))
    inside = fine_places(pos)[0]
    px[:, 0:256] = jnp.zeros((16, 256), F32)
    qx[:, NX * 256 :] = jnp.zeros((16, 256), F32)
    cfm[:, 896:1024] = jnp.zeros((128, 128), F32)
    array = lax.broadcasted_iota(jnp.int32, (8, 128), 0)
    edge = (lane8 >= 96) & ((array == 2) | (array == 5))
    for x in range(NX):
        first, second = slice(256 * x, 256 * x + 128), slice(256 * x + 128, 256 * x + 256)
        turned = roll(rows_in[x], 64)
        at = 64 * (x % 8)
        under = from_below(pos, got_first, got_second, slice(at, at + 64))
        over = from_above(pos, got_first, got_second, slice(at, at + 64))
        if x >= 8:
            under = roll(under, 64)
        else:
            over = roll(over, 64)
        r[:, first] = jnp.where(low, under, turned)
        r[:, second] = jnp.where(low, turned, over)
        places = [slice(512 + 128 * h + 8 * x, 520 + 128 * h + 8 * x) for h in range(2)]
        blocks = (
            [from_below(pos, got_first, got_second, p) for p in places]
            + [own[p] for p in places]
            + [from_above(pos, got_first, got_second, p) for p in places]
        )
        minus = jnp.where(array == 2, roll(roll(blocks[0], 3, 0), 96), roll(roll(blocks[0], 6, 0), 64))
        gather[pl.ds(x, 8, stride=16), :] = jnp.where(edge, minus, 0.0)
        for m in range(6):
            gather[pl.ds(128 * (m + 1) + x, 8, stride=16), :] = blocks[m]
        for half, at in enumerate((first, second)):
            acc = jnp.zeros((8, 128), F32)
            for row in range(8):
                n = 8 * half + row
                acc = jnp.where(
                    lane8 // 16 == row,
                    roll(blocks[1 + n // 4], 16 * row - (n % 4) * 32 - 8),
                    acc,
                )
            coef[:, at] = acc
    for m in range(7):
        cfm[:, 128 * m : 128 * m + 128] = gather[128 * m : 128 * m + 128, :]
    fine_weights(pos, coef, w)
    wide_inside = jnp.concatenate([inside] * (CHUNK // 256), axis=1)
    for c in range(CHUNKS):
        at = slice(CHUNK * c, CHUNK * (c + 1))
        inverse = fine_inverse(coef, w, diag_w, diag_e, wide_inside, at)
        inv[:, at] = inverse
        update = inverse * r[:, at] / MIDDLE
        u[:, at] = update
        sol[:, at] = update
    fine_apply(u, r, w, coef, wide, spread, px, qx, 0, sol, inv)
    fine_apply(u, r, w, coef, wide, spread, px, qx, 1, sol, inv)
    fine_apply(u, r, w, coef, wide, spread, px, qx, None, sol, inv)
    lane16 = lanes((16, 128)) % 16 // 4
    for c in range(CHUNKS):
        at = slice(CHUNK * c, CHUNK * (c + 1))
        rhs = mm(down[...], stack_hlh(r[:, at]))
        diag = mid_diag_e[...] * coef[0:1, at] + mm(mid_diag_w[...], kinds_of(w, at))
        update = jnp.where(wide_inside, 1.0 / diag, 0.0) * rhs / MIDDLE
        for n in range(CHUNK // 256):
            x = (CHUNK // 256) * c + n
            for half in range(2):
                piece = update[:, 256 * n + 128 * half : 256 * n + 128 * half + 128]
                held[pl.ds(128 * half + x, 8, stride=16), :] = piece
    packed = moved(jnp.concatenate([held[0:128, :], held[128:256, :]], axis=1), pack[...])
    send_up[0:128, :] = packed
    send_down[0:128, :] = packed
    for x in range(NX):
        first, second = slice(256 * x, 256 * x + 128), slice(256 * x + 128, 256 * x + 256)
        mine = jnp.where(low, roll(r[:, first], 64), roll(r[:, second], 64))
        up = jnp.zeros((16, 128), F32)
        dn = jnp.zeros((16, 128), F32)
        for j in range(4):
            part = mine[16 * j : 16 * j + 16]
            up = jnp.where(lane16 == j, roll(part, 4 * j - 8), up)
            dn = jnp.where(lane16 == j, roll(part, 4 * j - 4), dn)
        send_up[128 + 16 * x : 144 + 16 * x, :] = up
        send_down[128 + 16 * x : 144 + 16 * x, :] = dn
    lane = lanes((64, 128))
    for x in range(8):
        a, b = [
            compacted(sol[:, 256 * n : 256 * n + 128], sol[:, 256 * n + 128 : 256 * n + 256], lane)
            for n in (x, x + 8)
        ]
        keep[x] = jnp.where(low, a, roll(b, 64))


def mid_z_body(parity, own, dn, up, r, slab, first, second, frz):
    low = lanes((64, 128)) < 64
    l16 = lanes((16, 128)) % 16
    for x in range(NX):
        at = 256 * x
        mine = jnp.where(low, roll(r[:, at : at + 128], 64), roll(r[:, at + 128 : at + 256], 64))
        pack_dn = dn[128 + 16 * x : 144 + 16 * x, :]
        pack_up = up[128 + 16 * x : 144 + 16 * x, :]
        for j in range(4):
            rows = slice(16 * j, 16 * j + 16)
            part = jnp.where(l16 < 4, roll(pack_dn, -4 * j), mine[rows])
            part = jnp.where(l16 >= 12, roll(pack_up, 12 - 4 * j), part)
            frz[x, rows, :] = part
    for x in range(8):
        fwd = jnp.where(low, roll(frz[x], 64), frz[x + 8])
        bwd = jnp.where(low, frz[x], roll(frz[x + 8], 64))
        put(parity, first, second, slice(384 + 64 * x, 448 + 64 * x), fwd, bwd)
    lane = lanes((128, 128))
    tiles = []
    for m in range(4):
        acc = jnp.zeros((128, 128), F32)
        for n in range(4):
            y = 4 * (m - 1) + n
            if y < -1 or y > 8:
                continue
            to = 32 * n
            at = 12 * (y + 1)
            rows = slice(0, 128)
            acc = jnp.where((lane >= to + 12) & (lane < to + 20), roll(own[rows, :], to + 11 - at), acc)
            acc = jnp.where((lane >= to + 3) & (lane < to + 12), roll(dn[rows, :], to + 3 - at), acc)
            acc = jnp.where((lane >= to + 20) & (lane < to + 29), roll(up[rows, :], to + 19 - at), acc)
        if 1 <= m <= 2:
            slab[:, 128 * (m - 1) : 128 * m] = acc
        tiles.append(acc)
    for m in range(3):
        put(parity, first, second, slice(128 * m, 128 * m + 128), tiles[m], tiles[m + 1])


LOWS = ((0, 1, 2, 3), (0, 1, 4, 5), (0, 2, 4, 6))
HIGHS = ((4, 5, 6, 7), (2, 3, 6, 7), (1, 3, 5, 7))


def ahead(v, d):
    if d == 0:
        return roll(v, -1, 0)
    return roll(v, -32 if d == 1 else -1, 1)


def behind(v, d):
    if d == 0:
        return roll(v, 1, 0)
    return roll(v, 32 if d == 1 else 1, 1)


def mid_setup(pos, scal, cfm, sel, faces, inv, diag):
    place = lanes((16, 1024))
    x_at = lax.broadcasted_iota(jnp.int32, (16, 1024), 0)
    y_at = pos[0] * 8 - 12 + place // 32
    z_at = pos[1] * 8 - 12 + place % 32
    domain = (y_at >= 0) & (y_at < NY) & (z_at >= 0) & (z_at < NZ)
    known = domain & (place >= 128) & (place < 896) & (place % 32 >= 4) & (place % 32 < 28)
    lasts = (x_at < NX - 1, y_at < NY - 1, z_at < NZ - 1)
    for d in range(3):
        is_open = domain & lasts[d] & (cfm[64 + 16 * d : 80 + 16 * d, :] == 0.0)
        sel[d] = jnp.where(is_open, cfm[16 + 16 * d : 32 + 16 * d, :], 4.0)
    coef = cfm[0:16, :]

    for d in range(3):
        for c in range(8):
            at = slice(128 * c, 128 * c + 128)
            kind = sel[d, :, at]
            ones = [kind == float(k) for k in range(KINDS)]
            for i in range(4):
                for j in range(i, 4):
                    value = jnp.zeros((16, 128), F32)
                    for k in range(KINDS):
                        value = jnp.where(ones[k], scal[64 + 16 * k + 4 * i + j], value)
                    faces[d, 4 * i + j, :, at] = value
    if inv is None:
        return known
    for i in range(8):
        total = coef * scal[9 * i]
        for d in range(3):
            if i in HIGHS[d]:
                total = total + faces[d, 5 * HIGHS[d].index(i)]
            else:
                total = total + behind(faces[d, 5 * LOWS[d].index(i)], d)
        if diag is not None:
            diag[i] = total
        inv[i] = jnp.where(known, 1.0 / total, 0.0)
    return known


def mid_apply(v, r, scal, cfm, faces, jump, flux):
    for d in range(3):
        for j in range(4):
            jump[j] = v[HIGHS[d][j]] - ahead(v[LOWS[d][j]], d)

        for c in range(8):
            at = slice(128 * c, 128 * c + 128)
            jumps = [jump[j, :, at] for j in range(4)]
            for i in range(4):
                total = faces[d, i, :, at] * jumps[0]
                for j in range(1, 4):
                    total = total + faces[d, 4 * min(i, j) + max(i, j), :, at] * jumps[j]
                flux[4 * d + i, :, at] = total

    for c in range(1, 7):
        at = slice(128 * c, 128 * c + 128)
        values = [v[j, :, at] for j in range(8)]
        coef = cfm[0:16, at]
        for i in range(8):
            total = scal[8 * i] * values[0]
            for j in range(1, 8):
                total = total + scal[8 * i + j] * values[j]
            r[i, :, at] = r[i, :, at] - coef * total
    for d in range(3):
        for j in range(4):
            value = flux[4 * d + j]
            r[HIGHS[d][j]] = r[HIGHS[d][j]] - value
            r[LOWS[d][j]] = r[LOWS[d][j]] + behind(value, d)


def mid_step(step, u, r, sol, inv):
    keep, gain = STEPS[step]
    for i in range(8):
        new = keep * u[i] + gain * (inv[i] * r[i])
        u[i] = new
        sol[i] = sol[i] + new


def mid_pre_body(
    pos, scal, slab, got_first, got_second, cfm, level, coarse, send_up, send_down,
    sel, faces, inv, diag, u, sol, r, jump, flux,
):
    for i in range(8):
        rows = slice(16 * i, 16 * i + 16)
        for m in range(3):
            at = slice(128 * m + 16 * i, 128 * m + 16 * i + 16)
            u[i, :, 128 * m : 128 * m + 128] = from_below(pos, got_first, got_second, at)
            u[i, :, 128 * (m + 5) : 128 * (m + 6)] = from_above(pos, got_first, got_second, at)
        u[i, :, 384:640] = slab[rows, :]
    mid_setup(pos, scal, cfm, sel, faces, inv, diag)
    for i in range(8):
        r[i] = (MIDDLE * diag[i]) * u[i]
        sol[i] = u[i]
    mid_apply(u, r, scal, cfm, faces, jump, flux)
    mid_step(0, u, r, sol, inv)
    mid_apply(u, r, scal, cfm, faces, jump, flux)
    mid_step(1, u, r, sol, inv)
    mid_apply(u, r, scal, cfm, faces, jump, flux)
    level[0] = sol[:, :, 128:896]
    level[1] = r[:, :, 128:896]
    total = r[0]
    for i in range(1, 8):
        total = total + r[i]
    coarse[0] = total
    center = cfm[0:16, :] * scal[128]
    for d in range(3):
        kind = sel[d]
        value = jnp.zeros((16, 1024), F32)
        for k in range(KINDS):
            value = jnp.where(kind == float(k), scal[129 + k], value)
        coarse[2 + d] = value
        center = center + value + behind(value, d)
    coarse[1] = center
    l32 = lanes((16, 768)) % 32
    for out, first in ((send_up, 6), (send_down, 18)):
        acc = jnp.zeros((16, 768), F32)
        for f in range(4):
            acc = jnp.where(l32 // 8 == f, roll(coarse[f, :, 128:896], 8 * f - first), acc)
        out[0] = acc
        out[1] = roll(coarse[4, :, 128:896], -first)


def coarse_z_body(parity, own, dn, up, slab, first, second):
    lane = lanes((16, 128))
    for f in range(5):
        part = 0 if f < 4 else 1
        shift = 8 * f if f < 4 else 0
        for m in range(10):
            acc = jnp.zeros((16, 128), F32)
            for n in range(2):
                y = 2 * m + n - 6
                tile, at = (y + 12) // 4, 32 * ((y + 12) % 4)
                to = 64 * n
                mine = own[f, :, 128 * tile : 128 * tile + 128]
                left = dn[part, :, 128 * (tile - 1) : 128 * tile]
                right = up[part, :, 128 * (tile - 1) : 128 * tile]
                acc = jnp.where(
                    (lane >= to + 22) & (lane < to + 42), roll(mine, to + 22 - (at + 6)), acc
                )
                acc = jnp.where(
                    (lane >= to + 14) & (lane < to + 22), roll(left, to + 14 - (at + shift)), acc
                )
                acc = jnp.where(
                    (lane >= to + 42) & (lane < to + 50), roll(right, to + 42 - (at + shift)), acc
                )
            slab[f, :, 128 * m : 128 * m + 128] = acc
        for m in range(4):
            at = (f, slice(None), slice(128 * m, 128 * m + 128))
            after = (f, slice(None), slice(128 * (m + 6), 128 * (m + 7)))
            put(parity, first, second, at, slab[at], slab[after])


def settle(v, basis, j):
    lane = lanes((16, 128))
    for m in range(6):
        acc = jnp.zeros((16, 128), F32)
        for n in range(4):
            y = 4 * m + n - 8
            tile, at = (y + 14) // 2, 64 * ((y + 14) % 2)
            to = 32 * n
            piece = roll(v[:, 128 * tile : 128 * tile + 128], to + 5 - (at + 21))
            acc = jnp.where((lane >= to + 5) & (lane < to + 27), piece, acc)
        basis[j, :, 128 * m : 128 * m + 128] = acc


def two_sum(a, b):
    s = a + b
    t = s - a
    return s, (a - (s - t)) + (b - t)


def halves(a):
    t = a * 4097.0
    high = t - (t - a)
    return high, a - high


def two_prod(a, b):
    ah, al = halves(a)
    bh, bl = halves(b)
    p = a * b
    return p, ((ah * bh - p) + ah * bl + al * bh) + al * bl


def pair_mul(a, b):
    p, e = two_prod(a[0], b[0])
    return two_sum(p, e + (a[0] * b[1] + a[1] * b[0]))


def pair_sub(a, b):
    s, e = two_sum(a[0], -b[0])
    return two_sum(s, e + (a[1] - b[1]))


def pair_div(a, b):
    first = a[0] / b[0]
    rest = pair_sub(a, pair_mul((first, jnp.zeros_like(first)), b))
    return two_sum(first, rest[0] / b[0])


START = (0, 9, 17, 24, 30, 35, 39, 42)
PAIRS = sum(9 - i for i in range(BASIS))


def krylov_body(pos, scal, own, got_first, got_second, basis, gram, field, hold):
    for f in range(5):
        field[f, :, 0:512] = from_below(pos, got_first, got_second, f)
        field[f, :, 512:1792] = own[f]
        field[f, :, 1792:2304] = from_above(pos, got_first, got_second, f)
    center, half = scal[133], scal[134]
    lane8 = lanes((8, 128))

    def apply(v):
        total = field[1] * v
        for d in range(3):
            cond = field[2 + d]
            axis, step = ((0, 1), (1, 64), (1, 1))[d]
            total = total - cond * roll(v, -step, axis) - roll(cond * v, step, axis)
        return total

    def compact(v):
        acc = jnp.zeros((8, 128), F32)
        for t in range(2):
            for y in range(8):
                tile, at = (y + 14) // 2, 64 * ((y + 14) % 2) + 28
                to = 64 * t + 8 * y
                piece = v[8 * t : 8 * t + 8, 128 * tile : 128 * tile + 128]
                acc = jnp.where((lane8 >= to) & (lane8 < to + 8), roll(piece, to - at), acc)
        return acc

    before = None
    now = field[0]
    for j in range(BASIS):
        settle(now, basis, j)
        hold[j] = compact(now)
        image = apply(now)
        hold[BASIS + j] = compact(image)
        if j + 1 < BASIS:
            nxt = (image - center * now) * half
            if j > 0:
                nxt = 2.0 * nxt - before
            before, now = now, nxt
    high_rows, low_rows = [], []
    for i in range(BASIS):
        for j in range(i, BASIS + 1):
            other = hold[BASIS + j] if j < BASIS else hold[0]
            p, e = two_prod(hold[i], other)
            high_rows.append(p)
            low_rows.append(e)
    high = jnp.stack(high_rows)
    low = jnp.stack(low_rows)
    for axis, shifts in ((1, (4, 2, 1)), (2, (64, 32, 16, 8, 4, 2, 1))):
        for s in shifts:
            high, e = two_sum(high, roll(high, s, axis))
            low = low + roll(low, s, axis) + e
    row = jnp.zeros((8, 128), F32)
    for n in range(PAIRS):
        row = jnp.where(lane8 == n, high[n], row)
        row = jnp.where(lane8 == 64 + n, low[n], row)
    for m in range(2):
        gram[8 * m : 8 * m + 8, :] = row


def summed(gram):
    count = gram.shape[0] // 8
    high = gram[...].reshape(count, 8, 128)
    low = jnp.zeros((count, 8, 128), F32)
    while count > 1:
        count //= 2
        high, e = two_sum(high[:count], high[count : 2 * count])
        low = low[:count] + low[count : 2 * count] + e
    high, low = high[0], low[0]
    for s in (4, 2, 1):
        high, e = two_sum(high, roll(high, s, 0))
        low = low + roll(low, s, 0) + e
    return two_sum(high, low + roll(high, 64))


def gram_body(gram, out):
    high, low = summed(gram)
    row = jnp.where(lanes((8, 128)) < 64, high, roll(low, 64))
    for m in range(4):
        out[8 * m : 8 * m + 8, :] = row


def mid_post(pos, scal, gram, basis, cfm, level, out, sel, faces, inv, u, r, sol, jump, flux):
    high, low = summed(gram)
    lane = lanes((8, 128))
    sub = lax.broadcasted_iota(jnp.int32, (8, 128), 0)
    mat_h = jnp.zeros((8, 128), F32)
    mat_l = jnp.zeros((8, 128), F32)
    for i in range(BASIS):
        here = (sub == i) & (lane >= i) & (lane <= BASIS)
        mat_h = jnp.where(here, roll(high, i - START[i]), mat_h)
        mat_l = jnp.where(here, roll(low, i - START[i]), mat_l)
        for j in range(i + 1, BASIS):
            here = (sub == j) & (lane == i)
            shift = i - (START[i] + j - i)
            mat_h = jnp.where(here, roll(high, shift), mat_h)
            mat_l = jnp.where(here, roll(low, shift), mat_l)

    def spread_at(v, row, col):
        return jnp.broadcast_to(v[row : row + 1, col : col + 1], (8, 128))

    answers = []
    pivots = []
    for k in range(BASIS):
        start = spread_at(high, 0, START[k])
        piv = (spread_at(mat_h, k, k), spread_at(mat_l, k, k))
        good = jnp.abs(piv[0]) > 1e-12 * jnp.abs(start)
        safe = (jnp.where(good, piv[0], 1.0), jnp.where(good, piv[1], 0.0))
        pivots.append((safe, good))
        row = (
            jnp.broadcast_to(mat_h[k : k + 1, :], (8, 128)),
            jnp.broadcast_to(mat_l[k : k + 1, :], (8, 128)),
        )
        col = (
            jnp.broadcast_to(mat_h[:, k : k + 1], (8, 128)),
            jnp.broadcast_to(mat_l[:, k : k + 1], (8, 128)),
        )
        factor = pair_div(col, safe)
        use = good & (sub != k)
        factor = (jnp.where(use, factor[0], 0.0), jnp.where(use, factor[1], 0.0))
        mat_h, mat_l = pair_sub((mat_h, mat_l), pair_mul(factor, row))
    for k in range(BASIS):
        safe, good = pivots[k]
        value = pair_div((spread_at(mat_h, k, BASIS), spread_at(mat_l, k, BASIS)), safe)[0]
        answers.append(jnp.where(good, value, 0.0))
    weights = [jnp.concatenate([a, a], axis=0) for a in answers]
    lane16 = lanes((16, 128))
    for m in range(8):
        total = jnp.zeros((16, 128), F32)
        if 1 <= m <= 6:
            at = slice(128 * (m - 1), 128 * m)
            for j in range(BASIS):
                total = total + weights[j] * basis[j, :, at]
        for i in range(8):
            u[i, :, 128 * m : 128 * m + 128] = total
    mid_setup(pos, scal, cfm, sel, faces, inv, None)
    ends = jnp.zeros((16, 128), F32)
    for i in range(8):
        for ref in (r, sol):
            ref[i, :, 0:128] = ends
            ref[i, :, 896:1024] = ends
        r[i, :, 128:896] = level[1, i]
        sol[i, :, 128:896] = level[0, i] + u[i, :, 128:896]
    mid_apply(u, r, scal, cfm, faces, jump, flux)
    for i in range(8):
        new = inv[i] * r[i] / MIDDLE
        u[i] = new
        sol[i] = sol[i] + new
    mid_apply(u, r, scal, cfm, faces, jump, flux)
    mid_step(0, u, r, sol, inv)
    mid_apply(u, r, scal, cfm, faces, jump, flux)
    mid_step(1, u, r, sol, inv)
    for i in range(8):
        for half in range(2):
            acc = jnp.zeros((16, 128), F32)
            for n in range(8):
                y = 8 * half + n - 4
                tile, at = (y + 12) // 4, 32 * ((y + 12) % 4) + 8
                acc = jnp.where(
                    lane16 // 16 == n,
                    roll(sol[i, :, 128 * tile : 128 * tile + 128], 16 * n - at),
                    acc,
                )
            out[128 * half + 16 * i : 128 * half + 16 * i + 16, :] = acc


def post_body(
    pos, scal, gram, basis, cfm, level, keep, frz, got_first, got_second, coef, wide, spread,
    lift, diag_w, diag_e, out,
    sel, faces, mid_inv, mid_u, mid_r, mid_sol, jump, flux, mid, w, inv, u, r, sol, px, qx,
):
    fine_weights(pos, coef, w)
    wide_inside = jnp.concatenate([fine_places(pos)[0]] * (CHUNK // 256), axis=1)
    for c in range(CHUNKS):
        at = slice(CHUNK * c, CHUNK * (c + 1))
        inv[:, at] = fine_inverse(coef, w, diag_w, diag_e, wide_inside, at)
    mid_post(
        pos, scal, gram, basis, cfm, level, mid, sel, faces, mid_inv, mid_u, mid_r,
        mid_sol, jump, flux,
    )
    low = lanes((64, 128)) < 64
    px[:, 0:256] = jnp.zeros((16, 256), F32)
    qx[:, NX * 256 :] = jnp.zeros((16, 256), F32)
    for x in range(NX):
        first, second = slice(256 * x, 256 * x + 128), slice(256 * x + 128, 256 * x + 256)
        turned = roll(frz[x], 64)
        at = 384 + 64 * (x % 8)
        down = from_below(pos, got_first, got_second, slice(at, at + 64))
        over = from_above(pos, got_first, got_second, slice(at, at + 64))
        if x >= 8:
            down = roll(down, 64)
        else:
            over = roll(over, 64)
        r[:, first] = jnp.where(low, down, turned)
        r[:, second] = jnp.where(low, turned, over)
    planes = CHUNK // 256
    for c in range(CHUNKS):
        at = slice(CHUNK * c, CHUNK * (c + 1))
        pieces = [
            mid[pl.ds(128 * half + planes * c + n, 8, stride=16), :]
            for n in range(planes)
            for half in range(2)
        ]
        high, rest = split3(jnp.concatenate(pieces, axis=1))
        stacked = jnp.concatenate([high, rest, high, jnp.zeros((8, CHUNK), F32)], axis=0)
        lifted = mm(lift[...], stacked.astype(BF16))
        u[:, at] = lifted
        sol[:, at] = lifted
    fine_apply(u, r, w, coef, wide, spread, px, qx, None, sol, inv)
    for c in range(CHUNKS):
        at = slice(CHUNK * c, CHUNK * (c + 1))
        new = inv[:, at] * r[:, at] / MIDDLE
        u[:, at] = new
        sol[:, at] = sol[:, at] + new
    fine_apply(u, r, w, coef, wide, spread, px, qx, 0, sol, inv)
    fine_apply(u, r, w, coef, wide, spread, px, qx, 1, sol, inv)
    fine_apply(u, r, w, coef, wide, spread, px, qx, None, sol, inv)
    lane = lanes((64, 128))
    for x in range(NX):
        acc = jnp.zeros((64, 128), F32)
        for part, ref in enumerate((sol, r)):
            for y in range(8):
                half, at = (y + 4) // 8, 16 * ((y + 4) % 8) + 4
                start = 256 * x + 128 * half
                acc = jnp.where(
                    lane // 8 == 8 * part + y,
                    roll(ref[:, start : start + 128], 64 * part + 8 * y - at),
                    acc,
                )
        kept = keep[x % 8] if x < 8 else roll(keep[x % 8], 64)
        out[x] = acc + jnp.where(low, kept, 0.0)


def unpack_body(got, first, second):
    low = lanes((64, 128)) < 64
    for part, out in enumerate((first, second)):
        held = []
        for g in range(8):
            a, b = got[ORDER[g]], got[ORDER[g + 8]]
            if part == 0:
                held.append(jnp.where(low, a, roll(b, 64)))
            else:
                held.append(jnp.where(low, roll(a, 64), b))
        for y, rows in enumerate(exchange(held, 8)):
            out[pl.ds(y, 64, stride=8), :] = rows


def trace_tables():
    high = np.zeros((3, 16, 64), np.float32)
    low = np.zeros((3, 16, 64), np.float32)
    for p in range(4):
        for q in range(4):
            for d in range(3):
                for table, at in ((high, 3), (low, 0)):
                    index = [p, q]
                    index.insert(d, at)
                    table[d, 4 * p + q, 16 * index[0] + 4 * index[1] + index[2]] = 1.0
    return high, low


def mid_traces():
    high = np.zeros((3, 4, 8), np.float32)
    low = np.zeros((3, 4, 8), np.float32)
    for d in range(3):
        for n in range(4):
            high[d, n, HIGHS[d][n]] = 1.0
            low[d, n, LOWS[d][n]] = 1.0
    return high, low


def prolong_tables():
    half = np.float32(0.5)
    one = np.float32(1.0)
    node = np.array([-1.0, -1.0 / math.sqrt(5.0), 1.0 / math.sqrt(5.0), 1.0], np.float32)
    table = np.stack([(one - node) * half, (one + node) * half], axis=1)
    volume = (
        table[:, None, None, :, None, None]
        * table[None, :, None, None, :, None]
        * table[None, None, :, None, None, :]
    ).reshape(64, 8)
    surface = (table[:, None, :, None] * table[None, :, None, :]).reshape(16, 4)
    return volume, surface


def cut(x):
    return lax.reduce_precision(x, 8, 7)


def two_parts(x):
    high = cut(x)
    return high, cut(x - high)


def three_parts(x):
    high = cut(x)
    rest = x - high
    mid = cut(rest)
    return high, mid, cut(rest - mid)


def tables(element, faces):
    volume, surface = prolong_tables()
    elem_mid = jnp.dot(volume.T, jnp.dot(element, volume, precision=HIGHEST), precision=HIGHEST)
    eye = np.eye(16, dtype=np.float32)
    face_mid = jnp.einsum("kij,jb->kib", faces, surface, precision=HIGHEST)
    face_mid = jnp.einsum("ia,kib->kab", surface, face_mid, precision=HIGHEST)
    elem_coarse = jnp.sum(elem_mid)
    face_coarse = jnp.sum(face_mid, axis=(1, 2))
    high, low = trace_tables()
    both = np.concatenate([high, low], axis=0)
    rows = jnp.einsum("kij,djm->dkim", faces, both, precision=HIGHEST).reshape(384, 64)
    wide = jnp.concatenate([element, rows], axis=0)
    wh, wl = two_parts(wide)
    wide = jnp.concatenate([wh, wh, wl], axis=1).astype(BF16)
    spread = np.concatenate([high[1], -low[1], high[2], -low[2]], axis=0).T
    spread = np.concatenate([spread, spread], axis=1)
    face_diag = jnp.sum(faces * eye, axis=2)
    diag = jnp.einsum("dim,ki->mdk", both, face_diag, precision=HIGHEST).reshape(64, 24)
    diag_w = jnp.concatenate(three_parts(diag) + (jnp.zeros((64, 8), F32),), axis=1).astype(BF16)
    diag_e = jnp.sum(element * np.eye(64, dtype=np.float32), axis=1, keepdims=True)
    mh, ml = mid_traces()
    both = np.concatenate([mh, ml], axis=0)
    face_diag = jnp.sum(face_mid * eye[:4, :4], axis=2)
    diag = jnp.einsum("dim,ki->mdk", both, face_diag, precision=HIGHEST).reshape(8, 24)
    mid_diag_w = jnp.concatenate(three_parts(diag) + (jnp.zeros((8, 8), F32),), axis=1).astype(BF16)
    mid_diag_e = jnp.sum(elem_mid * eye[:8, :8], axis=1, keepdims=True)
    vh = volume.astype(BF16).astype(np.float32)
    vl = (volume - vh).astype(BF16).astype(np.float32)
    down = jnp.asarray(np.concatenate([vh.T, vh.T, vl.T], axis=1), BF16)
    lift = jnp.asarray(np.concatenate([vh, vh, vl, np.zeros((64, 8), np.float32)], axis=1), BF16)
    least = 0.1 * elem_coarse
    most = 1.35 * elem_coarse + 9.0 * jnp.max(jnp.abs(face_coarse))
    half = 0.5 * (most - least)
    half = jnp.where(jnp.abs(half) > 0.0, half, 1.0)
    scal = jnp.concatenate(
        [
            elem_mid.reshape(-1),
            face_mid.reshape(-1),
            elem_coarse[None],
            face_coarse,
            (0.5 * (most + least))[None],
            (1.0 / half)[None],
            jnp.zeros((9,), F32),
        ]
    )
    return (
        wide,
        jnp.asarray(spread, BF16),
        diag_w,
        diag_e,
        down,
        mid_diag_w,
        mid_diag_e,
        lift,
        scal,
    )


def local(residual, coefficient, element, faces, kind, flag):
    y_first = [(i, i ^ 1) for i in range(16)]
    y_second = [p for i in range(1, 15, 2) for p in ((i, i + 1), (i + 1, i))]

    def z_index(zb):
        return ORDER[zb % 16] * 2 + zb // 16

    z_up = [(z_index(i), z_index(i + 1)) for i in range(31)]
    z_dn = [(z_index(i + 1), z_index(i)) for i in range(31)]
    z_axes = ("gx", "lvl")
    side = lax.axis_index("lvl")
    chip = lax.axis_index("gx")
    pos = jnp.stack(
        [
            lax.axis_index("yz"),
            side * 16 + jnp.where(chip % 2 == 0, chip // 2, 15 - chip // 2),
        ]
    ).astype(jnp.int32)
    res = residual.reshape(512, 128)
    slots = call(
        slots_body,
        "slots",
        [f32s(16, 40, 128)],
        (0,) * 4,
        [pltpu.VMEM((128, 128), F32)],
        limit=LARGE_LIMIT,
    )(res, coefficient.reshape(8, 128), kind.reshape(48, 128), flag.reshape(48, 128))[0]
    element, faces, slots = lax.optimization_barrier((element, faces, slots))
    wide, spread, diag_w, diag_e, down, mid_diag_w, mid_diag_e, lift, scal = tables(element, faces)
    parity = jnp.broadcast_to((lax.axis_index("yz") % 2).astype(F32), (8, 128))
    own = lax.all_to_all(slots, "gx", 0, 0, tiled=True)
    own, wide, diag_w, diag_e, mid_diag_w, mid_diag_e, scal, parity, pos = lax.optimization_barrier(
        (own, wide, diag_w, diag_e, mid_diag_w, mid_diag_e, scal, parity, pos)
    )
    dn = lax.ppermute(own[:, 16:40], z_axes, z_up)
    up = lax.ppermute(own[:, 0:24], z_axes, z_dn)
    place_values, place_kinds, pack = place_tables()
    rows, own, other = call(
        join_body,
        "join",
        [f32s(NX, 64, 128), f32s(768, 128), f32s(768, 128)],
        (0,) * 6,
    )(parity, own, dn, up, place_values, place_kinds)
    got_first = lax.ppermute(own, "yz", y_first)
    got_second = lax.ppermute(other, "yz", y_second)
    plane = (64, NX * 256)
    strip = (16, NX * 256 + 256)
    keep, r, coef, cfm, send_up, send_down = call(
        fine_pre_body,
        "fine_pre",
        [
            f32s(8, 64, 128),
            f32s(*plane),
            f32s(8, NX * 256),
            f32s(128, 1024),
            f32s(384, 128),
            f32s(384, 128),
        ],
        (1,) + (0,) * 12,
        [
            pltpu.VMEM(plane, F32),
            pltpu.VMEM((24, NX * 256), F32),
            pltpu.VMEM(plane, F32),
            pltpu.VMEM(plane, F32),
            pltpu.VMEM(strip, F32),
            pltpu.VMEM(strip, F32),
            pltpu.VMEM((896, 128), F32),
            pltpu.VMEM((256, 128), F32),
        ],
    )(
        pos, rows, own, got_first, got_second, wide, spread, diag_w, diag_e, down, mid_diag_w, mid_diag_e, pack
    )
    dn = lax.ppermute(send_up, z_axes, z_up)
    up = lax.ppermute(send_down, z_axes, z_dn)
    slab, first, second, frz = call(
        mid_z_body,
        "mid_z",
        [f32s(128, 256), f32s(896, 128), f32s(896, 128), f32s(NX, 64, 128)],
        (0,) * 5,
    )(parity, send_up, dn, up, r)
    got_first = lax.ppermute(first, "yz", y_first)
    got_second = lax.ppermute(second, "yz", y_second)
    mid = (8, 16, 1024)
    mid_scratch = [
        pltpu.VMEM((3, 16, 1024), F32),
        pltpu.VMEM((3, 16, 16, 1024), F32),
        pltpu.VMEM(mid, F32),
    ]
    tail_scratch = [pltpu.VMEM((4, 16, 1024), F32), pltpu.VMEM((12, 16, 1024), F32)]
    level, coarse, send_up, send_down = call(
        mid_pre_body,
        "mid_pre",
        [f32s(2, 8, 16, 768), f32s(5, 16, 1024), f32s(2, 16, 768), f32s(2, 16, 768)],
        (1, 1, 0, 0, 0, 0),
        mid_scratch
        + [pltpu.VMEM(mid, F32)] * 4
        + tail_scratch,
    )(pos, scal, slab, got_first, got_second, cfm)
    dn = lax.ppermute(send_up, z_axes, z_up)
    up = lax.ppermute(send_down, z_axes, z_dn)
    coarse_slab, first, second = call(
        coarse_z_body,
        "coarse_z",
        [f32s(5, 16, 1280), f32s(5, 16, 512), f32s(5, 16, 512)],
        (0,) * 4,
    )(parity, coarse, dn, up)
    coarse_first = lax.ppermute(first, "yz", y_first)
    coarse_second = lax.ppermute(second, "yz", y_second)
    basis, gram = call(
        krylov_body,
        "krylov",
        [f32s(BASIS, 16, 768), f32s(16, 128)],
        (1, 1, 0, 0, 0),
        [
            pltpu.VMEM((5, 16, 2304), F32),
            pltpu.VMEM((2 * BASIS, 8, 128), F32),
        ],
    )(pos, scal, coarse_slab, coarse_first, coarse_second)
    gram = lax.all_to_all(gram, "yz", 0, 0, tiled=True)
    gram = call(gram_body, "gram", [f32s(32, 128)], (0,))(gram)[0]
    gram = lax.all_to_all(gram, z_axes, 0, 0, tiled=True)
    packed = call(
        post_body,
        "post",
        [f32s(16, 64, 128)],
        (1, 1) + (0,) * 14,
        mid_scratch
        + [pltpu.VMEM(mid, F32)] * 3
        + tail_scratch
        + [
            pltpu.VMEM((256, 128), F32),
            pltpu.VMEM((24, NX * 256), F32),
            pltpu.VMEM(plane, F32),
            pltpu.VMEM(plane, F32),
            pltpu.VMEM(plane, F32),
            pltpu.VMEM(plane, F32),
            pltpu.VMEM(strip, F32),
            pltpu.VMEM(strip, F32),
        ],
        limit=LARGE_LIMIT,
    )(
        pos, scal, gram, basis, cfm, level, keep, frz, got_first, got_second, coef, wide, spread,
        lift, diag_w, diag_e,
    )[0]
    got = lax.all_to_all(packed, "gx", 0, 0, tiled=True)
    correction, rest = call(unpack_body, "unpack", [f32s(512, 128), f32s(512, 128)], (0,))(got)
    return (correction.reshape(64, 1, 8, 128), rest.reshape(64, 1, 8, 128))


def solution(mesh):
    in_specs = (
        P(None, "gx", "yz", "lvl"),
        P("gx", "yz", "lvl"),
        P(),
        P(),
        P(None, "gx", "yz", "lvl"),
        P(None, "gx", "yz", "lvl"),
    )
    out_specs = (P(None, "gx", "yz", "lvl"), P(None, "gx", "yz", "lvl"))
    return jax.shard_map(local, mesh=mesh, in_specs=in_specs, out_specs=out_specs, check_vma=False)
```

```python
import functools
import math

import jax
import jax.numpy as jnp
import numpy as np
from jax import lax
from jax.experimental import pallas as pl
from jax.experimental.pallas import tpu as pltpu
from jax.sharding import PartitionSpec as P

NX = 16
NY = 128
NZ = 256
KINDS = 4
F32 = jnp.float32
BF16 = jnp.bfloat16
HIGHEST = lax.Precision.HIGHEST
LOW_EIG = 0.3
HIGH_EIG = 3.0
MIDDLE = 0.5 * (HIGH_EIG + LOW_EIG)
SPREAD = 0.5 * (HIGH_EIG - LOW_EIG)
SCALED = MIDDLE / SPREAD
RHO0 = 1.0 / SCALED
RHO1 = 1.0 / (2.0 * SCALED - RHO0)
RHO2 = 1.0 / (2.0 * SCALED - RHO1)
STEPS = ((RHO1 * RHO0, 2.0 * RHO1 / SPREAD), (RHO2 * RHO1, 2.0 * RHO2 / SPREAD))
BASIS = 8
ORDER = tuple(2 * n if n < 8 else 2 * (15 - n) + 1 for n in range(16))
VMEM_LIMIT = 24 * 2**20
LARGE_LIMIT = 60 * 2**20


def lanes(shape):
    return lax.broadcasted_iota(jnp.int32, shape, len(shape) - 1)


def roll(x, shift, axis=None):
    axis = x.ndim - 1 if axis is None else axis
    shift = shift % x.shape[axis]
    return x if shift == 0 else pltpu.roll(x, shift, axis)


SPACES = {
    0: pl.BlockSpec(memory_space=pltpu.VMEM),
    1: pl.BlockSpec(memory_space=pltpu.SMEM),
}


def call(body, name, out_shape, in_specs, scratch=(), out_specs=None, limit=VMEM_LIMIT):
    out_specs = out_specs or (0,) * len(out_shape)
    return pl.pallas_call(
        body,
        out_shape=list(out_shape),
        in_specs=[SPACES[i] for i in in_specs],
        out_specs=[SPACES[i] for i in out_specs],
        scratch_shapes=list(scratch),
        compiler_params=pltpu.CompilerParams(vmem_limit_bytes=limit),
        cost_estimate=pl.CostEstimate(flops=1000000, bytes_accessed=1000000, transcendentals=0),
        name=name,
    )


def position():
    chip = lax.axis_index("gx")
    up = lax.rem(chip, 2) == 0
    block = jnp.where(up, lax.div(chip, 2), 15 - lax.div(chip, 2))
    return lax.axis_index("yz"), lax.axis_index("lvl") * 16 + block


def even(pos):
    return lax.rem(pos[0], 2) == 0


def put(parity, first, second, at, fwd, bwd):
    is_even = jnp.broadcast_to(parity[0:1, :], fwd.shape) == 0.0
    first[at] = jnp.where(is_even, fwd, bwd)
    second[at] = jnp.where(is_even, bwd, fwd)


def from_below(pos, first, second, at):
    return jnp.where(even(pos), second[at], first[at])


def from_above(pos, first, second, at):
    return jnp.where(even(pos), first[at], second[at])


def f32s(*shape):
    return jax.ShapeDtypeStruct(shape, F32)


def split3(x):
    high = x.astype(BF16).astype(F32)
    low = x - high
    return high, low


def stack_hlh(x):
    high, low = split3(x)
    return jnp.concatenate([high, low, high], axis=0).astype(BF16)


def mm(a, b):
    return jnp.dot(a, b, preferred_element_type=F32)


def exchange(arrays, lane_block):
    arrays = list(arrays)
    group = lanes(arrays[0].shape) // lane_block
    for bit in (1, 2, 4):
        upper = (group // bit) % 2 == 1
        for n in range(8):
            if n & bit:
                continue
            a, b = arrays[n], arrays[n | bit]
            arrays[n] = jnp.where(upper, roll(b, lane_block * bit), a)
            arrays[n | bit] = jnp.where(upper, b, roll(a, -lane_block * bit))
    return arrays


def slots_body(res, coef, kind, flag, out, cf):
    for n in range(16):
        cf[8 * n : 8 * n + 8, :] = jnp.zeros((8, 128), F32)
    cf[0:8, :] = coef[...]
    for first, ref in ((8, kind), (32, flag)):
        for n in range(3):
            at = 8 * (2 * n + 1)
            cf[first + 8 * n : first + 8 * n + 8, :] = ref[at : at + 8, :].astype(F32)
    for first, ref in ((80, kind), (104, flag)):
        for n in range(2):
            at = 8 * (2 * n + 2)
            cf[first + 8 * n : first + 8 * n + 8, :] = ref[at : at + 8, :].astype(F32)
    low = lanes((16, 128)) < 64
    low8 = lanes((8, 128)) < 64
    near = lanes((32, 128)) % 8 < 4
    values = exchange([res[pl.ds(y, 64, stride=8), :] for y in range(8)], 8)
    kinds = exchange([cf[pl.ds(y, 16, stride=8), :] for y in range(8)], 8)
    for j in range(8):
        first, second = ORDER[j], ORDER[j + 8]
        a, b = values[j][0:32], values[j][32:64]
        for at, v in (
            (0, jnp.where(near, a, roll(b, 4))),
            (24, jnp.where(near, roll(a, -4), b)),
        ):
            out[first, at : at + 16, :] = jnp.where(low, v[0:16], roll(v[16:32], 64))
            out[second, at : at + 16, :] = jnp.where(low, roll(v[0:16], 64), v[16:32])
        a, b = kinds[j][0:8], kinds[j][8:16]
        out[first, 16:24, :] = jnp.where(low8, a, roll(b, 64))
        out[second, 16:24, :] = jnp.where(low8, roll(a, 64), b)


def place_tables():
    values = np.zeros((512, 512), np.float32)
    kinds = np.zeros((384, 512), np.float32)
    pack = np.zeros((256, 128), np.float32)
    for half in range(2):
        for y in range(8):
            for z in range(8):
                lane = 64 * half + 8 * y + z
                to = 128 * (2 * (z // 4) + half) + 16 * y + z % 4
                for n, first in enumerate((4, 8, 12, 0)):
                    values[128 * n + lane, to + first] = 1.0
                for n, first in enumerate((12, 4, 20)):
                    kinds[128 * n + lane, 256 * half + 32 * y + first + z] = 1.0
    for y in range(-1, 9):
        for z in range(-1, 9):
            pack[16 * (y + 4) + z + 4, 12 * (y + 1) + z + 1] = 1.0
    return [jnp.asarray(v, BF16) for v in (values, kinds, pack)]


def three_rows(x):
    high = x.astype(BF16).astype(F32)
    rest = x - high
    mid = rest.astype(BF16).astype(F32)
    return jnp.concatenate([high, mid, rest - mid], axis=0).astype(BF16)


def moved(x, table):
    count = x.shape[0]
    out = mm(three_rows(x), table)
    return out[0:count] + out[count : 2 * count] + out[2 * count :]


def join_body(parity, own, dn, up, place_values, place_kinds, rows, first, second):
    parts = (own[:, 0:16, :], own[:, 24:40, :], up[:, 0:16, :], dn[:, 8:24, :])
    values = jnp.concatenate([v.reshape(256, 128) for v in parts], axis=1)
    out = moved(values, place_values[...])
    for x in range(NX):
        for n in range(4):
            rows[x, 16 * n : 16 * n + 16, :] = out[16 * x : 16 * x + 16, 128 * n : 128 * n + 128]
    low = lanes((64, 128)) < 64
    for x in range(8):
        fwd = jnp.where(low, roll(rows[x], 64), rows[x + 8])
        bwd = jnp.where(low, rows[x], roll(rows[x + 8], 64))
        put(parity, first, second, slice(64 * x, 64 * x + 64), fwd, bwd)
    parts = (own[:, 16:24, :], dn[:, 0:8, :], up[:, 16:24, :])
    kinds = jnp.concatenate([v.reshape(128, 128) for v in parts], axis=1)
    out = moved(kinds, place_kinds[...])
    array = lax.broadcasted_iota(jnp.int32, (128, 128), 0) % 8
    edge = (lanes((128, 128)) % 32 == 3) & ((array == 3) | (array == 6))
    lane = lanes((128, 128))
    for h in range(2):
        minus = out[:, 256 + 128 * h : 384 + 128 * h]
        plus = jnp.where(edge, roll(minus, -1), out[:, 128 * h : 128 * h + 128])
        if h == 0:
            plus = jnp.where((array == 7) & (lane < 32), roll(minus, 5, 0), plus)
            plus = jnp.where(
                (array == 7) & (lane >= 32) & (lane < 64), roll(roll(minus, 2, 0), 32), plus
            )
        first[512 + 128 * h : 640 + 128 * h, :] = plus
        second[512 + 128 * h : 640 + 128 * h, :] = plus


CHUNK = 4096
CHUNKS = NX * 256 // CHUNK


def fine_apply(u, r, w, coef, wide, spread, px, qx, step, sol, inv):
    for c in range(CHUNKS):
        at = slice(CHUNK * c, CHUNK * (c + 1))
        after = slice(CHUNK * c + 256, CHUNK * (c + 1) + 256)
        prod = mm(wide[...], stack_hlh(u[:, at]))

        def pick(base, row):
            total = w[row : row + 1, at] * prod[base : base + 16]
            for k in range(1, KINDS):
                total = total + w[row + k : row + k + 1, at] * prod[base + 16 * k : base + 16 * k + 16]
            return total

        px[:, after] = pick(64, 0)
        py = pick(128, 4)
        pz = pick(192, 8)
        qx[:, at] = pick(256, 12)
        qy = pick(320, 16)
        qz = pick(384, 20)
        flux = jnp.concatenate(
            [py - roll(qy, -16), roll(py, 16) - qy, pz - roll(qz, -1), roll(pz, 1) - qz], axis=0
        )
        high, low = split3(flux)
        faces = mm(spread[...], jnp.concatenate([high, low], axis=0).astype(BF16))
        r[:, at] = r[:, at] - (coef[0:1, at] * prod[0:64] + faces)

    for c in range(CHUNKS):
        at = slice(CHUNK * c, CHUNK * (c + 1))
        after = slice(CHUNK * c + 256, CHUNK * (c + 1) + 256)
        r[48:64, at] = r[48:64, at] - (px[:, after] - qx[:, after])
        r[0:16, at] = r[0:16, at] + (px[:, at] - qx[:, at])
        if step is not None:
            keep, gain = STEPS[step]
            new = keep * u[:, at] + gain * (inv[:, at] * r[:, at])
            u[:, at] = new
            sol[:, at] = sol[:, at] + new


def fine_places(pos):
    place = lanes((1, 256))
    y_at = pos[0] * 8 - 4 + place // 16
    z_at = pos[1] * 8 - 4 + place % 16
    inside = (y_at >= 0) & (y_at < NY) & (z_at >= 0) & (z_at < NZ)
    return inside, inside & (y_at < NY - 1), inside & (z_at < NZ - 1)


def fine_weights(pos, coef, w):
    inside, has_y, has_z = fine_places(pos)
    w[12:16, 0:256] = jnp.zeros((4, 256), F32)
    for x in range(NX):
        at = slice(256 * x, 256 * x + 256)
        rows = coef[:, at]
        opens = [
            inside & (rows[4:5] == 0.0) if x < NX - 1 else jnp.zeros((1, 256), jnp.bool_),
            has_y & (rows[5:6] == 0.0),
            has_z & (rows[6:7] == 0.0),
        ]
        plus = [
            [jnp.where(opens[d] & (rows[1 + d : 2 + d] == float(k)), 1.0, 0.0) for k in range(KINDS)]
            for d in range(3)
        ]
        plus_all = jnp.concatenate(plus[0] + plus[1] + plus[2], axis=0)
        w[0:12, at] = plus_all
        if x < NX - 1:
            w[12:16, 256 * x + 256 : 256 * x + 512] = plus_all[0:4]
        w[16:20, at] = roll(plus_all[4:8], 16)
        w[20:24, at] = roll(plus_all[8:12], 1)


def kinds_of(w, at):
    ws = w[:, at]
    return jnp.concatenate([ws, ws, ws, jnp.zeros((8, CHUNK), F32)], axis=0).astype(BF16)


def fine_inverse(coef, w, diag_w, diag_e, inside, at):
    diag = diag_e[...] * coef[0:1, at] + mm(diag_w[...], kinds_of(w, at))
    return jnp.where(inside, 1.0 / diag, 0.0)


def compacted(first, second, lane):
    v = roll(jnp.where(lane < 64, roll(first, 64), roll(second, 64)), -4)
    for size in (8, 16, 32):
        v = jnp.where(lane % (4 * size) < size, v, roll(v, -size))
    return v


def fine_pre_body(
    rows_in,
    own,
    got_first,
    got_second,
    wide,
    spread,
    diag_w,
    diag_e,
    down,
    mid_diag_w,
    mid_diag_e,
    pack,
    keep,
    r,
    coef,
    cfm,
    send_up,
    send_down,
    sol,
    w,
    inv,
    u,
    px,
    qx,
    gather,
    held,
):
    pos = position()
    low = lanes((64, 128)) < 64
    lane8 = lanes((8, 128))
    inside = fine_places(pos)[0]
    px[:, 0:256] = jnp.zeros((16, 256), F32)
    qx[:, NX * 256 :] = jnp.zeros((16, 256), F32)
    cfm[:, 896:1024] = jnp.zeros((128, 128), F32)
    array = lax.broadcasted_iota(jnp.int32, (8, 128), 0)
    edge = (lane8 >= 96) & ((array == 2) | (array == 5))
    for x in range(NX):
        first, second = slice(256 * x, 256 * x + 128), slice(256 * x + 128, 256 * x + 256)
        turned = roll(rows_in[x], 64)
        at = 64 * (x % 8)
        under = from_below(pos, got_first, got_second, slice(at, at + 64))
        over = from_above(pos, got_first, got_second, slice(at, at + 64))
        if x >= 8:
            under = roll(under, 64)
        else:
            over = roll(over, 64)
        r[:, first] = jnp.where(low, under, turned)
        r[:, second] = jnp.where(low, turned, over)
        places = [slice(512 + 128 * h + 8 * x, 520 + 128 * h + 8 * x) for h in range(2)]
        blocks = (
            [from_below(pos, got_first, got_second, p) for p in places]
            + [own[p] for p in places]
            + [from_above(pos, got_first, got_second, p) for p in places]
        )
        minus = jnp.where(array == 2, roll(roll(blocks[0], 3, 0), 96), roll(roll(blocks[0], 6, 0), 64))
        gather[pl.ds(x, 8, stride=16), :] = jnp.where(edge, minus, 0.0)
        for m in range(6):
            gather[pl.ds(128 * (m + 1) + x, 8, stride=16), :] = blocks[m]
        for half, at in enumerate((first, second)):
            acc = jnp.zeros((8, 128), F32)
            for row in range(8):
                n = 8 * half + row
                acc = jnp.where(
                    lane8 // 16 == row,
                    roll(blocks[1 + n // 4], 16 * row - (n % 4) * 32 - 8),
                    acc,
                )
            coef[:, at] = acc
    for m in range(7):
        cfm[:, 128 * m : 128 * m + 128] = gather[128 * m : 128 * m + 128, :]
    fine_weights(pos, coef, w)
    wide_inside = jnp.concatenate([inside] * (CHUNK // 256), axis=1)
    for c in range(CHUNKS):
        at = slice(CHUNK * c, CHUNK * (c + 1))
        inverse = fine_inverse(coef, w, diag_w, diag_e, wide_inside, at)
        inv[:, at] = inverse
        update = inverse * r[:, at] / MIDDLE
        u[:, at] = update
        sol[:, at] = update
    fine_apply(u, r, w, coef, wide, spread, px, qx, 0, sol, inv)
    fine_apply(u, r, w, coef, wide, spread, px, qx, 1, sol, inv)
    fine_apply(u, r, w, coef, wide, spread, px, qx, None, sol, inv)
    lane16 = lanes((16, 128)) % 16 // 4
    for c in range(CHUNKS):
        at = slice(CHUNK * c, CHUNK * (c + 1))
        rhs = mm(down[...], stack_hlh(r[:, at]))
        diag = mid_diag_e[...] * coef[0:1, at] + mm(mid_diag_w[...], kinds_of(w, at))
        update = jnp.where(wide_inside, 1.0 / diag, 0.0) * rhs / MIDDLE
        for n in range(CHUNK // 256):
            x = (CHUNK // 256) * c + n
            for half in range(2):
                piece = update[:, 256 * n + 128 * half : 256 * n + 128 * half + 128]
                held[pl.ds(128 * half + x, 8, stride=16), :] = piece
    packed = moved(jnp.concatenate([held[0:128, :], held[128:256, :]], axis=1), pack[...])
    send_up[0:128, :] = packed
    send_down[0:128, :] = packed
    for x in range(NX):
        first, second = slice(256 * x, 256 * x + 128), slice(256 * x + 128, 256 * x + 256)
        mine = jnp.where(low, roll(r[:, first], 64), roll(r[:, second], 64))
        up = jnp.zeros((16, 128), F32)
        dn = jnp.zeros((16, 128), F32)
        for j in range(4):
            part = mine[16 * j : 16 * j + 16]
            up = jnp.where(lane16 == j, roll(part, 4 * j - 8), up)
            dn = jnp.where(lane16 == j, roll(part, 4 * j - 4), dn)
        send_up[128 + 16 * x : 144 + 16 * x, :] = up
        send_down[128 + 16 * x : 144 + 16 * x, :] = dn
    lane = lanes((64, 128))
    for x in range(8):
        a, b = [
            compacted(sol[:, 256 * n : 256 * n + 128], sol[:, 256 * n + 128 : 256 * n + 256], lane)
            for n in (x, x + 8)
        ]
        keep[x] = jnp.where(low, a, roll(b, 64))


def mid_z_body(parity, own, dn, up, r, slab, first, second, frz):
    low = lanes((64, 128)) < 64
    l16 = lanes((16, 128)) % 16
    for x in range(NX):
        at = 256 * x
        mine = jnp.where(low, roll(r[:, at : at + 128], 64), roll(r[:, at + 128 : at + 256], 64))
        pack_dn = dn[128 + 16 * x : 144 + 16 * x, :]
        pack_up = up[128 + 16 * x : 144 + 16 * x, :]
        for j in range(4):
            rows = slice(16 * j, 16 * j + 16)
            part = jnp.where(l16 < 4, roll(pack_dn, -4 * j), mine[rows])
            part = jnp.where(l16 >= 12, roll(pack_up, 12 - 4 * j), part)
            frz[x, rows, :] = part
    for x in range(8):
        fwd = jnp.where(low, roll(frz[x], 64), frz[x + 8])
        bwd = jnp.where(low, frz[x], roll(frz[x + 8], 64))
        put(parity, first, second, slice(384 + 64 * x, 448 + 64 * x), fwd, bwd)
    lane = lanes((128, 128))
    tiles = []
    for m in range(4):
        acc = jnp.zeros((128, 128), F32)
        for n in range(4):
            y = 4 * (m - 1) + n
            if y < -1 or y > 8:
                continue
            to = 32 * n
            at = 12 * (y + 1)
            rows = slice(0, 128)
            acc = jnp.where((lane >= to + 12) & (lane < to + 20), roll(own[rows, :], to + 11 - at), acc)
            acc = jnp.where((lane >= to + 3) & (lane < to + 12), roll(dn[rows, :], to + 3 - at), acc)
            acc = jnp.where((lane >= to + 20) & (lane < to + 29), roll(up[rows, :], to + 19 - at), acc)
        if 1 <= m <= 2:
            slab[:, 128 * (m - 1) : 128 * m] = acc
        tiles.append(acc)
    for m in range(3):
        put(parity, first, second, slice(128 * m, 128 * m + 128), tiles[m], tiles[m + 1])


LOWS = ((0, 1, 2, 3), (0, 1, 4, 5), (0, 2, 4, 6))
HIGHS = ((4, 5, 6, 7), (2, 3, 6, 7), (1, 3, 5, 7))


def ahead(v, d):
    if d == 0:
        return roll(v, -1, 0)
    return roll(v, -32 if d == 1 else -1, 1)


def behind(v, d):
    if d == 0:
        return roll(v, 1, 0)
    return roll(v, 32 if d == 1 else 1, 1)


def mid_setup(pos, scal, cfm, sel, faces, inv, diag):
    place = lanes((16, 1024))
    x_at = lax.broadcasted_iota(jnp.int32, (16, 1024), 0)
    y_at = pos[0] * 8 - 12 + place // 32
    z_at = pos[1] * 8 - 12 + place % 32
    domain = (y_at >= 0) & (y_at < NY) & (z_at >= 0) & (z_at < NZ)
    known = domain & (place >= 128) & (place < 896) & (place % 32 >= 4) & (place % 32 < 28)
    lasts = (x_at < NX - 1, y_at < NY - 1, z_at < NZ - 1)
    for d in range(3):
        is_open = domain & lasts[d] & (cfm[64 + 16 * d : 80 + 16 * d, :] == 0.0)
        sel[d] = jnp.where(is_open, cfm[16 + 16 * d : 32 + 16 * d, :], 4.0)
    coef = cfm[0:16, :]

    for d in range(3):
        for c in range(8):
            at = slice(128 * c, 128 * c + 128)
            kind = sel[d, :, at]
            ones = [kind == float(k) for k in range(KINDS)]
            for i in range(4):
                for j in range(i, 4):
                    value = jnp.zeros((16, 128), F32)
                    for k in range(KINDS):
                        value = jnp.where(ones[k], scal[64 + 16 * k + 4 * i + j], value)
                    faces[d, 4 * i + j, :, at] = value
    if inv is None:
        return known
    for i in range(8):
        total = coef * scal[9 * i]
        for d in range(3):
            if i in HIGHS[d]:
                total = total + faces[d, 5 * HIGHS[d].index(i)]
            else:
                total = total + behind(faces[d, 5 * LOWS[d].index(i)], d)
        if diag is not None:
            diag[i] = total
        inv[i] = jnp.where(known, 1.0 / total, 0.0)
    return known


def mid_apply(v, r, scal, cfm, faces, jump, flux):
    for d in range(3):
        for j in range(4):
            jump[j] = v[HIGHS[d][j]] - ahead(v[LOWS[d][j]], d)

        for c in range(8):
            at = slice(128 * c, 128 * c + 128)
            jumps = [jump[j, :, at] for j in range(4)]
            for i in range(4):
                total = faces[d, i, :, at] * jumps[0]
                for j in range(1, 4):
                    total = total + faces[d, 4 * min(i, j) + max(i, j), :, at] * jumps[j]
                flux[4 * d + i, :, at] = total

    for c in range(1, 7):
        at = slice(128 * c, 128 * c + 128)
        values = [v[j, :, at] for j in range(8)]
        coef = cfm[0:16, at]
        for i in range(8):
            total = scal[8 * i] * values[0]
            for j in range(1, 8):
                total = total + scal[8 * i + j] * values[j]
            r[i, :, at] = r[i, :, at] - coef * total
    for d in range(3):
        for j in range(4):
            value = flux[4 * d + j]
            r[HIGHS[d][j]] = r[HIGHS[d][j]] - value
            r[LOWS[d][j]] = r[LOWS[d][j]] + behind(value, d)


def mid_step(step, u, r, sol, inv):
    keep, gain = STEPS[step]
    for i in range(8):
        new = keep * u[i] + gain * (inv[i] * r[i])
        u[i] = new
        sol[i] = sol[i] + new


def mid_pre_body(
    scal, slab, got_first, got_second, cfm, level, coarse, send_up, send_down,
    sel, faces, inv, diag, u, sol, r, jump, flux,
):
    pos = position()
    for i in range(8):
        rows = slice(16 * i, 16 * i + 16)
        for m in range(3):
            at = slice(128 * m + 16 * i, 128 * m + 16 * i + 16)
            u[i, :, 128 * m : 128 * m + 128] = from_below(pos, got_first, got_second, at)
            u[i, :, 128 * (m + 5) : 128 * (m + 6)] = from_above(pos, got_first, got_second, at)
        u[i, :, 384:640] = slab[rows, :]
    mid_setup(pos, scal, cfm, sel, faces, inv, diag)
    for i in range(8):
        r[i] = (MIDDLE * diag[i]) * u[i]
        sol[i] = u[i]
    mid_apply(u, r, scal, cfm, faces, jump, flux)
    mid_step(0, u, r, sol, inv)
    mid_apply(u, r, scal, cfm, faces, jump, flux)
    mid_step(1, u, r, sol, inv)
    mid_apply(u, r, scal, cfm, faces, jump, flux)
    level[0] = sol[:, :, 128:896]
    level[1] = r[:, :, 128:896]
    total = r[0]
    for i in range(1, 8):
        total = total + r[i]
    coarse[0] = total
    center = cfm[0:16, :] * scal[128]
    for d in range(3):
        kind = sel[d]
        value = jnp.zeros((16, 1024), F32)
        for k in range(KINDS):
            value = jnp.where(kind == float(k), scal[129 + k], value)
        coarse[2 + d] = value
        center = center + value + behind(value, d)
    coarse[1] = center
    l32 = lanes((16, 768)) % 32
    for out, first in ((send_up, 6), (send_down, 18)):
        acc = jnp.zeros((16, 768), F32)
        for f in range(4):
            acc = jnp.where(l32 // 8 == f, roll(coarse[f, :, 128:896], 8 * f - first), acc)
        out[0] = acc
        out[1] = roll(coarse[4, :, 128:896], -first)


def coarse_z_body(parity, own, dn, up, slab, first, second):
    lane = lanes((16, 128))
    for f in range(5):
        part = 0 if f < 4 else 1
        shift = 8 * f if f < 4 else 0
        for m in range(10):
            acc = jnp.zeros((16, 128), F32)
            for n in range(2):
                y = 2 * m + n - 6
                tile, at = (y + 12) // 4, 32 * ((y + 12) % 4)
                to = 64 * n
                mine = own[f, :, 128 * tile : 128 * tile + 128]
                left = dn[part, :, 128 * (tile - 1) : 128 * tile]
                right = up[part, :, 128 * (tile - 1) : 128 * tile]
                acc = jnp.where(
                    (lane >= to + 22) & (lane < to + 42), roll(mine, to + 22 - (at + 6)), acc
                )
                acc = jnp.where(
                    (lane >= to + 14) & (lane < to + 22), roll(left, to + 14 - (at + shift)), acc
                )
                acc = jnp.where(
                    (lane >= to + 42) & (lane < to + 50), roll(right, to + 42 - (at + shift)), acc
                )
            slab[f, :, 128 * m : 128 * m + 128] = acc
        for m in range(4):
            at = (f, slice(None), slice(128 * m, 128 * m + 128))
            after = (f, slice(None), slice(128 * (m + 6), 128 * (m + 7)))
            put(parity, first, second, at, slab[at], slab[after])


def settle(v, basis, j):
    lane = lanes((16, 128))
    for m in range(6):
        acc = jnp.zeros((16, 128), F32)
        for n in range(4):
            y = 4 * m + n - 8
            tile, at = (y + 14) // 2, 64 * ((y + 14) % 2)
            to = 32 * n
            piece = roll(v[:, 128 * tile : 128 * tile + 128], to + 5 - (at + 21))
            acc = jnp.where((lane >= to + 5) & (lane < to + 27), piece, acc)
        basis[j, :, 128 * m : 128 * m + 128] = acc


def two_sum(a, b):
    s = a + b
    t = s - a
    return s, (a - (s - t)) + (b - t)


def halves(a):
    t = a * 4097.0
    high = t - (t - a)
    return high, a - high


def two_prod(a, b):
    ah, al = halves(a)
    bh, bl = halves(b)
    p = a * b
    return p, ((ah * bh - p) + ah * bl + al * bh) + al * bl


def pair_mul(a, b):
    p, e = two_prod(a[0], b[0])
    return two_sum(p, e + (a[0] * b[1] + a[1] * b[0]))


def pair_sub(a, b):
    s, e = two_sum(a[0], -b[0])
    return two_sum(s, e + (a[1] - b[1]))


def pair_div(a, b):
    first = a[0] / b[0]
    rest = pair_sub(a, pair_mul((first, jnp.zeros_like(first)), b))
    return two_sum(first, rest[0] / b[0])


START = (0, 9, 17, 24, 30, 35, 39, 42)
PAIRS = sum(9 - i for i in range(BASIS))


def krylov_body(scal, own, got_first, got_second, basis, gram, field, hold):
    pos = position()
    for f in range(5):
        field[f, :, 0:512] = from_below(pos, got_first, got_second, f)
        field[f, :, 512:1792] = own[f]
        field[f, :, 1792:2304] = from_above(pos, got_first, got_second, f)
    center, half = scal[133], scal[134]
    lane8 = lanes((8, 128))

    def apply(v):
        total = field[1] * v
        for d in range(3):
            cond = field[2 + d]
            axis, step = ((0, 1), (1, 64), (1, 1))[d]
            total = total - cond * roll(v, -step, axis) - roll(cond * v, step, axis)
        return total

    def compact(v):
        acc = jnp.zeros((8, 128), F32)
        for t in range(2):
            for y in range(8):
                tile, at = (y + 14) // 2, 64 * ((y + 14) % 2) + 28
                to = 64 * t + 8 * y
                piece = v[8 * t : 8 * t + 8, 128 * tile : 128 * tile + 128]
                acc = jnp.where((lane8 >= to) & (lane8 < to + 8), roll(piece, to - at), acc)
        return acc

    before = None
    now = field[0]
    for j in range(BASIS):
        settle(now, basis, j)
        hold[j] = compact(now)
        image = apply(now)
        hold[BASIS + j] = compact(image)
        if j + 1 < BASIS:
            nxt = (image - center * now) * half
            if j > 0:
                nxt = 2.0 * nxt - before
            before, now = now, nxt
    high_rows, low_rows = [], []
    for i in range(BASIS):
        for j in range(i, BASIS + 1):
            other = hold[BASIS + j] if j < BASIS else hold[0]
            p, e = two_prod(hold[i], other)
            high_rows.append(p)
            low_rows.append(e)
    high = jnp.stack(high_rows)
    low = jnp.stack(low_rows)
    for axis, shifts in ((1, (4, 2, 1)), (2, (64, 32, 16, 8, 4, 2, 1))):
        for s in shifts:
            high, e = two_sum(high, roll(high, s, axis))
            low = low + roll(low, s, axis) + e
    row = jnp.zeros((8, 128), F32)
    for n in range(PAIRS):
        row = jnp.where(lane8 == n, high[n], row)
        row = jnp.where(lane8 == 64 + n, low[n], row)
    for m in range(2):
        gram[8 * m : 8 * m + 8, :] = row


def summed(gram):
    count = gram.shape[0] // 8
    high = gram[...].reshape(count, 8, 128)
    low = jnp.zeros((count, 8, 128), F32)
    while count > 1:
        count //= 2
        high, e = two_sum(high[:count], high[count : 2 * count])
        low = low[:count] + low[count : 2 * count] + e
    high, low = high[0], low[0]
    for s in (4, 2, 1):
        high, e = two_sum(high, roll(high, s, 0))
        low = low + roll(low, s, 0) + e
    return two_sum(high, low + roll(high, 64))


def gram_body(gram, out):
    high, low = summed(gram)
    row = jnp.where(lanes((8, 128)) < 64, high, roll(low, 64))
    for m in range(4):
        out[8 * m : 8 * m + 8, :] = row


def mid_post(pos, scal, gram, basis, cfm, level, out, sel, faces, inv, u, r, sol, jump, flux):
    high, low = summed(gram)
    lane = lanes((8, 128))
    sub = lax.broadcasted_iota(jnp.int32, (8, 128), 0)
    mat_h = jnp.zeros((8, 128), F32)
    mat_l = jnp.zeros((8, 128), F32)
    for i in range(BASIS):
        here = (sub == i) & (lane >= i) & (lane <= BASIS)
        mat_h = jnp.where(here, roll(high, i - START[i]), mat_h)
        mat_l = jnp.where(here, roll(low, i - START[i]), mat_l)
        for j in range(i + 1, BASIS):
            here = (sub == j) & (lane == i)
            shift = i - (START[i] + j - i)
            mat_h = jnp.where(here, roll(high, shift), mat_h)
            mat_l = jnp.where(here, roll(low, shift), mat_l)

    def spread_at(v, row, col):
        return jnp.broadcast_to(v[row : row + 1, col : col + 1], (8, 128))

    answers = []
    pivots = []
    for k in range(BASIS):
        start = spread_at(high, 0, START[k])
        piv = (spread_at(mat_h, k, k), spread_at(mat_l, k, k))
        good = jnp.abs(piv[0]) > 1e-12 * jnp.abs(start)
        safe = (jnp.where(good, piv[0], 1.0), jnp.where(good, piv[1], 0.0))
        pivots.append((safe, good))
        row = (
            jnp.broadcast_to(mat_h[k : k + 1, :], (8, 128)),
            jnp.broadcast_to(mat_l[k : k + 1, :], (8, 128)),
        )
        col = (
            jnp.broadcast_to(mat_h[:, k : k + 1], (8, 128)),
            jnp.broadcast_to(mat_l[:, k : k + 1], (8, 128)),
        )
        factor = pair_div(col, safe)
        use = good & (sub != k)
        factor = (jnp.where(use, factor[0], 0.0), jnp.where(use, factor[1], 0.0))
        mat_h, mat_l = pair_sub((mat_h, mat_l), pair_mul(factor, row))
    for k in range(BASIS):
        safe, good = pivots[k]
        value = pair_div((spread_at(mat_h, k, BASIS), spread_at(mat_l, k, BASIS)), safe)[0]
        answers.append(jnp.where(good, value, 0.0))
    weights = [jnp.concatenate([a, a], axis=0) for a in answers]
    lane16 = lanes((16, 128))
    for m in range(8):
        total = jnp.zeros((16, 128), F32)
        if 1 <= m <= 6:
            at = slice(128 * (m - 1), 128 * m)
            for j in range(BASIS):
                total = total + weights[j] * basis[j, :, at]
        for i in range(8):
            u[i, :, 128 * m : 128 * m + 128] = total
    mid_setup(pos, scal, cfm, sel, faces, inv, None)
    ends = jnp.zeros((16, 128), F32)
    for i in range(8):
        for ref in (r, sol):
            ref[i, :, 0:128] = ends
            ref[i, :, 896:1024] = ends
        r[i, :, 128:896] = level[1, i]
        sol[i, :, 128:896] = level[0, i] + u[i, :, 128:896]
    mid_apply(u, r, scal, cfm, faces, jump, flux)
    for i in range(8):
        new = inv[i] * r[i] / MIDDLE
        u[i] = new
        sol[i] = sol[i] + new
    mid_apply(u, r, scal, cfm, faces, jump, flux)
    mid_step(0, u, r, sol, inv)
    mid_apply(u, r, scal, cfm, faces, jump, flux)
    mid_step(1, u, r, sol, inv)
    for i in range(8):
        for half in range(2):
            acc = jnp.zeros((16, 128), F32)
            for n in range(8):
                y = 8 * half + n - 4
                tile, at = (y + 12) // 4, 32 * ((y + 12) % 4) + 8
                acc = jnp.where(
                    lane16 // 16 == n,
                    roll(sol[i, :, 128 * tile : 128 * tile + 128], 16 * n - at),
                    acc,
                )
            out[128 * half + 16 * i : 128 * half + 16 * i + 16, :] = acc


def post_body(
    scal, gram, basis, cfm, level, keep, frz, got_first, got_second, coef, wide, spread,
    lift, diag_w, diag_e, out,
    sel, faces, mid_inv, mid_u, mid_r, mid_sol, jump, flux, mid, w, inv, u, r, sol, px, qx,
):
    pos = position()
    fine_weights(pos, coef, w)
    wide_inside = jnp.concatenate([fine_places(pos)[0]] * (CHUNK // 256), axis=1)
    for c in range(CHUNKS):
        at = slice(CHUNK * c, CHUNK * (c + 1))
        inv[:, at] = fine_inverse(coef, w, diag_w, diag_e, wide_inside, at)
    mid_post(
        pos, scal, gram, basis, cfm, level, mid, sel, faces, mid_inv, mid_u, mid_r,
        mid_sol, jump, flux,
    )
    low = lanes((64, 128)) < 64
    px[:, 0:256] = jnp.zeros((16, 256), F32)
    qx[:, NX * 256 :] = jnp.zeros((16, 256), F32)
    for x in range(NX):
        first, second = slice(256 * x, 256 * x + 128), slice(256 * x + 128, 256 * x + 256)
        turned = roll(frz[x], 64)
        at = 384 + 64 * (x % 8)
        down = from_below(pos, got_first, got_second, slice(at, at + 64))
        over = from_above(pos, got_first, got_second, slice(at, at + 64))
        if x >= 8:
            down = roll(down, 64)
        else:
            over = roll(over, 64)
        r[:, first] = jnp.where(low, down, turned)
        r[:, second] = jnp.where(low, turned, over)
    planes = CHUNK // 256
    for c in range(CHUNKS):
        at = slice(CHUNK * c, CHUNK * (c + 1))
        pieces = [
            mid[pl.ds(128 * half + planes * c + n, 8, stride=16), :]
            for n in range(planes)
            for half in range(2)
        ]
        high, rest = split3(jnp.concatenate(pieces, axis=1))
        stacked = jnp.concatenate([high, rest, high, jnp.zeros((8, CHUNK), F32)], axis=0)
        lifted = mm(lift[...], stacked.astype(BF16))
        u[:, at] = lifted
        sol[:, at] = lifted
    fine_apply(u, r, w, coef, wide, spread, px, qx, None, sol, inv)
    for c in range(CHUNKS):
        at = slice(CHUNK * c, CHUNK * (c + 1))
        new = inv[:, at] * r[:, at] / MIDDLE
        u[:, at] = new
        sol[:, at] = sol[:, at] + new
    fine_apply(u, r, w, coef, wide, spread, px, qx, 0, sol, inv)
    fine_apply(u, r, w, coef, wide, spread, px, qx, 1, sol, inv)
    fine_apply(u, r, w, coef, wide, spread, px, qx, None, sol, inv)
    lane = lanes((64, 128))
    for x in range(NX):
        acc = jnp.zeros((64, 128), F32)
        for part, ref in enumerate((sol, r)):
            for y in range(8):
                half, at = (y + 4) // 8, 16 * ((y + 4) % 8) + 4
                start = 256 * x + 128 * half
                acc = jnp.where(
                    lane // 8 == 8 * part + y,
                    roll(ref[:, start : start + 128], 64 * part + 8 * y - at),
                    acc,
                )
        kept = keep[x % 8] if x < 8 else roll(keep[x % 8], 64)
        out[x] = acc + jnp.where(low, kept, 0.0)


def unpack_body(got, first, second):
    low = lanes((64, 128)) < 64
    for part, out in enumerate((first, second)):
        held = []
        for g in range(8):
            a, b = got[ORDER[g]], got[ORDER[g + 8]]
            if part == 0:
                held.append(jnp.where(low, a, roll(b, 64)))
            else:
                held.append(jnp.where(low, roll(a, 64), b))
        for y, rows in enumerate(exchange(held, 8)):
            out[pl.ds(y, 64, stride=8), :] = rows


def trace_tables():
    high = np.zeros((3, 16, 64), np.float32)
    low = np.zeros((3, 16, 64), np.float32)
    for p in range(4):
        for q in range(4):
            for d in range(3):
                for table, at in ((high, 3), (low, 0)):
                    index = [p, q]
                    index.insert(d, at)
                    table[d, 4 * p + q, 16 * index[0] + 4 * index[1] + index[2]] = 1.0
    return high, low


def mid_traces():
    high = np.zeros((3, 4, 8), np.float32)
    low = np.zeros((3, 4, 8), np.float32)
    for d in range(3):
        for n in range(4):
            high[d, n, HIGHS[d][n]] = 1.0
            low[d, n, LOWS[d][n]] = 1.0
    return high, low


def prolong_tables():
    half = np.float32(0.5)
    one = np.float32(1.0)
    node = np.array([-1.0, -1.0 / math.sqrt(5.0), 1.0 / math.sqrt(5.0), 1.0], np.float32)
    table = np.stack([(one - node) * half, (one + node) * half], axis=1)
    volume = (
        table[:, None, None, :, None, None]
        * table[None, :, None, None, :, None]
        * table[None, None, :, None, None, :]
    ).reshape(64, 8)
    surface = (table[:, None, :, None] * table[None, :, None, :]).reshape(16, 4)
    return volume, surface


def cut(x):
    return lax.reduce_precision(x, 8, 7)


def two_parts(x):
    high = cut(x)
    return high, cut(x - high)


def three_parts(x):
    high = cut(x)
    rest = x - high
    mid = cut(rest)
    return high, mid, cut(rest - mid)


def tables(element, faces):
    volume, surface = prolong_tables()
    elem_mid = jnp.dot(volume.T, jnp.dot(element, volume, precision=HIGHEST), precision=HIGHEST)
    eye = np.eye(16, dtype=np.float32)
    face_mid = jnp.einsum("kij,jb->kib", faces, surface, precision=HIGHEST)
    face_mid = jnp.einsum("ia,kib->kab", surface, face_mid, precision=HIGHEST)
    elem_coarse = jnp.sum(elem_mid)
    face_coarse = jnp.sum(face_mid, axis=(1, 2))
    high, low = trace_tables()
    both = np.concatenate([high, low], axis=0)
    rows = jnp.einsum("kij,djm->dkim", faces, both, precision=HIGHEST).reshape(384, 64)
    wide = jnp.concatenate([element, rows], axis=0)
    wh, wl = two_parts(wide)
    wide = jnp.concatenate([wh, wh, wl], axis=1).astype(BF16)
    spread = np.concatenate([high[1], -low[1], high[2], -low[2]], axis=0).T
    spread = np.concatenate([spread, spread], axis=1)
    face_diag = jnp.sum(faces * eye, axis=2)
    diag = jnp.einsum("dim,ki->mdk", both, face_diag, precision=HIGHEST).reshape(64, 24)
    diag_w = jnp.concatenate(three_parts(diag) + (jnp.zeros((64, 8), F32),), axis=1).astype(BF16)
    diag_e = jnp.sum(element * np.eye(64, dtype=np.float32), axis=1, keepdims=True)
    mh, ml = mid_traces()
    both = np.concatenate([mh, ml], axis=0)
    face_diag = jnp.sum(face_mid * eye[:4, :4], axis=2)
    diag = jnp.einsum("dim,ki->mdk", both, face_diag, precision=HIGHEST).reshape(8, 24)
    mid_diag_w = jnp.concatenate(three_parts(diag) + (jnp.zeros((8, 8), F32),), axis=1).astype(BF16)
    mid_diag_e = jnp.sum(elem_mid * eye[:8, :8], axis=1, keepdims=True)
    vh = volume.astype(BF16).astype(np.float32)
    vl = (volume - vh).astype(BF16).astype(np.float32)
    down = jnp.asarray(np.concatenate([vh.T, vh.T, vl.T], axis=1), BF16)
    lift = jnp.asarray(np.concatenate([vh, vh, vl, np.zeros((64, 8), np.float32)], axis=1), BF16)
    least = 0.1 * elem_coarse
    most = 1.35 * elem_coarse + 9.0 * jnp.max(jnp.abs(face_coarse))
    half = 0.5 * (most - least)
    half = jnp.where(jnp.abs(half) > 0.0, half, 1.0)
    scal = jnp.concatenate(
        [
            elem_mid.reshape(-1),
            face_mid.reshape(-1),
            elem_coarse[None],
            face_coarse,
            (0.5 * (most + least))[None],
            (1.0 / half)[None],
            jnp.zeros((9,), F32),
        ]
    )
    return (
        wide,
        jnp.asarray(spread, BF16),
        diag_w,
        diag_e,
        down,
        mid_diag_w,
        mid_diag_e,
        lift,
        scal,
    )


def local(residual, coefficient, element, faces, kind, flag):
    y_first = [(i, i ^ 1) for i in range(16)]
    y_second = [p for i in range(1, 15, 2) for p in ((i, i + 1), (i + 1, i))]

    def z_index(zb):
        return ORDER[zb % 16] * 2 + zb // 16

    z_up = [(z_index(i), z_index(i + 1)) for i in range(31)]
    z_dn = [(z_index(i + 1), z_index(i)) for i in range(31)]
    z_axes = ("gx", "lvl")
    res = residual.reshape(512, 128)
    slots = call(
        slots_body,
        "slots",
        [f32s(16, 40, 128)],
        (0,) * 4,
        [pltpu.VMEM((128, 128), F32)],
        limit=LARGE_LIMIT,
    )(res, coefficient.reshape(8, 128), kind.reshape(48, 128), flag.reshape(48, 128))[0]
    element, faces, slots = lax.optimization_barrier((element, faces, slots))
    wide, spread, diag_w, diag_e, down, mid_diag_w, mid_diag_e, lift, scal = tables(element, faces)
    parity = jnp.broadcast_to((lax.axis_index("yz") % 2).astype(F32), (8, 128))
    own = lax.all_to_all(slots, "gx", 0, 0, tiled=True)
    own, wide, diag_w, diag_e, mid_diag_w, mid_diag_e, scal, parity = lax.optimization_barrier(
        (own, wide, diag_w, diag_e, mid_diag_w, mid_diag_e, scal, parity)
    )
    dn = lax.ppermute(own[:, 16:40], z_axes, z_up)
    up = lax.ppermute(own[:, 0:24], z_axes, z_dn)
    place_values, place_kinds, pack = place_tables()
    rows, own, other = call(
        join_body,
        "join",
        [f32s(NX, 64, 128), f32s(768, 128), f32s(768, 128)],
        (0,) * 6,
    )(parity, own, dn, up, place_values, place_kinds)
    got_first = lax.ppermute(own, "yz", y_first)
    got_second = lax.ppermute(other, "yz", y_second)
    plane = (64, NX * 256)
    strip = (16, NX * 256 + 256)
    keep, r, coef, cfm, send_up, send_down = call(
        fine_pre_body,
        "fine_pre",
        [
            f32s(8, 64, 128),
            f32s(*plane),
            f32s(8, NX * 256),
            f32s(128, 1024),
            f32s(384, 128),
            f32s(384, 128),
        ],
        (0,) * 12,
        [
            pltpu.VMEM(plane, F32),
            pltpu.VMEM((24, NX * 256), F32),
            pltpu.VMEM(plane, F32),
            pltpu.VMEM(plane, F32),
            pltpu.VMEM(strip, F32),
            pltpu.VMEM(strip, F32),
            pltpu.VMEM((896, 128), F32),
            pltpu.VMEM((256, 128), F32),
        ],
    )(
        rows, own, got_first, got_second, wide, spread, diag_w, diag_e, down, mid_diag_w, mid_diag_e, pack
    )
    dn = lax.ppermute(send_up, z_axes, z_up)
    up = lax.ppermute(send_down, z_axes, z_dn)
    slab, first, second, frz = call(
        mid_z_body,
        "mid_z",
        [f32s(128, 256), f32s(896, 128), f32s(896, 128), f32s(NX, 64, 128)],
        (0,) * 5,
    )(parity, send_up, dn, up, r)
    got_first = lax.ppermute(first, "yz", y_first)
    got_second = lax.ppermute(second, "yz", y_second)
    mid = (8, 16, 1024)
    mid_scratch = [
        pltpu.VMEM((3, 16, 1024), F32),
        pltpu.VMEM((3, 16, 16, 1024), F32),
        pltpu.VMEM(mid, F32),
    ]
    tail_scratch = [pltpu.VMEM((4, 16, 1024), F32), pltpu.VMEM((12, 16, 1024), F32)]
    level, coarse, send_up, send_down = call(
        mid_pre_body,
        "mid_pre",
        [f32s(2, 8, 16, 768), f32s(5, 16, 1024), f32s(2, 16, 768), f32s(2, 16, 768)],
        (1, 0, 0, 0, 0),
        mid_scratch
        + [pltpu.VMEM(mid, F32)] * 4
        + tail_scratch,
    )(scal, slab, got_first, got_second, cfm)
    dn = lax.ppermute(send_up, z_axes, z_up)
    up = lax.ppermute(send_down, z_axes, z_dn)
    coarse_slab, first, second = call(
        coarse_z_body,
        "coarse_z",
        [f32s(5, 16, 1280), f32s(5, 16, 512), f32s(5, 16, 512)],
        (0,) * 4,
    )(parity, coarse, dn, up)
    coarse_first = lax.ppermute(first, "yz", y_first)
    coarse_second = lax.ppermute(second, "yz", y_second)
    basis, gram = call(
        krylov_body,
        "krylov",
        [f32s(BASIS, 16, 768), f32s(16, 128)],
        (1, 0, 0, 0),
        [
            pltpu.VMEM((5, 16, 2304), F32),
            pltpu.VMEM((2 * BASIS, 8, 128), F32),
        ],
    )(scal, coarse_slab, coarse_first, coarse_second)
    gram = lax.all_to_all(gram, "yz", 0, 0, tiled=True)
    gram = call(gram_body, "gram", [f32s(32, 128)], (0,))(gram)[0]
    gram = lax.all_to_all(gram, z_axes, 0, 0, tiled=True)
    packed = call(
        post_body,
        "post",
        [f32s(16, 64, 128)],
        (1,) + (0,) * 14,
        mid_scratch
        + [pltpu.VMEM(mid, F32)] * 3
        + tail_scratch
        + [
            pltpu.VMEM((256, 128), F32),
            pltpu.VMEM((24, NX * 256), F32),
            pltpu.VMEM(plane, F32),
            pltpu.VMEM(plane, F32),
            pltpu.VMEM(plane, F32),
            pltpu.VMEM(plane, F32),
            pltpu.VMEM(strip, F32),
            pltpu.VMEM(strip, F32),
        ],
        limit=LARGE_LIMIT,
    )(
        scal, gram, basis, cfm, level, keep, frz, got_first, got_second, coef, wide, spread,
        lift, diag_w, diag_e,
    )[0]
    got = lax.all_to_all(packed, "gx", 0, 0, tiled=True)
    correction, rest = call(unpack_body, "unpack", [f32s(512, 128), f32s(512, 128)], (0,))(got)
    return (correction.reshape(64, 1, 8, 128), rest.reshape(64, 1, 8, 128))


def solution(mesh):
    in_specs = (
        P(None, "gx", "yz", "lvl"),
        P("gx", "yz", "lvl"),
        P(),
        P(),
        P(None, "gx", "yz", "lvl"),
        P(None, "gx", "yz", "lvl"),
    )
    out_specs = (P(None, "gx", "yz", "lvl"), P(None, "gx", "yz", "lvl"))
    return jax.shard_map(local, mesh=mesh, in_specs=in_specs, out_specs=out_specs, check_vma=False)
```

```python
import functools
import math

import jax
import jax.numpy as jnp
import numpy as np
from jax import lax
from jax.experimental import pallas as pl
from jax.experimental.pallas import tpu as pltpu
from jax.sharding import PartitionSpec as P

NX = 16
NY = 128
NZ = 256
KINDS = 4
F32 = jnp.float32
BF16 = jnp.bfloat16
HIGHEST = lax.Precision.HIGHEST
LOW_EIG = 0.3
HIGH_EIG = 3.0
MIDDLE = 0.5 * (HIGH_EIG + LOW_EIG)
SPREAD = 0.5 * (HIGH_EIG - LOW_EIG)
SCALED = MIDDLE / SPREAD
RHO0 = 1.0 / SCALED
RHO1 = 1.0 / (2.0 * SCALED - RHO0)
RHO2 = 1.0 / (2.0 * SCALED - RHO1)
STEPS = ((RHO1 * RHO0, 2.0 * RHO1 / SPREAD), (RHO2 * RHO1, 2.0 * RHO2 / SPREAD))
BASIS = 8
ORDER = tuple(2 * n if n < 8 else 2 * (15 - n) + 1 for n in range(16))
VMEM_LIMIT = 24 * 2**20
LARGE_LIMIT = 60 * 2**20


def lanes(shape):
    return lax.broadcasted_iota(jnp.int32, shape, len(shape) - 1)


def roll(x, shift, axis=None):
    axis = x.ndim - 1 if axis is None else axis
    shift = shift % x.shape[axis]
    return x if shift == 0 else pltpu.roll(x, shift, axis)


SPACES = {
    0: pl.BlockSpec(memory_space=pltpu.VMEM),
    1: pl.BlockSpec(memory_space=pltpu.SMEM),
}


def call(body, name, out_shape, in_specs, scratch=(), out_specs=None, limit=VMEM_LIMIT):
    out_specs = out_specs or (0,) * len(out_shape)
    return pl.pallas_call(
        body,
        out_shape=list(out_shape),
        in_specs=[SPACES[i] for i in in_specs],
        out_specs=[SPACES[i] for i in out_specs],
        scratch_shapes=list(scratch),
        compiler_params=pltpu.CompilerParams(vmem_limit_bytes=limit),
        cost_estimate=pl.CostEstimate(flops=1000000, bytes_accessed=1000000, transcendentals=0),
        name=name,
    )


def position():
    chip = lax.axis_index("gx")
    up = lax.rem(chip, 2) == 0
    block = jnp.where(up, lax.div(chip, 2), 15 - lax.div(chip, 2))
    return lax.axis_index("yz"), lax.axis_index("lvl") * 16 + block


def even(pos):
    return lax.rem(pos[0], 2) == 0


def put(parity, first, second, at, fwd, bwd):
    is_even = jnp.broadcast_to(parity[0:1, :], fwd.shape) == 0.0
    first[at] = jnp.where(is_even, fwd, bwd)
    second[at] = jnp.where(is_even, bwd, fwd)


def from_below(pos, first, second, at):
    return jnp.where(even(pos), second[at], first[at])


def from_above(pos, first, second, at):
    return jnp.where(even(pos), first[at], second[at])


def f32s(*shape):
    return jax.ShapeDtypeStruct(shape, F32)


def split3(x):
    high = x.astype(BF16).astype(F32)
    low = x - high
    return high, low


def stack_hlh(x):
    high, low = split3(x)
    return jnp.concatenate([high, low, high], axis=0).astype(BF16)


def mm(a, b):
    return jnp.dot(a, b, preferred_element_type=F32)


def exchange(arrays, lane_block):
    arrays = list(arrays)
    group = lanes(arrays[0].shape) // lane_block
    for bit in (1, 2, 4):
        upper = (group // bit) % 2 == 1
        for n in range(8):
            if n & bit:
                continue
            a, b = arrays[n], arrays[n | bit]
            arrays[n] = jnp.where(upper, roll(b, lane_block * bit), a)
            arrays[n | bit] = jnp.where(upper, b, roll(a, -lane_block * bit))
    return arrays


def slots_body(res, coef, kind, flag, out, cf):
    for n in range(16):
        cf[8 * n : 8 * n + 8, :] = jnp.zeros((8, 128), F32)
    cf[0:8, :] = coef[...]
    for first, ref in ((8, kind), (32, flag)):
        for n in range(3):
            at = 8 * (2 * n + 1)
            cf[first + 8 * n : first + 8 * n + 8, :] = ref[at : at + 8, :].astype(F32)
    for first, ref in ((80, kind), (104, flag)):
        for n in range(2):
            at = 8 * (2 * n + 2)
            cf[first + 8 * n : first + 8 * n + 8, :] = ref[at : at + 8, :].astype(F32)
    low = lanes((16, 128)) < 64
    low8 = lanes((8, 128)) < 64
    near = lanes((32, 128)) % 8 < 4
    values = exchange([res[pl.ds(y, 64, stride=8), :] for y in range(8)], 8)
    kinds = exchange([cf[pl.ds(y, 16, stride=8), :] for y in range(8)], 8)
    for j in range(8):
        first, second = ORDER[j], ORDER[j + 8]
        a, b = values[j][0:32], values[j][32:64]
        for at, v in (
            (0, jnp.where(near, a, roll(b, 4))),
            (24, jnp.where(near, roll(a, -4), b)),
        ):
            out[first, at : at + 16, :] = jnp.where(low, v[0:16], roll(v[16:32], 64))
            out[second, at : at + 16, :] = jnp.where(low, roll(v[0:16], 64), v[16:32])
        a, b = kinds[j][0:8], kinds[j][8:16]
        out[first, 16:24, :] = jnp.where(low8, a, roll(b, 64))
        out[second, 16:24, :] = jnp.where(low8, roll(a, 64), b)


def place_tables():
    values = np.zeros((512, 512), np.float32)
    kinds = np.zeros((384, 512), np.float32)
    pack = np.zeros((256, 128), np.float32)
    for half in range(2):
        for y in range(8):
            for z in range(8):
                lane = 64 * half + 8 * y + z
                to = 128 * (2 * (z // 4) + half) + 16 * y + z % 4
                for n, first in enumerate((4, 8, 12, 0)):
                    values[128 * n + lane, to + first] = 1.0
                for n, first in enumerate((12, 4, 20)):
                    kinds[128 * n + lane, 256 * half + 32 * y + first + z] = 1.0
    for y in range(-1, 9):
        for z in range(-1, 9):
            pack[16 * (y + 4) + z + 4, 12 * (y + 1) + z + 1] = 1.0
    return [jnp.asarray(v, BF16) for v in (values, kinds, pack)]


def three_rows(x):
    high = x.astype(BF16).astype(F32)
    rest = x - high
    mid = rest.astype(BF16).astype(F32)
    return jnp.concatenate([high, mid, rest - mid], axis=0).astype(BF16)


def moved(x, table):
    count = x.shape[0]
    out = mm(three_rows(x), table)
    return out[0:count] + out[count : 2 * count] + out[2 * count :]


def join_body(parity, own, dn, up, place_values, place_kinds, rows, first, second):
    parts = (own[:, 0:16, :], own[:, 24:40, :], up[:, 0:16, :], dn[:, 8:24, :])
    values = jnp.concatenate([v.reshape(256, 128) for v in parts], axis=1)
    out = moved(values, place_values[...])
    for x in range(NX):
        for n in range(4):
            rows[x, 16 * n : 16 * n + 16, :] = out[16 * x : 16 * x + 16, 128 * n : 128 * n + 128]
    low = lanes((64, 128)) < 64
    for x in range(8):
        fwd = jnp.where(low, roll(rows[x], 64), rows[x + 8])
        bwd = jnp.where(low, rows[x], roll(rows[x + 8], 64))
        put(parity, first, second, slice(64 * x, 64 * x + 64), fwd, bwd)
    parts = (own[:, 16:24, :], dn[:, 0:8, :], up[:, 16:24, :])
    kinds = jnp.concatenate([v.reshape(128, 128) for v in parts], axis=1)
    out = moved(kinds, place_kinds[...])
    array = lax.broadcasted_iota(jnp.int32, (128, 128), 0) % 8
    edge = (lanes((128, 128)) % 32 == 3) & ((array == 3) | (array == 6))
    lane = lanes((128, 128))
    for h in range(2):
        minus = out[:, 256 + 128 * h : 384 + 128 * h]
        plus = jnp.where(edge, roll(minus, -1), out[:, 128 * h : 128 * h + 128])
        if h == 0:
            plus = jnp.where((array == 7) & (lane < 32), roll(minus, 5, 0), plus)
            plus = jnp.where(
                (array == 7) & (lane >= 32) & (lane < 64), roll(roll(minus, 2, 0), 32), plus
            )
        first[512 + 128 * h : 640 + 128 * h, :] = plus
        second[512 + 128 * h : 640 + 128 * h, :] = plus


CHUNK = 4096
CHUNKS = NX * 256 // CHUNK


def fine_apply(u, r, w, coef, wide, spread, px, qx, step, sol, inv):
    for c in range(CHUNKS):
        at = slice(CHUNK * c, CHUNK * (c + 1))
        after = slice(CHUNK * c + 256, CHUNK * (c + 1) + 256)
        prod = mm(wide[...], stack_hlh(u[:, at]))

        def pick(base, row):
            total = w[row : row + 1, at] * prod[base : base + 16]
            for k in range(1, KINDS):
                total = total + w[row + k : row + k + 1, at] * prod[base + 16 * k : base + 16 * k + 16]
            return total

        px[:, after] = pick(64, 0)
        py = pick(128, 4)
        pz = pick(192, 8)
        qx[:, at] = pick(256, 12)
        qy = pick(320, 16)
        qz = pick(384, 20)
        flux = jnp.concatenate(
            [py - roll(qy, -16), roll(py, 16) - qy, pz - roll(qz, -1), roll(pz, 1) - qz], axis=0
        )
        high, low = split3(flux)
        faces = mm(spread[...], jnp.concatenate([high, low], axis=0).astype(BF16))
        r[:, at] = r[:, at] - (coef[0:1, at] * prod[0:64] + faces)

    for c in range(CHUNKS):
        at = slice(CHUNK * c, CHUNK * (c + 1))
        after = slice(CHUNK * c + 256, CHUNK * (c + 1) + 256)
        r[48:64, at] = r[48:64, at] - (px[:, after] - qx[:, after])
        r[0:16, at] = r[0:16, at] + (px[:, at] - qx[:, at])
        if step is not None:
            keep, gain = STEPS[step]
            new = keep * u[:, at] + gain * (inv[:, at] * r[:, at])
            u[:, at] = new
            sol[:, at] = sol[:, at] + new


def fine_places(pos):
    place = lanes((1, 256))
    y_at = pos[0] * 8 - 4 + place // 16
    z_at = pos[1] * 8 - 4 + place % 16
    inside = (y_at >= 0) & (y_at < NY) & (z_at >= 0) & (z_at < NZ)
    return inside, inside & (y_at < NY - 1), inside & (z_at < NZ - 1)


def fine_weights(pos, coef, w):
    inside, has_y, has_z = fine_places(pos)
    w[12:16, 0:256] = jnp.zeros((4, 256), F32)
    for x in range(NX):
        at = slice(256 * x, 256 * x + 256)
        rows = coef[:, at]
        opens = [
            inside & (rows[4:5] == 0.0) if x < NX - 1 else jnp.zeros((1, 256), jnp.bool_),
            has_y & (rows[5:6] == 0.0),
            has_z & (rows[6:7] == 0.0),
        ]
        plus = [
            [jnp.where(opens[d] & (rows[1 + d : 2 + d] == float(k)), 1.0, 0.0) for k in range(KINDS)]
            for d in range(3)
        ]
        plus_all = jnp.concatenate(plus[0] + plus[1] + plus[2], axis=0)
        w[0:12, at] = plus_all
        if x < NX - 1:
            w[12:16, 256 * x + 256 : 256 * x + 512] = plus_all[0:4]
        w[16:20, at] = roll(plus_all[4:8], 16)
        w[20:24, at] = roll(plus_all[8:12], 1)


def kinds_of(w, at):
    ws = w[:, at]
    return jnp.concatenate([ws, ws, ws, jnp.zeros((8, CHUNK), F32)], axis=0).astype(BF16)


def fine_inverse(coef, w, diag_w, diag_e, inside, at):
    diag = diag_e[...] * coef[0:1, at] + mm(diag_w[...], kinds_of(w, at))
    return jnp.where(inside, 1.0 / diag, 0.0)


def compacted(first, second, lane):
    v = roll(jnp.where(lane < 64, roll(first, 64), roll(second, 64)), -4)
    for size in (8, 16, 32):
        v = jnp.where(lane % (4 * size) < size, v, roll(v, -size))
    return v


def fine_pre_body(
    rows_in,
    own,
    got_first,
    got_second,
    wide,
    spread,
    diag_w,
    diag_e,
    down,
    mid_diag_w,
    mid_diag_e,
    pack,
    keep,
    r,
    coef,
    cfm,
    send_up,
    send_down,
    sol,
    w,
    inv,
    u,
    px,
    qx,
    gather,
    held,
):
    pos = position()
    low = lanes((64, 128)) < 64
    lane8 = lanes((8, 128))
    inside = fine_places(pos)[0]
    px[:, 0:256] = jnp.zeros((16, 256), F32)
    qx[:, NX * 256 :] = jnp.zeros((16, 256), F32)
    cfm[:, 896:1024] = jnp.zeros((128, 128), F32)
    array = lax.broadcasted_iota(jnp.int32, (8, 128), 0)
    edge = (lane8 >= 96) & ((array == 2) | (array == 5))
    for x in range(NX):
        first, second = slice(256 * x, 256 * x + 128), slice(256 * x + 128, 256 * x + 256)
        turned = roll(rows_in[x], 64)
        at = 64 * (x % 8)
        under = from_below(pos, got_first, got_second, slice(at, at + 64))
        over = from_above(pos, got_first, got_second, slice(at, at + 64))
        if x >= 8:
            under = roll(under, 64)
        else:
            over = roll(over, 64)
        r[:, first] = jnp.where(low, under, turned)
        r[:, second] = jnp.where(low, turned, over)
        places = [slice(512 + 128 * h + 8 * x, 520 + 128 * h + 8 * x) for h in range(2)]
        blocks = (
            [from_below(pos, got_first, got_second, p) for p in places]
            + [own[p] for p in places]
            + [from_above(pos, got_first, got_second, p) for p in places]
        )
        minus = jnp.where(array == 2, roll(roll(blocks[0], 3, 0), 96), roll(roll(blocks[0], 6, 0), 64))
        gather[pl.ds(x, 8, stride=16), :] = jnp.where(edge, minus, 0.0)
        for m in range(6):
            gather[pl.ds(128 * (m + 1) + x, 8, stride=16), :] = blocks[m]
        for half, at in enumerate((first, second)):
            acc = jnp.zeros((8, 128), F32)
            for row in range(8):
                n = 8 * half + row
                acc = jnp.where(
                    lane8 // 16 == row,
                    roll(blocks[1 + n // 4], 16 * row - (n % 4) * 32 - 8),
                    acc,
                )
            coef[:, at] = acc
    for m in range(7):
        cfm[:, 128 * m : 128 * m + 128] = gather[128 * m : 128 * m + 128, :]
    fine_weights(pos, coef, w)
    wide_inside = jnp.concatenate([inside] * (CHUNK // 256), axis=1)
    for c in range(CHUNKS):
        at = slice(CHUNK * c, CHUNK * (c + 1))
        inverse = fine_inverse(coef, w, diag_w, diag_e, wide_inside, at)
        inv[:, at] = inverse
        update = inverse * r[:, at] / MIDDLE
        u[:, at] = update
        sol[:, at] = update
    fine_apply(u, r, w, coef, wide, spread, px, qx, 0, sol, inv)
    fine_apply(u, r, w, coef, wide, spread, px, qx, 1, sol, inv)
    fine_apply(u, r, w, coef, wide, spread, px, qx, None, sol, inv)
    lane16 = lanes((16, 128)) % 16 // 4
    for c in range(CHUNKS):
        at = slice(CHUNK * c, CHUNK * (c + 1))
        rhs = mm(down[...], stack_hlh(r[:, at]))
        diag = mid_diag_e[...] * coef[0:1, at] + mm(mid_diag_w[...], kinds_of(w, at))
        update = jnp.where(wide_inside, 1.0 / diag, 0.0) * rhs / MIDDLE
        for n in range(CHUNK // 256):
            x = (CHUNK // 256) * c + n
            for half in range(2):
                piece = update[:, 256 * n + 128 * half : 256 * n + 128 * half + 128]
                held[pl.ds(128 * half + x, 8, stride=16), :] = piece
    packed = moved(jnp.concatenate([held[0:128, :], held[128:256, :]], axis=1), pack[...])
    send_up[0:128, :] = packed
    send_down[0:128, :] = packed
    for x in range(NX):
        first, second = slice(256 * x, 256 * x + 128), slice(256 * x + 128, 256 * x + 256)
        mine = jnp.where(low, roll(r[:, first], 64), roll(r[:, second], 64))
        up = jnp.zeros((16, 128), F32)
        dn = jnp.zeros((16, 128), F32)
        for j in range(4):
            part = mine[16 * j : 16 * j + 16]
            up = jnp.where(lane16 == j, roll(part, 4 * j - 8), up)
            dn = jnp.where(lane16 == j, roll(part, 4 * j - 4), dn)
        send_up[128 + 16 * x : 144 + 16 * x, :] = up
        send_down[128 + 16 * x : 144 + 16 * x, :] = dn
    lane = lanes((64, 128))
    for x in range(8):
        a, b = [
            compacted(sol[:, 256 * n : 256 * n + 128], sol[:, 256 * n + 128 : 256 * n + 256], lane)
            for n in (x, x + 8)
        ]
        keep[x] = jnp.where(low, a, roll(b, 64))


def mid_z_body(parity, own, dn, up, r, slab, first, second, frz):
    low = lanes((64, 128)) < 64
    l16 = lanes((16, 128)) % 16
    for x in range(NX):
        at = 256 * x
        mine = jnp.where(low, roll(r[:, at : at + 128], 64), roll(r[:, at + 128 : at + 256], 64))
        pack_dn = dn[128 + 16 * x : 144 + 16 * x, :]
        pack_up = up[128 + 16 * x : 144 + 16 * x, :]
        for j in range(4):
            rows = slice(16 * j, 16 * j + 16)
            part = jnp.where(l16 < 4, roll(pack_dn, -4 * j), mine[rows])
            part = jnp.where(l16 >= 12, roll(pack_up, 12 - 4 * j), part)
            frz[x, rows, :] = part
    for x in range(8):
        fwd = jnp.where(low, roll(frz[x], 64), frz[x + 8])
        bwd = jnp.where(low, frz[x], roll(frz[x + 8], 64))
        put(parity, first, second, slice(384 + 64 * x, 448 + 64 * x), fwd, bwd)
    lane = lanes((128, 128))
    tiles = []
    for m in range(4):
        acc = jnp.zeros((128, 128), F32)
        for n in range(4):
            y = 4 * (m - 1) + n
            if y < -1 or y > 8:
                continue
            to = 32 * n
            at = 12 * (y + 1)
            rows = slice(0, 128)
            acc = jnp.where((lane >= to + 12) & (lane < to + 20), roll(own[rows, :], to + 11 - at), acc)
            acc = jnp.where((lane >= to + 3) & (lane < to + 12), roll(dn[rows, :], to + 3 - at), acc)
            acc = jnp.where((lane >= to + 20) & (lane < to + 29), roll(up[rows, :], to + 19 - at), acc)
        if 1 <= m <= 2:
            slab[:, 128 * (m - 1) : 128 * m] = acc
        tiles.append(acc)
    for m in range(3):
        put(parity, first, second, slice(128 * m, 128 * m + 128), tiles[m], tiles[m + 1])


LOWS = ((0, 1, 2, 3), (0, 1, 4, 5), (0, 2, 4, 6))
HIGHS = ((4, 5, 6, 7), (2, 3, 6, 7), (1, 3, 5, 7))


def ahead(v, d):
    if d == 0:
        return roll(v, -1, 0)
    return roll(v, -32 if d == 1 else -1, 1)


def behind(v, d):
    if d == 0:
        return roll(v, 1, 0)
    return roll(v, 32 if d == 1 else 1, 1)


def mid_setup(pos, scal, cfm, sel, faces, inv, diag):
    place = lanes((16, 1024))
    x_at = lax.broadcasted_iota(jnp.int32, (16, 1024), 0)
    y_at = pos[0] * 8 - 12 + place // 32
    z_at = pos[1] * 8 - 12 + place % 32
    domain = (y_at >= 0) & (y_at < NY) & (z_at >= 0) & (z_at < NZ)
    known = domain & (place >= 128) & (place < 896) & (place % 32 >= 4) & (place % 32 < 28)
    lasts = (x_at < NX - 1, y_at < NY - 1, z_at < NZ - 1)
    for d in range(3):
        is_open = domain & lasts[d] & (cfm[64 + 16 * d : 80 + 16 * d, :] == 0.0)
        sel[d] = jnp.where(is_open, cfm[16 + 16 * d : 32 + 16 * d, :], 4.0)
    coef = cfm[0:16, :]

    for d in range(3):
        for c in range(8):
            at = slice(128 * c, 128 * c + 128)
            kind = sel[d, :, at]
            ones = [kind == float(k) for k in range(KINDS)]
            for i in range(4):
                for j in range(i, 4):
                    value = jnp.zeros((16, 128), F32)
                    for k in range(KINDS):
                        value = jnp.where(ones[k], scal[64 + 16 * k + 4 * i + j], value)
                    faces[d, 4 * i + j, :, at] = value
    if inv is None:
        return known
    for i in range(8):
        total = coef * scal[9 * i]
        for d in range(3):
            if i in HIGHS[d]:
                total = total + faces[d, 5 * HIGHS[d].index(i)]
            else:
                total = total + behind(faces[d, 5 * LOWS[d].index(i)], d)
        if diag is not None:
            diag[i] = total
        inv[i] = jnp.where(known, 1.0 / total, 0.0)
    return known


def mid_apply(v, r, scal, cfm, faces, jump, flux):
    for d in range(3):
        for j in range(4):
            jump[j] = v[HIGHS[d][j]] - ahead(v[LOWS[d][j]], d)

        for c in range(8):
            at = slice(128 * c, 128 * c + 128)
            jumps = [jump[j, :, at] for j in range(4)]
            for i in range(4):
                total = faces[d, i, :, at] * jumps[0]
                for j in range(1, 4):
                    total = total + faces[d, 4 * min(i, j) + max(i, j), :, at] * jumps[j]
                flux[4 * d + i, :, at] = total

    for c in range(1, 7):
        at = slice(128 * c, 128 * c + 128)
        values = [v[j, :, at] for j in range(8)]
        coef = cfm[0:16, at]
        for i in range(8):
            total = scal[8 * i] * values[0]
            for j in range(1, 8):
                total = total + scal[8 * i + j] * values[j]
            r[i, :, at] = r[i, :, at] - coef * total
    for d in range(3):
        for j in range(4):
            value = flux[4 * d + j]
            r[HIGHS[d][j]] = r[HIGHS[d][j]] - value
            r[LOWS[d][j]] = r[LOWS[d][j]] + behind(value, d)


def mid_step(step, u, r, sol, inv):
    keep, gain = STEPS[step]
    for i in range(8):
        new = keep * u[i] + gain * (inv[i] * r[i])
        u[i] = new
        sol[i] = sol[i] + new


def mid_pre_body(
    scal, slab, got_first, got_second, cfm, level, coarse, send_up, send_down,
    sel, faces, inv, diag, u, sol, r, jump, flux,
):
    pos = position()
    for i in range(8):
        rows = slice(16 * i, 16 * i + 16)
        for m in range(3):
            at = slice(128 * m + 16 * i, 128 * m + 16 * i + 16)
            u[i, :, 128 * m : 128 * m + 128] = from_below(pos, got_first, got_second, at)
            u[i, :, 128 * (m + 5) : 128 * (m + 6)] = from_above(pos, got_first, got_second, at)
        u[i, :, 384:640] = slab[rows, :]
    mid_setup(pos, scal, cfm, sel, faces, inv, diag)
    for i in range(8):
        r[i] = (MIDDLE * diag[i]) * u[i]
        sol[i] = u[i]
    mid_apply(u, r, scal, cfm, faces, jump, flux)
    mid_step(0, u, r, sol, inv)
    mid_apply(u, r, scal, cfm, faces, jump, flux)
    mid_step(1, u, r, sol, inv)
    mid_apply(u, r, scal, cfm, faces, jump, flux)
    level[0] = sol[:, :, 128:896]
    level[1] = r[:, :, 128:896]
    total = r[0]
    for i in range(1, 8):
        total = total + r[i]
    coarse[0] = total
    center = cfm[0:16, :] * scal[128]
    for d in range(3):
        kind = sel[d]
        value = jnp.zeros((16, 1024), F32)
        for k in range(KINDS):
            value = jnp.where(kind == float(k), scal[129 + k], value)
        coarse[2 + d] = value
        center = center + value + behind(value, d)
    coarse[1] = center
    l32 = lanes((16, 768)) % 32
    for out, first in ((send_up, 6), (send_down, 18)):
        acc = jnp.zeros((16, 768), F32)
        for f in range(4):
            acc = jnp.where(l32 // 8 == f, roll(coarse[f, :, 128:896], 8 * f - first), acc)
        out[0] = acc
        out[1] = roll(coarse[4, :, 128:896], -first)


def coarse_z_body(parity, own, dn, up, slab, first, second):
    lane = lanes((16, 128))
    for f in range(5):
        part = 0 if f < 4 else 1
        shift = 8 * f if f < 4 else 0
        for m in range(10):
            acc = jnp.zeros((16, 128), F32)
            for n in range(2):
                y = 2 * m + n - 6
                tile, at = (y + 12) // 4, 32 * ((y + 12) % 4)
                to = 64 * n
                mine = own[f, :, 128 * tile : 128 * tile + 128]
                left = dn[part, :, 128 * (tile - 1) : 128 * tile]
                right = up[part, :, 128 * (tile - 1) : 128 * tile]
                acc = jnp.where(
                    (lane >= to + 22) & (lane < to + 42), roll(mine, to + 22 - (at + 6)), acc
                )
                acc = jnp.where(
                    (lane >= to + 14) & (lane < to + 22), roll(left, to + 14 - (at + shift)), acc
                )
                acc = jnp.where(
                    (lane >= to + 42) & (lane < to + 50), roll(right, to + 42 - (at + shift)), acc
                )
            slab[f, :, 128 * m : 128 * m + 128] = acc
        for m in range(4):
            at = (f, slice(None), slice(128 * m, 128 * m + 128))
            after = (f, slice(None), slice(128 * (m + 6), 128 * (m + 7)))
            put(parity, first, second, at, slab[at], slab[after])


def settle(v, basis, j):
    lane = lanes((16, 128))
    for m in range(6):
        acc = jnp.zeros((16, 128), F32)
        for n in range(4):
            y = 4 * m + n - 8
            tile, at = (y + 14) // 2, 64 * ((y + 14) % 2)
            to = 32 * n
            piece = roll(v[:, 128 * tile : 128 * tile + 128], to + 5 - (at + 21))
            acc = jnp.where((lane >= to + 5) & (lane < to + 27), piece, acc)
        basis[j, :, 128 * m : 128 * m + 128] = acc


def two_sum(a, b):
    s = a + b
    t = s - a
    return s, (a - (s - t)) + (b - t)


def halves(a):
    t = a * 4097.0
    high = t - (t - a)
    return high, a - high


def two_prod(a, b):
    ah, al = halves(a)
    bh, bl = halves(b)
    p = a * b
    return p, ((ah * bh - p) + ah * bl + al * bh) + al * bl


def pair_mul(a, b):
    p, e = two_prod(a[0], b[0])
    return two_sum(p, e + (a[0] * b[1] + a[1] * b[0]))


def pair_sub(a, b):
    s, e = two_sum(a[0], -b[0])
    return two_sum(s, e + (a[1] - b[1]))


def pair_div(a, b):
    first = a[0] / b[0]
    rest = pair_sub(a, pair_mul((first, jnp.zeros_like(first)), b))
    return two_sum(first, rest[0] / b[0])


START = (0, 9, 17, 24, 30, 35, 39, 42)
PAIRS = sum(9 - i for i in range(BASIS))


def krylov_body(interval, own, got_first, got_second, basis, gram, field, hold):
    pos = position()
    for f in range(5):
        field[f, :, 0:512] = from_below(pos, got_first, got_second, f)
        field[f, :, 512:1792] = own[f]
        field[f, :, 1792:2304] = from_above(pos, got_first, got_second, f)
    center = jnp.concatenate([interval[0:1, :]] * 18, axis=1)
    half = jnp.concatenate([interval[8:9, :]] * 18, axis=1)
    lane8 = lanes((8, 128))

    def apply(v):
        total = field[1] * v
        for d in range(3):
            cond = field[2 + d]
            axis, step = ((0, 1), (1, 64), (1, 1))[d]
            total = total - cond * roll(v, -step, axis) - roll(cond * v, step, axis)
        return total

    def compact(v):
        acc = jnp.zeros((8, 128), F32)
        for t in range(2):
            for y in range(8):
                tile, at = (y + 14) // 2, 64 * ((y + 14) % 2) + 28
                to = 64 * t + 8 * y
                piece = v[8 * t : 8 * t + 8, 128 * tile : 128 * tile + 128]
                acc = jnp.where((lane8 >= to) & (lane8 < to + 8), roll(piece, to - at), acc)
        return acc

    before = None
    now = field[0]
    for j in range(BASIS):
        settle(now, basis, j)
        hold[j] = compact(now)
        image = apply(now)
        hold[BASIS + j] = compact(image)
        if j + 1 < BASIS:
            nxt = (image - center * now) * half
            if j > 0:
                nxt = 2.0 * nxt - before
            before, now = now, nxt
    high_rows, low_rows = [], []
    for i in range(BASIS):
        for j in range(i, BASIS + 1):
            other = hold[BASIS + j] if j < BASIS else hold[0]
            p, e = two_prod(hold[i], other)
            high_rows.append(p)
            low_rows.append(e)
    high = jnp.stack(high_rows)
    low = jnp.stack(low_rows)
    for axis, shifts in ((1, (4, 2, 1)), (2, (64, 32, 16, 8, 4, 2, 1))):
        for s in shifts:
            high, e = two_sum(high, roll(high, s, axis))
            low = low + roll(low, s, axis) + e
    row = jnp.zeros((8, 128), F32)
    for n in range(PAIRS):
        row = jnp.where(lane8 == n, high[n], row)
        row = jnp.where(lane8 == 64 + n, low[n], row)
    for m in range(2):
        gram[8 * m : 8 * m + 8, :] = row


def summed(gram):
    count = gram.shape[0] // 8
    high = gram[...].reshape(count, 8, 128)
    low = jnp.zeros((count, 8, 128), F32)
    while count > 1:
        count //= 2
        high, e = two_sum(high[:count], high[count : 2 * count])
        low = low[:count] + low[count : 2 * count] + e
    high, low = high[0], low[0]
    for s in (4, 2, 1):
        high, e = two_sum(high, roll(high, s, 0))
        low = low + roll(low, s, 0) + e
    return two_sum(high, low + roll(high, 64))


def gram_body(gram, out):
    high, low = summed(gram)
    row = jnp.where(lanes((8, 128)) < 64, high, roll(low, 64))
    for m in range(4):
        out[8 * m : 8 * m + 8, :] = row


def mid_post(pos, scal, gram, basis, cfm, level, out, sel, faces, inv, u, r, sol, jump, flux):
    high, low = summed(gram)
    lane = lanes((8, 128))
    sub = lax.broadcasted_iota(jnp.int32, (8, 128), 0)
    mat_h = jnp.zeros((8, 128), F32)
    mat_l = jnp.zeros((8, 128), F32)
    for i in range(BASIS):
        here = (sub == i) & (lane >= i) & (lane <= BASIS)
        mat_h = jnp.where(here, roll(high, i - START[i]), mat_h)
        mat_l = jnp.where(here, roll(low, i - START[i]), mat_l)
        for j in range(i + 1, BASIS):
            here = (sub == j) & (lane == i)
            shift = i - (START[i] + j - i)
            mat_h = jnp.where(here, roll(high, shift), mat_h)
            mat_l = jnp.where(here, roll(low, shift), mat_l)

    def spread_at(v, row, col):
        return jnp.broadcast_to(v[row : row + 1, col : col + 1], (8, 128))

    answers = []
    pivots = []
    for k in range(BASIS):
        start = spread_at(high, 0, START[k])
        piv = (spread_at(mat_h, k, k), spread_at(mat_l, k, k))
        good = jnp.abs(piv[0]) > 1e-12 * jnp.abs(start)
        safe = (jnp.where(good, piv[0], 1.0), jnp.where(good, piv[1], 0.0))
        pivots.append((safe, good))
        row = (
            jnp.broadcast_to(mat_h[k : k + 1, :], (8, 128)),
            jnp.broadcast_to(mat_l[k : k + 1, :], (8, 128)),
        )
        col = (
            jnp.broadcast_to(mat_h[:, k : k + 1], (8, 128)),
            jnp.broadcast_to(mat_l[:, k : k + 1], (8, 128)),
        )
        factor = pair_div(col, safe)
        use = good & (sub != k)
        factor = (jnp.where(use, factor[0], 0.0), jnp.where(use, factor[1], 0.0))
        mat_h, mat_l = pair_sub((mat_h, mat_l), pair_mul(factor, row))
    for k in range(BASIS):
        safe, good = pivots[k]
        value = pair_div((spread_at(mat_h, k, BASIS), spread_at(mat_l, k, BASIS)), safe)[0]
        answers.append(jnp.where(good, value, 0.0))
    weights = [jnp.concatenate([a, a], axis=0) for a in answers]
    lane16 = lanes((16, 128))
    for m in range(8):
        total = jnp.zeros((16, 128), F32)
        if 1 <= m <= 6:
            at = slice(128 * (m - 1), 128 * m)
            for j in range(BASIS):
                total = total + weights[j] * basis[j, :, at]
        for i in range(8):
            u[i, :, 128 * m : 128 * m + 128] = total
    mid_setup(pos, scal, cfm, sel, faces, inv, None)
    ends = jnp.zeros((16, 128), F32)
    for i in range(8):
        for ref in (r, sol):
            ref[i, :, 0:128] = ends
            ref[i, :, 896:1024] = ends
        r[i, :, 128:896] = level[1, i]
        sol[i, :, 128:896] = level[0, i] + u[i, :, 128:896]
    mid_apply(u, r, scal, cfm, faces, jump, flux)
    for i in range(8):
        new = inv[i] * r[i] / MIDDLE
        u[i] = new
        sol[i] = sol[i] + new
    mid_apply(u, r, scal, cfm, faces, jump, flux)
    mid_step(0, u, r, sol, inv)
    mid_apply(u, r, scal, cfm, faces, jump, flux)
    mid_step(1, u, r, sol, inv)
    for i in range(8):
        for half in range(2):
            acc = jnp.zeros((16, 128), F32)
            for n in range(8):
                y = 8 * half + n - 4
                tile, at = (y + 12) // 4, 32 * ((y + 12) % 4) + 8
                acc = jnp.where(
                    lane16 // 16 == n,
                    roll(sol[i, :, 128 * tile : 128 * tile + 128], 16 * n - at),
                    acc,
                )
            out[128 * half + 16 * i : 128 * half + 16 * i + 16, :] = acc


def post_body(
    scal, gram, basis, cfm, level, keep, frz, got_first, got_second, coef, wide, spread,
    lift, diag_w, diag_e, out,
    sel, faces, mid_inv, mid_u, mid_r, mid_sol, jump, flux, mid, w, inv, u, r, sol, px, qx,
):
    pos = position()
    fine_weights(pos, coef, w)
    wide_inside = jnp.concatenate([fine_places(pos)[0]] * (CHUNK // 256), axis=1)
    for c in range(CHUNKS):
        at = slice(CHUNK * c, CHUNK * (c + 1))
        inv[:, at] = fine_inverse(coef, w, diag_w, diag_e, wide_inside, at)
    mid_post(
        pos, scal, gram, basis, cfm, level, mid, sel, faces, mid_inv, mid_u, mid_r,
        mid_sol, jump, flux,
    )
    low = lanes((64, 128)) < 64
    px[:, 0:256] = jnp.zeros((16, 256), F32)
    qx[:, NX * 256 :] = jnp.zeros((16, 256), F32)
    for x in range(NX):
        first, second = slice(256 * x, 256 * x + 128), slice(256 * x + 128, 256 * x + 256)
        turned = roll(frz[x], 64)
        at = 384 + 64 * (x % 8)
        down = from_below(pos, got_first, got_second, slice(at, at + 64))
        over = from_above(pos, got_first, got_second, slice(at, at + 64))
        if x >= 8:
            down = roll(down, 64)
        else:
            over = roll(over, 64)
        r[:, first] = jnp.where(low, down, turned)
        r[:, second] = jnp.where(low, turned, over)
    planes = CHUNK // 256
    for c in range(CHUNKS):
        at = slice(CHUNK * c, CHUNK * (c + 1))
        pieces = [
            mid[pl.ds(128 * half + planes * c + n, 8, stride=16), :]
            for n in range(planes)
            for half in range(2)
        ]
        high, rest = split3(jnp.concatenate(pieces, axis=1))
        stacked = jnp.concatenate([high, rest, high, jnp.zeros((8, CHUNK), F32)], axis=0)
        lifted = mm(lift[...], stacked.astype(BF16))
        u[:, at] = lifted
        sol[:, at] = lifted
    fine_apply(u, r, w, coef, wide, spread, px, qx, None, sol, inv)
    for c in range(CHUNKS):
        at = slice(CHUNK * c, CHUNK * (c + 1))
        new = inv[:, at] * r[:, at] / MIDDLE
        u[:, at] = new
        sol[:, at] = sol[:, at] + new
    fine_apply(u, r, w, coef, wide, spread, px, qx, 0, sol, inv)
    fine_apply(u, r, w, coef, wide, spread, px, qx, 1, sol, inv)
    fine_apply(u, r, w, coef, wide, spread, px, qx, None, sol, inv)
    lane = lanes((64, 128))
    for x in range(NX):
        acc = jnp.zeros((64, 128), F32)
        for part, ref in enumerate((sol, r)):
            for y in range(8):
                half, at = (y + 4) // 8, 16 * ((y + 4) % 8) + 4
                start = 256 * x + 128 * half
                acc = jnp.where(
                    lane // 8 == 8 * part + y,
                    roll(ref[:, start : start + 128], 64 * part + 8 * y - at),
                    acc,
                )
        kept = keep[x % 8] if x < 8 else roll(keep[x % 8], 64)
        out[x] = acc + jnp.where(low, kept, 0.0)


def unpack_body(got, first, second):
    low = lanes((64, 128)) < 64
    for part, out in enumerate((first, second)):
        held = []
        for g in range(8):
            a, b = got[ORDER[g]], got[ORDER[g + 8]]
            if part == 0:
                held.append(jnp.where(low, a, roll(b, 64)))
            else:
                held.append(jnp.where(low, roll(a, 64), b))
        for y, rows in enumerate(exchange(held, 8)):
            out[pl.ds(y, 64, stride=8), :] = rows


def trace_tables():
    high = np.zeros((3, 16, 64), np.float32)
    low = np.zeros((3, 16, 64), np.float32)
    for p in range(4):
        for q in range(4):
            for d in range(3):
                for table, at in ((high, 3), (low, 0)):
                    index = [p, q]
                    index.insert(d, at)
                    table[d, 4 * p + q, 16 * index[0] + 4 * index[1] + index[2]] = 1.0
    return high, low


def mid_traces():
    high = np.zeros((3, 4, 8), np.float32)
    low = np.zeros((3, 4, 8), np.float32)
    for d in range(3):
        for n in range(4):
            high[d, n, HIGHS[d][n]] = 1.0
            low[d, n, LOWS[d][n]] = 1.0
    return high, low


def prolong_tables():
    half = np.float32(0.5)
    one = np.float32(1.0)
    node = np.array([-1.0, -1.0 / math.sqrt(5.0), 1.0 / math.sqrt(5.0), 1.0], np.float32)
    table = np.stack([(one - node) * half, (one + node) * half], axis=1)
    volume = (
        table[:, None, None, :, None, None]
        * table[None, :, None, None, :, None]
        * table[None, None, :, None, None, :]
    ).reshape(64, 8)
    surface = (table[:, None, :, None] * table[None, :, None, :]).reshape(16, 4)
    return volume, surface


def cut(x):
    return lax.reduce_precision(x, 8, 7)


def two_parts(x):
    high = cut(x)
    return high, cut(x - high)


def three_parts(x):
    high = cut(x)
    rest = x - high
    mid = cut(rest)
    return high, mid, cut(rest - mid)


def tables(element, faces):
    volume, surface = prolong_tables()
    elem_mid = jnp.dot(volume.T, jnp.dot(element, volume, precision=HIGHEST), precision=HIGHEST)
    eye = np.eye(16, dtype=np.float32)
    face_mid = jnp.einsum("kij,jb->kib", faces, surface, precision=HIGHEST)
    face_mid = jnp.einsum("ia,kib->kab", surface, face_mid, precision=HIGHEST)
    elem_coarse = jnp.sum(elem_mid)
    face_coarse = jnp.sum(face_mid, axis=(1, 2))
    high, low = trace_tables()
    both = np.concatenate([high, low], axis=0)
    rows = jnp.einsum("kij,djm->dkim", faces, both, precision=HIGHEST).reshape(384, 64)
    wide = jnp.concatenate([element, rows], axis=0)
    wh, wl = two_parts(wide)
    wide = jnp.concatenate([wh, wh, wl], axis=1).astype(BF16)
    spread = np.concatenate([high[1], -low[1], high[2], -low[2]], axis=0).T
    spread = np.concatenate([spread, spread], axis=1)
    face_diag = jnp.sum(faces * eye, axis=2)
    diag = jnp.einsum("dim,ki->mdk", both, face_diag, precision=HIGHEST).reshape(64, 24)
    diag_w = jnp.concatenate(three_parts(diag) + (jnp.zeros((64, 8), F32),), axis=1).astype(BF16)
    diag_e = jnp.sum(element * np.eye(64, dtype=np.float32), axis=1, keepdims=True)
    mh, ml = mid_traces()
    both = np.concatenate([mh, ml], axis=0)
    face_diag = jnp.sum(face_mid * eye[:4, :4], axis=2)
    diag = jnp.einsum("dim,ki->mdk", both, face_diag, precision=HIGHEST).reshape(8, 24)
    mid_diag_w = jnp.concatenate(three_parts(diag) + (jnp.zeros((8, 8), F32),), axis=1).astype(BF16)
    mid_diag_e = jnp.sum(elem_mid * eye[:8, :8], axis=1, keepdims=True)
    vh = volume.astype(BF16).astype(np.float32)
    vl = (volume - vh).astype(BF16).astype(np.float32)
    down = jnp.asarray(np.concatenate([vh.T, vh.T, vl.T], axis=1), BF16)
    lift = jnp.asarray(np.concatenate([vh, vh, vl, np.zeros((64, 8), np.float32)], axis=1), BF16)
    least = 0.1 * elem_coarse
    most = 1.35 * elem_coarse + 9.0 * jnp.max(jnp.abs(face_coarse))
    half = 0.5 * (most - least)
    half = jnp.where(jnp.abs(half) > 0.0, half, 1.0)
    scal = jnp.concatenate(
        [
            elem_mid.reshape(-1),
            face_mid.reshape(-1),
            elem_coarse[None],
            face_coarse,
            (0.5 * (most + least))[None],
            (1.0 / half)[None],
            jnp.zeros((9,), F32),
        ]
    )
    return (
        wide,
        jnp.asarray(spread, BF16),
        diag_w,
        diag_e,
        down,
        mid_diag_w,
        mid_diag_e,
        lift,
        scal,
    )


def local(residual, coefficient, element, faces, kind, flag):
    y_first = [(i, i ^ 1) for i in range(16)]
    y_second = [p for i in range(1, 15, 2) for p in ((i, i + 1), (i + 1, i))]

    def z_index(zb):
        return ORDER[zb % 16] * 2 + zb // 16

    z_up = [(z_index(i), z_index(i + 1)) for i in range(31)]
    z_dn = [(z_index(i + 1), z_index(i)) for i in range(31)]
    z_axes = ("gx", "lvl")
    res = residual.reshape(512, 128)
    slots = call(
        slots_body,
        "slots",
        [f32s(16, 40, 128)],
        (0,) * 4,
        [pltpu.VMEM((128, 128), F32)],
        limit=LARGE_LIMIT,
    )(res, coefficient.reshape(8, 128), kind.reshape(48, 128), flag.reshape(48, 128))[0]
    element, faces, slots = lax.optimization_barrier((element, faces, slots))
    wide, spread, diag_w, diag_e, down, mid_diag_w, mid_diag_e, lift, scal = tables(element, faces)
    interval = jnp.repeat(jnp.broadcast_to(scal[133:135, None], (2, 128)), 8, axis=0)
    parity = jnp.broadcast_to((lax.axis_index("yz") % 2).astype(F32), (8, 128))
    own = lax.all_to_all(slots, "gx", 0, 0, tiled=True)
    own, wide, diag_w, diag_e, mid_diag_w, mid_diag_e, scal, parity, interval = lax.optimization_barrier(
        (own, wide, diag_w, diag_e, mid_diag_w, mid_diag_e, scal, parity, interval)
    )
    dn = lax.ppermute(own[:, 16:40], z_axes, z_up)
    up = lax.ppermute(own[:, 0:24], z_axes, z_dn)
    place_values, place_kinds, pack = place_tables()
    rows, own, other = call(
        join_body,
        "join",
        [f32s(NX, 64, 128), f32s(768, 128), f32s(768, 128)],
        (0,) * 6,
    )(parity, own, dn, up, place_values, place_kinds)
    got_first = lax.ppermute(own, "yz", y_first)
    got_second = lax.ppermute(other, "yz", y_second)
    plane = (64, NX * 256)
    strip = (16, NX * 256 + 256)
    keep, r, coef, cfm, send_up, send_down = call(
        fine_pre_body,
        "fine_pre",
        [
            f32s(8, 64, 128),
            f32s(*plane),
            f32s(8, NX * 256),
            f32s(128, 1024),
            f32s(384, 128),
            f32s(384, 128),
        ],
        (0,) * 12,
        [
            pltpu.VMEM(plane, F32),
            pltpu.VMEM((24, NX * 256), F32),
            pltpu.VMEM(plane, F32),
            pltpu.VMEM(plane, F32),
            pltpu.VMEM(strip, F32),
            pltpu.VMEM(strip, F32),
            pltpu.VMEM((896, 128), F32),
            pltpu.VMEM((256, 128), F32),
        ],
    )(
        rows, own, got_first, got_second, wide, spread, diag_w, diag_e, down, mid_diag_w, mid_diag_e, pack
    )
    dn = lax.ppermute(send_up, z_axes, z_up)
    up = lax.ppermute(send_down, z_axes, z_dn)
    slab, first, second, frz = call(
        mid_z_body,
        "mid_z",
        [f32s(128, 256), f32s(896, 128), f32s(896, 128), f32s(NX, 64, 128)],
        (0,) * 5,
    )(parity, send_up, dn, up, r)
    got_first = lax.ppermute(first, "yz", y_first)
    got_second = lax.ppermute(second, "yz", y_second)
    mid = (8, 16, 1024)
    mid_scratch = [
        pltpu.VMEM((3, 16, 1024), F32),
        pltpu.VMEM((3, 16, 16, 1024), F32),
        pltpu.VMEM(mid, F32),
    ]
    tail_scratch = [pltpu.VMEM((4, 16, 1024), F32), pltpu.VMEM((12, 16, 1024), F32)]
    level, coarse, send_up, send_down = call(
        mid_pre_body,
        "mid_pre",
        [f32s(2, 8, 16, 768), f32s(5, 16, 1024), f32s(2, 16, 768), f32s(2, 16, 768)],
        (1, 0, 0, 0, 0),
        mid_scratch
        + [pltpu.VMEM(mid, F32)] * 4
        + tail_scratch,
    )(scal, slab, got_first, got_second, cfm)
    dn = lax.ppermute(send_up, z_axes, z_up)
    up = lax.ppermute(send_down, z_axes, z_dn)
    coarse_slab, first, second = call(
        coarse_z_body,
        "coarse_z",
        [f32s(5, 16, 1280), f32s(5, 16, 512), f32s(5, 16, 512)],
        (0,) * 4,
    )(parity, coarse, dn, up)
    coarse_first = lax.ppermute(first, "yz", y_first)
    coarse_second = lax.ppermute(second, "yz", y_second)
    basis, gram = call(
        krylov_body,
        "krylov",
        [f32s(BASIS, 16, 768), f32s(16, 128)],
        (0, 0, 0, 0),
        [
            pltpu.VMEM((5, 16, 2304), F32),
            pltpu.VMEM((2 * BASIS, 8, 128), F32),
        ],
    )(interval, coarse_slab, coarse_first, coarse_second)
    gram = lax.all_to_all(gram, "yz", 0, 0, tiled=True)
    gram = call(gram_body, "gram", [f32s(32, 128)], (0,))(gram)[0]
    gram = lax.all_to_all(gram, z_axes, 0, 0, tiled=True)
    packed = call(
        post_body,
        "post",
        [f32s(16, 64, 128)],
        (1,) + (0,) * 14,
        mid_scratch
        + [pltpu.VMEM(mid, F32)] * 3
        + tail_scratch
        + [
            pltpu.VMEM((256, 128), F32),
            pltpu.VMEM((24, NX * 256), F32),
            pltpu.VMEM(plane, F32),
            pltpu.VMEM(plane, F32),
            pltpu.VMEM(plane, F32),
            pltpu.VMEM(plane, F32),
            pltpu.VMEM(strip, F32),
            pltpu.VMEM(strip, F32),
        ],
        limit=LARGE_LIMIT,
    )(
        scal, gram, basis, cfm, level, keep, frz, got_first, got_second, coef, wide, spread,
        lift, diag_w, diag_e,
    )[0]
    got = lax.all_to_all(packed, "gx", 0, 0, tiled=True)
    correction, rest = call(unpack_body, "unpack", [f32s(512, 128), f32s(512, 128)], (0,))(got)
    return (correction.reshape(64, 1, 8, 128), rest.reshape(64, 1, 8, 128))


def solution(mesh):
    in_specs = (
        P(None, "gx", "yz", "lvl"),
        P("gx", "yz", "lvl"),
        P(),
        P(),
        P(None, "gx", "yz", "lvl"),
        P(None, "gx", "yz", "lvl"),
    )
    out_specs = (P(None, "gx", "yz", "lvl"), P(None, "gx", "yz", "lvl"))
    return jax.shard_map(local, mesh=mesh, in_specs=in_specs, out_specs=out_specs, check_vma=False)
```
